32 devices in a mesh: fs: 8 (over y, x, core), tp: 4 (over z).
Axes of the slice: x: 2, y: 2, z: 4, core: 2. Of those that a mesh axis runs over, the one named last changes fastest.
Arguments:
- tokens: bfloat16 [2048, 2048], P('fs'), may hold values from -6 to 6
- cotangent: bfloat16 [2048, 2048], P('fs'), may hold values from -6 to 6
- qkv_weight: bfloat16 [3, 2048, 2048], P(None, 'fs', 'tp'), may hold values from -0.125 to 0.125
- out_weight: bfloat16 [2048, 2048], P('tp', 'fs'), may hold values from -1.5 to 1.5
- norm_gains: bfloat16 [2, 2048], P(None, 'fs'), may hold values from 0.5 to 1.5
- router_weight: bfloat16 [8, 2048], P(None, 'fs'), may hold values from -0.0625 to 0.0625
- shared_gate: bfloat16 [2048], P('fs'), may hold values from -0.125 to 0.125
- expert_gate_up: bfloat16 [8, 2048, 2, 1408], P(None, 'fs', None, 'tp'), may hold values from -0.125 to 0.125
- expert_down: bfloat16 [8, 1408, 2048], P(None, 'tp', 'fs'), may hold values from -0.625 to 0.625
- shared_gate_up: bfloat16 [2048, 2, 5632], P('fs', None, 'tp'), may hold values from -0.125 to 0.125
- shared_down: bfloat16 [5632, 2048], P('tp', 'fs'), may hold values from -0.15625 to 0.15625
- routes: int32 [2048, 4], P('fs'), may hold values from 0 to 7, all different within a row
- doc_start: int32 [2048], P('fs'), may hold values from 0 to 1023, as said below
Outputs:
- output: bfloat16 [2048, 2048], P('fs', 'tp')
- input_grad: float32 [2048, 2048], P('fs')
- grad_qkv_weight: float32 [3, 2048, 2048], P(None, 'fs', 'tp')
- grad_out_weight: float32 [2048, 2048], P('tp', 'fs')
- grad_norm_gains: float32 [2, 2048], P(None, 'fs')
- grad_router_weight: float32 [8, 2048], P(None, 'fs')
- grad_shared_gate: float32 [2048], P('fs')
- grad_expert_gate_up: float32 [8, 2048, 2, 1408], P(None, 'fs', None, 'tp')
- grad_expert_down: float32 [8, 1408, 2048], P(None, 'tp', 'fs')
- grad_shared_gate_up: float32 [2048, 2, 5632], P('fs', None, 'tp')
- grad_shared_down: float32 [5632, 2048], P('tp', 'fs')
The draws below stay inside these ranges and needn't reach their ends.
Inputs may be any that keep to these rules, and one draw needn't show every extreme that they name: `routes`: each token names 4 different experts; every expert is named by some token. `doc_start`: every sequence holds three documents; the second begins within the first 128 positions and ends within the last 128.
All inputs are finite; a program needn't handle non-finite values.
Results may differ from the reference program's by a relative error of at most 0.029.
Values may be sent and summed in bfloat16 or wider, within the bound.
A program may use at most 320 MiB of HBM per device.

```python
import jax
import jax.numpy as jnp
from jax import lax

D = 2048
HD = 128
FFE = 1408
FFS = 5632
E = 8
TOP = 4
SEQ_DEV = 128
SEQS = 2
LEN = 1024
TOK_DEV = 256
TOKENS = 2048
N_FS = 8


def draw_doc_start(key, part):
    key = jax.random.fold_in(key, 7)
    first_key, second_key = jax.random.split(key)
    first_cut = jax.random.randint(first_key, (SEQS,), 1, SEQ_DEV)
    second_cut = jax.random.randint(second_key, (SEQS,), LEN - SEQ_DEV + 1, LEN)
    row_index = jnp.arange(TOKENS)
    sequence = row_index % TOK_DEV // SEQ_DEV
    position = row_index // TOK_DEV * SEQ_DEV + row_index % SEQ_DEV
    lower = first_cut[sequence]
    upper = second_cut[sequence]
    return jnp.where(position >= upper, upper, jnp.where(position >= lower, lower, 0)).astype(jnp.int32)


def block_levels(key, dims, cuts, smallest, high):
    def one(dim, blocks):
        heights = jax.random.uniform(jax.random.fold_in(jax.random.fold_in(key, 6), dim), (blocks,), jnp.float32, smallest / len(cuts), high / len(cuts))
        return jnp.repeat(jnp.exp(heights), dims[dim] // blocks).reshape((-1,) + (1,) * (len(dims) - dim - 1))

    loudness = one(*cuts[0])
    for cut in cuts[1:]:
        loudness = loudness * one(*cut)
    return loudness


def different_ones(stream_key, rows, number_of, top, lift):
    order = jax.random.permutation(jax.random.fold_in(stream_key, 1), number_of)
    boost = order
    for power in range(3):
        boost = boost * boost // number_of
    boost = boost * lift // number_of
    chance = jax.random.randint(jax.random.fold_in(stream_key, 2), (rows, number_of), 0, 4096) + boost
    holders = jax.random.permutation(jax.random.fold_in(stream_key, 3), rows)[jnp.arange(number_of) % rows]
    chance = jnp.where(jnp.arange(rows)[:, None] == holders[None, :], 1 << 14, chance)
    score = chance * number_of + jnp.arange(number_of)
    return lax.top_k(score.astype(jnp.int32), top)[1].astype(jnp.int32)


def scatter_about(key, shape, width, bound, shards=(), kind=jnp.bfloat16):
    entries = width * jax.random.normal(key, shape, jnp.float32)
    if shards:
        entries = entries * block_levels(key, shape, shards, -0.22, 0.18)
    return jnp.clip(entries, -bound, bound).astype(kind)


def setup_inputs(seed: int = 0) -> dict:
    splits = jax.random.split(jax.random.key(seed), 14)
    tokens = scatter_about(splits[0], (TOKENS, D), 1.0, 6.0, ((0, 8),))
    cotangent = scatter_about(splits[1], (TOKENS, D), 1.0, 6.0, ((0, 8),))
    qkv_weight = scatter_about(splits[2], (3, D, D), D ** -0.5, 0.125, ((1, 8), (2, 4)))
    out_weight = scatter_about(splits[3], (D, D), (max(D // 128, 1)) ** -0.5, 1.5, ((0, 4), (1, 8)))
    norm_gains = jnp.clip(1.0 + 0.1 * jax.random.normal(splits[4], (2, D), jnp.float32), 0.5, 1.5).astype(jnp.bfloat16)
    router_weight = scatter_about(splits[5], (E, D), (4 * D) ** -0.5, 0.0625, ((1, 8),))
    shared_gate = scatter_about(splits[6], (D,), D ** -0.5, 0.125, ((0, 8),))
    expert_gate_up = scatter_about(splits[7], (E, D, 2, FFE), D ** -0.5, 0.125, ((1, 8), (3, 4)))
    expert_down = scatter_about(splits[8], (E, FFE, D), (max(FFE // 16, 1)) ** -0.5, 0.625, ((1, 4), (2, 8)))
    shared_gate_up = scatter_about(splits[9], (D, 2, FFS), D ** -0.5, 0.125, ((0, 8), (2, 4)))
    shared_down = scatter_about(splits[10], (FFS, D), (max(FFS // 4, 1)) ** -0.5, 0.15625, ((0, 4), (1, 8)))
    routes = different_ones(splits[11], TOKENS, E, TOP, 4096)
    doc_start = draw_doc_start(jax.random.fold_in(splits[13], 71), 0)
    return dict(tokens=tokens, cotangent=cotangent, qkv_weight=qkv_weight, out_weight=out_weight, norm_gains=norm_gains, router_weight=router_weight, shared_gate=shared_gate, expert_gate_up=expert_gate_up, expert_down=expert_down, shared_gate_up=shared_gate_up, shared_down=shared_down, routes=routes, doc_start=doc_start)


NORM_EPS = 1e-06
NEG_FILL = -1e+30
ROPE_BASE = 1000000.0
HIGHEST = lax.Precision.HIGHEST

@jax.custom_vjp
def low(v):
    return lax.optimization_barrier(v.astype(jnp.bfloat16)).astype(jnp.float32)

@jax.custom_vjp
def low_back(v):
    return v

def low_keep(v):
    return (low(v), None)

def low_pass(kept, grad):
    return (grad,)

def back_keep(v):
    return (v, None)

def back_low(kept, grad):
    return (low(grad),)
low.defvjp(low_keep, low_pass)
low_back.defvjp(back_keep, back_low)

def both_round(values):
    return low(low_back(values))

def rms_norm(values):
    return values * lax.rsqrt(lax.optimization_barrier(jnp.mean(values * values, axis=1, keepdims=True)) + NORM_EPS)

def rope_tables(positions):
    half_size = HD // 2
    frequency = ROPE_BASE ** (-(jnp.arange(half_size, dtype=jnp.float32) * 2.0 / HD))
    angles = positions.astype(jnp.float32)[:, None] * frequency[None, :]
    return (jnp.cos(angles), jnp.sin(angles))

def rotate(values, cosine, sine_table):
    shaped = values.reshape(values.shape[0], -1, HD)
    half_size = HD // 2
    first_half = shaped[..., :half_size]
    second_half = shaped[..., half_size:]
    cos_part = cosine[:, None, :]
    sin_part = sine_table[:, None, :]
    turned = jnp.concatenate([first_half * cos_part - second_half * sin_part, second_half * cos_part + first_half * sin_part], axis=-1)
    return turned.reshape(values.shape)

def to_sequences(values):
    width_in = values.shape[-1]
    return values.reshape(N_FS, SEQS, SEQ_DEV, width_in).transpose(1, 0, 2, 3).reshape(SEQS, LEN, width_in)

def from_sequences(values):
    width_in = values.shape[-1]
    return values.reshape(SEQS, N_FS, SEQ_DEV, width_in).transpose(1, 0, 2, 3).reshape(TOKENS, width_in)

def attend_sequence(query_seq, key_seq, value_seq, start_seq):
    block_size = min(512, LEN)
    block_count = LEN // block_size
    key_positions = jnp.arange(LEN)

    def one_block(inputs):
        query_block, start_block, offset = inputs
        query_positions = offset + jnp.arange(block_size)
        scores = jnp.einsum('qhd,khd->hqk', query_block, key_seq, precision=HIGHEST) * HD ** (-0.5)
        scores = low_back(scores)
        allowed = (key_positions[None, :] <= query_positions[:, None]) & (key_positions[None, :] >= start_block[:, None])
        scores = jnp.where(allowed[None], scores, NEG_FILL)
        weights = low(jax.nn.softmax(scores, axis=-1))
        return jnp.einsum('hqk,khd->qhd', weights, value_seq, precision=HIGHEST)
    return lax.map(jax.checkpoint(one_block), (query_seq.reshape(block_count, block_size, -1, HD), start_seq.reshape(block_count, block_size), jnp.arange(block_count) * block_size))

def forward(tokens, qkv_weight, out_weight, norm_gains, router_weight, shared_gate, expert_gate_up, expert_down, shared_gate_up, shared_down, routes, doc_start):
    row_index = jnp.arange(TOKENS)
    positions = row_index // TOK_DEV * SEQ_DEV + row_index % SEQ_DEV
    cosine, sine_table = rope_tables(positions)
    normed_one = rms_norm(tokens)
    hidden_one = low(normed_one * norm_gains[0][None, :])
    projected = jnp.einsum('td,jdf->jtf', hidden_one, qkv_weight, precision=HIGHEST)
    query_rows = low(rotate(low_back(projected[0]), cosine, sine_table))
    key_rows = low(rotate(low_back(projected[1]), cosine, sine_table))
    value_rows = both_round(projected[2])
    starts = doc_start.reshape(N_FS, SEQS, SEQ_DEV).transpose(1, 0, 2).reshape(SEQS, LEN)
    per_sequence = lax.map(lambda inputs: attend_sequence(*inputs), (to_sequences(query_rows).reshape(SEQS, LEN, -1, HD), to_sequences(key_rows).reshape(SEQS, LEN, -1, HD), to_sequences(value_rows).reshape(SEQS, LEN, -1, HD), starts))
    attended = both_round(from_sequences(per_sequence.reshape(SEQS, LEN, D)))
    branch = low_back(jnp.dot(attended, out_weight, precision=HIGHEST))
    residual = tokens + branch
    hidden_two = low(rms_norm(residual) * norm_gains[1][None, :])

    def mixture(inputs):
        rows_in, route_rows = inputs
        logits = low_back(jnp.einsum('td,ed->te', rows_in, router_weight, precision=HIGHEST))
        router_probs = jax.nn.softmax(logits, axis=-1)
        chosen = lax.optimization_barrier(jnp.sum((route_rows[:, :, None] == jnp.arange(E)[None, None, :]).astype(jnp.float32), axis=1))
        gate_weights = router_probs * chosen
        gate_up = low_back(jnp.einsum('td,edkf->tekf', rows_in, expert_gate_up, precision=HIGHEST))
        active = jax.nn.silu(gate_up[:, :, 0]) * gate_up[:, :, 1]
        hidden = low(gate_weights[:, :, None] * active)
        shared_in = low_back(jnp.einsum('td,dkf->tkf', rows_in, shared_gate_up, precision=HIGHEST))
        shared_active = jax.nn.silu(shared_in[:, 0]) * shared_in[:, 1]
        gate_logit = low_back(jnp.dot(rows_in, shared_gate, precision=HIGHEST))
        shared_hidden = low(jax.nn.sigmoid(gate_logit)[:, None] * shared_active)
        routed_out = jnp.einsum('tef,efd->td', hidden, expert_down, precision=HIGHEST)
        return routed_out + jnp.dot(shared_hidden, shared_down, precision=HIGHEST)
    block_rows = min(2048, TOKENS)
    mixed_rows = lax.map(jax.checkpoint(mixture), (hidden_two.reshape(TOKENS // block_rows, block_rows, D), routes.reshape(TOKENS // block_rows, block_rows, TOP)))
    return residual + mixed_rows.reshape(TOKENS, D)

def reference(tokens, cotangent, qkv_weight, out_weight, norm_gains, router_weight, shared_gate, expert_gate_up, expert_down, shared_gate_up, shared_down, routes, doc_start):
    floats = (tokens.astype(jnp.float32), qkv_weight.astype(jnp.float32), out_weight.astype(jnp.float32), norm_gains.astype(jnp.float32), router_weight.astype(jnp.float32), shared_gate.astype(jnp.float32), expert_gate_up.astype(jnp.float32), expert_down.astype(jnp.float32), shared_gate_up.astype(jnp.float32), shared_down.astype(jnp.float32))

    def forward_floats(*arrays):
        return forward(*arrays, routes, doc_start)
    result, pullback = jax.vjp(forward_floats, *floats)
    grads = pullback(cotangent.astype(jnp.float32))
    return (result.astype(jnp.bfloat16), grads[0], grads[1], grads[2], grads[3], grads[4], grads[5], grads[6], grads[7], grads[8], grads[9])
```

```python
import math

import jax
import jax.numpy as jnp
from jax import lax
from jax.sharding import PartitionSpec as P

HD = 128
E = 8
SEQ_DEV = 128
SIDE = 128


NORM_EPS = 1e-06
NEG_FILL = -1e30
ROPE_BASE = 1000000.0


def rope_tables(positions):
    half_size = HD // 2
    frequency = ROPE_BASE ** (-(jnp.arange(half_size, dtype=jnp.float32) * 2.0 / HD))
    angles = positions.astype(jnp.float32)[:, None] * frequency[None, :]
    return (jnp.cos(angles), jnp.sin(angles))


def rotate(values, cosine, sine_table):
    shaped = values.reshape(values.shape[0], -1, HD)
    half_size = HD // 2
    first_half = shaped[..., :half_size]
    second_half = shaped[..., half_size:]
    cos_part = cosine[:, None, :]
    sin_part = sine_table[:, None, :]
    turned = jnp.concatenate(
        [
            first_half * cos_part - second_half * sin_part,
            second_half * cos_part + first_half * sin_part,
        ],
        axis=-1,
    )
    return turned.reshape(values.shape)


def key_mask(query_pos, query_start, first_dev, group_size):
    key_pos = (first_dev + jnp.arange(group_size, dtype=jnp.int32)[:, None]) * SEQ_DEV + jnp.arange(
        SEQ_DEV, dtype=jnp.int32
    )[None, :]
    key_pos = key_pos[None, None, :, :]
    return (key_pos <= query_pos[None, :, None, None]) & (key_pos >= query_start[:, :, None, None])


def shards_gathered(
    tokens,
    cotangent,
    qkv_weight,
    out_weight,
    norm_gains,
    router_weight,
    shared_gate,
    expert_gate_up,
    expert_down,
    shared_gate_up,
    shared_down,
    routes,
    doc_start,
):
    tok_rows = tokens.shape[0]
    seq_count = tok_rows // SEQ_DEV
    local_width = qkv_weight.shape[2]
    head_count = local_width // HD
    out_width = tokens.shape[1] // lax.axis_size("tp")
    score_scale = HD ** (-0.5)
    fs_index = lax.axis_index("fs")
    tp_index = lax.axis_index("tp")
    query_pos = fs_index * SEQ_DEV + jnp.arange(SEQ_DEV, dtype=jnp.int32)
    positions = jnp.tile(query_pos, seq_count)
    query_start = doc_start.reshape(seq_count, SEQ_DEV)
    cosine, sine_table = rope_tables(positions)
    group_limit = max(1, 512 // SEQ_DEV)
    qkv_full, out_full, gains_full, router_full, shared_gate_full = (
        lax.all_gather(qkv_weight, "fs", axis=1, tiled=True),
        lax.all_gather(out_weight, "fs", axis=1, tiled=True),
        lax.all_gather(norm_gains, "fs", axis=1, tiled=True),
        lax.all_gather(router_weight, "fs", axis=1, tiled=True),
        lax.all_gather(shared_gate, "fs", axis=0, tiled=True),
    )
    token_float = tokens.astype(jnp.float32)
    rstd_one = lax.rsqrt(jnp.mean(token_float * token_float, axis=1, keepdims=True) + NORM_EPS)
    normed_one = token_float * rstd_one
    hidden_one = (normed_one * gains_full[0].astype(jnp.float32)[None, :]).astype(jnp.bfloat16)
    projected = jnp.einsum("td,jdf->jtf", hidden_one, qkv_full, preferred_element_type=jnp.float32)
    query_rows = rotate(projected[0], cosine, sine_table).astype(jnp.bfloat16)
    key_own = rotate(projected[1], cosine, sine_table).astype(jnp.bfloat16)
    value_own = projected[2].astype(jnp.bfloat16)
    query_heads = query_rows.reshape(seq_count, SEQ_DEV, head_count, HD)

    def score_block(key_group, first_dev):
        allowed = key_mask(query_pos, query_start, first_dev, key_group.shape[0])[:, None]
        scores = (
            jnp.einsum(
                "pqhd,gpkhd->phqgk", query_heads, key_group, preferred_element_type=jnp.float32
            )
            * score_scale
        )
        return (jnp.where(allowed, scores, NEG_FILL), allowed)

    def forward_update(running, key_group, value_group, first_dev):
        run_max, run_sum, accumulated = running
        scores, allowed = score_block(key_group, first_dev)
        new_max = jnp.maximum(run_max, jnp.max(scores, axis=(3, 4)))
        weights = jnp.where(allowed, jnp.exp(scores - new_max[..., None, None]), 0.0)
        factor = jnp.exp(run_max - new_max)
        new_sum = run_sum * factor + jnp.sum(weights, axis=(3, 4))
        mixed_part = jnp.einsum(
            "phqgk,gpkhd->pqhd",
            weights.astype(jnp.bfloat16),
            value_group,
            preferred_element_type=jnp.float32,
        )
        new_accum = accumulated * jnp.transpose(factor, (0, 2, 1))[..., None] + mixed_part
        return (new_max, new_sum, new_accum)

    initial = (
        jnp.full((seq_count, head_count, SEQ_DEV), NEG_FILL, jnp.float32),
        jnp.zeros((seq_count, head_count, SEQ_DEV), jnp.float32),
        jnp.zeros((seq_count, SEQ_DEV, head_count, HD), jnp.float32),
    )
    running = initial
    key_piece = lax.all_gather(key_own, "fs", axis=0, tiled=True)
    value_piece = lax.all_gather(value_own, "fs", axis=0, tiled=True)
    shard_count = key_piece.shape[0] // tok_rows
    group_size = math.gcd(shard_count, group_limit)
    step_count = shard_count // group_size
    shaped = (step_count, group_size, seq_count, SEQ_DEV, head_count, HD)
    first_dev = jnp.int32(0) // tok_rows

    def one_step(carried, inputs):
        key_group, value_group, group_index = inputs
        start_dev = group_index * group_size
        updated = lax.cond(
            start_dev <= fs_index,
            lambda state_in: forward_update(state_in, key_group, value_group, start_dev),
            lambda state_in: state_in,
            carried,
        )
        return (updated, None)

    running, ignored = lax.scan(
        one_step,
        running,
        (
            key_piece.reshape(shaped),
            value_piece.reshape(shaped),
            jnp.arange(step_count, dtype=jnp.int32),
        ),
    )
    run_max, run_sum, accumulated = running
    attended_heads = (accumulated / jnp.transpose(run_sum, (0, 2, 1))[..., None]).astype(
        jnp.bfloat16
    )
    log_total = run_max + jnp.log(run_sum)
    attended = attended_heads.reshape(tok_rows, local_width)
    branch_part = jnp.dot(attended, out_full, preferred_element_type=jnp.float32)
    branch = lax.psum(branch_part.astype(jnp.bfloat16), "tp").astype(jnp.float32)
    residual = token_float + branch
    rstd_two = lax.rsqrt(jnp.mean(residual * residual, axis=1, keepdims=True) + NORM_EPS)
    normed_two = residual * rstd_two
    hidden_two = (normed_two * gains_full[1].astype(jnp.float32)[None, :]).astype(jnp.bfloat16)
    expert_gate_all, expert_down_all, shared_up_all, shared_down_all = (
        lax.all_gather(expert_gate_up, "fs", axis=1, tiled=True),
        lax.all_gather(expert_down, "fs", axis=2, tiled=True),
        lax.all_gather(shared_gate_up, "fs", axis=0, tiled=True),
        lax.all_gather(shared_down, "fs", axis=1, tiled=True),
    )
    logits = jnp.einsum("td,ed->te", hidden_two, router_full, preferred_element_type=jnp.float32)
    router_probs = jax.nn.softmax(logits, axis=-1)
    chosen = jnp.sum(
        (routes[:, :, None] == jnp.arange(E, dtype=jnp.int32)[None, None, :]).astype(jnp.float32),
        axis=1,
    )
    gate_weights = router_probs * chosen
    gate_up = jnp.einsum(
        "td,edkf->tekf", hidden_two, expert_gate_all, preferred_element_type=jnp.float32
    )
    gate_part = gate_up[:, :, 0]
    up_part = gate_up[:, :, 1]
    gate_sigmoid = jax.nn.sigmoid(gate_part)
    active = gate_part * gate_sigmoid * up_part
    hidden = (gate_weights[:, :, None] * active).astype(jnp.bfloat16)
    shared_in = jnp.einsum(
        "td,dkf->tkf", hidden_two, shared_up_all, preferred_element_type=jnp.float32
    )
    shared_gate_in = shared_in[:, 0]
    shared_up_in = shared_in[:, 1]
    shared_sigmoid = jax.nn.sigmoid(shared_gate_in)
    shared_active = shared_gate_in * shared_sigmoid * shared_up_in
    gate_logit = jnp.einsum(
        "td,d->t", hidden_two, shared_gate_full, preferred_element_type=jnp.float32
    )
    gate_value = jax.nn.sigmoid(gate_logit)
    shared_hidden = (gate_value[:, None] * shared_active).astype(jnp.bfloat16)
    mixture_part = jnp.einsum(
        "tef,efd->td", hidden, expert_down_all, preferred_element_type=jnp.float32
    ) + jnp.dot(shared_hidden, shared_down_all, preferred_element_type=jnp.float32)
    mixture = lax.psum_scatter(
        mixture_part.astype(jnp.bfloat16), "tp", scatter_dimension=1, tiled=True
    ).astype(jnp.float32)
    output = (
        lax.dynamic_slice_in_dim(residual, tp_index * out_width, out_width, 1) + mixture
    ).astype(jnp.bfloat16)
    qkv_back, out_back, gains_back, router_back, shared_gate_back = (
        lax.all_gather(qkv_weight, "fs", axis=1, tiled=True),
        lax.all_gather(out_weight, "fs", axis=1, tiled=True),
        lax.all_gather(norm_gains, "fs", axis=1, tiled=True),
        lax.all_gather(router_weight, "fs", axis=1, tiled=True),
        lax.all_gather(shared_gate, "fs", axis=0, tiled=True),
    )
    expert_gate_back, expert_down_back, shared_up_back, shared_down_back = (
        lax.all_gather(expert_gate_up, "fs", axis=1, tiled=True),
        lax.all_gather(expert_down, "fs", axis=2, tiled=True),
        lax.all_gather(shared_gate_up, "fs", axis=0, tiled=True),
        lax.all_gather(shared_down, "fs", axis=1, tiled=True),
    )
    hidden_grad = jnp.einsum(
        "td,efd->tef", cotangent, expert_down_back, preferred_element_type=jnp.float32
    )
    expert_down_grad = jnp.einsum(
        "tef,td->efd", hidden, cotangent, preferred_element_type=jnp.float32
    )
    shared_grad = jnp.einsum(
        "td,fd->tf", cotangent, shared_down_back, preferred_element_type=jnp.float32
    )
    shared_down_grad = jnp.einsum(
        "tf,td->fd", shared_hidden, cotangent, preferred_element_type=jnp.float32
    )
    gate_dot = jnp.sum(active * hidden_grad, axis=2)
    shared_dot = jnp.sum(shared_active * shared_grad, axis=1)
    active_grad = gate_weights[:, :, None] * hidden_grad
    gate_grad = active_grad * up_part * gate_sigmoid * (1.0 + gate_part * (1.0 - gate_sigmoid))
    up_grad = active_grad * gate_part * gate_sigmoid
    gate_up_grad = jnp.stack([gate_grad, up_grad], axis=2).astype(jnp.bfloat16)
    shared_active_grad = gate_value[:, None] * shared_grad
    shared_gate_grad = (
        shared_active_grad
        * shared_up_in
        * shared_sigmoid
        * (1.0 + shared_gate_in * (1.0 - shared_sigmoid))
    )
    shared_unit_grad = shared_active_grad * shared_gate_in * shared_sigmoid
    shared_up_grad = jnp.stack([shared_gate_grad, shared_unit_grad], axis=1).astype(jnp.bfloat16)
    expert_gate_grad = jnp.einsum(
        "td,tekf->edkf", hidden_two, gate_up_grad, preferred_element_type=jnp.float32
    )
    shared_proj_grad = jnp.einsum(
        "td,tkf->dkf", hidden_two, shared_up_grad, preferred_element_type=jnp.float32
    )
    input_part = jnp.einsum(
        "tekf,edkf->td", gate_up_grad, expert_gate_back, preferred_element_type=jnp.float32
    ) + jnp.einsum(
        "tkf,dkf->td", shared_up_grad, shared_up_back, preferred_element_type=jnp.float32
    )
    input_sum, gate_sum, shared_sum = (
        lax.psum(input_part.astype(jnp.bfloat16), "tp").astype(jnp.float32),
        lax.psum(gate_dot.astype(jnp.bfloat16), "tp").astype(jnp.float32),
        lax.psum(shared_dot.astype(jnp.bfloat16), "tp").astype(jnp.float32),
    )
    chosen_grad = chosen * gate_sum
    logit_grad = (
        router_probs * (chosen_grad - jnp.sum(router_probs * chosen_grad, axis=1, keepdims=True))
    ).astype(jnp.bfloat16)
    gate_logit_grad = (shared_sum * gate_value * (1.0 - gate_value)).astype(jnp.bfloat16)
    router_grad = jnp.einsum(
        "te,td->ed", logit_grad, hidden_two, preferred_element_type=jnp.float32
    )
    shared_vector_grad = jnp.einsum(
        "t,td->d", gate_logit_grad, hidden_two, preferred_element_type=jnp.float32
    )
    two_grad = (
        input_sum
        + jnp.einsum("te,ed->td", logit_grad, router_back, preferred_element_type=jnp.float32)
        + gate_logit_grad.astype(jnp.float32)[:, None]
        * shared_gate_back.astype(jnp.float32)[None, :]
    )
    scaled_two = two_grad * gains_back[1].astype(jnp.float32)[None, :]
    gain_two_grad = jnp.sum(two_grad * normed_two, axis=0)
    residual_grad = cotangent.astype(jnp.float32) + rstd_two * (
        scaled_two - normed_two * jnp.mean(scaled_two * normed_two, axis=1, keepdims=True)
    )
    branch_grad = residual_grad.astype(jnp.bfloat16)
    out_grad = jnp.einsum("tf,td->fd", attended, branch_grad, preferred_element_type=jnp.float32)
    attended_grad = jnp.einsum(
        "td,fd->tf", branch_grad, out_back, preferred_element_type=jnp.float32
    ).astype(jnp.bfloat16)
    grad_heads = attended_grad.reshape(seq_count, SEQ_DEV, head_count, HD)
    delta_rows = jnp.einsum(
        "pqhd,pqhd->phq", grad_heads, attended_heads, preferred_element_type=jnp.float32
    )
    key_all, value_all = (
        lax.all_gather(key_own, "fs", axis=0, tiled=True),
        lax.all_gather(value_own, "fs", axis=0, tiled=True),
    )
    device_count = key_all.shape[0] // tok_rows
    back_group = math.gcd(device_count, group_limit)
    back_steps = device_count // back_group
    back_shape = (back_steps, back_group, seq_count, SEQ_DEV, head_count, HD)

    def backward_update(key_group, value_group, start_dev):
        scores, allowed = score_block(key_group, start_dev)
        probs_block = jnp.where(allowed, jnp.exp(scores - log_total[..., None, None]), 0.0)
        weights_grad = jnp.einsum(
            "pqhd,gpkhd->phqgk", grad_heads, value_group, preferred_element_type=jnp.float32
        )
        score_grad = (probs_block * (weights_grad - delta_rows[..., None, None])).astype(
            jnp.bfloat16
        )
        query_part = (
            jnp.einsum(
                "phqgk,gpkhd->pqhd", score_grad, key_group, preferred_element_type=jnp.float32
            )
            * score_scale
        )
        key_part = (
            jnp.einsum(
                "phqgk,pqhd->gpkhd", score_grad, query_heads, preferred_element_type=jnp.float32
            )
            * score_scale
        )
        value_part = jnp.einsum(
            "phqgk,pqhd->gpkhd",
            probs_block.astype(jnp.bfloat16),
            grad_heads,
            preferred_element_type=jnp.float32,
        )
        return (query_part, key_part, value_part)

    empty_grads = (
        jnp.zeros((seq_count, SEQ_DEV, head_count, HD), jnp.float32),
        jnp.zeros((back_group, seq_count, SEQ_DEV, head_count, HD), jnp.float32),
        jnp.zeros((back_group, seq_count, SEQ_DEV, head_count, HD), jnp.float32),
    )
    scan_inputs = (
        key_all.reshape(back_shape),
        value_all.reshape(back_shape),
        jnp.arange(back_steps, dtype=jnp.int32),
    )

    def back_step(query_acc, inputs):
        key_group, value_group, group_index = inputs
        start_dev = group_index * back_group
        query_part, key_part, value_part = lax.cond(
            start_dev <= fs_index,
            lambda ignored_in: backward_update(key_group, value_group, start_dev),
            lambda ignored_in: empty_grads,
            key_group,
        )
        term_rows = jnp.concatenate(
            [
                key_part.reshape(back_group * tok_rows, local_width),
                value_part.reshape(back_group * tok_rows, local_width),
            ],
            axis=1,
        )
        return (query_acc + query_part, term_rows)

    query_grad, key_value_terms = lax.scan(back_step, empty_grads[0], scan_inputs)
    key_value_sum = lax.psum_scatter(
        key_value_terms.reshape(device_count * tok_rows, 2 * local_width).astype(jnp.bfloat16),
        "fs",
        scatter_dimension=0,
        tiled=True,
    ).astype(jnp.float32)
    key_grad_rows = key_value_sum[:, :local_width]
    value_grad_rows = key_value_sum[:, local_width:]
    projected_grad = jnp.stack(
        [
            rotate(query_grad.reshape(tok_rows, local_width), cosine, -sine_table),
            rotate(key_grad_rows, cosine, -sine_table),
            value_grad_rows,
        ],
        axis=0,
    ).astype(jnp.bfloat16)
    qkv_grad = jnp.einsum(
        "td,jtf->jdf", hidden_one, projected_grad, preferred_element_type=jnp.float32
    )
    one_part = jnp.einsum(
        "jtf,jdf->td", projected_grad, qkv_back, preferred_element_type=jnp.float32
    )
    one_grad = lax.psum(one_part.astype(jnp.bfloat16), "tp").astype(jnp.float32)
    scaled_one = one_grad * gains_back[0].astype(jnp.float32)[None, :]
    gain_one_grad = jnp.sum(one_grad * normed_one, axis=0)
    input_grad = residual_grad + rstd_one * (
        scaled_one - normed_one * jnp.mean(scaled_one * normed_one, axis=1, keepdims=True)
    )
    gains_grad = jnp.stack([gain_one_grad, gain_two_grad], axis=0)
    reduced = (
        lax.psum_scatter(
            qkv_grad.astype(jnp.bfloat16), "fs", scatter_dimension=1, tiled=True
        ).astype(jnp.float32),
        lax.psum_scatter(
            out_grad.astype(jnp.bfloat16), "fs", scatter_dimension=1, tiled=True
        ).astype(jnp.float32),
        lax.psum_scatter(
            gains_grad.astype(jnp.bfloat16), "fs", scatter_dimension=1, tiled=True
        ).astype(jnp.float32),
        lax.psum_scatter(
            router_grad.astype(jnp.bfloat16), "fs", scatter_dimension=1, tiled=True
        ).astype(jnp.float32),
        lax.psum_scatter(
            shared_vector_grad.astype(jnp.bfloat16), "fs", scatter_dimension=0, tiled=True
        ).astype(jnp.float32),
        lax.psum_scatter(
            expert_gate_grad.astype(jnp.bfloat16), "fs", scatter_dimension=1, tiled=True
        ).astype(jnp.float32),
        lax.psum_scatter(
            expert_down_grad.astype(jnp.bfloat16), "fs", scatter_dimension=2, tiled=True
        ).astype(jnp.float32),
        lax.psum_scatter(
            shared_proj_grad.astype(jnp.bfloat16), "fs", scatter_dimension=0, tiled=True
        ).astype(jnp.float32),
        lax.psum_scatter(
            shared_down_grad.astype(jnp.bfloat16), "fs", scatter_dimension=1, tiled=True
        ).astype(jnp.float32),
    )
    return (
        output,
        input_grad,
        reduced[0],
        reduced[1],
        reduced[2],
        reduced[3],
        reduced[4],
        reduced[5],
        reduced[6],
        reduced[7],
        reduced[8],
    )


def shards_units(
    tokens,
    cotangent,
    qkv_weight,
    out_weight,
    norm_gains,
    router_weight,
    shared_gate,
    expert_gate_up,
    expert_down,
    shared_gate_up,
    shared_down,
    routes,
    doc_start,
):
    tok_rows = tokens.shape[0]
    seq_count = tok_rows // SEQ_DEV
    local_width = qkv_weight.shape[2]
    head_count = local_width // HD
    out_width = tokens.shape[1] // lax.axis_size("tp")
    score_scale = HD ** (-0.5)
    fs_index = lax.axis_index("fs")
    tp_index = lax.axis_index("tp")
    query_pos = fs_index * SEQ_DEV + jnp.arange(SEQ_DEV, dtype=jnp.int32)
    positions = jnp.tile(query_pos, seq_count)
    query_start = doc_start.reshape(seq_count, SEQ_DEV)
    cosine, sine_table = rope_tables(positions)
    group_limit = max(1, 512 // SEQ_DEV)
    fs_size = lax.axis_size("fs")
    width = tokens.shape[1]
    small = jnp.concatenate([norm_gains, router_weight, shared_gate[None]], axis=0)
    small_full = lax.all_gather(small, "fs", axis=1, tiled=True)
    gains_full = small_full[:2]
    router_full = small_full[2 : 2 + E]
    shared_gate_full = small_full[2 + E]
    qkv_full = lax.all_gather(qkv_weight, "fs", axis=1, tiled=True)
    out_full = lax.all_gather(out_weight, "fs", axis=1, tiled=True)
    routed_units = expert_down.shape[1]
    shared_units = shared_down.shape[0] // fs_size
    units = routed_units + shared_units
    block = expert_down.shape[2]
    expert_up_slabs = jnp.transpose(expert_gate_up, (0, 2, 3, 1))
    shared_up_slabs = jnp.transpose(
        shared_gate_up.reshape(block, 2, fs_size, shared_units), (2, 1, 3, 0)
    )
    up_slabs = jnp.concatenate([expert_up_slabs, shared_up_slabs], axis=2)
    down_slabs = jnp.concatenate(
        [expert_down, shared_down.reshape(fs_size, shared_units, block)], axis=1
    )
    slabs = jnp.concatenate([up_slabs, down_slabs[:, None]], axis=1)
    slabs = lax.all_to_all(slabs, "fs", 0, 0, tiled=True)
    cotangent_all = lax.all_gather(cotangent, "fs", axis=0, tiled=True)
    token_float = tokens.astype(jnp.float32)
    rstd_one = lax.rsqrt(jnp.mean(token_float * token_float, axis=1, keepdims=True) + NORM_EPS)
    normed_one = token_float * rstd_one
    hidden_one = (normed_one * gains_full[0].astype(jnp.float32)[None, :]).astype(jnp.bfloat16)
    projected = jnp.einsum("td,jdf->jtf", hidden_one, qkv_full, preferred_element_type=jnp.float32)
    query_rows = rotate(projected[0], cosine, sine_table).astype(jnp.bfloat16)
    key_own = rotate(projected[1], cosine, sine_table).astype(jnp.bfloat16)
    value_own = projected[2].astype(jnp.bfloat16)
    query_heads = query_rows.reshape(seq_count, SEQ_DEV, head_count, HD)

    def score_block(key_group, first_dev):
        allowed = key_mask(query_pos, query_start, first_dev, key_group.shape[0])[:, None]
        scores = (
            jnp.einsum(
                "pqhd,gpkhd->phqgk", query_heads, key_group, preferred_element_type=jnp.float32
            )
            * score_scale
        )
        return (jnp.where(allowed, scores, NEG_FILL), allowed)

    def forward_update(running, key_group, value_group, first_dev):
        run_max, run_sum, accumulated = running
        scores, allowed = score_block(key_group, first_dev)
        new_max = jnp.maximum(run_max, jnp.max(scores, axis=(3, 4)))
        weights = jnp.where(allowed, jnp.exp(scores - new_max[..., None, None]), 0.0)
        factor = jnp.exp(run_max - new_max)
        new_sum = run_sum * factor + jnp.sum(weights, axis=(3, 4))
        mixed_part = jnp.einsum(
            "phqgk,gpkhd->pqhd",
            weights.astype(jnp.bfloat16),
            value_group,
            preferred_element_type=jnp.float32,
        )
        new_accum = accumulated * jnp.transpose(factor, (0, 2, 1))[..., None] + mixed_part
        return (new_max, new_sum, new_accum)

    initial = (
        jnp.full((seq_count, head_count, SEQ_DEV), NEG_FILL, jnp.float32),
        jnp.zeros((seq_count, head_count, SEQ_DEV), jnp.float32),
        jnp.zeros((seq_count, SEQ_DEV, head_count, HD), jnp.float32),
    )
    running = initial
    key_piece = lax.all_gather(key_own, "fs", axis=0, tiled=True)
    value_piece = lax.all_gather(value_own, "fs", axis=0, tiled=True)
    shard_count = key_piece.shape[0] // tok_rows
    group_size = math.gcd(shard_count, group_limit)
    step_count = shard_count // group_size
    shaped = (step_count, group_size, seq_count, SEQ_DEV, head_count, HD)
    first_dev = jnp.int32(0) // tok_rows

    def one_step(carried, inputs):
        key_group, value_group, group_index = inputs
        start_dev = group_index * group_size
        updated = lax.cond(
            start_dev <= fs_index,
            lambda state_in: forward_update(state_in, key_group, value_group, start_dev),
            lambda state_in: state_in,
            carried,
        )
        return (updated, None)

    running, ignored = lax.scan(
        one_step,
        running,
        (
            key_piece.reshape(shaped),
            value_piece.reshape(shaped),
            jnp.arange(step_count, dtype=jnp.int32),
        ),
    )
    run_max, run_sum, accumulated = running
    attended_heads = (accumulated / jnp.transpose(run_sum, (0, 2, 1))[..., None]).astype(
        jnp.bfloat16
    )
    log_total = run_max + jnp.log(run_sum)
    attended = attended_heads.reshape(tok_rows, local_width)
    branch_part = jnp.dot(attended, out_full, preferred_element_type=jnp.float32)
    branch = lax.psum(branch_part.astype(jnp.bfloat16), "tp").astype(jnp.float32)
    residual = token_float + branch
    rstd_two = lax.rsqrt(jnp.mean(residual * residual, axis=1, keepdims=True) + NORM_EPS)
    normed_two = residual * rstd_two
    hidden_two = (normed_two * gains_full[1].astype(jnp.float32)[None, :]).astype(jnp.bfloat16)
    logits = jnp.einsum("td,ed->te", hidden_two, router_full, preferred_element_type=jnp.float32)
    router_probs = jax.nn.softmax(logits, axis=-1)
    chosen = jnp.sum(
        (routes[:, :, None] == jnp.arange(E, dtype=jnp.int32)[None, None, :]).astype(jnp.float32),
        axis=1,
    )
    gate_weights = router_probs * chosen
    gate_logit = jnp.einsum(
        "td,d->t", hidden_two, shared_gate_full, preferred_element_type=jnp.float32
    )
    gate_value = jax.nn.sigmoid(gate_logit)
    scales = jnp.concatenate([gate_weights, gate_value[:, None]], axis=1)
    scales_high = scales.astype(jnp.bfloat16)
    scales_low = (scales - scales_high.astype(jnp.float32)).astype(jnp.bfloat16)
    sent = jnp.concatenate(
        [
            hidden_two,
            scales_high,
            scales_low,
            jnp.zeros((tok_rows, SIDE - 2 * (E + 1)), jnp.bfloat16),
        ],
        axis=1,
    )
    hidden_all = lax.all_gather(sent, "fs", axis=0, tiled=True)
    side_all = hidden_all[:, width : width + 2 * (E + 1)].astype(jnp.float32)
    scales_all = side_all[:, : E + 1] + side_all[:, E + 1 :]
    two_all = hidden_all[:, :width]
    mine = (jnp.arange(E, dtype=jnp.int32) == fs_index).astype(jnp.float32)
    routed_scale = jnp.sum(scales_all[:, :E] * mine[None, :], axis=1, keepdims=True)
    is_routed = jnp.arange(units, dtype=jnp.int32)[None, :] < routed_units
    scale = jnp.where(is_routed, routed_scale, scales_all[:, E:])
    weights_by_unit = jnp.transpose(slabs, (1, 2, 0, 3)).reshape(3, units, width)
    gate_part = jnp.einsum(
        "td,ud->tu", two_all, weights_by_unit[0], preferred_element_type=jnp.float32
    )
    up_part = jnp.einsum(
        "td,ud->tu", two_all, weights_by_unit[1], preferred_element_type=jnp.float32
    )
    hidden_grad = jnp.einsum(
        "td,ud->tu", cotangent_all, weights_by_unit[2], preferred_element_type=jnp.float32
    )
    gate_sigmoid = jax.nn.sigmoid(gate_part)
    silu = gate_part * gate_sigmoid
    active = silu * up_part
    hidden = (scale * active).astype(jnp.bfloat16)
    dots = active * hidden_grad
    routed_dot = jnp.sum(jnp.where(is_routed, dots, 0.0), axis=1, keepdims=True)
    shared_dot = jnp.sum(jnp.where(is_routed, 0.0, dots), axis=1, keepdims=True)
    active_grad = scale * hidden_grad
    gate_grad = (
        active_grad * up_part * gate_sigmoid * (1.0 + gate_part * (1.0 - gate_sigmoid))
    ).astype(jnp.bfloat16)
    up_grad = (active_grad * silu).astype(jnp.bfloat16)
    mixture_part = jnp.einsum(
        "tu,ud->td", hidden, weights_by_unit[2], preferred_element_type=jnp.float32
    )
    mixture_own = lax.psum_scatter(
        mixture_part.astype(jnp.bfloat16), "fs", scatter_dimension=0, tiled=True
    )
    mixture = lax.psum_scatter(
        mixture_own, "tp", scatter_dimension=1, tiled=True
    ).astype(jnp.float32)
    output = (
        lax.dynamic_slice_in_dim(residual, tp_index * out_width, out_width, 1) + mixture
    ).astype(jnp.bfloat16)
    input_part = jnp.einsum(
        "tu,ud->td", gate_grad, weights_by_unit[0], preferred_element_type=jnp.float32
    ) + jnp.einsum(
        "tu,ud->td", up_grad, weights_by_unit[1], preferred_element_type=jnp.float32
    )
    side_part = jnp.concatenate(
        [
            routed_dot * mine[None, :],
            shared_dot,
            jnp.zeros((input_part.shape[0], SIDE - E - 1), jnp.float32),
        ],
        axis=1,
    )
    back_part = jnp.concatenate([input_part, side_part], axis=1).astype(jnp.bfloat16)
    back_own = lax.psum_scatter(back_part, "fs", scatter_dimension=0, tiled=True)
    back_sum = lax.psum(back_own, "tp").astype(jnp.float32)
    input_sum = back_sum[:, :width]
    gate_sum = back_sum[:, width : width + E]
    shared_sum = back_sum[:, width + E]
    grad_by_unit = jnp.stack(
        [
            jnp.einsum("tu,td->ud", gate_grad, two_all, preferred_element_type=jnp.float32),
            jnp.einsum("tu,td->ud", up_grad, two_all, preferred_element_type=jnp.float32),
            jnp.einsum("tu,td->ud", hidden, cotangent_all, preferred_element_type=jnp.float32),
        ],
        axis=0,
    ).astype(jnp.bfloat16)
    grad_slabs = jnp.transpose(grad_by_unit.reshape(3, units, fs_size, block), (2, 0, 1, 3))
    grad_slabs = lax.all_to_all(grad_slabs, "fs", 0, 0, tiled=True)
    chosen_grad = chosen * gate_sum
    logit_grad = (
        router_probs * (chosen_grad - jnp.sum(router_probs * chosen_grad, axis=1, keepdims=True))
    ).astype(jnp.bfloat16)
    gate_logit_grad = (shared_sum * gate_value * (1.0 - gate_value)).astype(jnp.bfloat16)
    router_grad = jnp.einsum(
        "te,td->ed", logit_grad, hidden_two, preferred_element_type=jnp.float32
    )
    shared_vector_grad = jnp.einsum(
        "t,td->d", gate_logit_grad, hidden_two, preferred_element_type=jnp.float32
    )
    two_grad = (
        input_sum
        + jnp.einsum("te,ed->td", logit_grad, router_full, preferred_element_type=jnp.float32)
        + gate_logit_grad.astype(jnp.float32)[:, None]
        * shared_gate_full.astype(jnp.float32)[None, :]
    )
    scaled_two = two_grad * gains_full[1].astype(jnp.float32)[None, :]
    gain_two_grad = jnp.sum(two_grad * normed_two, axis=0)
    residual_grad = cotangent.astype(jnp.float32) + rstd_two * (
        scaled_two - normed_two * jnp.mean(scaled_two * normed_two, axis=1, keepdims=True)
    )
    branch_grad = residual_grad.astype(jnp.bfloat16)
    out_grad = jnp.einsum("tf,td->fd", attended, branch_grad, preferred_element_type=jnp.float32)
    attended_grad = jnp.einsum(
        "td,fd->tf", branch_grad, out_full, preferred_element_type=jnp.float32
    ).astype(jnp.bfloat16)
    grad_heads = attended_grad.reshape(seq_count, SEQ_DEV, head_count, HD)
    delta_rows = jnp.einsum(
        "pqhd,pqhd->phq", grad_heads, attended_heads, preferred_element_type=jnp.float32
    )
    key_all, value_all = key_piece, value_piece
    device_count = key_all.shape[0] // tok_rows
    back_group = math.gcd(device_count, group_limit)
    back_steps = device_count // back_group
    back_shape = (back_steps, back_group, seq_count, SEQ_DEV, head_count, HD)

    def backward_update(key_group, value_group, start_dev):
        scores, allowed = score_block(key_group, start_dev)
        probs_block = jnp.where(allowed, jnp.exp(scores - log_total[..., None, None]), 0.0)
        weights_grad = jnp.einsum(
            "pqhd,gpkhd->phqgk", grad_heads, value_group, preferred_element_type=jnp.float32
        )
        score_grad = (probs_block * (weights_grad - delta_rows[..., None, None])).astype(
            jnp.bfloat16
        )
        query_part = (
            jnp.einsum(
                "phqgk,gpkhd->pqhd", score_grad, key_group, preferred_element_type=jnp.float32
            )
            * score_scale
        )
        key_part = (
            jnp.einsum(
                "phqgk,pqhd->gpkhd", score_grad, query_heads, preferred_element_type=jnp.float32
            )
            * score_scale
        )
        value_part = jnp.einsum(
            "phqgk,pqhd->gpkhd",
            probs_block.astype(jnp.bfloat16),
            grad_heads,
            preferred_element_type=jnp.float32,
        )
        return (query_part, key_part, value_part)

    empty_grads = (
        jnp.zeros((seq_count, SEQ_DEV, head_count, HD), jnp.float32),
        jnp.zeros((back_group, seq_count, SEQ_DEV, head_count, HD), jnp.float32),
        jnp.zeros((back_group, seq_count, SEQ_DEV, head_count, HD), jnp.float32),
    )
    scan_inputs = (
        key_all.reshape(back_shape),
        value_all.reshape(back_shape),
        jnp.arange(back_steps, dtype=jnp.int32),
    )

    def back_step(query_acc, inputs):
        key_group, value_group, group_index = inputs
        start_dev = group_index * back_group
        query_part, key_part, value_part = lax.cond(
            start_dev <= fs_index,
            lambda ignored_in: backward_update(key_group, value_group, start_dev),
            lambda ignored_in: empty_grads,
            key_group,
        )
        term_rows = jnp.concatenate(
            [
                key_part.reshape(back_group * tok_rows, local_width),
                value_part.reshape(back_group * tok_rows, local_width),
            ],
            axis=1,
        )
        return (query_acc + query_part, term_rows)

    query_grad, key_value_terms = lax.scan(back_step, empty_grads[0], scan_inputs)
    key_value_sum = lax.psum_scatter(
        key_value_terms.reshape(device_count * tok_rows, 2 * local_width).astype(jnp.bfloat16),
        "fs",
        scatter_dimension=0,
        tiled=True,
    ).astype(jnp.float32)
    key_grad_rows = key_value_sum[:, :local_width]
    value_grad_rows = key_value_sum[:, local_width:]
    projected_grad = jnp.stack(
        [
            rotate(query_grad.reshape(tok_rows, local_width), cosine, -sine_table),
            rotate(key_grad_rows, cosine, -sine_table),
            value_grad_rows,
        ],
        axis=0,
    ).astype(jnp.bfloat16)
    qkv_grad = jnp.einsum(
        "td,jtf->jdf", hidden_one, projected_grad, preferred_element_type=jnp.float32
    )
    one_part = jnp.einsum(
        "jtf,jdf->td", projected_grad, qkv_full, preferred_element_type=jnp.float32
    )
    one_grad = lax.psum(one_part.astype(jnp.bfloat16), "tp").astype(jnp.float32)
    scaled_one = one_grad * gains_full[0].astype(jnp.float32)[None, :]
    gain_one_grad = jnp.sum(one_grad * normed_one, axis=0)
    input_grad = residual_grad + rstd_one * (
        scaled_one - normed_one * jnp.mean(scaled_one * normed_one, axis=1, keepdims=True)
    )
    gains_grad = jnp.stack([gain_one_grad, gain_two_grad], axis=0)
    small_grad = jnp.concatenate(
        [gains_grad, router_grad, shared_vector_grad[None]], axis=0
    ).astype(jnp.bfloat16)
    small_own = lax.psum_scatter(small_grad, "fs", scatter_dimension=1, tiled=True).astype(
        jnp.float32
    )
    qkv_own = lax.psum_scatter(
        qkv_grad.astype(jnp.bfloat16), "fs", scatter_dimension=1, tiled=True
    ).astype(jnp.float32)
    out_own = lax.psum_scatter(
        out_grad.astype(jnp.bfloat16), "fs", scatter_dimension=1, tiled=True
    ).astype(jnp.float32)
    own = grad_slabs.astype(jnp.float32)
    expert_up_own = jnp.transpose(own[:, :2, :routed_units], (0, 3, 1, 2))
    expert_down_own = own[:, 2, :routed_units]
    shared_up_own = jnp.transpose(own[:, :2, routed_units:], (3, 1, 0, 2)).reshape(
        shared_gate_up.shape
    )
    shared_down_own = own[:, 2, routed_units:].reshape(shared_down.shape)
    return (
        output,
        input_grad,
        qkv_own,
        out_own,
        small_own[:2],
        small_own[2 : 2 + E],
        small_own[2 + E],
        expert_up_own,
        expert_down_own,
        shared_up_own,
        shared_down_own,
    )


def solution(mesh):
    return jax.shard_map(
        shards_units if mesh.shape["fs"] == E else shards_gathered,
        mesh=mesh,
        in_specs=(
            P("fs", None),
            P("fs", None),
            P(None, "fs", "tp"),
            P("tp", "fs"),
            P(None, "fs"),
            P(None, "fs"),
            P("fs"),
            P(None, "fs", None, "tp"),
            P(None, "tp", "fs"),
            P("fs", None, "tp"),
            P("tp", "fs"),
            P("fs", None),
            P("fs"),
        ),
        out_specs=(
            P("fs", "tp"),
            P("fs", None),
            P(None, "fs", "tp"),
            P("tp", "fs"),
            P(None, "fs"),
            P(None, "fs"),
            P("fs"),
            P(None, "fs", None, "tp"),
            P(None, "tp", "fs"),
            P("fs", None, "tp"),
            P("tp", "fs"),
        ),
        check_vma=False,
    )
```

```python
import math

import jax
import jax.numpy as jnp
from jax import lax
from jax.experimental import pallas as pl
from jax.experimental.pallas import tpu as pltpu
from jax.sharding import PartitionSpec as P

HD = 128
E = 8
SEQ_DEV = 128
SIDE = 128


NORM_EPS = 1e-06
NEG_FILL = -1e30
ROPE_BASE = 1000000.0


def rope_tables(positions):
    half_size = HD // 2
    frequency = ROPE_BASE ** (-(jnp.arange(half_size, dtype=jnp.float32) * 2.0 / HD))
    angles = positions.astype(jnp.float32)[:, None] * frequency[None, :]
    return (jnp.cos(angles), jnp.sin(angles))


def rotate(values, cosine, sine_table):
    shaped = values.reshape(values.shape[0], -1, HD)
    half_size = HD // 2
    first_half = shaped[..., :half_size]
    second_half = shaped[..., half_size:]
    cos_part = cosine[:, None, :]
    sin_part = sine_table[:, None, :]
    turned = jnp.concatenate(
        [
            first_half * cos_part - second_half * sin_part,
            second_half * cos_part + first_half * sin_part,
        ],
        axis=-1,
    )
    return turned.reshape(values.shape)


def key_mask(query_pos, query_start, first_dev, group_size):
    key_pos = (first_dev + jnp.arange(group_size, dtype=jnp.int32)[:, None]) * SEQ_DEV + jnp.arange(
        SEQ_DEV, dtype=jnp.int32
    )[None, :]
    key_pos = key_pos[None, None, :, :]
    return (key_pos <= query_pos[None, :, None, None]) & (key_pos >= query_start[:, :, None, None])


def shards_gathered(
    tokens,
    cotangent,
    qkv_weight,
    out_weight,
    norm_gains,
    router_weight,
    shared_gate,
    expert_gate_up,
    expert_down,
    shared_gate_up,
    shared_down,
    routes,
    doc_start,
):
    tok_rows = tokens.shape[0]
    seq_count = tok_rows // SEQ_DEV
    local_width = qkv_weight.shape[2]
    head_count = local_width // HD
    out_width = tokens.shape[1] // lax.axis_size("tp")
    score_scale = HD ** (-0.5)
    fs_index = lax.axis_index("fs")
    tp_index = lax.axis_index("tp")
    query_pos = fs_index * SEQ_DEV + jnp.arange(SEQ_DEV, dtype=jnp.int32)
    positions = jnp.tile(query_pos, seq_count)
    query_start = doc_start.reshape(seq_count, SEQ_DEV)
    cosine, sine_table = rope_tables(positions)
    group_limit = max(1, 512 // SEQ_DEV)
    qkv_full, out_full, gains_full, router_full, shared_gate_full = (
        lax.all_gather(qkv_weight, "fs", axis=1, tiled=True),
        lax.all_gather(out_weight, "fs", axis=1, tiled=True),
        lax.all_gather(norm_gains, "fs", axis=1, tiled=True),
        lax.all_gather(router_weight, "fs", axis=1, tiled=True),
        lax.all_gather(shared_gate, "fs", axis=0, tiled=True),
    )
    token_float = tokens.astype(jnp.float32)
    rstd_one = lax.rsqrt(jnp.mean(token_float * token_float, axis=1, keepdims=True) + NORM_EPS)
    normed_one = token_float * rstd_one
    hidden_one = (normed_one * gains_full[0].astype(jnp.float32)[None, :]).astype(jnp.bfloat16)
    projected = jnp.einsum("td,jdf->jtf", hidden_one, qkv_full, preferred_element_type=jnp.float32)
    query_rows = rotate(projected[0], cosine, sine_table).astype(jnp.bfloat16)
    key_own = rotate(projected[1], cosine, sine_table).astype(jnp.bfloat16)
    value_own = projected[2].astype(jnp.bfloat16)
    query_heads = query_rows.reshape(seq_count, SEQ_DEV, head_count, HD)

    def score_block(key_group, first_dev):
        allowed = key_mask(query_pos, query_start, first_dev, key_group.shape[0])[:, None]
        scores = (
            jnp.einsum(
                "pqhd,gpkhd->phqgk", query_heads, key_group, preferred_element_type=jnp.float32
            )
            * score_scale
        )
        return (jnp.where(allowed, scores, NEG_FILL), allowed)

    def forward_update(running, key_group, value_group, first_dev):
        run_max, run_sum, accumulated = running
        scores, allowed = score_block(key_group, first_dev)
        new_max = jnp.maximum(run_max, jnp.max(scores, axis=(3, 4)))
        weights = jnp.where(allowed, jnp.exp(scores - new_max[..., None, None]), 0.0)
        factor = jnp.exp(run_max - new_max)
        new_sum = run_sum * factor + jnp.sum(weights, axis=(3, 4))
        mixed_part = jnp.einsum(
            "phqgk,gpkhd->pqhd",
            weights.astype(jnp.bfloat16),
            value_group,
            preferred_element_type=jnp.float32,
        )
        new_accum = accumulated * jnp.transpose(factor, (0, 2, 1))[..., None] + mixed_part
        return (new_max, new_sum, new_accum)

    initial = (
        jnp.full((seq_count, head_count, SEQ_DEV), NEG_FILL, jnp.float32),
        jnp.zeros((seq_count, head_count, SEQ_DEV), jnp.float32),
        jnp.zeros((seq_count, SEQ_DEV, head_count, HD), jnp.float32),
    )
    running = initial
    key_piece = lax.all_gather(key_own, "fs", axis=0, tiled=True)
    value_piece = lax.all_gather(value_own, "fs", axis=0, tiled=True)
    shard_count = key_piece.shape[0] // tok_rows
    group_size = math.gcd(shard_count, group_limit)
    step_count = shard_count // group_size
    shaped = (step_count, group_size, seq_count, SEQ_DEV, head_count, HD)
    first_dev = jnp.int32(0) // tok_rows

    def one_step(carried, inputs):
        key_group, value_group, group_index = inputs
        start_dev = group_index * group_size
        updated = lax.cond(
            start_dev <= fs_index,
            lambda state_in: forward_update(state_in, key_group, value_group, start_dev),
            lambda state_in: state_in,
            carried,
        )
        return (updated, None)

    running, ignored = lax.scan(
        one_step,
        running,
        (
            key_piece.reshape(shaped),
            value_piece.reshape(shaped),
            jnp.arange(step_count, dtype=jnp.int32),
        ),
    )
    run_max, run_sum, accumulated = running
    attended_heads = (accumulated / jnp.transpose(run_sum, (0, 2, 1))[..., None]).astype(
        jnp.bfloat16
    )
    log_total = run_max + jnp.log(run_sum)
    attended = attended_heads.reshape(tok_rows, local_width)
    branch_part = jnp.dot(attended, out_full, preferred_element_type=jnp.float32)
    branch = lax.psum(branch_part.astype(jnp.bfloat16), "tp").astype(jnp.float32)
    residual = token_float + branch
    rstd_two = lax.rsqrt(jnp.mean(residual * residual, axis=1, keepdims=True) + NORM_EPS)
    normed_two = residual * rstd_two
    hidden_two = (normed_two * gains_full[1].astype(jnp.float32)[None, :]).astype(jnp.bfloat16)
    expert_gate_all, expert_down_all, shared_up_all, shared_down_all = (
        lax.all_gather(expert_gate_up, "fs", axis=1, tiled=True),
        lax.all_gather(expert_down, "fs", axis=2, tiled=True),
        lax.all_gather(shared_gate_up, "fs", axis=0, tiled=True),
        lax.all_gather(shared_down, "fs", axis=1, tiled=True),
    )
    logits = jnp.einsum("td,ed->te", hidden_two, router_full, preferred_element_type=jnp.float32)
    router_probs = jax.nn.softmax(logits, axis=-1)
    chosen = jnp.sum(
        (routes[:, :, None] == jnp.arange(E, dtype=jnp.int32)[None, None, :]).astype(jnp.float32),
        axis=1,
    )
    gate_weights = router_probs * chosen
    gate_up = jnp.einsum(
        "td,edkf->tekf", hidden_two, expert_gate_all, preferred_element_type=jnp.float32
    )
    gate_part = gate_up[:, :, 0]
    up_part = gate_up[:, :, 1]
    gate_sigmoid = jax.nn.sigmoid(gate_part)
    active = gate_part * gate_sigmoid * up_part
    hidden = (gate_weights[:, :, None] * active).astype(jnp.bfloat16)
    shared_in = jnp.einsum(
        "td,dkf->tkf", hidden_two, shared_up_all, preferred_element_type=jnp.float32
    )
    shared_gate_in = shared_in[:, 0]
    shared_up_in = shared_in[:, 1]
    shared_sigmoid = jax.nn.sigmoid(shared_gate_in)
    shared_active = shared_gate_in * shared_sigmoid * shared_up_in
    gate_logit = jnp.einsum(
        "td,d->t", hidden_two, shared_gate_full, preferred_element_type=jnp.float32
    )
    gate_value = jax.nn.sigmoid(gate_logit)
    shared_hidden = (gate_value[:, None] * shared_active).astype(jnp.bfloat16)
    mixture_part = jnp.einsum(
        "tef,efd->td", hidden, expert_down_all, preferred_element_type=jnp.float32
    ) + jnp.dot(shared_hidden, shared_down_all, preferred_element_type=jnp.float32)
    mixture = lax.psum_scatter(
        mixture_part.astype(jnp.bfloat16), "tp", scatter_dimension=1, tiled=True
    ).astype(jnp.float32)
    output = (
        lax.dynamic_slice_in_dim(residual, tp_index * out_width, out_width, 1) + mixture
    ).astype(jnp.bfloat16)
    qkv_back, out_back, gains_back, router_back, shared_gate_back = (
        lax.all_gather(qkv_weight, "fs", axis=1, tiled=True),
        lax.all_gather(out_weight, "fs", axis=1, tiled=True),
        lax.all_gather(norm_gains, "fs", axis=1, tiled=True),
        lax.all_gather(router_weight, "fs", axis=1, tiled=True),
        lax.all_gather(shared_gate, "fs", axis=0, tiled=True),
    )
    expert_gate_back, expert_down_back, shared_up_back, shared_down_back = (
        lax.all_gather(expert_gate_up, "fs", axis=1, tiled=True),
        lax.all_gather(expert_down, "fs", axis=2, tiled=True),
        lax.all_gather(shared_gate_up, "fs", axis=0, tiled=True),
        lax.all_gather(shared_down, "fs", axis=1, tiled=True),
    )
    hidden_grad = jnp.einsum(
        "td,efd->tef", cotangent, expert_down_back, preferred_element_type=jnp.float32
    )
    expert_down_grad = jnp.einsum(
        "tef,td->efd", hidden, cotangent, preferred_element_type=jnp.float32
    )
    shared_grad = jnp.einsum(
        "td,fd->tf", cotangent, shared_down_back, preferred_element_type=jnp.float32
    )
    shared_down_grad = jnp.einsum(
        "tf,td->fd", shared_hidden, cotangent, preferred_element_type=jnp.float32
    )
    gate_dot = jnp.sum(active * hidden_grad, axis=2)
    shared_dot = jnp.sum(shared_active * shared_grad, axis=1)
    active_grad = gate_weights[:, :, None] * hidden_grad
    gate_grad = active_grad * up_part * gate_sigmoid * (1.0 + gate_part * (1.0 - gate_sigmoid))
    up_grad = active_grad * gate_part * gate_sigmoid
    gate_up_grad = jnp.stack([gate_grad, up_grad], axis=2).astype(jnp.bfloat16)
    shared_active_grad = gate_value[:, None] * shared_grad
    shared_gate_grad = (
        shared_active_grad
        * shared_up_in
        * shared_sigmoid
        * (1.0 + shared_gate_in * (1.0 - shared_sigmoid))
    )
    shared_unit_grad = shared_active_grad * shared_gate_in * shared_sigmoid
    shared_up_grad = jnp.stack([shared_gate_grad, shared_unit_grad], axis=1).astype(jnp.bfloat16)
    expert_gate_grad = jnp.einsum(
        "td,tekf->edkf", hidden_two, gate_up_grad, preferred_element_type=jnp.float32
    )
    shared_proj_grad = jnp.einsum(
        "td,tkf->dkf", hidden_two, shared_up_grad, preferred_element_type=jnp.float32
    )
    input_part = jnp.einsum(
        "tekf,edkf->td", gate_up_grad, expert_gate_back, preferred_element_type=jnp.float32
    ) + jnp.einsum(
        "tkf,dkf->td", shared_up_grad, shared_up_back, preferred_element_type=jnp.float32
    )
    input_sum, gate_sum, shared_sum = (
        lax.psum(input_part.astype(jnp.bfloat16), "tp").astype(jnp.float32),
        lax.psum(gate_dot.astype(jnp.bfloat16), "tp").astype(jnp.float32),
        lax.psum(shared_dot.astype(jnp.bfloat16), "tp").astype(jnp.float32),
    )
    chosen_grad = chosen * gate_sum
    logit_grad = (
        router_probs * (chosen_grad - jnp.sum(router_probs * chosen_grad, axis=1, keepdims=True))
    ).astype(jnp.bfloat16)
    gate_logit_grad = (shared_sum * gate_value * (1.0 - gate_value)).astype(jnp.bfloat16)
    router_grad = jnp.einsum(
        "te,td->ed", logit_grad, hidden_two, preferred_element_type=jnp.float32
    )
    shared_vector_grad = jnp.einsum(
        "t,td->d", gate_logit_grad, hidden_two, preferred_element_type=jnp.float32
    )
    two_grad = (
        input_sum
        + jnp.einsum("te,ed->td", logit_grad, router_back, preferred_element_type=jnp.float32)
        + gate_logit_grad.astype(jnp.float32)[:, None]
        * shared_gate_back.astype(jnp.float32)[None, :]
    )
    scaled_two = two_grad * gains_back[1].astype(jnp.float32)[None, :]
    gain_two_grad = jnp.sum(two_grad * normed_two, axis=0)
    residual_grad = cotangent.astype(jnp.float32) + rstd_two * (
        scaled_two - normed_two * jnp.mean(scaled_two * normed_two, axis=1, keepdims=True)
    )
    branch_grad = residual_grad.astype(jnp.bfloat16)
    out_grad = jnp.einsum("tf,td->fd", attended, branch_grad, preferred_element_type=jnp.float32)
    attended_grad = jnp.einsum(
        "td,fd->tf", branch_grad, out_back, preferred_element_type=jnp.float32
    ).astype(jnp.bfloat16)
    grad_heads = attended_grad.reshape(seq_count, SEQ_DEV, head_count, HD)
    delta_rows = jnp.einsum(
        "pqhd,pqhd->phq", grad_heads, attended_heads, preferred_element_type=jnp.float32
    )
    key_all, value_all = (
        lax.all_gather(key_own, "fs", axis=0, tiled=True),
        lax.all_gather(value_own, "fs", axis=0, tiled=True),
    )
    device_count = key_all.shape[0] // tok_rows
    back_group = math.gcd(device_count, group_limit)
    back_steps = device_count // back_group
    back_shape = (back_steps, back_group, seq_count, SEQ_DEV, head_count, HD)

    def backward_update(key_group, value_group, start_dev):
        scores, allowed = score_block(key_group, start_dev)
        probs_block = jnp.where(allowed, jnp.exp(scores - log_total[..., None, None]), 0.0)
        weights_grad = jnp.einsum(
            "pqhd,gpkhd->phqgk", grad_heads, value_group, preferred_element_type=jnp.float32
        )
        score_grad = (probs_block * (weights_grad - delta_rows[..., None, None])).astype(
            jnp.bfloat16
        )
        query_part = (
            jnp.einsum(
                "phqgk,gpkhd->pqhd", score_grad, key_group, preferred_element_type=jnp.float32
            )
            * score_scale
        )
        key_part = (
            jnp.einsum(
                "phqgk,pqhd->gpkhd", score_grad, query_heads, preferred_element_type=jnp.float32
            )
            * score_scale
        )
        value_part = jnp.einsum(
            "phqgk,pqhd->gpkhd",
            probs_block.astype(jnp.bfloat16),
            grad_heads,
            preferred_element_type=jnp.float32,
        )
        return (query_part, key_part, value_part)

    empty_grads = (
        jnp.zeros((seq_count, SEQ_DEV, head_count, HD), jnp.float32),
        jnp.zeros((back_group, seq_count, SEQ_DEV, head_count, HD), jnp.float32),
        jnp.zeros((back_group, seq_count, SEQ_DEV, head_count, HD), jnp.float32),
    )
    scan_inputs = (
        key_all.reshape(back_shape),
        value_all.reshape(back_shape),
        jnp.arange(back_steps, dtype=jnp.int32),
    )

    def back_step(query_acc, inputs):
        key_group, value_group, group_index = inputs
        start_dev = group_index * back_group
        query_part, key_part, value_part = lax.cond(
            start_dev <= fs_index,
            lambda ignored_in: backward_update(key_group, value_group, start_dev),
            lambda ignored_in: empty_grads,
            key_group,
        )
        term_rows = jnp.concatenate(
            [
                key_part.reshape(back_group * tok_rows, local_width),
                value_part.reshape(back_group * tok_rows, local_width),
            ],
            axis=1,
        )
        return (query_acc + query_part, term_rows)

    query_grad, key_value_terms = lax.scan(back_step, empty_grads[0], scan_inputs)
    key_value_sum = lax.psum_scatter(
        key_value_terms.reshape(device_count * tok_rows, 2 * local_width).astype(jnp.bfloat16),
        "fs",
        scatter_dimension=0,
        tiled=True,
    ).astype(jnp.float32)
    key_grad_rows = key_value_sum[:, :local_width]
    value_grad_rows = key_value_sum[:, local_width:]
    projected_grad = jnp.stack(
        [
            rotate(query_grad.reshape(tok_rows, local_width), cosine, -sine_table),
            rotate(key_grad_rows, cosine, -sine_table),
            value_grad_rows,
        ],
        axis=0,
    ).astype(jnp.bfloat16)
    qkv_grad = jnp.einsum(
        "td,jtf->jdf", hidden_one, projected_grad, preferred_element_type=jnp.float32
    )
    one_part = jnp.einsum(
        "jtf,jdf->td", projected_grad, qkv_back, preferred_element_type=jnp.float32
    )
    one_grad = lax.psum(one_part.astype(jnp.bfloat16), "tp").astype(jnp.float32)
    scaled_one = one_grad * gains_back[0].astype(jnp.float32)[None, :]
    gain_one_grad = jnp.sum(one_grad * normed_one, axis=0)
    input_grad = residual_grad + rstd_one * (
        scaled_one - normed_one * jnp.mean(scaled_one * normed_one, axis=1, keepdims=True)
    )
    gains_grad = jnp.stack([gain_one_grad, gain_two_grad], axis=0)
    reduced = (
        lax.psum_scatter(
            qkv_grad.astype(jnp.bfloat16), "fs", scatter_dimension=1, tiled=True
        ).astype(jnp.float32),
        lax.psum_scatter(
            out_grad.astype(jnp.bfloat16), "fs", scatter_dimension=1, tiled=True
        ).astype(jnp.float32),
        lax.psum_scatter(
            gains_grad.astype(jnp.bfloat16), "fs", scatter_dimension=1, tiled=True
        ).astype(jnp.float32),
        lax.psum_scatter(
            router_grad.astype(jnp.bfloat16), "fs", scatter_dimension=1, tiled=True
        ).astype(jnp.float32),
        lax.psum_scatter(
            shared_vector_grad.astype(jnp.bfloat16), "fs", scatter_dimension=0, tiled=True
        ).astype(jnp.float32),
        lax.psum_scatter(
            expert_gate_grad.astype(jnp.bfloat16), "fs", scatter_dimension=1, tiled=True
        ).astype(jnp.float32),
        lax.psum_scatter(
            expert_down_grad.astype(jnp.bfloat16), "fs", scatter_dimension=2, tiled=True
        ).astype(jnp.float32),
        lax.psum_scatter(
            shared_proj_grad.astype(jnp.bfloat16), "fs", scatter_dimension=0, tiled=True
        ).astype(jnp.float32),
        lax.psum_scatter(
            shared_down_grad.astype(jnp.bfloat16), "fs", scatter_dimension=1, tiled=True
        ).astype(jnp.float32),
    )
    return (
        output,
        input_grad,
        reduced[0],
        reduced[1],
        reduced[2],
        reduced[3],
        reduced[4],
        reduced[5],
        reduced[6],
        reduced[7],
        reduced[8],
    )


MESH = pl.DeviceIdType.MESH
X_BIT, Y_BIT, CORE_BIT = 2, 4, 1
QUARTERS = 4
SMALL = 16


def flip(index, bit):
    return index + bit - 2 * bit * ((index // bit) % 2)


class Links:
    def __init__(self, send, recv, local):
        self.fs = lax.axis_index("fs")
        self.tp = lax.axis_index("tp")
        self.send, self.recv, self.local = send, recv, local
        self.used = 0
        self.used_local = 0

    def peer(self, bits):
        where = self.fs
        for bit in (X_BIT, Y_BIT, CORE_BIT):
            if bits & bit:
                where = flip(where, bit)
        return where

    def along(self, step):
        return lax.rem(self.tp + step, QUARTERS)

    def remote(self, source, target, device, landing):
        i = self.used
        self.used += 1
        out = pltpu.make_async_remote_copy(
            src_ref=source,
            dst_ref=target,
            send_sem=self.send.at[i],
            recv_sem=self.recv.at[i],
            device_id=device,
            device_id_type=MESH,
        )
        back = pltpu.make_async_remote_copy(
            src_ref=landing,
            dst_ref=landing,
            send_sem=self.send.at[i],
            recv_sem=self.recv.at[i],
            device_id=device,
            device_id_type=MESH,
        )
        return out, back

    def inside(self, source, target):
        i = self.used_local
        self.used_local += 1
        return pltpu.make_async_copy(source, target, self.local.at[i])

    def greet(self, plane, column):
        barrier = pltpu.get_barrier_semaphore()
        for bits in plane:
            pl.semaphore_signal(
                barrier, inc=1, device_id=(self.peer(bits), self.tp), device_id_type=MESH
            )
        for step in column:
            pl.semaphore_signal(
                barrier, inc=1, device_id=(self.fs, self.along(step)), device_id_type=MESH
            )
        pl.semaphore_wait(barrier, len(plane) + len(column))


class Gather:
    def __init__(self, links, source, place, half):
        self.links = links
        fs, tp = links.fs, links.tp

        def to(bits, what, landing, origin=None):
            return links.remote(
                what if origin is None else origin, what, (links.peer(bits), tp), landing
            )

        p = links.peer
        self.keep = links.inside(source, place(fs))
        self.to_x = to(X_BIT, place(fs), place(p(X_BIT)), source)
        self.to_y = to(Y_BIT, place(fs), place(p(Y_BIT)), source)
        self.to_c = to(CORE_BIT, place(fs), place(p(CORE_BIT)), source)
        xy = X_BIT + Y_BIT
        self.x_on = to(Y_BIT, half(p(X_BIT), 0), half(p(xy), 0))
        self.y_on = to(X_BIT, half(p(Y_BIT), 1), half(p(xy), 1))
        self.x_core = to(CORE_BIT, place(p(X_BIT)), place(p(X_BIT + CORE_BIT)))
        self.y_core = to(CORE_BIT, place(p(Y_BIT)), place(p(Y_BIT + CORE_BIT)))
        self.d_core = [
            to(CORE_BIT, half(p(xy), h), half(p(xy + CORE_BIT), h)) for h in range(2)
        ]

    def first(self):
        self.to_x[0].start()
        self.to_y[0].start()
        self.to_c[0].start()
        self.keep.start()

    def second(self):
        self.to_x[1].wait_recv()
        self.x_on[0].start()
        self.x_core[0].start()
        self.to_y[1].wait_recv()
        self.y_on[0].start()
        self.y_core[0].start()

    def third(self):
        self.x_on[1].wait_recv()
        self.d_core[0][0].start()
        self.y_on[1].wait_recv()
        self.d_core[1][0].start()

    def last(self):
        self.keep.wait()
        for out, back in (self.to_c, self.x_core, self.y_core, *self.d_core):
            back.wait_recv()
        for out, back in (
            self.to_x,
            self.to_y,
            self.to_c,
            self.x_on,
            self.y_on,
            self.x_core,
            self.y_core,
            *self.d_core,
        ):
            out.wait_send()


def turn(values, cosine, sine_signed):
    parts = []
    for h in range(values.shape[1] // HD):
        v = values[:, h * HD : (h + 1) * HD]
        parts.append(v * cosine + pltpu.roll(v, HD // 2, 1) * sine_signed)
    return jnp.concatenate(parts, axis=1)


def matmul(a, b):
    return jnp.dot(a, b, preferred_element_type=jnp.float32)


def matmul_nt(a, b):
    return lax.dot_general(a, b, (((1,), (1,)), ((), ())), preferred_element_type=jnp.float32)


def matmul_tn(a, b):
    return lax.dot_general(a, b, (((0,), (0,)), ((), ())), preferred_element_type=jnp.float32)


def forward_kernel(
    tokens_ref,
    cotangent_ref,
    qkv_ref,
    out_ref,
    small_ref,
    slabs_ref,
    cos_ref,
    sin_ref,
    start_ref,
    routes_ref,
    two_ref,
    residual_ref,
    scales_ref,
    attended_ref,
    query_ref,
    slabs_all,
    cotangent_all,
    kv_out,
    qkv_out,
    out_out,
    small_out,
    qkv_full,
    out_full,
    small_full,
    kv_own,
    kv_full,
    hidden_buf,
    branch_buf,
    branch_in,
    send,
    recv,
    local,
):
    links = Links(send, recv, local)
    fs, tp = links.fs, links.tp
    rows, width = tokens_ref.shape
    block = width // E
    local_width = qkv_ref.shape[2]
    heads = local_width // HD
    seqs = rows // SEQ_DEV
    quarter = rows // QUARTERS

    def at_rows(index, size):
        return pl.ds(pl.multiple_of(index * size, size), size)

    links.greet(range(1, 8), range(1, QUARTERS))
    small = Gather(
        links, small_ref, lambda f: small_full.at[f], lambda f, h: small_full.at[f, :, pl.ds(h * 128, 128)]
    )
    qkv = Gather(
        links,
        qkv_ref,
        lambda f: qkv_full.at[:, at_rows(f, block)],
        lambda f, h: qkv_full.at[:, pl.ds(pl.multiple_of(f * block + h * (block // 2), block // 2), block // 2)],
    )
    outs = Gather(
        links,
        out_ref,
        lambda f: out_full.at[f],
        lambda f, h: out_full.at[f, pl.ds(h * (local_width // 2), local_width // 2)],
    )
    small.first()
    qkv.first()
    small.second()
    small.third()
    small.last()
    tokens = tokens_ref[...].astype(jnp.float32)
    rstd_one = lax.rsqrt(jnp.mean(tokens * tokens, axis=1, keepdims=True) + NORM_EPS)
    for b in range(E):
        cols = slice(b * block, (b + 1) * block)
        gain = small_full[b, 0:1, :].astype(jnp.float32)
        hidden_buf[:, cols] = (tokens[:, cols] * rstd_one * gain).astype(jnp.bfloat16)
    qkv.second()
    qkv.third()
    outs.first()
    qkv.last()
    hidden = hidden_buf[...]
    cosine, sine = cos_ref[...], sin_ref[...]
    kv_own[:, :local_width] = turn(matmul(hidden, qkv_full[1]), cosine, sine).astype(jnp.bfloat16)
    kv_own[:, local_width:] = matmul(hidden, qkv_full[2]).astype(jnp.bfloat16)
    kv = Gather(
        links,
        kv_own,
        lambda f: kv_full.at[f],
        lambda f, h: kv_full.at[f, pl.ds(h * SEQ_DEV, SEQ_DEV)],
    )
    kv.first()
    qkv_keep = links.inside(qkv_full, qkv_out)
    qkv_keep.start()
    query_ref[...] = turn(matmul(hidden, qkv_full[0]), cosine, sine).astype(jnp.bfloat16)
    outs.second()
    kv.second()
    outs.third()
    kv.third()
    slab_copies = []
    for bits in (6, 7, 2, 3, 4, 5, 1):
        peer = links.peer(bits)
        slab_copies.append(
            links.remote(slabs_ref.at[peer], slabs_all.at[fs], (peer, tp), slabs_all.at[peer])
        )
    for out, back in slab_copies:
        out.start()
    slab_own = links.inside(slabs_ref.at[fs], slabs_all.at[fs])
    slab_own.start()
    cot = Gather(
        links,
        cotangent_ref,
        lambda f: cotangent_all.at[f],
        lambda f, h: cotangent_all.at[f, pl.ds(h * SEQ_DEV, SEQ_DEV)],
    )
    cot.first()
    kv.last()
    kv_keep = links.inside(kv_full, kv_out)
    kv_keep.start()
    length = E * SEQ_DEV
    key_pos = lax.broadcasted_iota(jnp.int32, (SEQ_DEV, length), 1)
    query_pos = fs * SEQ_DEV + lax.broadcasted_iota(jnp.int32, (SEQ_DEV, length), 0)
    for s in range(seqs):
        here = slice(s * SEQ_DEV, (s + 1) * SEQ_DEV)
        allowed = (key_pos <= query_pos) & (key_pos >= start_ref[here, :])
        for h in range(heads):
            cols = slice(h * HD, (h + 1) * HD)
            vcols = slice(local_width + h * HD, local_width + (h + 1) * HD)
            keys = kv_full[:, here, cols].reshape(length, HD)
            values = kv_full[:, here, vcols].reshape(length, HD)
            scores = matmul_nt(query_ref[here, cols], keys) * (HD ** (-0.5))
            scores = jnp.where(allowed, scores, NEG_FILL)
            top = jnp.max(scores, axis=1, keepdims=True)
            weights = jnp.exp(scores - top)
            weights = weights / jnp.sum(weights, axis=1, keepdims=True)
            attended_ref[here, cols] = matmul(weights.astype(jnp.bfloat16), values).astype(
                jnp.bfloat16
            )
    outs.last()
    out_keep = links.inside(out_full, out_out)
    out_keep.start()
    small_keep = links.inside(small_full, small_out)
    small_keep.start()
    attended = attended_ref[...]
    for b in range(E):
        branch_buf[:, b * block : (b + 1) * block] = matmul(attended, out_full[b]).astype(
            jnp.bfloat16
        )
    branch = []
    for step in range(1, QUARTERS):
        peer = links.along(step)
        branch.append(
            links.remote(
                branch_buf.at[at_rows(peer, quarter)],
                branch_in.at[step - 1],
                (fs, peer),
                branch_in.at[step - 1],
            )
        )
    for out, back in branch:
        out.start()
    cot.second()
    for out, back in branch:
        back.wait_recv()
    mine = at_rows(tp, quarter)
    total = branch_buf[mine, :].astype(jnp.float32)
    for step in range(1, QUARTERS):
        total = total + branch_in[step - 1].astype(jnp.float32)
    residual = tokens_ref[mine, :].astype(jnp.float32) + total
    residual_ref[...] = residual
    rstd_two = lax.rsqrt(jnp.mean(residual * residual, axis=1, keepdims=True) + NORM_EPS)
    logits = jnp.zeros((quarter, SMALL), jnp.float32)
    for b in range(E):
        cols = slice(b * block, (b + 1) * block)
        gain = small_full[b, 1:2, :].astype(jnp.float32)
        part = (residual[:, cols] * rstd_two * gain).astype(jnp.bfloat16)
        two_ref[:, cols] = part
        logits = logits + matmul_nt(part, small_full[b])
    lane = lax.broadcasted_iota(jnp.int32, (quarter, SMALL), 1)
    routed = (lane >= 2) & (lane < 2 + E)
    masked = jnp.where(routed, logits, NEG_FILL)
    odds = jnp.exp(masked - jnp.max(masked, axis=1, keepdims=True))
    odds = jnp.where(routed, odds, 0.0)
    probs = odds / jnp.sum(odds, axis=1, keepdims=True)
    routes = routes_ref[mine, :]
    chosen = jnp.zeros((quarter, SMALL), jnp.float32)
    for k in range(routes.shape[1]):
        chosen = chosen + (routes[:, k : k + 1] == lane - 2).astype(jnp.float32)
    gate_value = 1.0 / (1.0 + jnp.exp(-logits))
    scales = jnp.where(lane == 2 + E, gate_value, probs * chosen)
    scales_ref[...] = jnp.concatenate([scales, probs, chosen], axis=1)
    cot.third()
    cot.last()
    for out, back in slab_copies:
        back.wait_recv()
    slab_own.wait()
    for out, back in slab_copies + branch:
        out.wait_send()
    for copy in (qkv_keep, kv_keep, out_keep, small_keep):
        copy.wait()


def forward_call(tokens, cotangent, qkv_weight, out_weight, small, slabs, cosine, sine, start, routes):
    rows, width = tokens.shape
    block = width // E
    local_width = qkv_weight.shape[2]
    quarter = rows // QUARTERS
    bf, f32 = jnp.bfloat16, jnp.float32
    sds = jax.ShapeDtypeStruct
    vmem = pl.BlockSpec(memory_space=pltpu.VMEM)
    hbm = pl.BlockSpec(memory_space=pl.ANY)
    outs = [
        (sds((quarter, width), bf), vmem),
        (sds((quarter, width), f32), vmem),
        (sds((quarter, 3 * SMALL), f32), vmem),
        (sds((rows, local_width), bf), vmem),
        (sds((rows, local_width), bf), vmem),
        (sds(slabs.shape, bf), hbm),
        (sds((E, rows, width), bf), hbm),
        (sds((E, rows, 2 * local_width), bf), hbm),
        (sds((3, width, local_width), bf), hbm),
        (sds((E, local_width, block), bf), hbm),
        (sds((E, SMALL, block), bf), hbm),
    ]
    return pl.pallas_call(
        forward_kernel,
        name="attention_forward",
        out_shape=[o[0] for o in outs],
        in_specs=[vmem, hbm, hbm, hbm, hbm, hbm, vmem, vmem, vmem, vmem],
        out_specs=[o[1] for o in outs],
        scratch_shapes=[
            pltpu.VMEM((3, width, local_width), bf),
            pltpu.VMEM((E, local_width, block), bf),
            pltpu.VMEM((E, SMALL, block), bf),
            pltpu.VMEM((rows, 2 * local_width), bf),
            pltpu.VMEM((E, rows, 2 * local_width), bf),
            pltpu.VMEM((rows, width), bf),
            pltpu.VMEM((rows, width), bf),
            pltpu.VMEM((QUARTERS - 1, quarter, width), bf),
            pltpu.SemaphoreType.DMA((64,)),
            pltpu.SemaphoreType.DMA((64,)),
            pltpu.SemaphoreType.DMA((16,)),
        ],
        compiler_params=pltpu.CompilerParams(
            collective_id=1, has_side_effects=True, vmem_limit_bytes=56 * 2**20
        ),
    )(tokens, cotangent, qkv_weight, out_weight, small, slabs, cosine, sine, start, routes)


def shards_units(
    tokens,
    cotangent,
    qkv_weight,
    out_weight,
    norm_gains,
    router_weight,
    shared_gate,
    expert_gate_up,
    expert_down,
    shared_gate_up,
    shared_down,
    routes,
    doc_start,
):
    tok_rows, width = tokens.shape
    seq_count = tok_rows // SEQ_DEV
    local_width = qkv_weight.shape[2]
    head_count = local_width // HD
    quarter = tok_rows // QUARTERS
    score_scale = HD ** (-0.5)
    fs_index = lax.axis_index("fs")
    tp_index = lax.axis_index("tp")
    fs_size = E
    query_pos = fs_index * SEQ_DEV + jnp.arange(SEQ_DEV, dtype=jnp.int32)
    positions = jnp.tile(query_pos, seq_count)
    half_cos, half_sin = rope_tables(positions)
    cosine = jnp.concatenate([half_cos, half_cos], axis=1)
    sine = jnp.concatenate([-half_sin, half_sin], axis=1)
    small = jnp.concatenate(
        [
            norm_gains,
            router_weight,
            shared_gate[None],
            jnp.zeros((SMALL - 3 - E, shared_gate.shape[0]), jnp.bfloat16),
        ],
        axis=0,
    )
    routed_units = expert_down.shape[1]
    shared_units = shared_down.shape[0] // fs_size
    units = routed_units + shared_units
    block = expert_down.shape[2]
    expert_up_slabs = jnp.transpose(expert_gate_up, (0, 2, 3, 1))
    shared_up_slabs = jnp.transpose(
        shared_gate_up.reshape(block, 2, fs_size, shared_units), (2, 1, 3, 0)
    )
    up_slabs = jnp.concatenate([expert_up_slabs, shared_up_slabs], axis=2)
    down_slabs = jnp.concatenate(
        [expert_down, shared_down.reshape(fs_size, shared_units, block)], axis=1
    )
    slabs = jnp.concatenate([up_slabs, down_slabs[:, None]], axis=1)
    (
        two_rows,
        residual_rows,
        router_rows,
        attended,
        query_rows,
        slabs,
        cotangent_all,
        kv_all,
        qkv_full,
        out_full,
        small_full,
    ) = forward_call(
        tokens,
        cotangent,
        qkv_weight,
        out_weight,
        small,
        slabs.reshape(fs_size, 3 * units, block),
        cosine,
        sine,
        doc_start[:, None],
        routes,
    )
    cotangent_all = cotangent_all.reshape(-1, width)
    slabs = slabs.reshape(fs_size, 3, units, block)
    small_rows = jnp.transpose(small_full, (1, 0, 2)).reshape(SMALL, width)
    scale_rows = router_rows[:, 2 : 3 + E]
    probs_rows = router_rows[:, SMALL + 2 : SMALL + 2 + E]
    chosen_rows = router_rows[:, 2 * SMALL + 2 : 2 * SMALL + 2 + E]
    scales_high = scale_rows.astype(jnp.bfloat16)
    scales_low = (scale_rows - scales_high.astype(jnp.float32)).astype(jnp.bfloat16)
    sent = jnp.concatenate(
        [
            two_rows,
            scales_high,
            scales_low,
            jnp.zeros((quarter, SIDE - 2 * (E + 1)), jnp.bfloat16),
        ],
        axis=1,
    )
    hidden_all = lax.all_gather(sent, ("fs", "tp"), axis=0, tiled=True)
    side_all = hidden_all[:, width : width + 2 * (E + 1)].astype(jnp.float32)
    scales_all = side_all[:, : E + 1] + side_all[:, E + 1 :]
    two_all = hidden_all[:, :width]
    mine = (jnp.arange(E, dtype=jnp.int32) == fs_index).astype(jnp.float32)
    routed_scale = jnp.sum(scales_all[:, :E] * mine[None, :], axis=1, keepdims=True)
    is_routed = jnp.arange(units, dtype=jnp.int32)[None, :] < routed_units
    scale = jnp.where(is_routed, routed_scale, scales_all[:, E:])
    weights_by_unit = jnp.transpose(slabs, (1, 2, 0, 3)).reshape(3, units, width)
    gate_part = jnp.einsum(
        "td,ud->tu", two_all, weights_by_unit[0], preferred_element_type=jnp.float32
    )
    up_part = jnp.einsum(
        "td,ud->tu", two_all, weights_by_unit[1], preferred_element_type=jnp.float32
    )
    hidden_grad = jnp.einsum(
        "td,ud->tu", cotangent_all, weights_by_unit[2], preferred_element_type=jnp.float32
    )
    gate_sigmoid = jax.nn.sigmoid(gate_part)
    silu = gate_part * gate_sigmoid
    active = silu * up_part
    hidden = (scale * active).astype(jnp.bfloat16)
    dots = active * hidden_grad
    routed_dot = jnp.sum(jnp.where(is_routed, dots, 0.0), axis=1, keepdims=True)
    shared_dot = jnp.sum(jnp.where(is_routed, 0.0, dots), axis=1, keepdims=True)
    active_grad = scale * hidden_grad
    gate_grad = (
        active_grad * up_part * gate_sigmoid * (1.0 + gate_part * (1.0 - gate_sigmoid))
    ).astype(jnp.bfloat16)
    up_grad = (active_grad * silu).astype(jnp.bfloat16)
    mixture_part = jnp.einsum(
        "tu,ud->td", hidden, weights_by_unit[2], preferred_element_type=jnp.float32
    )
    mixture_own = lax.psum_scatter(
        mixture_part.astype(jnp.bfloat16), "fs", scatter_dimension=0, tiled=True
    )
    residual_placed = lax.dynamic_update_slice(
        jnp.zeros((tok_rows, width), jnp.float32), residual_rows, (tp_index * quarter, 0)
    )
    output = lax.psum_scatter(
        (mixture_own.astype(jnp.float32) + residual_placed).astype(jnp.bfloat16),
        "tp",
        scatter_dimension=1,
        tiled=True,
    )
    input_part = jnp.einsum(
        "tu,ud->td", gate_grad, weights_by_unit[0], preferred_element_type=jnp.float32
    ) + jnp.einsum(
        "tu,ud->td", up_grad, weights_by_unit[1], preferred_element_type=jnp.float32
    )
    side_part = jnp.concatenate(
        [
            routed_dot * mine[None, :],
            shared_dot,
            jnp.zeros((input_part.shape[0], SIDE - E - 1), jnp.float32),
        ],
        axis=1,
    )
    back_part = jnp.concatenate([input_part, side_part], axis=1).astype(jnp.bfloat16)
    back_own = lax.psum_scatter(back_part, "fs", scatter_dimension=0, tiled=True)
    back_rows = lax.psum_scatter(back_own, "tp", scatter_dimension=0, tiled=True).astype(
        jnp.float32
    )
    input_sum = back_rows[:, :width]
    gate_sum = back_rows[:, width : width + E]
    shared_sum = back_rows[:, width + E]
    grad_by_unit = jnp.stack(
        [
            jnp.einsum("tu,td->ud", gate_grad, two_all, preferred_element_type=jnp.float32),
            jnp.einsum("tu,td->ud", up_grad, two_all, preferred_element_type=jnp.float32),
            jnp.einsum("tu,td->ud", hidden, cotangent_all, preferred_element_type=jnp.float32),
        ],
        axis=0,
    ).astype(jnp.bfloat16)
    grad_slabs = jnp.transpose(grad_by_unit.reshape(3, units, fs_size, block), (2, 0, 1, 3))
    grad_slabs = lax.all_to_all(grad_slabs, "fs", 0, 0, tiled=True)
    token_rows = lax.dynamic_slice_in_dim(tokens, tp_index * quarter, quarter, 0).astype(
        jnp.float32
    )
    cotangent_rows = lax.dynamic_slice_in_dim(cotangent, tp_index * quarter, quarter, 0).astype(
        jnp.float32
    )
    rstd_one = lax.rsqrt(jnp.mean(token_rows * token_rows, axis=1, keepdims=True) + NORM_EPS)
    normed_one = token_rows * rstd_one
    rstd_two = lax.rsqrt(jnp.mean(residual_rows * residual_rows, axis=1, keepdims=True) + NORM_EPS)
    normed_two = residual_rows * rstd_two
    gate_value = scale_rows[:, E]
    chosen_grad = chosen_rows * gate_sum
    logit_grad = (
        probs_rows * (chosen_grad - jnp.sum(probs_rows * chosen_grad, axis=1, keepdims=True))
    ).astype(jnp.bfloat16)
    gate_logit_grad = (shared_sum * gate_value * (1.0 - gate_value)).astype(jnp.bfloat16)
    router_grad = jnp.einsum("te,td->ed", logit_grad, two_rows, preferred_element_type=jnp.float32)
    shared_vector_grad = jnp.einsum(
        "t,td->d", gate_logit_grad, two_rows, preferred_element_type=jnp.float32
    )
    two_grad = (
        input_sum
        + jnp.einsum(
            "te,ed->td", logit_grad, small_rows[2 : 2 + E], preferred_element_type=jnp.float32
        )
        + gate_logit_grad.astype(jnp.float32)[:, None]
        * small_rows[2 + E].astype(jnp.float32)[None, :]
    )
    scaled_two = two_grad * small_rows[1].astype(jnp.float32)[None, :]
    gain_two_grad = jnp.sum(two_grad * normed_two, axis=0)
    residual_grad = cotangent_rows + rstd_two * (
        scaled_two - normed_two * jnp.mean(scaled_two * normed_two, axis=1, keepdims=True)
    )
    branch_grad = lax.all_gather(residual_grad.astype(jnp.bfloat16), "tp", axis=0, tiled=True)
    out_grad = jnp.einsum("tf,td->fd", attended, branch_grad, preferred_element_type=jnp.float32)
    attended_grad = jnp.einsum(
        "tbd,bfd->tf",
        branch_grad.reshape(tok_rows, fs_size, block),
        out_full,
        preferred_element_type=jnp.float32,
    ).astype(jnp.bfloat16)
    grad_heads = attended_grad.reshape(seq_count, SEQ_DEV, head_count, HD)
    query_heads = query_rows.reshape(seq_count, SEQ_DEV, head_count, HD)
    kv_heads = kv_all.reshape(fs_size, seq_count, SEQ_DEV, 2, head_count, HD)
    key_heads, value_heads = kv_heads[:, :, :, 0], kv_heads[:, :, :, 1]
    query_start = doc_start.reshape(seq_count, SEQ_DEV)
    allowed = key_mask(query_pos, query_start, 0, fs_size)[:, None]
    scores = (
        jnp.einsum("pqhd,gpkhd->phqgk", query_heads, key_heads, preferred_element_type=jnp.float32)
        * score_scale
    )
    scores = jnp.where(allowed, scores, NEG_FILL)
    exps = jnp.exp(scores - jnp.max(scores, axis=(3, 4), keepdims=True))
    probs = exps / jnp.sum(exps, axis=(3, 4), keepdims=True)
    weights_grad = jnp.einsum(
        "pqhd,gpkhd->phqgk", grad_heads, value_heads, preferred_element_type=jnp.float32
    )
    delta = jnp.sum(probs * weights_grad, axis=(3, 4), keepdims=True)
    score_grad = (probs * (weights_grad - delta)).astype(jnp.bfloat16)
    query_grad = (
        jnp.einsum("phqgk,gpkhd->pqhd", score_grad, key_heads, preferred_element_type=jnp.float32)
        * score_scale
    )
    key_grad = (
        jnp.einsum(
            "phqgk,pqhd->gpkhd", score_grad, query_heads, preferred_element_type=jnp.float32
        )
        * score_scale
    )
    value_grad = jnp.einsum(
        "phqgk,pqhd->gpkhd",
        probs.astype(jnp.bfloat16),
        grad_heads,
        preferred_element_type=jnp.float32,
    )
    terms = jnp.concatenate(
        [
            key_grad.reshape(fs_size * tok_rows, local_width),
            value_grad.reshape(fs_size * tok_rows, local_width),
        ],
        axis=1,
    ).astype(jnp.bfloat16)
    key_value_sum = lax.psum_scatter(terms, "fs", scatter_dimension=0, tiled=True).astype(
        jnp.float32
    )
    projected_grad = jnp.stack(
        [
            rotate(query_grad.reshape(tok_rows, local_width), half_cos, -half_sin),
            rotate(key_value_sum[:, :local_width], half_cos, -half_sin),
            key_value_sum[:, local_width:],
        ],
        axis=0,
    ).astype(jnp.bfloat16)
    token_all = tokens.astype(jnp.float32)
    rstd_all = lax.rsqrt(jnp.mean(token_all * token_all, axis=1, keepdims=True) + NORM_EPS)
    hidden_one = (token_all * rstd_all * small_rows[0].astype(jnp.float32)[None, :]).astype(
        jnp.bfloat16
    )
    qkv_grad = jnp.einsum(
        "td,jtf->jdf", hidden_one, projected_grad, preferred_element_type=jnp.float32
    )
    one_part = jnp.einsum(
        "jtf,jdf->td", projected_grad, qkv_full, preferred_element_type=jnp.float32
    )
    one_grad = lax.psum_scatter(
        one_part.astype(jnp.bfloat16), "tp", scatter_dimension=0, tiled=True
    ).astype(jnp.float32)
    scaled_one = one_grad * small_rows[0].astype(jnp.float32)[None, :]
    gain_one_grad = jnp.sum(one_grad * normed_one, axis=0)
    input_grad_rows = residual_grad + rstd_one * (
        scaled_one - normed_one * jnp.mean(scaled_one * normed_one, axis=1, keepdims=True)
    )
    input_grad = lax.all_gather(
        input_grad_rows.astype(jnp.bfloat16), "tp", axis=0, tiled=True
    ).astype(jnp.float32)
    small_grad = jnp.concatenate(
        [gain_one_grad[None], gain_two_grad[None], router_grad, shared_vector_grad[None]], axis=0
    )
    small_own = lax.psum(
        lax.psum_scatter(
            small_grad.astype(jnp.bfloat16), "fs", scatter_dimension=1, tiled=True
        ),
        "tp",
    ).astype(jnp.float32)
    qkv_own = lax.psum_scatter(
        qkv_grad.astype(jnp.bfloat16), "fs", scatter_dimension=1, tiled=True
    ).astype(jnp.float32)
    out_own = lax.psum_scatter(
        out_grad.astype(jnp.bfloat16), "fs", scatter_dimension=1, tiled=True
    ).astype(jnp.float32)
    own = grad_slabs.astype(jnp.float32)
    expert_up_own = jnp.transpose(own[:, :2, :routed_units], (0, 3, 1, 2))
    expert_down_own = own[:, 2, :routed_units]
    shared_up_own = jnp.transpose(own[:, :2, routed_units:], (3, 1, 0, 2)).reshape(
        shared_gate_up.shape
    )
    shared_down_own = own[:, 2, routed_units:].reshape(shared_down.shape)
    return (
        output,
        input_grad,
        qkv_own,
        out_own,
        small_own[:2],
        small_own[2 : 2 + E],
        small_own[2 + E],
        expert_up_own,
        expert_down_own,
        shared_up_own,
        shared_down_own,
    )


def solution(mesh):
    return jax.shard_map(
        shards_units if dict(mesh.shape) == {"fs": E, "tp": QUARTERS} else shards_gathered,
        mesh=mesh,
        in_specs=(
            P("fs", None),
            P("fs", None),
            P(None, "fs", "tp"),
            P("tp", "fs"),
            P(None, "fs"),
            P(None, "fs"),
            P("fs"),
            P(None, "fs", None, "tp"),
            P(None, "tp", "fs"),
            P("fs", None, "tp"),
            P("tp", "fs"),
            P("fs", None),
            P("fs"),
        ),
        out_specs=(
            P("fs", "tp"),
            P("fs", None),
            P(None, "fs", "tp"),
            P("tp", "fs"),
            P(None, "fs"),
            P(None, "fs"),
            P("fs"),
            P(None, "fs", None, "tp"),
            P(None, "tp", "fs"),
            P("fs", None, "tp"),
            P("tp", "fs"),
        ),
        check_vma=False,
    )
```

```python
import functools
import math

import jax
import jax.numpy as jnp
from jax import lax
from jax.experimental import pallas as pl
from jax.experimental.pallas import tpu as pltpu
from jax.sharding import PartitionSpec as P

HD = 128
E = 8
SEQ_DEV = 128
SIDE = 128


NORM_EPS = 1e-06
NEG_FILL = -1e30
ROPE_BASE = 1000000.0


def rope_tables(positions):
    half_size = HD // 2
    frequency = ROPE_BASE ** (-(jnp.arange(half_size, dtype=jnp.float32) * 2.0 / HD))
    angles = positions.astype(jnp.float32)[:, None] * frequency[None, :]
    return (jnp.cos(angles), jnp.sin(angles))


def rotate(values, cosine, sine_table):
    shaped = values.reshape(values.shape[0], -1, HD)
    half_size = HD // 2
    first_half = shaped[..., :half_size]
    second_half = shaped[..., half_size:]
    cos_part = cosine[:, None, :]
    sin_part = sine_table[:, None, :]
    turned = jnp.concatenate(
        [
            first_half * cos_part - second_half * sin_part,
            second_half * cos_part + first_half * sin_part,
        ],
        axis=-1,
    )
    return turned.reshape(values.shape)


def key_mask(query_pos, query_start, first_dev, group_size):
    key_pos = (first_dev + jnp.arange(group_size, dtype=jnp.int32)[:, None]) * SEQ_DEV + jnp.arange(
        SEQ_DEV, dtype=jnp.int32
    )[None, :]
    key_pos = key_pos[None, None, :, :]
    return (key_pos <= query_pos[None, :, None, None]) & (key_pos >= query_start[:, :, None, None])


def shards_gathered(
    tokens,
    cotangent,
    qkv_weight,
    out_weight,
    norm_gains,
    router_weight,
    shared_gate,
    expert_gate_up,
    expert_down,
    shared_gate_up,
    shared_down,
    routes,
    doc_start,
):
    tok_rows = tokens.shape[0]
    seq_count = tok_rows // SEQ_DEV
    local_width = qkv_weight.shape[2]
    head_count = local_width // HD
    out_width = tokens.shape[1] // lax.axis_size("tp")
    score_scale = HD ** (-0.5)
    fs_index = lax.axis_index("fs")
    tp_index = lax.axis_index("tp")
    query_pos = fs_index * SEQ_DEV + jnp.arange(SEQ_DEV, dtype=jnp.int32)
    positions = jnp.tile(query_pos, seq_count)
    query_start = doc_start.reshape(seq_count, SEQ_DEV)
    cosine, sine_table = rope_tables(positions)
    group_limit = max(1, 512 // SEQ_DEV)
    qkv_full, out_full, gains_full, router_full, shared_gate_full = (
        lax.all_gather(qkv_weight, "fs", axis=1, tiled=True),
        lax.all_gather(out_weight, "fs", axis=1, tiled=True),
        lax.all_gather(norm_gains, "fs", axis=1, tiled=True),
        lax.all_gather(router_weight, "fs", axis=1, tiled=True),
        lax.all_gather(shared_gate, "fs", axis=0, tiled=True),
    )
    token_float = tokens.astype(jnp.float32)
    rstd_one = lax.rsqrt(jnp.mean(token_float * token_float, axis=1, keepdims=True) + NORM_EPS)
    normed_one = token_float * rstd_one
    hidden_one = (normed_one * gains_full[0].astype(jnp.float32)[None, :]).astype(jnp.bfloat16)
    projected = jnp.einsum("td,jdf->jtf", hidden_one, qkv_full, preferred_element_type=jnp.float32)
    query_rows = rotate(projected[0], cosine, sine_table).astype(jnp.bfloat16)
    key_own = rotate(projected[1], cosine, sine_table).astype(jnp.bfloat16)
    value_own = projected[2].astype(jnp.bfloat16)
    query_heads = query_rows.reshape(seq_count, SEQ_DEV, head_count, HD)

    def score_block(key_group, first_dev):
        allowed = key_mask(query_pos, query_start, first_dev, key_group.shape[0])[:, None]
        scores = (
            jnp.einsum(
                "pqhd,gpkhd->phqgk", query_heads, key_group, preferred_element_type=jnp.float32
            )
            * score_scale
        )
        return (jnp.where(allowed, scores, NEG_FILL), allowed)

    def forward_update(running, key_group, value_group, first_dev):
        run_max, run_sum, accumulated = running
        scores, allowed = score_block(key_group, first_dev)
        new_max = jnp.maximum(run_max, jnp.max(scores, axis=(3, 4)))
        weights = jnp.where(allowed, jnp.exp(scores - new_max[..., None, None]), 0.0)
        factor = jnp.exp(run_max - new_max)
        new_sum = run_sum * factor + jnp.sum(weights, axis=(3, 4))
        mixed_part = jnp.einsum(
            "phqgk,gpkhd->pqhd",
            weights.astype(jnp.bfloat16),
            value_group,
            preferred_element_type=jnp.float32,
        )
        new_accum = accumulated * jnp.transpose(factor, (0, 2, 1))[..., None] + mixed_part
        return (new_max, new_sum, new_accum)

    initial = (
        jnp.full((seq_count, head_count, SEQ_DEV), NEG_FILL, jnp.float32),
        jnp.zeros((seq_count, head_count, SEQ_DEV), jnp.float32),
        jnp.zeros((seq_count, SEQ_DEV, head_count, HD), jnp.float32),
    )
    running = initial
    key_piece = lax.all_gather(key_own, "fs", axis=0, tiled=True)
    value_piece = lax.all_gather(value_own, "fs", axis=0, tiled=True)
    shard_count = key_piece.shape[0] // tok_rows
    group_size = math.gcd(shard_count, group_limit)
    step_count = shard_count // group_size
    shaped = (step_count, group_size, seq_count, SEQ_DEV, head_count, HD)
    first_dev = jnp.int32(0) // tok_rows

    def one_step(carried, inputs):
        key_group, value_group, group_index = inputs
        start_dev = group_index * group_size
        updated = lax.cond(
            start_dev <= fs_index,
            lambda state_in: forward_update(state_in, key_group, value_group, start_dev),
            lambda state_in: state_in,
            carried,
        )
        return (updated, None)

    running, ignored = lax.scan(
        one_step,
        running,
        (
            key_piece.reshape(shaped),
            value_piece.reshape(shaped),
            jnp.arange(step_count, dtype=jnp.int32),
        ),
    )
    run_max, run_sum, accumulated = running
    attended_heads = (accumulated / jnp.transpose(run_sum, (0, 2, 1))[..., None]).astype(
        jnp.bfloat16
    )
    log_total = run_max + jnp.log(run_sum)
    attended = attended_heads.reshape(tok_rows, local_width)
    branch_part = jnp.dot(attended, out_full, preferred_element_type=jnp.float32)
    branch = lax.psum(branch_part.astype(jnp.bfloat16), "tp").astype(jnp.float32)
    residual = token_float + branch
    rstd_two = lax.rsqrt(jnp.mean(residual * residual, axis=1, keepdims=True) + NORM_EPS)
    normed_two = residual * rstd_two
    hidden_two = (normed_two * gains_full[1].astype(jnp.float32)[None, :]).astype(jnp.bfloat16)
    expert_gate_all, expert_down_all, shared_up_all, shared_down_all = (
        lax.all_gather(expert_gate_up, "fs", axis=1, tiled=True),
        lax.all_gather(expert_down, "fs", axis=2, tiled=True),
        lax.all_gather(shared_gate_up, "fs", axis=0, tiled=True),
        lax.all_gather(shared_down, "fs", axis=1, tiled=True),
    )
    logits = jnp.einsum("td,ed->te", hidden_two, router_full, preferred_element_type=jnp.float32)
    router_probs = jax.nn.softmax(logits, axis=-1)
    chosen = jnp.sum(
        (routes[:, :, None] == jnp.arange(E, dtype=jnp.int32)[None, None, :]).astype(jnp.float32),
        axis=1,
    )
    gate_weights = router_probs * chosen
    gate_up = jnp.einsum(
        "td,edkf->tekf", hidden_two, expert_gate_all, preferred_element_type=jnp.float32
    )
    gate_part = gate_up[:, :, 0]
    up_part = gate_up[:, :, 1]
    gate_sigmoid = jax.nn.sigmoid(gate_part)
    active = gate_part * gate_sigmoid * up_part
    hidden = (gate_weights[:, :, None] * active).astype(jnp.bfloat16)
    shared_in = jnp.einsum(
        "td,dkf->tkf", hidden_two, shared_up_all, preferred_element_type=jnp.float32
    )
    shared_gate_in = shared_in[:, 0]
    shared_up_in = shared_in[:, 1]
    shared_sigmoid = jax.nn.sigmoid(shared_gate_in)
    shared_active = shared_gate_in * shared_sigmoid * shared_up_in
    gate_logit = jnp.einsum(
        "td,d->t", hidden_two, shared_gate_full, preferred_element_type=jnp.float32
    )
    gate_value = jax.nn.sigmoid(gate_logit)
    shared_hidden = (gate_value[:, None] * shared_active).astype(jnp.bfloat16)
    mixture_part = jnp.einsum(
        "tef,efd->td", hidden, expert_down_all, preferred_element_type=jnp.float32
    ) + jnp.dot(shared_hidden, shared_down_all, preferred_element_type=jnp.float32)
    mixture = lax.psum_scatter(
        mixture_part.astype(jnp.bfloat16), "tp", scatter_dimension=1, tiled=True
    ).astype(jnp.float32)
    output = (
        lax.dynamic_slice_in_dim(residual, tp_index * out_width, out_width, 1) + mixture
    ).astype(jnp.bfloat16)
    qkv_back, out_back, gains_back, router_back, shared_gate_back = (
        lax.all_gather(qkv_weight, "fs", axis=1, tiled=True),
        lax.all_gather(out_weight, "fs", axis=1, tiled=True),
        lax.all_gather(norm_gains, "fs", axis=1, tiled=True),
        lax.all_gather(router_weight, "fs", axis=1, tiled=True),
        lax.all_gather(shared_gate, "fs", axis=0, tiled=True),
    )
    expert_gate_back, expert_down_back, shared_up_back, shared_down_back = (
        lax.all_gather(expert_gate_up, "fs", axis=1, tiled=True),
        lax.all_gather(expert_down, "fs", axis=2, tiled=True),
        lax.all_gather(shared_gate_up, "fs", axis=0, tiled=True),
        lax.all_gather(shared_down, "fs", axis=1, tiled=True),
    )
    hidden_grad = jnp.einsum(
        "td,efd->tef", cotangent, expert_down_back, preferred_element_type=jnp.float32
    )
    expert_down_grad = jnp.einsum(
        "tef,td->efd", hidden, cotangent, preferred_element_type=jnp.float32
    )
    shared_grad = jnp.einsum(
        "td,fd->tf", cotangent, shared_down_back, preferred_element_type=jnp.float32
    )
    shared_down_grad = jnp.einsum(
        "tf,td->fd", shared_hidden, cotangent, preferred_element_type=jnp.float32
    )
    gate_dot = jnp.sum(active * hidden_grad, axis=2)
    shared_dot = jnp.sum(shared_active * shared_grad, axis=1)
    active_grad = gate_weights[:, :, None] * hidden_grad
    gate_grad = active_grad * up_part * gate_sigmoid * (1.0 + gate_part * (1.0 - gate_sigmoid))
    up_grad = active_grad * gate_part * gate_sigmoid
    gate_up_grad = jnp.stack([gate_grad, up_grad], axis=2).astype(jnp.bfloat16)
    shared_active_grad = gate_value[:, None] * shared_grad
    shared_gate_grad = (
        shared_active_grad
        * shared_up_in
        * shared_sigmoid
        * (1.0 + shared_gate_in * (1.0 - shared_sigmoid))
    )
    shared_unit_grad = shared_active_grad * shared_gate_in * shared_sigmoid
    shared_up_grad = jnp.stack([shared_gate_grad, shared_unit_grad], axis=1).astype(jnp.bfloat16)
    expert_gate_grad = jnp.einsum(
        "td,tekf->edkf", hidden_two, gate_up_grad, preferred_element_type=jnp.float32
    )
    shared_proj_grad = jnp.einsum(
        "td,tkf->dkf", hidden_two, shared_up_grad, preferred_element_type=jnp.float32
    )
    input_part = jnp.einsum(
        "tekf,edkf->td", gate_up_grad, expert_gate_back, preferred_element_type=jnp.float32
    ) + jnp.einsum(
        "tkf,dkf->td", shared_up_grad, shared_up_back, preferred_element_type=jnp.float32
    )
    input_sum, gate_sum, shared_sum = (
        lax.psum(input_part.astype(jnp.bfloat16), "tp").astype(jnp.float32),
        lax.psum(gate_dot.astype(jnp.bfloat16), "tp").astype(jnp.float32),
        lax.psum(shared_dot.astype(jnp.bfloat16), "tp").astype(jnp.float32),
    )
    chosen_grad = chosen * gate_sum
    logit_grad = (
        router_probs * (chosen_grad - jnp.sum(router_probs * chosen_grad, axis=1, keepdims=True))
    ).astype(jnp.bfloat16)
    gate_logit_grad = (shared_sum * gate_value * (1.0 - gate_value)).astype(jnp.bfloat16)
    router_grad = jnp.einsum(
        "te,td->ed", logit_grad, hidden_two, preferred_element_type=jnp.float32
    )
    shared_vector_grad = jnp.einsum(
        "t,td->d", gate_logit_grad, hidden_two, preferred_element_type=jnp.float32
    )
    two_grad = (
        input_sum
        + jnp.einsum("te,ed->td", logit_grad, router_back, preferred_element_type=jnp.float32)
        + gate_logit_grad.astype(jnp.float32)[:, None]
        * shared_gate_back.astype(jnp.float32)[None, :]
    )
    scaled_two = two_grad * gains_back[1].astype(jnp.float32)[None, :]
    gain_two_grad = jnp.sum(two_grad * normed_two, axis=0)
    residual_grad = cotangent.astype(jnp.float32) + rstd_two * (
        scaled_two - normed_two * jnp.mean(scaled_two * normed_two, axis=1, keepdims=True)
    )
    branch_grad = residual_grad.astype(jnp.bfloat16)
    out_grad = jnp.einsum("tf,td->fd", attended, branch_grad, preferred_element_type=jnp.float32)
    attended_grad = jnp.einsum(
        "td,fd->tf", branch_grad, out_back, preferred_element_type=jnp.float32
    ).astype(jnp.bfloat16)
    grad_heads = attended_grad.reshape(seq_count, SEQ_DEV, head_count, HD)
    delta_rows = jnp.einsum(
        "pqhd,pqhd->phq", grad_heads, attended_heads, preferred_element_type=jnp.float32
    )
    key_all, value_all = (
        lax.all_gather(key_own, "fs", axis=0, tiled=True),
        lax.all_gather(value_own, "fs", axis=0, tiled=True),
    )
    device_count = key_all.shape[0] // tok_rows
    back_group = math.gcd(device_count, group_limit)
    back_steps = device_count // back_group
    back_shape = (back_steps, back_group, seq_count, SEQ_DEV, head_count, HD)

    def backward_update(key_group, value_group, start_dev):
        scores, allowed = score_block(key_group, start_dev)
        probs_block = jnp.where(allowed, jnp.exp(scores - log_total[..., None, None]), 0.0)
        weights_grad = jnp.einsum(
            "pqhd,gpkhd->phqgk", grad_heads, value_group, preferred_element_type=jnp.float32
        )
        score_grad = (probs_block * (weights_grad - delta_rows[..., None, None])).astype(
            jnp.bfloat16
        )
        query_part = (
            jnp.einsum(
                "phqgk,gpkhd->pqhd", score_grad, key_group, preferred_element_type=jnp.float32
            )
            * score_scale
        )
        key_part = (
            jnp.einsum(
                "phqgk,pqhd->gpkhd", score_grad, query_heads, preferred_element_type=jnp.float32
            )
            * score_scale
        )
        value_part = jnp.einsum(
            "phqgk,pqhd->gpkhd",
            probs_block.astype(jnp.bfloat16),
            grad_heads,
            preferred_element_type=jnp.float32,
        )
        return (query_part, key_part, value_part)

    empty_grads = (
        jnp.zeros((seq_count, SEQ_DEV, head_count, HD), jnp.float32),
        jnp.zeros((back_group, seq_count, SEQ_DEV, head_count, HD), jnp.float32),
        jnp.zeros((back_group, seq_count, SEQ_DEV, head_count, HD), jnp.float32),
    )
    scan_inputs = (
        key_all.reshape(back_shape),
        value_all.reshape(back_shape),
        jnp.arange(back_steps, dtype=jnp.int32),
    )

    def back_step(query_acc, inputs):
        key_group, value_group, group_index = inputs
        start_dev = group_index * back_group
        query_part, key_part, value_part = lax.cond(
            start_dev <= fs_index,
            lambda ignored_in: backward_update(key_group, value_group, start_dev),
            lambda ignored_in: empty_grads,
            key_group,
        )
        term_rows = jnp.concatenate(
            [
                key_part.reshape(back_group * tok_rows, local_width),
                value_part.reshape(back_group * tok_rows, local_width),
            ],
            axis=1,
        )
        return (query_acc + query_part, term_rows)

    query_grad, key_value_terms = lax.scan(back_step, empty_grads[0], scan_inputs)
    key_value_sum = lax.psum_scatter(
        key_value_terms.reshape(device_count * tok_rows, 2 * local_width).astype(jnp.bfloat16),
        "fs",
        scatter_dimension=0,
        tiled=True,
    ).astype(jnp.float32)
    key_grad_rows = key_value_sum[:, :local_width]
    value_grad_rows = key_value_sum[:, local_width:]
    projected_grad = jnp.stack(
        [
            rotate(query_grad.reshape(tok_rows, local_width), cosine, -sine_table),
            rotate(key_grad_rows, cosine, -sine_table),
            value_grad_rows,
        ],
        axis=0,
    ).astype(jnp.bfloat16)
    qkv_grad = jnp.einsum(
        "td,jtf->jdf", hidden_one, projected_grad, preferred_element_type=jnp.float32
    )
    one_part = jnp.einsum(
        "jtf,jdf->td", projected_grad, qkv_back, preferred_element_type=jnp.float32
    )
    one_grad = lax.psum(one_part.astype(jnp.bfloat16), "tp").astype(jnp.float32)
    scaled_one = one_grad * gains_back[0].astype(jnp.float32)[None, :]
    gain_one_grad = jnp.sum(one_grad * normed_one, axis=0)
    input_grad = residual_grad + rstd_one * (
        scaled_one - normed_one * jnp.mean(scaled_one * normed_one, axis=1, keepdims=True)
    )
    gains_grad = jnp.stack([gain_one_grad, gain_two_grad], axis=0)
    reduced = (
        lax.psum_scatter(
            qkv_grad.astype(jnp.bfloat16), "fs", scatter_dimension=1, tiled=True
        ).astype(jnp.float32),
        lax.psum_scatter(
            out_grad.astype(jnp.bfloat16), "fs", scatter_dimension=1, tiled=True
        ).astype(jnp.float32),
        lax.psum_scatter(
            gains_grad.astype(jnp.bfloat16), "fs", scatter_dimension=1, tiled=True
        ).astype(jnp.float32),
        lax.psum_scatter(
            router_grad.astype(jnp.bfloat16), "fs", scatter_dimension=1, tiled=True
        ).astype(jnp.float32),
        lax.psum_scatter(
            shared_vector_grad.astype(jnp.bfloat16), "fs", scatter_dimension=0, tiled=True
        ).astype(jnp.float32),
        lax.psum_scatter(
            expert_gate_grad.astype(jnp.bfloat16), "fs", scatter_dimension=1, tiled=True
        ).astype(jnp.float32),
        lax.psum_scatter(
            expert_down_grad.astype(jnp.bfloat16), "fs", scatter_dimension=2, tiled=True
        ).astype(jnp.float32),
        lax.psum_scatter(
            shared_proj_grad.astype(jnp.bfloat16), "fs", scatter_dimension=0, tiled=True
        ).astype(jnp.float32),
        lax.psum_scatter(
            shared_down_grad.astype(jnp.bfloat16), "fs", scatter_dimension=1, tiled=True
        ).astype(jnp.float32),
    )
    return (
        output,
        input_grad,
        reduced[0],
        reduced[1],
        reduced[2],
        reduced[3],
        reduced[4],
        reduced[5],
        reduced[6],
        reduced[7],
        reduced[8],
    )


MESH = pl.DeviceIdType.MESH
X_BIT, Y_BIT, CORE_BIT = 2, 4, 1
QUARTERS = 4
SMALL = 16


def flip(index, bit):
    return index + bit - 2 * bit * ((index // bit) % 2)


class Links:
    def __init__(self, send, recv, local):
        self.fs = lax.axis_index("fs")
        self.tp = lax.axis_index("tp")
        self.send, self.recv, self.local = send, recv, local
        self.used = 0
        self.used_local = 0

    def peer(self, bits):
        where = self.fs
        for bit in (X_BIT, Y_BIT, CORE_BIT):
            if bits & bit:
                where = flip(where, bit)
        return where

    def along(self, step):
        return lax.rem(self.tp + step, QUARTERS)

    def remote(self, source, target, device, landing):
        i = self.used
        self.used += 1
        out = pltpu.make_async_remote_copy(
            src_ref=source,
            dst_ref=target,
            send_sem=self.send.at[i],
            recv_sem=self.recv.at[i],
            device_id=device,
            device_id_type=MESH,
        )
        back = pltpu.make_async_remote_copy(
            src_ref=landing,
            dst_ref=landing,
            send_sem=self.send.at[i],
            recv_sem=self.recv.at[i],
            device_id=device,
            device_id_type=MESH,
        )
        return out, back

    def inside(self, source, target):
        i = self.used_local
        self.used_local += 1
        return pltpu.make_async_copy(source, target, self.local.at[i])

    def greet(self, plane, column):
        barrier = pltpu.get_barrier_semaphore()
        for bits in plane:
            pl.semaphore_signal(
                barrier, inc=1, device_id=(self.peer(bits), self.tp), device_id_type=MESH
            )
        for step in column:
            pl.semaphore_signal(
                barrier, inc=1, device_id=(self.fs, self.along(step)), device_id_type=MESH
            )
        pl.semaphore_wait(barrier, len(plane) + len(column))


class Gather:
    def __init__(self, links, source, place, half):
        self.links = links
        fs, tp = links.fs, links.tp

        def to(bits, what, landing, origin=None):
            return links.remote(
                what if origin is None else origin, what, (links.peer(bits), tp), landing
            )

        p = links.peer
        self.keep = None if source is None else links.inside(source, place(fs))
        self.to_x = to(X_BIT, place(fs), place(p(X_BIT)), source)
        self.to_y = to(Y_BIT, place(fs), place(p(Y_BIT)), source)
        self.to_c = to(CORE_BIT, place(fs), place(p(CORE_BIT)), source)
        xy = X_BIT + Y_BIT
        self.x_on = to(Y_BIT, half(p(X_BIT), 0), half(p(xy), 0))
        self.y_on = to(X_BIT, half(p(Y_BIT), 1), half(p(xy), 1))
        self.x_core = to(CORE_BIT, place(p(X_BIT)), place(p(X_BIT + CORE_BIT)))
        self.y_core = to(CORE_BIT, place(p(Y_BIT)), place(p(Y_BIT + CORE_BIT)))
        self.d_core = [
            to(CORE_BIT, half(p(xy), h), half(p(xy + CORE_BIT), h)) for h in range(2)
        ]

    def first(self):
        self.to_x[0].start()
        self.to_y[0].start()
        self.to_c[0].start()
        if self.keep is not None:
            self.keep.start()

    def second(self):
        self.to_x[1].wait_recv()
        self.x_on[0].start()
        self.x_core[0].start()
        self.to_y[1].wait_recv()
        self.y_on[0].start()
        self.y_core[0].start()

    def third(self):
        self.x_on[1].wait_recv()
        self.d_core[0][0].start()
        self.y_on[1].wait_recv()
        self.d_core[1][0].start()

    def last(self):
        if self.keep is not None:
            self.keep.wait()
        for out, back in (self.to_c, self.x_core, self.y_core, *self.d_core):
            back.wait_recv()
        for out, back in (
            self.to_x,
            self.to_y,
            self.to_c,
            self.x_on,
            self.y_on,
            self.x_core,
            self.y_core,
            *self.d_core,
        ):
            out.wait_send()


def turn(values, cosine, sine_signed):
    parts = []
    for h in range(values.shape[1] // HD):
        v = values[:, h * HD : (h + 1) * HD]
        parts.append(v * cosine + pltpu.roll(v, HD // 2, 1) * sine_signed)
    return jnp.concatenate(parts, axis=1)


def matmul(a, b):
    return jnp.dot(a, b, preferred_element_type=jnp.float32)


def matmul_nt(a, b):
    return lax.dot_general(a, b, (((1,), (1,)), ((), ())), preferred_element_type=jnp.float32)


def matmul_tn(a, b):
    return lax.dot_general(a, b, (((0,), (0,)), ((), ())), preferred_element_type=jnp.float32)


def forward_kernel(
    tokens_ref,
    cotangent_ref,
    qkv_ref,
    out_ref,
    small_ref,
    slabs_ref,
    cos_ref,
    sin_ref,
    start_ref,
    routes_ref,
    two_ref,
    residual_ref,
    scales_ref,
    attended_ref,
    query_ref,
    slabs_all,
    cotangent_all,
    kv_out,
    qkv_out,
    out_out,
    small_out,
    qkv_full,
    out_full,
    small_full,
    kv_own,
    kv_full,
    hidden_buf,
    branch_buf,
    branch_in,
    send,
    recv,
    local,
):
    links = Links(send, recv, local)
    fs, tp = links.fs, links.tp
    rows, width = tokens_ref.shape
    block = width // E
    local_width = qkv_ref.shape[2]
    heads = local_width // HD
    seqs = rows // SEQ_DEV
    quarter = rows // QUARTERS

    def at_rows(index, size):
        return pl.ds(pl.multiple_of(index * size, size), size)

    links.greet(range(1, 8), range(1, QUARTERS))
    small = Gather(
        links, small_ref, lambda f: small_full.at[f], lambda f, h: small_full.at[f, :, pl.ds(h * 128, 128)]
    )
    qkv = Gather(
        links,
        qkv_ref,
        lambda f: qkv_full.at[:, at_rows(f, block)],
        lambda f, h: qkv_full.at[:, pl.ds(pl.multiple_of(f * block + h * (block // 2), block // 2), block // 2)],
    )
    outs = Gather(
        links,
        out_ref,
        lambda f: out_full.at[f],
        lambda f, h: out_full.at[f, pl.ds(h * (local_width // 2), local_width // 2)],
    )
    small.first()
    qkv.first()
    small.second()
    small.third()
    small.last()
    tokens = tokens_ref[...].astype(jnp.float32)
    rstd_one = lax.rsqrt(jnp.mean(tokens * tokens, axis=1, keepdims=True) + NORM_EPS)
    for b in range(E):
        cols = slice(b * block, (b + 1) * block)
        gain = small_full[b, 0:1, :].astype(jnp.float32)
        hidden_buf[:, cols] = (tokens[:, cols] * rstd_one * gain).astype(jnp.bfloat16)
    qkv.second()
    qkv.third()
    outs.first()
    qkv.last()
    hidden = hidden_buf[...]
    cosine, sine = cos_ref[...], sin_ref[...]
    kv_own[:, :local_width] = turn(matmul(hidden, qkv_full[1]), cosine, sine).astype(jnp.bfloat16)
    kv_own[:, local_width:] = matmul(hidden, qkv_full[2]).astype(jnp.bfloat16)
    kv = Gather(
        links,
        kv_own,
        lambda f: kv_full.at[f],
        lambda f, h: kv_full.at[f, pl.ds(h * SEQ_DEV, SEQ_DEV)],
    )
    kv.first()
    qkv_keep = links.inside(qkv_full, qkv_out)
    qkv_keep.start()
    query_ref[...] = turn(matmul(hidden, qkv_full[0]), cosine, sine).astype(jnp.bfloat16)
    outs.second()
    kv.second()
    outs.third()
    kv.third()
    slab_copies = []
    for bits in (6, 7, 2, 3, 4, 5, 1):
        peer = links.peer(bits)
        slab_copies.append(
            links.remote(slabs_ref.at[peer], slabs_all.at[fs], (peer, tp), slabs_all.at[peer])
        )
    for out, back in slab_copies:
        out.start()
    slab_own = links.inside(slabs_ref.at[fs], slabs_all.at[fs])
    slab_own.start()
    cot = Gather(
        links,
        cotangent_ref,
        lambda f: cotangent_all.at[f],
        lambda f, h: cotangent_all.at[f, pl.ds(h * SEQ_DEV, SEQ_DEV)],
    )
    cot.first()
    kv.last()
    kv_keep = links.inside(kv_full, kv_out)
    kv_keep.start()
    length = E * SEQ_DEV
    key_pos = lax.broadcasted_iota(jnp.int32, (SEQ_DEV, length), 1)
    query_pos = fs * SEQ_DEV + lax.broadcasted_iota(jnp.int32, (SEQ_DEV, length), 0)
    for s in range(seqs):
        here = slice(s * SEQ_DEV, (s + 1) * SEQ_DEV)
        allowed = (key_pos <= query_pos) & (key_pos >= start_ref[here, :])
        for h in range(heads):
            cols = slice(h * HD, (h + 1) * HD)
            vcols = slice(local_width + h * HD, local_width + (h + 1) * HD)
            keys = kv_full[:, here, cols].reshape(length, HD)
            values = kv_full[:, here, vcols].reshape(length, HD)
            scores = matmul_nt(query_ref[here, cols], keys) * (HD ** (-0.5))
            scores = jnp.where(allowed, scores, NEG_FILL)
            top = jnp.max(scores, axis=1, keepdims=True)
            weights = jnp.exp(scores - top)
            weights = weights / jnp.sum(weights, axis=1, keepdims=True)
            attended_ref[here, cols] = matmul(weights.astype(jnp.bfloat16), values).astype(
                jnp.bfloat16
            )
    outs.last()
    out_keep = links.inside(out_full, out_out)
    out_keep.start()
    small_keep = links.inside(small_full, small_out)
    small_keep.start()
    attended = attended_ref[...]
    for b in range(E):
        branch_buf[:, b * block : (b + 1) * block] = matmul(attended, out_full[b]).astype(
            jnp.bfloat16
        )
    branch = []
    for step in range(1, QUARTERS):
        peer = links.along(step)
        branch.append(
            links.remote(
                branch_buf.at[at_rows(peer, quarter)],
                branch_in.at[step - 1],
                (fs, peer),
                branch_in.at[step - 1],
            )
        )
    for out, back in branch:
        out.start()
    cot.second()
    for out, back in branch:
        back.wait_recv()
    mine = at_rows(tp, quarter)
    total = branch_buf[mine, :].astype(jnp.float32)
    for step in range(1, QUARTERS):
        total = total + branch_in[step - 1].astype(jnp.float32)
    residual = tokens_ref[mine, :].astype(jnp.float32) + total
    residual_ref[...] = residual
    rstd_two = lax.rsqrt(jnp.mean(residual * residual, axis=1, keepdims=True) + NORM_EPS)
    logits = jnp.zeros((quarter, SMALL), jnp.float32)
    for b in range(E):
        cols = slice(b * block, (b + 1) * block)
        gain = small_full[b, 1:2, :].astype(jnp.float32)
        part = (residual[:, cols] * rstd_two * gain).astype(jnp.bfloat16)
        two_ref[:, cols] = part
        logits = logits + matmul_nt(part, small_full[b])
    lane = lax.broadcasted_iota(jnp.int32, (quarter, SMALL), 1)
    routed = (lane >= 2) & (lane < 2 + E)
    masked = jnp.where(routed, logits, NEG_FILL)
    odds = jnp.exp(masked - jnp.max(masked, axis=1, keepdims=True))
    odds = jnp.where(routed, odds, 0.0)
    probs = odds / jnp.sum(odds, axis=1, keepdims=True)
    routes = routes_ref[mine, :]
    chosen = jnp.zeros((quarter, SMALL), jnp.float32)
    for k in range(routes.shape[1]):
        chosen = chosen + (routes[:, k : k + 1] == lane - 2).astype(jnp.float32)
    gate_value = 1.0 / (1.0 + jnp.exp(-logits))
    scales = jnp.where(lane == 2 + E, gate_value, probs * chosen)
    scales_ref[...] = jnp.concatenate([scales, probs, chosen], axis=1)
    high = scales.astype(jnp.bfloat16)
    low = (scales - high.astype(jnp.float32)).astype(jnp.bfloat16)
    two_ref[:, width:] = jnp.concatenate(
        [high, low, jnp.zeros((quarter, SIDE - 2 * SMALL), jnp.bfloat16)], axis=1
    )
    cot.third()
    cot.last()
    for out, back in slab_copies:
        back.wait_recv()
    slab_own.wait()
    for out, back in slab_copies + branch:
        out.wait_send()
    for copy in (qkv_keep, kv_keep, out_keep, small_keep):
        copy.wait()


def forward_call(tokens, cotangent, qkv_weight, out_weight, small, slabs, cosine, sine, start, routes):
    rows, width = tokens.shape
    block = width // E
    local_width = qkv_weight.shape[2]
    quarter = rows // QUARTERS
    bf, f32 = jnp.bfloat16, jnp.float32
    sds = jax.ShapeDtypeStruct
    vmem = pl.BlockSpec(memory_space=pltpu.VMEM)
    hbm = pl.BlockSpec(memory_space=pl.ANY)
    outs = [
        (sds((quarter, width + SIDE), bf), vmem),
        (sds((quarter, width), f32), vmem),
        (sds((quarter, 3 * SMALL), f32), vmem),
        (sds((rows, local_width), bf), vmem),
        (sds((rows, local_width), bf), vmem),
        (sds(slabs.shape, bf), hbm),
        (sds((E, rows, width), bf), hbm),
        (sds((E, rows, 2 * local_width), bf), hbm),
        (sds((3, width, local_width), bf), hbm),
        (sds((E, local_width, block), bf), hbm),
        (sds((E, SMALL, block), bf), hbm),
    ]
    return pl.pallas_call(
        forward_kernel,
        name="attention_forward",
        out_shape=[o[0] for o in outs],
        in_specs=[vmem, hbm, hbm, hbm, hbm, hbm, vmem, vmem, vmem, vmem],
        out_specs=[o[1] for o in outs],
        scratch_shapes=[
            pltpu.VMEM((3, width, local_width), bf),
            pltpu.VMEM((E, local_width, block), bf),
            pltpu.VMEM((E, SMALL, block), bf),
            pltpu.VMEM((rows, 2 * local_width), bf),
            pltpu.VMEM((E, rows, 2 * local_width), bf),
            pltpu.VMEM((rows, width), bf),
            pltpu.VMEM((rows, width), bf),
            pltpu.VMEM((QUARTERS - 1, quarter, width), bf),
            pltpu.SemaphoreType.DMA((64,)),
            pltpu.SemaphoreType.DMA((64,)),
            pltpu.SemaphoreType.DMA((16,)),
        ],
        compiler_params=pltpu.CompilerParams(
            collective_id=1, has_side_effects=True, vmem_limit_bytes=56 * 2**20
        ),
    )(tokens, cotangent, qkv_weight, out_weight, small, slabs, cosine, sine, start, routes)


def flip_by(index, bits):
    total = 0
    for bit in (1, 2, 4):
        a, b = (index // bit) % 2, (bits // bit) % 2
        total = total + bit * (a + b - 2 * a * b)
    return total


def expert_kernel(
    routed,
    two_ref,
    router_ref,
    residual_ref,
    cotangent_ref,
    cotangent_all,
    slabs_ref,
    small_ref,
    output_ref,
    branch_ref,
    back_ref,
    small_grad_ref,
    grads_out,
    two_all,
    cot_all,
    weights,
    units,
    first,
    parts,
    core_in,
    diag_in,
    side_in,
    rows_in,
    cols_in,
    staged,
    send,
    recv,
    local,
    credit,
):
    links = Links(send, recv, local)
    fs, tp = links.fs, links.tp
    quarter = two_ref.shape[0]
    rows = quarter * QUARTERS
    width = residual_ref.shape[1]
    block = width // E
    count = weights.shape[0] // 3
    out_width = output_ref.shape[1]
    back_width = width + SIDE
    whole = back_width + width

    def at_rows(index, size):
        return pl.ds(pl.multiple_of(index * size, size), size)

    links.greet(range(1, 8), range(1, QUARTERS))
    along = []
    for step in range(1, QUARTERS):
        here = two_all.at[fs, at_rows(tp, quarter)]
        landing = two_all.at[fs, at_rows(links.along(QUARTERS - step), quarter)]
        along.append(links.remote(two_ref, here, (fs, links.along(step)), landing))
    gathers = []
    for step in range(QUARTERS):
        q = links.along(QUARTERS - step) if step else tp
        gathers.append(
            Gather(
                links,
                two_ref if step == 0 else None,
                lambda f, q=q: two_all.at[f, at_rows(q, quarter)],
                lambda f, h, q=q: two_all.at[f, at_rows(q * 2 + h, quarter // 2)],
            )
        )
    gathers[0].first()
    for out, back in along:
        out.start()
    loads = [
        links.inside(slabs_ref.at[g], weights.at[:, pl.ds(g * block, block)]) for g in range(E)
    ]
    loads.append(links.inside(cotangent_all, cot_all))
    for load in loads:
        load.start()
    for step in range(1, QUARTERS):
        along[step - 1][1].wait_recv()
        gathers[step].first()
        gathers[step - 1].second()
        if step >= 2:
            gathers[step - 2].third()
    gathers[3].second()
    gathers[2].third()
    gathers[3].third()
    for load in loads:
        load.wait()
    for gather in gathers:
        gather.last()

    core_copies = []
    for i in range(4):
        core_copies.append(
            links.remote(
                parts.at[i % 2], core_in.at[i % 2], (links.peer(CORE_BIT), tp), core_in.at[i % 2]
            )
        )
    half_rows = rows // 2
    diag_y = links.remote(
        parts.at[2, pl.ds(0, half_rows)], diag_in.at[0], (links.peer(Y_BIT), tp), diag_in.at[0]
    )
    diag_x = links.remote(
        parts.at[2, pl.ds(half_rows, half_rows)],
        diag_in.at[1],
        (links.peer(X_BIT), tp),
        diag_in.at[1],
    )
    side_x = links.remote(parts.at[3], side_in.at[0], (links.peer(X_BIT), tp), side_in.at[0])
    side_y = links.remote(parts.at[4], side_in.at[1], (links.peer(Y_BIT), tp), side_in.at[1])

    sub = lax.broadcasted_iota(jnp.int32, (8, SIDE), 0)
    lane = lax.broadcasted_iota(jnp.int32, (8, SIDE), 1)
    mine, common = 2 + fs, 2 + E
    pick_in = (
        ((sub == 0) & ((lane == mine) | (lane == mine + SMALL)))
        | ((sub == 1) & ((lane == common) | (lane == common + SMALL)))
    ).astype(jnp.bfloat16)
    pick_out = (((sub == 0) & (lane == mine)) | ((sub == 1) & (lane == common))).astype(
        jnp.bfloat16
    )

    def one_block(index, slot):
        first[: 2 * count] = matmul_nt(weights[: 2 * count], two_all[index, :, :width])
        first[2 * count :] = matmul_nt(weights[2 * count :], cot_all[index])
        scale = matmul_nt(pick_in, two_all[index, :, width:])
        cols = pl.ds(pl.multiple_of(index * rows, rows), rows)
        dots = []
        for group, (low, high) in enumerate(((0, routed), (routed, count))):
            gate = first[low:high]
            up = first[count + low : count + high]
            grad = first[2 * count + low : 2 * count + high]
            by = scale[group : group + 1]
            sigmoid = 1.0 / (1.0 + jnp.exp(-gate))
            silu = gate * sigmoid
            active = silu * up
            units[2 * count + low : 2 * count + high, cols] = (by * active).astype(jnp.bfloat16)
            dots.append(jnp.sum(active * grad, axis=0, keepdims=True))
            active_grad = by * grad
            units[low:high, cols] = (
                active_grad * up * sigmoid * (1.0 + gate * (1.0 - sigmoid))
            ).astype(jnp.bfloat16)
            units[count + low : count + high, cols] = (active_grad * silu).astype(jnp.bfloat16)
        both = jnp.concatenate([*dots, jnp.zeros((6, rows), jnp.float32)], axis=0)
        parts[slot, :, width:back_width] = matmul_tn(both.astype(jnp.bfloat16), pick_out).astype(
            jnp.bfloat16
        )
        tile = 512
        for n in range(width // tile):
            at = slice(n * tile, (n + 1) * tile)
            parts[slot, :, at] = matmul_tn(units[: 2 * count, cols], weights[: 2 * count, at]).astype(
                jnp.bfloat16
            )
            beyond = slice(back_width + n * tile, back_width + (n + 1) * tile)
            parts[slot, :, beyond] = matmul_tn(
                units[2 * count :, cols], weights[2 * count :, at]
            ).astype(jnp.bfloat16)

    chunk = 32

    def add_in(slot, others):
        @pl.loop(0, rows // chunk)
        def _(r):
            at = pl.ds(pl.multiple_of(r * chunk, chunk), chunk)
            total = parts[slot, at, :].astype(jnp.float32)
            for ref in others:
                total = total + ref[at, :].astype(jnp.float32)
            parts[slot, at, :] = total.astype(jnp.bfloat16)

    def add_half(slot, ref, start):
        @pl.loop(0, half_rows // chunk)
        def _(r):
            at = pl.ds(pl.multiple_of(start + r * chunk, chunk), chunk)
            there = pl.ds(pl.multiple_of(r * chunk, chunk), chunk)
            total = parts[slot, at, :].astype(jnp.float32) + ref[there, :].astype(jnp.float32)
            parts[slot, at, :] = total.astype(jnp.bfloat16)

    def free_core():
        pl.semaphore_signal(
            credit, inc=1, device_id=(links.peer(CORE_BIT), tp), device_id_type=MESH
        )

    @pl.loop(0, 8)
    def _(t):
        pair = t // 2
        second = t % 2
        bits = 7 - 4 * pair + 6 * (pair // 2) - second
        index = flip_by(fs, bits)
        slot = second * (2 + pair - 3 * (pair // 3)) + (1 - second) * (pair % 2)

        @pl.when(t == 4)
        def _():
            core_copies[0][0].wait_send()

        @pl.when(t == 6)
        def _():
            core_copies[1][0].wait_send()

        @pl.when(t == 7)
        def _():
            diag_y[0].wait_send()
            diag_x[0].wait_send()

        one_block(index, slot)
        for i in range(4):

            @pl.when(t == 2 * i)
            def _(i=i):
                if i >= 2:
                    pl.semaphore_wait(credit, 1)
                core_copies[i][0].start()

        @pl.when(t == 1)
        def _():
            core_copies[0][1].wait_recv()
            add_in(2, [core_in.at[0]])
            free_core()
            diag_y[0].start()
            diag_x[0].start()

        @pl.when(t == 3)
        def _():
            core_copies[1][1].wait_recv()
            add_in(3, [core_in.at[1]])
            free_core()
            diag_y[1].wait_recv()
            add_half(3, diag_in.at[0], 0)
            side_x[0].start()

        @pl.when(t == 5)
        def _():
            core_copies[2][1].wait_recv()
            add_in(4, [core_in.at[0]])
            diag_x[1].wait_recv()
            add_half(4, diag_in.at[1], half_rows)
            side_y[0].start()

        @pl.when(t == 7)
        def _():
            core_copies[3][1].wait_recv()
            add_in(2, [core_in.at[1]])

    keeps = []

    def weight_grads(g):
        at = pl.ds(g * block, block)
        if g >= 2:
            keeps[g - 2].wait()
        hidden_cols = two_all[:, :, at].reshape(E * rows, block)
        staged[g % 2, : 2 * count] = matmul(units[: 2 * count], hidden_cols).astype(jnp.bfloat16)
        cot_cols = cot_all[:, :, at].reshape(E * rows, block)
        staged[g % 2, 2 * count :] = matmul(units[2 * count :], cot_cols).astype(jnp.bfloat16)
        keep = links.inside(staged.at[g % 2], grads_out.at[g])
        keep.start()
        keeps.append(keep)

    for g in range(E // 2):
        weight_grads(g)
    side_x[1].wait_recv()
    side_y[1].wait_recv()
    add_in(2, [side_in.at[0], side_in.at[1]])
    own = at_rows(tp, quarter)
    parts[2, own, back_width:] = (
        parts[2, own, back_width:].astype(jnp.float32) + residual_ref[...]
    ).astype(jnp.bfloat16)
    column = []
    for step in range(1, QUARTERS):
        peer = links.along(step)
        column.append(
            links.remote(
                parts.at[2, at_rows(peer, quarter), pl.ds(0, back_width)],
                rows_in.at[step - 1],
                (fs, peer),
                rows_in.at[step - 1],
            )
        )
    for step in range(1, QUARTERS):
        peer = links.along(step)
        column.append(
            links.remote(
                parts.at[2, :, pl.ds(pl.multiple_of(back_width + peer * out_width, 128), out_width)],
                cols_in.at[step - 1],
                (fs, peer),
                cols_in.at[step - 1],
            )
        )
    for out, back in column:
        out.start()
    for g in range(E // 2, E):
        weight_grads(g)
    for out, back in column[:3]:
        back.wait_recv()
    total = parts[2, own, :back_width].astype(jnp.float32)
    for step in range(1, QUARTERS):
        total = total + rows_in[step - 1].astype(jnp.float32)
    dots = total[:, width : width + SMALL]
    scales = router_ref[:, :SMALL]
    probs = router_ref[:, SMALL : 2 * SMALL]
    chosen = router_ref[:, 2 * SMALL :]
    chosen_grad = chosen * dots
    logit_grad = probs * (chosen_grad - jnp.sum(probs * chosen_grad, axis=1, keepdims=True))
    gate_lane = lax.broadcasted_iota(jnp.int32, (quarter, SMALL), 1) == 2 + E
    logit_grad = jnp.where(gate_lane, dots * scales * (1.0 - scales), logit_grad).astype(
        jnp.bfloat16
    )
    residual = residual_ref[...]
    rstd = lax.rsqrt(jnp.mean(residual * residual, axis=1, keepdims=True) + NORM_EPS)
    mean = jnp.zeros((quarter, 1), jnp.float32)
    for b in range(E):
        at = slice(b * block, (b + 1) * block)
        two_grad = total[:, at] + matmul(logit_grad, small_ref[b])
        normed = residual[:, at] * rstd
        gain = small_ref[b, 1:2, :].astype(jnp.float32)
        back_ref[:, at] = two_grad
        mean = mean + jnp.sum(two_grad * gain * normed, axis=1, keepdims=True)
        grads = matmul_tn(logit_grad, two_all[fs, own, at])
        sub = lax.broadcasted_iota(jnp.int32, (SMALL, block), 0)
        gain_grad = jnp.sum(two_grad * normed, axis=0, keepdims=True)
        small_grad_ref[:, at] = jnp.where(sub == 1, gain_grad, grads)
    mean = mean / width
    for b in range(E):
        at = slice(b * block, (b + 1) * block)
        gain = small_ref[b, 1:2, :].astype(jnp.float32)
        normed = residual[:, at] * rstd
        grad = cotangent_ref[own, at].astype(jnp.float32) + rstd * (
            back_ref[:, at] * gain - normed * mean
        )
        back_ref[:, at] = grad
        branch_ref[:, at] = grad.astype(jnp.bfloat16)
    for out, back in column[3:]:
        back.wait_recv()
    start = pl.multiple_of(back_width + tp * out_width, 128)
    total = parts[2, :, pl.ds(start, out_width)].astype(jnp.float32)
    for step in range(1, QUARTERS):
        total = total + cols_in[step - 1].astype(jnp.float32)
    output_ref[...] = total.astype(jnp.bfloat16)
    for out, back in along + core_copies[2:] + [side_x, side_y] + column:
        out.wait_send()
    for keep in keeps[-2:]:
        keep.wait()


def expert_call(
    two_rows, router_rows, residual_rows, cotangent, cotangent_all, slabs, small_full, out_width, routed
):
    quarter, width = residual_rows.shape
    rows = quarter * QUARTERS
    back_width = width + SIDE
    block = width // E
    bf, f32 = jnp.bfloat16, jnp.float32
    sds = jax.ShapeDtypeStruct
    vmem = pl.BlockSpec(memory_space=pltpu.VMEM)
    hbm = pl.BlockSpec(memory_space=pl.ANY)
    outs = [
        (sds((rows, out_width), bf), vmem),
        (sds((quarter, width), bf), vmem),
        (sds((quarter, width), f32), vmem),
        (sds((SMALL, width), f32), vmem),
        (sds(slabs.shape, bf), hbm),
    ]
    units = slabs.shape[1]
    return pl.pallas_call(
        functools.partial(expert_kernel, routed),
        name="experts",
        out_shape=[o[0] for o in outs],
        in_specs=[vmem, vmem, vmem, vmem, hbm, hbm, vmem],
        out_specs=[o[1] for o in outs],
        scratch_shapes=[
            pltpu.VMEM((E, rows, back_width), bf),
            pltpu.VMEM((E, rows, width), bf),
            pltpu.VMEM((units, width), bf),
            pltpu.VMEM((units, E * rows), bf),
            pltpu.VMEM((units, rows), f32),
            pltpu.VMEM((5, rows, back_width + width), bf),
            pltpu.VMEM((2, rows, back_width + width), bf),
            pltpu.VMEM((2, rows // 2, back_width + width), bf),
            pltpu.VMEM((2, rows, back_width + width), bf),
            pltpu.VMEM((QUARTERS - 1, quarter, back_width), bf),
            pltpu.VMEM((QUARTERS - 1, rows, out_width), bf),
            pltpu.VMEM((2, units, block), bf),
            pltpu.SemaphoreType.DMA((64,)),
            pltpu.SemaphoreType.DMA((64,)),
            pltpu.SemaphoreType.DMA((24,)),
            pltpu.SemaphoreType.REGULAR,
        ],
        compiler_params=pltpu.CompilerParams(
            collective_id=2, has_side_effects=True, vmem_limit_bytes=62 * 2**20
        ),
    )(two_rows, router_rows, residual_rows, cotangent, cotangent_all, slabs, small_full)


def shards_units(
    tokens,
    cotangent,
    qkv_weight,
    out_weight,
    norm_gains,
    router_weight,
    shared_gate,
    expert_gate_up,
    expert_down,
    shared_gate_up,
    shared_down,
    routes,
    doc_start,
):
    tok_rows, width = tokens.shape
    seq_count = tok_rows // SEQ_DEV
    local_width = qkv_weight.shape[2]
    head_count = local_width // HD
    quarter = tok_rows // QUARTERS
    score_scale = HD ** (-0.5)
    fs_index = lax.axis_index("fs")
    tp_index = lax.axis_index("tp")
    fs_size = E
    query_pos = fs_index * SEQ_DEV + jnp.arange(SEQ_DEV, dtype=jnp.int32)
    positions = jnp.tile(query_pos, seq_count)
    half_cos, half_sin = rope_tables(positions)
    cosine = jnp.concatenate([half_cos, half_cos], axis=1)
    sine = jnp.concatenate([-half_sin, half_sin], axis=1)
    small = jnp.concatenate(
        [
            norm_gains,
            router_weight,
            shared_gate[None],
            jnp.zeros((SMALL - 3 - E, shared_gate.shape[0]), jnp.bfloat16),
        ],
        axis=0,
    )
    routed_units = expert_down.shape[1]
    shared_units = shared_down.shape[0] // fs_size
    units = routed_units + shared_units
    block = expert_down.shape[2]
    expert_up_slabs = jnp.transpose(expert_gate_up, (0, 2, 3, 1))
    shared_up_slabs = jnp.transpose(
        shared_gate_up.reshape(block, 2, fs_size, shared_units), (2, 1, 3, 0)
    )
    up_slabs = jnp.concatenate([expert_up_slabs, shared_up_slabs], axis=2)
    down_slabs = jnp.concatenate(
        [expert_down, shared_down.reshape(fs_size, shared_units, block)], axis=1
    )
    slabs = jnp.concatenate([up_slabs, down_slabs[:, None]], axis=1)
    (
        two_rows,
        residual_rows,
        router_rows,
        attended,
        query_rows,
        slabs,
        cotangent_all,
        kv_all,
        qkv_full,
        out_full,
        small_full,
    ) = forward_call(
        tokens,
        cotangent,
        qkv_weight,
        out_weight,
        small,
        slabs.reshape(fs_size, 3 * units, block),
        cosine,
        sine,
        doc_start[:, None],
        routes,
    )
    output, branch_rows, residual_grad, small_grad, grad_slabs = expert_call(
        two_rows,
        router_rows,
        residual_rows,
        cotangent,
        cotangent_all,
        slabs,
        small_full,
        width // QUARTERS,
        routed_units,
    )
    grad_slabs = lax.all_to_all(
        grad_slabs.reshape(fs_size, 3, units, block), "fs", 0, 0, tiled=True
    )
    small_rows = jnp.transpose(small_full, (1, 0, 2)).reshape(SMALL, width)
    token_rows = lax.dynamic_slice_in_dim(tokens, tp_index * quarter, quarter, 0).astype(
        jnp.float32
    )
    rstd_one = lax.rsqrt(jnp.mean(token_rows * token_rows, axis=1, keepdims=True) + NORM_EPS)
    normed_one = token_rows * rstd_one
    branch_grad = lax.all_gather(branch_rows, "tp", axis=0, tiled=True)
    out_grad = jnp.einsum("tf,td->fd", attended, branch_grad, preferred_element_type=jnp.float32)
    attended_grad = jnp.einsum(
        "tbd,bfd->tf",
        branch_grad.reshape(tok_rows, fs_size, block),
        out_full,
        preferred_element_type=jnp.float32,
    ).astype(jnp.bfloat16)
    grad_heads = attended_grad.reshape(seq_count, SEQ_DEV, head_count, HD)
    query_heads = query_rows.reshape(seq_count, SEQ_DEV, head_count, HD)
    kv_heads = kv_all.reshape(fs_size, seq_count, SEQ_DEV, 2, head_count, HD)
    key_heads, value_heads = kv_heads[:, :, :, 0], kv_heads[:, :, :, 1]
    query_start = doc_start.reshape(seq_count, SEQ_DEV)
    allowed = key_mask(query_pos, query_start, 0, fs_size)[:, None]
    scores = (
        jnp.einsum("pqhd,gpkhd->phqgk", query_heads, key_heads, preferred_element_type=jnp.float32)
        * score_scale
    )
    scores = jnp.where(allowed, scores, NEG_FILL)
    exps = jnp.exp(scores - jnp.max(scores, axis=(3, 4), keepdims=True))
    probs = exps / jnp.sum(exps, axis=(3, 4), keepdims=True)
    weights_grad = jnp.einsum(
        "pqhd,gpkhd->phqgk", grad_heads, value_heads, preferred_element_type=jnp.float32
    )
    delta = jnp.sum(probs * weights_grad, axis=(3, 4), keepdims=True)
    score_grad = (probs * (weights_grad - delta)).astype(jnp.bfloat16)
    query_grad = (
        jnp.einsum("phqgk,gpkhd->pqhd", score_grad, key_heads, preferred_element_type=jnp.float32)
        * score_scale
    )
    key_grad = (
        jnp.einsum(
            "phqgk,pqhd->gpkhd", score_grad, query_heads, preferred_element_type=jnp.float32
        )
        * score_scale
    )
    value_grad = jnp.einsum(
        "phqgk,pqhd->gpkhd",
        probs.astype(jnp.bfloat16),
        grad_heads,
        preferred_element_type=jnp.float32,
    )
    terms = jnp.concatenate(
        [
            key_grad.reshape(fs_size * tok_rows, local_width),
            value_grad.reshape(fs_size * tok_rows, local_width),
        ],
        axis=1,
    ).astype(jnp.bfloat16)
    key_value_sum = lax.psum_scatter(terms, "fs", scatter_dimension=0, tiled=True).astype(
        jnp.float32
    )
    projected_grad = jnp.stack(
        [
            rotate(query_grad.reshape(tok_rows, local_width), half_cos, -half_sin),
            rotate(key_value_sum[:, :local_width], half_cos, -half_sin),
            key_value_sum[:, local_width:],
        ],
        axis=0,
    ).astype(jnp.bfloat16)
    token_all = tokens.astype(jnp.float32)
    rstd_all = lax.rsqrt(jnp.mean(token_all * token_all, axis=1, keepdims=True) + NORM_EPS)
    hidden_one = (token_all * rstd_all * small_rows[0].astype(jnp.float32)[None, :]).astype(
        jnp.bfloat16
    )
    qkv_grad = jnp.einsum(
        "td,jtf->jdf", hidden_one, projected_grad, preferred_element_type=jnp.float32
    )
    one_part = jnp.einsum(
        "jtf,jdf->td", projected_grad, qkv_full, preferred_element_type=jnp.float32
    )
    one_grad = lax.psum_scatter(
        one_part.astype(jnp.bfloat16), "tp", scatter_dimension=0, tiled=True
    ).astype(jnp.float32)
    scaled_one = one_grad * small_rows[0].astype(jnp.float32)[None, :]
    gain_one_grad = jnp.sum(one_grad * normed_one, axis=0)
    input_grad_rows = residual_grad + rstd_one * (
        scaled_one - normed_one * jnp.mean(scaled_one * normed_one, axis=1, keepdims=True)
    )
    input_grad = lax.all_gather(
        input_grad_rows.astype(jnp.bfloat16), "tp", axis=0, tiled=True
    ).astype(jnp.float32)
    small_grad = jnp.concatenate([gain_one_grad[None], small_grad[1 : 3 + E]], axis=0)
    small_own = lax.psum(
        lax.psum_scatter(
            small_grad.astype(jnp.bfloat16), "fs", scatter_dimension=1, tiled=True
        ),
        "tp",
    ).astype(jnp.float32)
    qkv_own = lax.psum_scatter(
        qkv_grad.astype(jnp.bfloat16), "fs", scatter_dimension=1, tiled=True
    ).astype(jnp.float32)
    out_own = lax.psum_scatter(
        out_grad.astype(jnp.bfloat16), "fs", scatter_dimension=1, tiled=True
    ).astype(jnp.float32)
    own = grad_slabs.astype(jnp.float32)
    expert_up_own = jnp.transpose(own[:, :2, :routed_units], (0, 3, 1, 2))
    expert_down_own = own[:, 2, :routed_units]
    shared_up_own = jnp.transpose(own[:, :2, routed_units:], (3, 1, 0, 2)).reshape(
        shared_gate_up.shape
    )
    shared_down_own = own[:, 2, routed_units:].reshape(shared_down.shape)
    return (
        output,
        input_grad,
        qkv_own,
        out_own,
        small_own[:2],
        small_own[2 : 2 + E],
        small_own[2 + E],
        expert_up_own,
        expert_down_own,
        shared_up_own,
        shared_down_own,
    )


def solution(mesh):
    return jax.shard_map(
        shards_units if dict(mesh.shape) == {"fs": E, "tp": QUARTERS} else shards_gathered,
        mesh=mesh,
        in_specs=(
            P("fs", None),
            P("fs", None),
            P(None, "fs", "tp"),
            P("tp", "fs"),
            P(None, "fs"),
            P(None, "fs"),
            P("fs"),
            P(None, "fs", None, "tp"),
            P(None, "tp", "fs"),
            P("fs", None, "tp"),
            P("tp", "fs"),
            P("fs", None),
            P("fs"),
        ),
        out_specs=(
            P("fs", "tp"),
            P("fs", None),
            P(None, "fs", "tp"),
            P("tp", "fs"),
            P(None, "fs"),
            P(None, "fs"),
            P("fs"),
            P(None, "fs", None, "tp"),
            P(None, "tp", "fs"),
            P("fs", None, "tp"),
            P("tp", "fs"),
        ),
        check_vma=False,
    )
```

```python
import functools
import math

import jax
import jax.numpy as jnp
from jax import lax
from jax.experimental import pallas as pl
from jax.experimental.pallas import tpu as pltpu
from jax.sharding import PartitionSpec as P

HD = 128
E = 8
SEQ_DEV = 128
SIDE = 128


NORM_EPS = 1e-06
NEG_FILL = -1e30
ROPE_BASE = 1000000.0


def rope_tables(positions):
    half_size = HD // 2
    frequency = ROPE_BASE ** (-(jnp.arange(half_size, dtype=jnp.float32) * 2.0 / HD))
    angles = positions.astype(jnp.float32)[:, None] * frequency[None, :]
    return (jnp.cos(angles), jnp.sin(angles))


def rotate(values, cosine, sine_table):
    shaped = values.reshape(values.shape[0], -1, HD)
    half_size = HD // 2
    first_half = shaped[..., :half_size]
    second_half = shaped[..., half_size:]
    cos_part = cosine[:, None, :]
    sin_part = sine_table[:, None, :]
    turned = jnp.concatenate(
        [
            first_half * cos_part - second_half * sin_part,
            second_half * cos_part + first_half * sin_part,
        ],
        axis=-1,
    )
    return turned.reshape(values.shape)


def key_mask(query_pos, query_start, first_dev, group_size):
    key_pos = (first_dev + jnp.arange(group_size, dtype=jnp.int32)[:, None]) * SEQ_DEV + jnp.arange(
        SEQ_DEV, dtype=jnp.int32
    )[None, :]
    key_pos = key_pos[None, None, :, :]
    return (key_pos <= query_pos[None, :, None, None]) & (key_pos >= query_start[:, :, None, None])


def shards_gathered(
    tokens,
    cotangent,
    qkv_weight,
    out_weight,
    norm_gains,
    router_weight,
    shared_gate,
    expert_gate_up,
    expert_down,
    shared_gate_up,
    shared_down,
    routes,
    doc_start,
):
    tok_rows = tokens.shape[0]
    seq_count = tok_rows // SEQ_DEV
    local_width = qkv_weight.shape[2]
    head_count = local_width // HD
    out_width = tokens.shape[1] // lax.axis_size("tp")
    score_scale = HD ** (-0.5)
    fs_index = lax.axis_index("fs")
    tp_index = lax.axis_index("tp")
    query_pos = fs_index * SEQ_DEV + jnp.arange(SEQ_DEV, dtype=jnp.int32)
    positions = jnp.tile(query_pos, seq_count)
    query_start = doc_start.reshape(seq_count, SEQ_DEV)
    cosine, sine_table = rope_tables(positions)
    group_limit = max(1, 512 // SEQ_DEV)
    qkv_full, out_full, gains_full, router_full, shared_gate_full = (
        lax.all_gather(qkv_weight, "fs", axis=1, tiled=True),
        lax.all_gather(out_weight, "fs", axis=1, tiled=True),
        lax.all_gather(norm_gains, "fs", axis=1, tiled=True),
        lax.all_gather(router_weight, "fs", axis=1, tiled=True),
        lax.all_gather(shared_gate, "fs", axis=0, tiled=True),
    )
    token_float = tokens.astype(jnp.float32)
    rstd_one = lax.rsqrt(jnp.mean(token_float * token_float, axis=1, keepdims=True) + NORM_EPS)
    normed_one = token_float * rstd_one
    hidden_one = (normed_one * gains_full[0].astype(jnp.float32)[None, :]).astype(jnp.bfloat16)
    projected = jnp.einsum("td,jdf->jtf", hidden_one, qkv_full, preferred_element_type=jnp.float32)
    query_rows = rotate(projected[0], cosine, sine_table).astype(jnp.bfloat16)
    key_own = rotate(projected[1], cosine, sine_table).astype(jnp.bfloat16)
    value_own = projected[2].astype(jnp.bfloat16)
    query_heads = query_rows.reshape(seq_count, SEQ_DEV, head_count, HD)

    def score_block(key_group, first_dev):
        allowed = key_mask(query_pos, query_start, first_dev, key_group.shape[0])[:, None]
        scores = (
            jnp.einsum(
                "pqhd,gpkhd->phqgk", query_heads, key_group, preferred_element_type=jnp.float32
            )
            * score_scale
        )
        return (jnp.where(allowed, scores, NEG_FILL), allowed)

    def forward_update(running, key_group, value_group, first_dev):
        run_max, run_sum, accumulated = running
        scores, allowed = score_block(key_group, first_dev)
        new_max = jnp.maximum(run_max, jnp.max(scores, axis=(3, 4)))
        weights = jnp.where(allowed, jnp.exp(scores - new_max[..., None, None]), 0.0)
        factor = jnp.exp(run_max - new_max)
        new_sum = run_sum * factor + jnp.sum(weights, axis=(3, 4))
        mixed_part = jnp.einsum(
            "phqgk,gpkhd->pqhd",
            weights.astype(jnp.bfloat16),
            value_group,
            preferred_element_type=jnp.float32,
        )
        new_accum = accumulated * jnp.transpose(factor, (0, 2, 1))[..., None] + mixed_part
        return (new_max, new_sum, new_accum)

    initial = (
        jnp.full((seq_count, head_count, SEQ_DEV), NEG_FILL, jnp.float32),
        jnp.zeros((seq_count, head_count, SEQ_DEV), jnp.float32),
        jnp.zeros((seq_count, SEQ_DEV, head_count, HD), jnp.float32),
    )
    running = initial
    key_piece = lax.all_gather(key_own, "fs", axis=0, tiled=True)
    value_piece = lax.all_gather(value_own, "fs", axis=0, tiled=True)
    shard_count = key_piece.shape[0] // tok_rows
    group_size = math.gcd(shard_count, group_limit)
    step_count = shard_count // group_size
    shaped = (step_count, group_size, seq_count, SEQ_DEV, head_count, HD)
    first_dev = jnp.int32(0) // tok_rows

    def one_step(carried, inputs):
        key_group, value_group, group_index = inputs
        start_dev = group_index * group_size
        updated = lax.cond(
            start_dev <= fs_index,
            lambda state_in: forward_update(state_in, key_group, value_group, start_dev),
            lambda state_in: state_in,
            carried,
        )
        return (updated, None)

    running, ignored = lax.scan(
        one_step,
        running,
        (
            key_piece.reshape(shaped),
            value_piece.reshape(shaped),
            jnp.arange(step_count, dtype=jnp.int32),
        ),
    )
    run_max, run_sum, accumulated = running
    attended_heads = (accumulated / jnp.transpose(run_sum, (0, 2, 1))[..., None]).astype(
        jnp.bfloat16
    )
    log_total = run_max + jnp.log(run_sum)
    attended = attended_heads.reshape(tok_rows, local_width)
    branch_part = jnp.dot(attended, out_full, preferred_element_type=jnp.float32)
    branch = lax.psum(branch_part.astype(jnp.bfloat16), "tp").astype(jnp.float32)
    residual = token_float + branch
    rstd_two = lax.rsqrt(jnp.mean(residual * residual, axis=1, keepdims=True) + NORM_EPS)
    normed_two = residual * rstd_two
    hidden_two = (normed_two * gains_full[1].astype(jnp.float32)[None, :]).astype(jnp.bfloat16)
    expert_gate_all, expert_down_all, shared_up_all, shared_down_all = (
        lax.all_gather(expert_gate_up, "fs", axis=1, tiled=True),
        lax.all_gather(expert_down, "fs", axis=2, tiled=True),
        lax.all_gather(shared_gate_up, "fs", axis=0, tiled=True),
        lax.all_gather(shared_down, "fs", axis=1, tiled=True),
    )
    logits = jnp.einsum("td,ed->te", hidden_two, router_full, preferred_element_type=jnp.float32)
    router_probs = jax.nn.softmax(logits, axis=-1)
    chosen = jnp.sum(
        (routes[:, :, None] == jnp.arange(E, dtype=jnp.int32)[None, None, :]).astype(jnp.float32),
        axis=1,
    )
    gate_weights = router_probs * chosen
    gate_up = jnp.einsum(
        "td,edkf->tekf", hidden_two, expert_gate_all, preferred_element_type=jnp.float32
    )
    gate_part = gate_up[:, :, 0]
    up_part = gate_up[:, :, 1]
    gate_sigmoid = jax.nn.sigmoid(gate_part)
    active = gate_part * gate_sigmoid * up_part
    hidden = (gate_weights[:, :, None] * active).astype(jnp.bfloat16)
    shared_in = jnp.einsum(
        "td,dkf->tkf", hidden_two, shared_up_all, preferred_element_type=jnp.float32
    )
    shared_gate_in = shared_in[:, 0]
    shared_up_in = shared_in[:, 1]
    shared_sigmoid = jax.nn.sigmoid(shared_gate_in)
    shared_active = shared_gate_in * shared_sigmoid * shared_up_in
    gate_logit = jnp.einsum(
        "td,d->t", hidden_two, shared_gate_full, preferred_element_type=jnp.float32
    )
    gate_value = jax.nn.sigmoid(gate_logit)
    shared_hidden = (gate_value[:, None] * shared_active).astype(jnp.bfloat16)
    mixture_part = jnp.einsum(
        "tef,efd->td", hidden, expert_down_all, preferred_element_type=jnp.float32
    ) + jnp.dot(shared_hidden, shared_down_all, preferred_element_type=jnp.float32)
    mixture = lax.psum_scatter(
        mixture_part.astype(jnp.bfloat16), "tp", scatter_dimension=1, tiled=True
    ).astype(jnp.float32)
    output = (
        lax.dynamic_slice_in_dim(residual, tp_index * out_width, out_width, 1) + mixture
    ).astype(jnp.bfloat16)
    qkv_back, out_back, gains_back, router_back, shared_gate_back = (
        lax.all_gather(qkv_weight, "fs", axis=1, tiled=True),
        lax.all_gather(out_weight, "fs", axis=1, tiled=True),
        lax.all_gather(norm_gains, "fs", axis=1, tiled=True),
        lax.all_gather(router_weight, "fs", axis=1, tiled=True),
        lax.all_gather(shared_gate, "fs", axis=0, tiled=True),
    )
    expert_gate_back, expert_down_back, shared_up_back, shared_down_back = (
        lax.all_gather(expert_gate_up, "fs", axis=1, tiled=True),
        lax.all_gather(expert_down, "fs", axis=2, tiled=True),
        lax.all_gather(shared_gate_up, "fs", axis=0, tiled=True),
        lax.all_gather(shared_down, "fs", axis=1, tiled=True),
    )
    hidden_grad = jnp.einsum(
        "td,efd->tef", cotangent, expert_down_back, preferred_element_type=jnp.float32
    )
    expert_down_grad = jnp.einsum(
        "tef,td->efd", hidden, cotangent, preferred_element_type=jnp.float32
    )
    shared_grad = jnp.einsum(
        "td,fd->tf", cotangent, shared_down_back, preferred_element_type=jnp.float32
    )
    shared_down_grad = jnp.einsum(
        "tf,td->fd", shared_hidden, cotangent, preferred_element_type=jnp.float32
    )
    gate_dot = jnp.sum(active * hidden_grad, axis=2)
    shared_dot = jnp.sum(shared_active * shared_grad, axis=1)
    active_grad = gate_weights[:, :, None] * hidden_grad
    gate_grad = active_grad * up_part * gate_sigmoid * (1.0 + gate_part * (1.0 - gate_sigmoid))
    up_grad = active_grad * gate_part * gate_sigmoid
    gate_up_grad = jnp.stack([gate_grad, up_grad], axis=2).astype(jnp.bfloat16)
    shared_active_grad = gate_value[:, None] * shared_grad
    shared_gate_grad = (
        shared_active_grad
        * shared_up_in
        * shared_sigmoid
        * (1.0 + shared_gate_in * (1.0 - shared_sigmoid))
    )
    shared_unit_grad = shared_active_grad * shared_gate_in * shared_sigmoid
    shared_up_grad = jnp.stack([shared_gate_grad, shared_unit_grad], axis=1).astype(jnp.bfloat16)
    expert_gate_grad = jnp.einsum(
        "td,tekf->edkf", hidden_two, gate_up_grad, preferred_element_type=jnp.float32
    )
    shared_proj_grad = jnp.einsum(
        "td,tkf->dkf", hidden_two, shared_up_grad, preferred_element_type=jnp.float32
    )
    input_part = jnp.einsum(
        "tekf,edkf->td", gate_up_grad, expert_gate_back, preferred_element_type=jnp.float32
    ) + jnp.einsum(
        "tkf,dkf->td", shared_up_grad, shared_up_back, preferred_element_type=jnp.float32
    )
    input_sum, gate_sum, shared_sum = (
        lax.psum(input_part.astype(jnp.bfloat16), "tp").astype(jnp.float32),
        lax.psum(gate_dot.astype(jnp.bfloat16), "tp").astype(jnp.float32),
        lax.psum(shared_dot.astype(jnp.bfloat16), "tp").astype(jnp.float32),
    )
    chosen_grad = chosen * gate_sum
    logit_grad = (
        router_probs * (chosen_grad - jnp.sum(router_probs * chosen_grad, axis=1, keepdims=True))
    ).astype(jnp.bfloat16)
    gate_logit_grad = (shared_sum * gate_value * (1.0 - gate_value)).astype(jnp.bfloat16)
    router_grad = jnp.einsum(
        "te,td->ed", logit_grad, hidden_two, preferred_element_type=jnp.float32
    )
    shared_vector_grad = jnp.einsum(
        "t,td->d", gate_logit_grad, hidden_two, preferred_element_type=jnp.float32
    )
    two_grad = (
        input_sum
        + jnp.einsum("te,ed->td", logit_grad, router_back, preferred_element_type=jnp.float32)
        + gate_logit_grad.astype(jnp.float32)[:, None]
        * shared_gate_back.astype(jnp.float32)[None, :]
    )
    scaled_two = two_grad * gains_back[1].astype(jnp.float32)[None, :]
    gain_two_grad = jnp.sum(two_grad * normed_two, axis=0)
    residual_grad = cotangent.astype(jnp.float32) + rstd_two * (
        scaled_two - normed_two * jnp.mean(scaled_two * normed_two, axis=1, keepdims=True)
    )
    branch_grad = residual_grad.astype(jnp.bfloat16)
    out_grad = jnp.einsum("tf,td->fd", attended, branch_grad, preferred_element_type=jnp.float32)
    attended_grad = jnp.einsum(
        "td,fd->tf", branch_grad, out_back, preferred_element_type=jnp.float32
    ).astype(jnp.bfloat16)
    grad_heads = attended_grad.reshape(seq_count, SEQ_DEV, head_count, HD)
    delta_rows = jnp.einsum(
        "pqhd,pqhd->phq", grad_heads, attended_heads, preferred_element_type=jnp.float32
    )
    key_all, value_all = (
        lax.all_gather(key_own, "fs", axis=0, tiled=True),
        lax.all_gather(value_own, "fs", axis=0, tiled=True),
    )
    device_count = key_all.shape[0] // tok_rows
    back_group = math.gcd(device_count, group_limit)
    back_steps = device_count // back_group
    back_shape = (back_steps, back_group, seq_count, SEQ_DEV, head_count, HD)

    def backward_update(key_group, value_group, start_dev):
        scores, allowed = score_block(key_group, start_dev)
        probs_block = jnp.where(allowed, jnp.exp(scores - log_total[..., None, None]), 0.0)
        weights_grad = jnp.einsum(
            "pqhd,gpkhd->phqgk", grad_heads, value_group, preferred_element_type=jnp.float32
        )
        score_grad = (probs_block * (weights_grad - delta_rows[..., None, None])).astype(
            jnp.bfloat16
        )
        query_part = (
            jnp.einsum(
                "phqgk,gpkhd->pqhd", score_grad, key_group, preferred_element_type=jnp.float32
            )
            * score_scale
        )
        key_part = (
            jnp.einsum(
                "phqgk,pqhd->gpkhd", score_grad, query_heads, preferred_element_type=jnp.float32
            )
            * score_scale
        )
        value_part = jnp.einsum(
            "phqgk,pqhd->gpkhd",
            probs_block.astype(jnp.bfloat16),
            grad_heads,
            preferred_element_type=jnp.float32,
        )
        return (query_part, key_part, value_part)

    empty_grads = (
        jnp.zeros((seq_count, SEQ_DEV, head_count, HD), jnp.float32),
        jnp.zeros((back_group, seq_count, SEQ_DEV, head_count, HD), jnp.float32),
        jnp.zeros((back_group, seq_count, SEQ_DEV, head_count, HD), jnp.float32),
    )
    scan_inputs = (
        key_all.reshape(back_shape),
        value_all.reshape(back_shape),
        jnp.arange(back_steps, dtype=jnp.int32),
    )

    def back_step(query_acc, inputs):
        key_group, value_group, group_index = inputs
        start_dev = group_index * back_group
        query_part, key_part, value_part = lax.cond(
            start_dev <= fs_index,
            lambda ignored_in: backward_update(key_group, value_group, start_dev),
            lambda ignored_in: empty_grads,
            key_group,
        )
        term_rows = jnp.concatenate(
            [
                key_part.reshape(back_group * tok_rows, local_width),
                value_part.reshape(back_group * tok_rows, local_width),
            ],
            axis=1,
        )
        return (query_acc + query_part, term_rows)

    query_grad, key_value_terms = lax.scan(back_step, empty_grads[0], scan_inputs)
    key_value_sum = lax.psum_scatter(
        key_value_terms.reshape(device_count * tok_rows, 2 * local_width).astype(jnp.bfloat16),
        "fs",
        scatter_dimension=0,
        tiled=True,
    ).astype(jnp.float32)
    key_grad_rows = key_value_sum[:, :local_width]
    value_grad_rows = key_value_sum[:, local_width:]
    projected_grad = jnp.stack(
        [
            rotate(query_grad.reshape(tok_rows, local_width), cosine, -sine_table),
            rotate(key_grad_rows, cosine, -sine_table),
            value_grad_rows,
        ],
        axis=0,
    ).astype(jnp.bfloat16)
    qkv_grad = jnp.einsum(
        "td,jtf->jdf", hidden_one, projected_grad, preferred_element_type=jnp.float32
    )
    one_part = jnp.einsum(
        "jtf,jdf->td", projected_grad, qkv_back, preferred_element_type=jnp.float32
    )
    one_grad = lax.psum(one_part.astype(jnp.bfloat16), "tp").astype(jnp.float32)
    scaled_one = one_grad * gains_back[0].astype(jnp.float32)[None, :]
    gain_one_grad = jnp.sum(one_grad * normed_one, axis=0)
    input_grad = residual_grad + rstd_one * (
        scaled_one - normed_one * jnp.mean(scaled_one * normed_one, axis=1, keepdims=True)
    )
    gains_grad = jnp.stack([gain_one_grad, gain_two_grad], axis=0)
    reduced = (
        lax.psum_scatter(
            qkv_grad.astype(jnp.bfloat16), "fs", scatter_dimension=1, tiled=True
        ).astype(jnp.float32),
        lax.psum_scatter(
            out_grad.astype(jnp.bfloat16), "fs", scatter_dimension=1, tiled=True
        ).astype(jnp.float32),
        lax.psum_scatter(
            gains_grad.astype(jnp.bfloat16), "fs", scatter_dimension=1, tiled=True
        ).astype(jnp.float32),
        lax.psum_scatter(
            router_grad.astype(jnp.bfloat16), "fs", scatter_dimension=1, tiled=True
        ).astype(jnp.float32),
        lax.psum_scatter(
            shared_vector_grad.astype(jnp.bfloat16), "fs", scatter_dimension=0, tiled=True
        ).astype(jnp.float32),
        lax.psum_scatter(
            expert_gate_grad.astype(jnp.bfloat16), "fs", scatter_dimension=1, tiled=True
        ).astype(jnp.float32),
        lax.psum_scatter(
            expert_down_grad.astype(jnp.bfloat16), "fs", scatter_dimension=2, tiled=True
        ).astype(jnp.float32),
        lax.psum_scatter(
            shared_proj_grad.astype(jnp.bfloat16), "fs", scatter_dimension=0, tiled=True
        ).astype(jnp.float32),
        lax.psum_scatter(
            shared_down_grad.astype(jnp.bfloat16), "fs", scatter_dimension=1, tiled=True
        ).astype(jnp.float32),
    )
    return (
        output,
        input_grad,
        reduced[0],
        reduced[1],
        reduced[2],
        reduced[3],
        reduced[4],
        reduced[5],
        reduced[6],
        reduced[7],
        reduced[8],
    )


MESH = pl.DeviceIdType.MESH
X_BIT, Y_BIT, CORE_BIT = 2, 4, 1
QUARTERS = 4
SMALL = 16


def flip(index, bit):
    return index + bit - 2 * bit * ((index // bit) % 2)


class Links:
    def __init__(self, send, recv, local):
        self.fs = lax.axis_index("fs")
        self.tp = lax.axis_index("tp")
        self.send, self.recv, self.local = send, recv, local
        self.used = 0
        self.used_local = 0

    def peer(self, bits):
        where = self.fs
        for bit in (X_BIT, Y_BIT, CORE_BIT):
            if bits & bit:
                where = flip(where, bit)
        return where

    def along(self, step):
        return lax.rem(self.tp + step, QUARTERS)

    def remote(self, source, target, device, landing):
        i = self.used
        self.used += 1
        out = pltpu.make_async_remote_copy(
            src_ref=source,
            dst_ref=target,
            send_sem=self.send.at[i],
            recv_sem=self.recv.at[i],
            device_id=device,
            device_id_type=MESH,
        )
        back = pltpu.make_async_remote_copy(
            src_ref=landing,
            dst_ref=landing,
            send_sem=self.send.at[i],
            recv_sem=self.recv.at[i],
            device_id=device,
            device_id_type=MESH,
        )
        return out, back

    def inside(self, source, target):
        i = self.used_local
        self.used_local += 1
        return pltpu.make_async_copy(source, target, self.local.at[i])

    def greet(self, plane, column):
        barrier = pltpu.get_barrier_semaphore()
        for bits in plane:
            pl.semaphore_signal(
                barrier, inc=1, device_id=(self.peer(bits), self.tp), device_id_type=MESH
            )
        for step in column:
            pl.semaphore_signal(
                barrier, inc=1, device_id=(self.fs, self.along(step)), device_id_type=MESH
            )
        pl.semaphore_wait(barrier, len(plane) + len(column))


class Gather:
    def __init__(self, links, source, place, half):
        self.links = links
        fs, tp = links.fs, links.tp

        def to(bits, what, landing, origin=None):
            return links.remote(
                what if origin is None else origin, what, (links.peer(bits), tp), landing
            )

        p = links.peer
        self.keep = None if source is None else links.inside(source, place(fs))
        self.to_x = to(X_BIT, place(fs), place(p(X_BIT)), source)
        self.to_y = to(Y_BIT, place(fs), place(p(Y_BIT)), source)
        self.to_c = to(CORE_BIT, place(fs), place(p(CORE_BIT)), source)
        xy = X_BIT + Y_BIT
        self.x_on = to(Y_BIT, half(p(X_BIT), 0), half(p(xy), 0))
        self.y_on = to(X_BIT, half(p(Y_BIT), 1), half(p(xy), 1))
        self.x_core = to(CORE_BIT, place(p(X_BIT)), place(p(X_BIT + CORE_BIT)))
        self.y_core = to(CORE_BIT, place(p(Y_BIT)), place(p(Y_BIT + CORE_BIT)))
        self.d_core = [
            to(CORE_BIT, half(p(xy), h), half(p(xy + CORE_BIT), h)) for h in range(2)
        ]

    def first(self):
        self.to_x[0].start()
        self.to_y[0].start()
        self.to_c[0].start()
        if self.keep is not None:
            self.keep.start()

    def second(self):
        self.to_x[1].wait_recv()
        self.x_on[0].start()
        self.x_core[0].start()
        self.to_y[1].wait_recv()
        self.y_on[0].start()
        self.y_core[0].start()

    def third(self):
        self.x_on[1].wait_recv()
        self.d_core[0][0].start()
        self.y_on[1].wait_recv()
        self.d_core[1][0].start()

    def last(self):
        if self.keep is not None:
            self.keep.wait()
        for out, back in (self.to_c, self.x_core, self.y_core, *self.d_core):
            back.wait_recv()
        for out, back in (
            self.to_x,
            self.to_y,
            self.to_c,
            self.x_on,
            self.y_on,
            self.x_core,
            self.y_core,
            *self.d_core,
        ):
            out.wait_send()


def turn(values, cosine, sine_signed):
    parts = []
    for h in range(values.shape[1] // HD):
        v = values[:, h * HD : (h + 1) * HD]
        parts.append(v * cosine + pltpu.roll(v, HD // 2, 1) * sine_signed)
    return jnp.concatenate(parts, axis=1)


def matmul(a, b):
    return jnp.dot(a, b, preferred_element_type=jnp.float32)


def matmul_nt(a, b):
    return lax.dot_general(a, b, (((1,), (1,)), ((), ())), preferred_element_type=jnp.float32)


def matmul_tn(a, b):
    return lax.dot_general(a, b, (((0,), (0,)), ((), ())), preferred_element_type=jnp.float32)


def forward_kernel(
    tokens_ref,
    cotangent_ref,
    qkv_ref,
    out_ref,
    small_ref,
    slabs_ref,
    cos_ref,
    sin_ref,
    start_ref,
    routes_ref,
    two_ref,
    residual_ref,
    scales_ref,
    attended_ref,
    query_ref,
    hidden_buf,
    slabs_all,
    cotangent_all,
    kv_out,
    qkv_out,
    out_out,
    small_out,
    qkv_full,
    out_full,
    small_full,
    kv_own,
    kv_full,
    branch_buf,
    branch_in,
    send,
    recv,
    local,
):
    links = Links(send, recv, local)
    fs, tp = links.fs, links.tp
    rows, width = tokens_ref.shape
    block = width // E
    local_width = qkv_ref.shape[2]
    heads = local_width // HD
    seqs = rows // SEQ_DEV
    quarter = rows // QUARTERS

    def at_rows(index, size):
        return pl.ds(pl.multiple_of(index * size, size), size)

    links.greet(range(1, 8), range(1, QUARTERS))
    small = Gather(
        links, small_ref, lambda f: small_full.at[f], lambda f, h: small_full.at[f, :, pl.ds(h * 128, 128)]
    )
    qkv = Gather(
        links,
        qkv_ref,
        lambda f: qkv_full.at[:, at_rows(f, block)],
        lambda f, h: qkv_full.at[:, pl.ds(pl.multiple_of(f * block + h * (block // 2), block // 2), block // 2)],
    )
    outs = Gather(
        links,
        out_ref,
        lambda f: out_full.at[f],
        lambda f, h: out_full.at[f, pl.ds(h * (local_width // 2), local_width // 2)],
    )
    small.first()
    qkv.first()
    small.second()
    small.third()
    small.last()
    tokens = tokens_ref[...].astype(jnp.float32)
    rstd_one = lax.rsqrt(jnp.mean(tokens * tokens, axis=1, keepdims=True) + NORM_EPS)
    for b in range(E):
        cols = slice(b * block, (b + 1) * block)
        gain = small_full[b, 0:1, :].astype(jnp.float32)
        hidden_buf[:, cols] = (tokens[:, cols] * rstd_one * gain).astype(jnp.bfloat16)
    qkv.second()
    qkv.third()
    outs.first()
    qkv.last()
    hidden = hidden_buf[...]
    cosine, sine = cos_ref[...], sin_ref[...]
    kv_own[:, :local_width] = turn(matmul(hidden, qkv_full[1]), cosine, sine).astype(jnp.bfloat16)
    kv_own[:, local_width:] = matmul(hidden, qkv_full[2]).astype(jnp.bfloat16)
    kv = Gather(
        links,
        kv_own,
        lambda f: kv_full.at[f],
        lambda f, h: kv_full.at[f, pl.ds(h * SEQ_DEV, SEQ_DEV)],
    )
    kv.first()
    qkv_keep = links.inside(qkv_full, qkv_out)
    qkv_keep.start()
    query_ref[...] = turn(matmul(hidden, qkv_full[0]), cosine, sine).astype(jnp.bfloat16)
    outs.second()
    kv.second()
    outs.third()
    kv.third()
    slab_copies = []
    for bits in (6, 7, 2, 3, 4, 5, 1):
        peer = links.peer(bits)
        slab_copies.append(
            links.remote(slabs_ref.at[peer], slabs_all.at[fs], (peer, tp), slabs_all.at[peer])
        )
    for out, back in slab_copies:
        out.start()
    slab_own = links.inside(slabs_ref.at[fs], slabs_all.at[fs])
    slab_own.start()
    cot = Gather(
        links,
        cotangent_ref,
        lambda f: cotangent_all.at[f],
        lambda f, h: cotangent_all.at[f, pl.ds(h * SEQ_DEV, SEQ_DEV)],
    )
    cot.first()
    kv.last()
    kv_keep = links.inside(kv_full, kv_out)
    kv_keep.start()
    length = E * SEQ_DEV
    key_pos = lax.broadcasted_iota(jnp.int32, (SEQ_DEV, length), 1)
    query_pos = fs * SEQ_DEV + lax.broadcasted_iota(jnp.int32, (SEQ_DEV, length), 0)
    for s in range(seqs):
        here = slice(s * SEQ_DEV, (s + 1) * SEQ_DEV)
        allowed = (key_pos <= query_pos) & (key_pos >= start_ref[here, :])
        for h in range(heads):
            cols = slice(h * HD, (h + 1) * HD)
            vcols = slice(local_width + h * HD, local_width + (h + 1) * HD)
            keys = kv_full[:, here, cols].reshape(length, HD)
            values = kv_full[:, here, vcols].reshape(length, HD)
            scores = matmul_nt(query_ref[here, cols], keys) * (HD ** (-0.5))
            scores = jnp.where(allowed, scores, NEG_FILL)
            top = jnp.max(scores, axis=1, keepdims=True)
            weights = jnp.exp(scores - top)
            weights = weights / jnp.sum(weights, axis=1, keepdims=True)
            attended_ref[here, cols] = matmul(weights.astype(jnp.bfloat16), values).astype(
                jnp.bfloat16
            )
    outs.last()
    out_keep = links.inside(out_full, out_out)
    out_keep.start()
    small_keep = links.inside(small_full, small_out)
    small_keep.start()
    attended = attended_ref[...]
    for b in range(E):
        branch_buf[:, b * block : (b + 1) * block] = matmul(attended, out_full[b]).astype(
            jnp.bfloat16
        )
    branch = []
    for step in range(1, QUARTERS):
        peer = links.along(step)
        branch.append(
            links.remote(
                branch_buf.at[at_rows(peer, quarter)],
                branch_in.at[step - 1],
                (fs, peer),
                branch_in.at[step - 1],
            )
        )
    for out, back in branch:
        out.start()
    cot.second()
    for out, back in branch:
        back.wait_recv()
    mine = at_rows(tp, quarter)
    total = branch_buf[mine, :].astype(jnp.float32)
    for step in range(1, QUARTERS):
        total = total + branch_in[step - 1].astype(jnp.float32)
    residual = tokens_ref[mine, :].astype(jnp.float32) + total
    residual_ref[...] = residual
    rstd_two = lax.rsqrt(jnp.mean(residual * residual, axis=1, keepdims=True) + NORM_EPS)
    logits = jnp.zeros((quarter, SMALL), jnp.float32)
    for b in range(E):
        cols = slice(b * block, (b + 1) * block)
        gain = small_full[b, 1:2, :].astype(jnp.float32)
        part = (residual[:, cols] * rstd_two * gain).astype(jnp.bfloat16)
        two_ref[:, cols] = part
        logits = logits + matmul_nt(part, small_full[b])
    lane = lax.broadcasted_iota(jnp.int32, (quarter, SMALL), 1)
    routed = (lane >= 2) & (lane < 2 + E)
    masked = jnp.where(routed, logits, NEG_FILL)
    odds = jnp.exp(masked - jnp.max(masked, axis=1, keepdims=True))
    odds = jnp.where(routed, odds, 0.0)
    probs = odds / jnp.sum(odds, axis=1, keepdims=True)
    routes = routes_ref[mine, :]
    chosen = jnp.zeros((quarter, SMALL), jnp.float32)
    for k in range(routes.shape[1]):
        chosen = chosen + (routes[:, k : k + 1] == lane - 2).astype(jnp.float32)
    gate_value = 1.0 / (1.0 + jnp.exp(-logits))
    scales = jnp.where(lane == 2 + E, gate_value, probs * chosen)
    scales_ref[...] = jnp.concatenate([scales, probs, chosen], axis=1)
    high = scales.astype(jnp.bfloat16)
    low = (scales - high.astype(jnp.float32)).astype(jnp.bfloat16)
    two_ref[:, width:] = jnp.concatenate(
        [high, low, jnp.zeros((quarter, SIDE - 2 * SMALL), jnp.bfloat16)], axis=1
    )
    cot.third()
    cot.last()
    for out, back in slab_copies:
        back.wait_recv()
    slab_own.wait()
    for out, back in slab_copies + branch:
        out.wait_send()
    for copy in (qkv_keep, kv_keep, out_keep, small_keep):
        copy.wait()


def forward_call(tokens, cotangent, qkv_weight, out_weight, small, slabs, cosine, sine, start, routes):
    rows, width = tokens.shape
    block = width // E
    local_width = qkv_weight.shape[2]
    quarter = rows // QUARTERS
    bf, f32 = jnp.bfloat16, jnp.float32
    sds = jax.ShapeDtypeStruct
    vmem = pl.BlockSpec(memory_space=pltpu.VMEM)
    hbm = pl.BlockSpec(memory_space=pl.ANY)
    outs = [
        (sds((quarter, width + SIDE), bf), vmem),
        (sds((quarter, width), f32), vmem),
        (sds((quarter, 3 * SMALL), f32), vmem),
        (sds((rows, local_width), bf), vmem),
        (sds((rows, local_width), bf), vmem),
        (sds((rows, width), bf), vmem),
        (sds(slabs.shape, bf), hbm),
        (sds((E, rows, width), bf), hbm),
        (sds((E, rows, 2 * local_width), bf), hbm),
        (sds((3, width, local_width), bf), hbm),
        (sds((E, local_width, block), bf), hbm),
        (sds((E, SMALL, block), bf), hbm),
    ]
    return pl.pallas_call(
        forward_kernel,
        name="attention_forward",
        out_shape=[o[0] for o in outs],
        in_specs=[vmem, hbm, hbm, hbm, hbm, hbm, vmem, vmem, vmem, vmem],
        out_specs=[o[1] for o in outs],
        scratch_shapes=[
            pltpu.VMEM((3, width, local_width), bf),
            pltpu.VMEM((E, local_width, block), bf),
            pltpu.VMEM((E, SMALL, block), bf),
            pltpu.VMEM((rows, 2 * local_width), bf),
            pltpu.VMEM((E, rows, 2 * local_width), bf),
            pltpu.VMEM((rows, width), bf),
            pltpu.VMEM((QUARTERS - 1, quarter, width), bf),
            pltpu.SemaphoreType.DMA((64,)),
            pltpu.SemaphoreType.DMA((64,)),
            pltpu.SemaphoreType.DMA((16,)),
        ],
        compiler_params=pltpu.CompilerParams(
            collective_id=1, has_side_effects=True, vmem_limit_bytes=56 * 2**20
        ),
    )(tokens, cotangent, qkv_weight, out_weight, small, slabs, cosine, sine, start, routes)


def flip_by(index, bits):
    total = 0
    for bit in (1, 2, 4):
        a, b = (index // bit) % 2, (bits // bit) % 2
        total = total + bit * (a + b - 2 * a * b)
    return total


def expert_kernel(
    routed,
    two_ref,
    router_ref,
    residual_ref,
    cotangent_ref,
    cotangent_all,
    slabs_ref,
    small_ref,
    output_ref,
    branch_ref,
    back_ref,
    small_grad_ref,
    grads_out,
    two_all,
    cot_all,
    weights,
    units,
    first,
    parts,
    core_in,
    diag_in,
    side_in,
    rows_in,
    cols_in,
    staged,
    send,
    recv,
    local,
    credit,
):
    links = Links(send, recv, local)
    fs, tp = links.fs, links.tp
    quarter = two_ref.shape[0]
    rows = quarter * QUARTERS
    width = residual_ref.shape[1]
    block = width // E
    count = weights.shape[0] // 3
    out_width = output_ref.shape[1]
    back_width = width + SIDE
    whole = back_width + width

    def at_rows(index, size):
        return pl.ds(pl.multiple_of(index * size, size), size)

    links.greet(range(1, 8), range(1, QUARTERS))
    along = []
    for step in range(1, QUARTERS):
        here = two_all.at[fs, at_rows(tp, quarter)]
        landing = two_all.at[fs, at_rows(links.along(QUARTERS - step), quarter)]
        along.append(links.remote(two_ref, here, (fs, links.along(step)), landing))
    gathers = []
    for step in range(QUARTERS):
        q = links.along(QUARTERS - step) if step else tp
        gathers.append(
            Gather(
                links,
                two_ref if step == 0 else None,
                lambda f, q=q: two_all.at[f, at_rows(q, quarter)],
                lambda f, h, q=q: two_all.at[f, at_rows(q * 2 + h, quarter // 2)],
            )
        )
    gathers[0].first()
    for out, back in along:
        out.start()
    loads = [
        links.inside(slabs_ref.at[g], weights.at[:, pl.ds(g * block, block)]) for g in range(E)
    ]
    loads.append(links.inside(cotangent_all, cot_all))
    for load in loads:
        load.start()
    for step in range(1, QUARTERS):
        along[step - 1][1].wait_recv()
        gathers[step].first()
        gathers[step - 1].second()
        if step >= 2:
            gathers[step - 2].third()
    gathers[3].second()
    gathers[2].third()
    gathers[3].third()
    for load in loads:
        load.wait()
    for gather in gathers:
        gather.last()

    core_copies = []
    for i in range(4):
        core_copies.append(
            links.remote(
                parts.at[i % 2], core_in.at[i % 2], (links.peer(CORE_BIT), tp), core_in.at[i % 2]
            )
        )
    half_rows = rows // 2
    diag_y = links.remote(
        parts.at[2, pl.ds(0, half_rows)], diag_in.at[0], (links.peer(Y_BIT), tp), diag_in.at[0]
    )
    diag_x = links.remote(
        parts.at[2, pl.ds(half_rows, half_rows)],
        diag_in.at[1],
        (links.peer(X_BIT), tp),
        diag_in.at[1],
    )
    side_x = links.remote(parts.at[3], side_in.at[0], (links.peer(X_BIT), tp), side_in.at[0])
    side_y = links.remote(parts.at[4], side_in.at[1], (links.peer(Y_BIT), tp), side_in.at[1])

    sub = lax.broadcasted_iota(jnp.int32, (8, SIDE), 0)
    lane = lax.broadcasted_iota(jnp.int32, (8, SIDE), 1)
    mine, common = 2 + fs, 2 + E
    pick_in = (
        ((sub == 0) & ((lane == mine) | (lane == mine + SMALL)))
        | ((sub == 1) & ((lane == common) | (lane == common + SMALL)))
    ).astype(jnp.bfloat16)
    pick_out = (((sub == 0) & (lane == mine)) | ((sub == 1) & (lane == common))).astype(
        jnp.bfloat16
    )

    def one_block(index, slot):
        first[: 2 * count] = matmul_nt(weights[: 2 * count], two_all[index, :, :width])
        first[2 * count :] = matmul_nt(weights[2 * count :], cot_all[index])
        scale = matmul_nt(pick_in, two_all[index, :, width:])
        cols = pl.ds(pl.multiple_of(index * rows, rows), rows)
        dots = []
        for group, (low, high) in enumerate(((0, routed), (routed, count))):
            gate = first[low:high]
            up = first[count + low : count + high]
            grad = first[2 * count + low : 2 * count + high]
            by = scale[group : group + 1]
            sigmoid = 1.0 / (1.0 + jnp.exp(-gate))
            silu = gate * sigmoid
            active = silu * up
            units[2 * count + low : 2 * count + high, cols] = (by * active).astype(jnp.bfloat16)
            dots.append(jnp.sum(active * grad, axis=0, keepdims=True))
            active_grad = by * grad
            units[low:high, cols] = (
                active_grad * up * sigmoid * (1.0 + gate * (1.0 - sigmoid))
            ).astype(jnp.bfloat16)
            units[count + low : count + high, cols] = (active_grad * silu).astype(jnp.bfloat16)
        both = jnp.concatenate([*dots, jnp.zeros((6, rows), jnp.float32)], axis=0)
        parts[slot, :, width:back_width] = matmul_tn(both.astype(jnp.bfloat16), pick_out).astype(
            jnp.bfloat16
        )
        tile = 512
        for n in range(width // tile):
            at = slice(n * tile, (n + 1) * tile)
            parts[slot, :, at] = matmul_tn(units[: 2 * count, cols], weights[: 2 * count, at]).astype(
                jnp.bfloat16
            )
            beyond = slice(back_width + n * tile, back_width + (n + 1) * tile)
            parts[slot, :, beyond] = matmul_tn(
                units[2 * count :, cols], weights[2 * count :, at]
            ).astype(jnp.bfloat16)

    chunk = 32

    def add_in(slot, others):
        @pl.loop(0, rows // chunk)
        def _(r):
            at = pl.ds(pl.multiple_of(r * chunk, chunk), chunk)
            total = parts[slot, at, :].astype(jnp.float32)
            for ref in others:
                total = total + ref[at, :].astype(jnp.float32)
            parts[slot, at, :] = total.astype(jnp.bfloat16)

    def add_half(slot, ref, start):
        @pl.loop(0, half_rows // chunk)
        def _(r):
            at = pl.ds(pl.multiple_of(start + r * chunk, chunk), chunk)
            there = pl.ds(pl.multiple_of(r * chunk, chunk), chunk)
            total = parts[slot, at, :].astype(jnp.float32) + ref[there, :].astype(jnp.float32)
            parts[slot, at, :] = total.astype(jnp.bfloat16)

    def free_core():
        pl.semaphore_signal(
            credit, inc=1, device_id=(links.peer(CORE_BIT), tp), device_id_type=MESH
        )

    @pl.loop(0, 8)
    def _(t):
        pair = t // 2
        second = t % 2
        bits = 7 - 4 * pair + 6 * (pair // 2) - second
        index = flip_by(fs, bits)
        slot = second * (2 + pair - 3 * (pair // 3)) + (1 - second) * (pair % 2)

        @pl.when(t == 4)
        def _():
            core_copies[0][0].wait_send()

        @pl.when(t == 6)
        def _():
            core_copies[1][0].wait_send()

        @pl.when(t == 7)
        def _():
            diag_y[0].wait_send()
            diag_x[0].wait_send()

        one_block(index, slot)
        for i in range(4):

            @pl.when(t == 2 * i)
            def _(i=i):
                if i >= 2:
                    pl.semaphore_wait(credit, 1)
                core_copies[i][0].start()

        @pl.when(t == 1)
        def _():
            core_copies[0][1].wait_recv()
            add_in(2, [core_in.at[0]])
            free_core()
            diag_y[0].start()
            diag_x[0].start()

        @pl.when(t == 3)
        def _():
            core_copies[1][1].wait_recv()
            add_in(3, [core_in.at[1]])
            free_core()
            diag_y[1].wait_recv()
            add_half(3, diag_in.at[0], 0)
            side_x[0].start()

        @pl.when(t == 5)
        def _():
            core_copies[2][1].wait_recv()
            add_in(4, [core_in.at[0]])
            diag_x[1].wait_recv()
            add_half(4, diag_in.at[1], half_rows)
            side_y[0].start()

        @pl.when(t == 7)
        def _():
            core_copies[3][1].wait_recv()
            add_in(2, [core_in.at[1]])

    keeps = []

    def weight_grads(g):
        at = pl.ds(g * block, block)
        if g >= 2:
            keeps[g - 2].wait()
        hidden_cols = two_all[:, :, at].reshape(E * rows, block)
        staged[g % 2, : 2 * count] = matmul(units[: 2 * count], hidden_cols).astype(jnp.bfloat16)
        cot_cols = cot_all[:, :, at].reshape(E * rows, block)
        staged[g % 2, 2 * count :] = matmul(units[2 * count :], cot_cols).astype(jnp.bfloat16)
        keep = links.inside(staged.at[g % 2], grads_out.at[g])
        keep.start()
        keeps.append(keep)

    for g in range(E // 2):
        weight_grads(g)
    side_x[1].wait_recv()
    side_y[1].wait_recv()
    add_in(2, [side_in.at[0], side_in.at[1]])
    own = at_rows(tp, quarter)
    parts[2, own, back_width:] = (
        parts[2, own, back_width:].astype(jnp.float32) + residual_ref[...]
    ).astype(jnp.bfloat16)
    column = []
    for step in range(1, QUARTERS):
        peer = links.along(step)
        column.append(
            links.remote(
                parts.at[2, at_rows(peer, quarter), pl.ds(0, back_width)],
                rows_in.at[step - 1],
                (fs, peer),
                rows_in.at[step - 1],
            )
        )
    for step in range(1, QUARTERS):
        peer = links.along(step)
        column.append(
            links.remote(
                parts.at[2, :, pl.ds(pl.multiple_of(back_width + peer * out_width, 128), out_width)],
                cols_in.at[step - 1],
                (fs, peer),
                cols_in.at[step - 1],
            )
        )
    for out, back in column:
        out.start()
    for g in range(E // 2, E):
        weight_grads(g)
    for out, back in column[:3]:
        back.wait_recv()
    total = parts[2, own, :back_width].astype(jnp.float32)
    for step in range(1, QUARTERS):
        total = total + rows_in[step - 1].astype(jnp.float32)
    dots = total[:, width : width + SMALL]
    scales = router_ref[:, :SMALL]
    probs = router_ref[:, SMALL : 2 * SMALL]
    chosen = router_ref[:, 2 * SMALL :]
    chosen_grad = chosen * dots
    logit_grad = probs * (chosen_grad - jnp.sum(probs * chosen_grad, axis=1, keepdims=True))
    gate_lane = lax.broadcasted_iota(jnp.int32, (quarter, SMALL), 1) == 2 + E
    logit_grad = jnp.where(gate_lane, dots * scales * (1.0 - scales), logit_grad).astype(
        jnp.bfloat16
    )
    residual = residual_ref[...]
    rstd = lax.rsqrt(jnp.mean(residual * residual, axis=1, keepdims=True) + NORM_EPS)
    mean = jnp.zeros((quarter, 1), jnp.float32)
    for b in range(E):
        at = slice(b * block, (b + 1) * block)
        two_grad = total[:, at] + matmul(logit_grad, small_ref[b])
        normed = residual[:, at] * rstd
        gain = small_ref[b, 1:2, :].astype(jnp.float32)
        back_ref[:, at] = two_grad
        mean = mean + jnp.sum(two_grad * gain * normed, axis=1, keepdims=True)
        grads = matmul_tn(logit_grad, two_all[fs, own, at])
        sub = lax.broadcasted_iota(jnp.int32, (SMALL, block), 0)
        gain_grad = jnp.sum(two_grad * normed, axis=0, keepdims=True)
        small_grad_ref[:, at] = jnp.where(sub == 1, gain_grad, grads)
    mean = mean / width
    for b in range(E):
        at = slice(b * block, (b + 1) * block)
        gain = small_ref[b, 1:2, :].astype(jnp.float32)
        normed = residual[:, at] * rstd
        grad = cotangent_ref[own, at].astype(jnp.float32) + rstd * (
            back_ref[:, at] * gain - normed * mean
        )
        back_ref[:, at] = grad
        branch_ref[:, at] = grad.astype(jnp.bfloat16)
    for out, back in column[3:]:
        back.wait_recv()
    start = pl.multiple_of(back_width + tp * out_width, 128)
    total = parts[2, :, pl.ds(start, out_width)].astype(jnp.float32)
    for step in range(1, QUARTERS):
        total = total + cols_in[step - 1].astype(jnp.float32)
    output_ref[...] = total.astype(jnp.bfloat16)
    for out, back in along + core_copies[2:] + [side_x, side_y] + column:
        out.wait_send()
    for keep in keeps[-2:]:
        keep.wait()


def expert_call(
    two_rows, router_rows, residual_rows, cotangent, cotangent_all, slabs, small_full, out_width, routed
):
    quarter, width = residual_rows.shape
    rows = quarter * QUARTERS
    back_width = width + SIDE
    block = width // E
    bf, f32 = jnp.bfloat16, jnp.float32
    sds = jax.ShapeDtypeStruct
    vmem = pl.BlockSpec(memory_space=pltpu.VMEM)
    hbm = pl.BlockSpec(memory_space=pl.ANY)
    outs = [
        (sds((rows, out_width), bf), vmem),
        (sds((quarter, width), bf), vmem),
        (sds((quarter, width), f32), vmem),
        (sds((SMALL, width), f32), vmem),
        (sds(slabs.shape, bf), hbm),
    ]
    units = slabs.shape[1]
    return pl.pallas_call(
        functools.partial(expert_kernel, routed),
        name="experts",
        out_shape=[o[0] for o in outs],
        in_specs=[vmem, vmem, vmem, vmem, hbm, hbm, vmem],
        out_specs=[o[1] for o in outs],
        scratch_shapes=[
            pltpu.VMEM((E, rows, back_width), bf),
            pltpu.VMEM((E, rows, width), bf),
            pltpu.VMEM((units, width), bf),
            pltpu.VMEM((units, E * rows), bf),
            pltpu.VMEM((units, rows), f32),
            pltpu.VMEM((5, rows, back_width + width), bf),
            pltpu.VMEM((2, rows, back_width + width), bf),
            pltpu.VMEM((2, rows // 2, back_width + width), bf),
            pltpu.VMEM((2, rows, back_width + width), bf),
            pltpu.VMEM((QUARTERS - 1, quarter, back_width), bf),
            pltpu.VMEM((QUARTERS - 1, rows, out_width), bf),
            pltpu.VMEM((2, units, block), bf),
            pltpu.SemaphoreType.DMA((64,)),
            pltpu.SemaphoreType.DMA((64,)),
            pltpu.SemaphoreType.DMA((24,)),
            pltpu.SemaphoreType.REGULAR,
        ],
        compiler_params=pltpu.CompilerParams(
            collective_id=2, has_side_effects=True, vmem_limit_bytes=62 * 2**20
        ),
    )(two_rows, router_rows, residual_rows, cotangent, cotangent_all, slabs, small_full)


class Scatter:
    def __init__(self, links, parts, core_in, diag_in, side_in):
        self.links, self.parts = links, parts
        self.core_in, self.diag_in, self.side_in = core_in, diag_in, side_in
        self.rows = parts.shape[1]
        p, tp = links.peer, links.tp
        half = self.rows // 2
        self.core = [
            links.remote(
                parts.at[p(bits + CORE_BIT)], core_in.at[i], (p(CORE_BIT), tp), core_in.at[i]
            )
            for i, bits in enumerate((6, 2, 4, 0))
        ]
        self.diag = [
            links.remote(
                parts.at[p(6), pl.ds(h * half, half)], diag_in.at[h], (p(bits), tp), diag_in.at[h]
            )
            for h, bits in enumerate((Y_BIT, X_BIT))
        ]
        self.side = [
            links.remote(parts.at[p(bits)], side_in.at[i], (p(bits), tp), side_in.at[i])
            for i, bits in enumerate((X_BIT, Y_BIT))
        ]

    def add(self, index, first, count, refs, target=None):
        chunk = 32

        @pl.loop(0, count // chunk)
        def _(r):
            here = pl.ds(pl.multiple_of(first + r * chunk, chunk), chunk)
            there = pl.ds(pl.multiple_of(r * chunk, chunk), chunk)
            total = self.parts[index, here, :].astype(jnp.float32)
            for ref in refs:
                total = total + ref[there, :].astype(jnp.float32)
            if target is None:
                self.parts[index, here, :] = total.astype(jnp.bfloat16)
            else:
                target[here, :] = total

    def to_core(self):
        for out, back in self.core:
            out.start()

    def diagonal(self):
        self.core[0][1].wait_recv()
        self.add(self.links.peer(6), 0, self.rows, [self.core_in.at[0]])
        for out, back in self.diag:
            out.start()

    def sideways(self, i):
        index = self.links.peer((X_BIT, Y_BIT)[i])
        self.core[1 + i][1].wait_recv()
        self.add(index, 0, self.rows, [self.core_in.at[1 + i]])
        self.diag[i][1].wait_recv()
        self.add(index, i * (self.rows // 2), self.rows // 2, [self.diag_in.at[i]])
        self.side[i][0].start()

    def finish(self, target):
        self.core[3][1].wait_recv()
        for out, back in self.side:
            back.wait_recv()
        self.add(
            self.links.fs,
            0,
            self.rows,
            [self.core_in.at[3], self.side_in.at[0], self.side_in.at[1]],
            target,
        )

    def sent(self):
        for out, back in self.core + self.diag + self.side:
            out.wait_send()


def backward_kernel(
    branch_ref,
    residual_ref,
    small_grad_ref,
    attended_ref,
    query_ref,
    hidden_ref,
    tokens_ref,
    kv_ref,
    qkv_ref,
    out_ref,
    small_ref,
    cos_ref,
    sin_ref,
    start_ref,
    slabs_ref,
    input_grad_ref,
    qkv_own,
    out_own,
    small_own,
    slabs_all,
    kv_full,
    qkv_full,
    out_full,
    branch_all,
    odds,
    query_grad,
    projected,
    kv_total,
    kv_parts,
    kv_core,
    kv_diag,
    kv_side,
    qkv_parts,
    qkv_core,
    qkv_diag,
    qkv_side,
    out_parts,
    out_core,
    out_diag,
    out_side,
    one_parts,
    one_in,
    grad_rows,
    small_parts,
    small_in,
    small_column,
    send,
    recv,
    local,
):
    links = Links(send, recv, local)
    fs, tp = links.fs, links.tp
    quarter, width = residual_ref.shape
    rows = quarter * QUARTERS
    block = width // E
    local_width = query_ref.shape[1]
    heads = local_width // HD
    seqs = rows // SEQ_DEV
    length = E * SEQ_DEV
    scale = HD ** (-0.5)

    def at_rows(index, size):
        return pl.ds(pl.multiple_of(index * size, size), size)

    own = at_rows(tp, quarter)
    links.greet(range(1, 8), range(1, QUARTERS))
    branch = []
    for step in range(1, QUARTERS):
        here = branch_all.at[own]
        landing = branch_all.at[at_rows(links.along(QUARTERS - step), quarter)]
        branch.append(links.remote(branch_ref, here, (fs, links.along(step)), landing))
    for out, back in branch:
        out.start()
    branch_all[own, :] = branch_ref[...]
    slab_copies = []
    for bits in (6, 7, 2, 3, 4, 5, 1):
        peer = links.peer(bits)
        slab_copies.append(
            links.remote(slabs_ref.at[peer], slabs_all.at[fs], (peer, tp), slabs_all.at[peer])
        )
    for out, back in slab_copies:
        out.start()
    slab_own = links.inside(slabs_ref.at[fs], slabs_all.at[fs])
    slab_own.start()
    kv_load = links.inside(kv_ref, kv_full)
    kv_load.start()
    out_load = links.inside(out_ref, out_full)
    out_load.start()
    qkv_load = links.inside(qkv_ref, qkv_full)
    qkv_load.start()
    kv_sum = Scatter(links, kv_parts, kv_core, kv_diag, kv_side)
    qkv_sum = Scatter(links, qkv_parts, qkv_core, qkv_diag, qkv_side)
    out_sum = Scatter(links, out_parts, out_core, out_diag, out_side)

    kv_load.wait()
    key_pos = lax.broadcasted_iota(jnp.int32, (SEQ_DEV, length), 1)
    query_pos = fs * SEQ_DEV + lax.broadcasted_iota(jnp.int32, (SEQ_DEV, length), 0)
    for s in range(seqs):
        here = slice(s * SEQ_DEV, (s + 1) * SEQ_DEV)
        allowed = (key_pos <= query_pos) & (key_pos >= start_ref[here, :])
        for h in range(heads):
            cols = slice(h * HD, (h + 1) * HD)
            keys = kv_full[:, here, cols].reshape(length, HD)
            scores = matmul_nt(query_ref[here, cols], keys) * scale
            scores = jnp.where(allowed, scores, NEG_FILL)
            top = jnp.max(scores, axis=1, keepdims=True)
            weights = jnp.exp(scores - top)
            odds[s * heads + h] = weights / jnp.sum(weights, axis=1, keepdims=True)
    out_load.wait()
    for out, back in branch:
        back.wait_recv()
    attended_grad = jnp.zeros((rows, local_width), jnp.float32)
    for b in range(E):
        attended_grad = attended_grad + matmul_nt(
            branch_all[:, b * block : (b + 1) * block], out_full[b]
        )
    query_grad[...] = attended_grad.astype(jnp.bfloat16)
    for s in range(seqs):
        here = slice(s * SEQ_DEV, (s + 1) * SEQ_DEV)
        for h in range(heads):
            cols = slice(h * HD, (h + 1) * HD)
            vcols = slice(local_width + h * HD, local_width + (h + 1) * HD)
            keys = kv_full[:, here, cols].reshape(length, HD)
            values = kv_full[:, here, vcols].reshape(length, HD)
            grad = query_grad[here, cols]
            probs = odds[s * heads + h]
            weights_grad = matmul_nt(grad, values)
            delta = jnp.sum(probs * weights_grad, axis=1, keepdims=True)
            score_grad = (probs * (weights_grad - delta)).astype(jnp.bfloat16)
            key_grad = matmul_tn(score_grad, query_ref[here, cols]) * scale
            value_grad = matmul_tn(probs.astype(jnp.bfloat16), grad)
            kv_parts[:, here, cols] = key_grad.astype(jnp.bfloat16).reshape(E, SEQ_DEV, HD)
            kv_parts[:, here, vcols] = value_grad.astype(jnp.bfloat16).reshape(E, SEQ_DEV, HD)
            projected[0, here, cols] = turn(
                matmul(score_grad, keys) * scale, cos_ref[here, :], -sin_ref[here, :]
            ).astype(jnp.bfloat16)
    kv_sum.to_core()
    attended = attended_ref[...]
    for b in range(E):
        cols = slice(b * block, (b + 1) * block)
        out_parts[b] = matmul_tn(attended, branch_all[:, cols]).astype(jnp.bfloat16)
    kv_sum.diagonal()
    out_sum.to_core()

    def weight_grad(j):
        for b in range(E):
            cols = slice(b * block, (b + 1) * block)
            qkv_parts[b, j * block : (j + 1) * block] = matmul_tn(
                hidden_ref[:, cols], projected[j]
            ).astype(jnp.bfloat16)

    weight_grad(0)
    kv_sum.sideways(0)
    kv_sum.sideways(1)
    out_sum.diagonal()
    qkv_load.wait()
    kv_sum.finish(kv_total)
    projected[1] = turn(kv_total[:, :local_width], cos_ref[...], -sin_ref[...]).astype(jnp.bfloat16)
    projected[2] = kv_total[:, local_width:].astype(jnp.bfloat16)
    for b in range(E):
        cols = slice(b * block, (b + 1) * block)
        part = jnp.zeros((rows, block), jnp.float32)
        for j in range(3):
            part = part + matmul_nt(projected[j], qkv_full[j, cols])
        one_parts[:, cols] = part.astype(jnp.bfloat16)
    column = []
    for step in range(1, QUARTERS):
        peer = links.along(step)
        column.append(
            links.remote(
                one_parts.at[at_rows(peer, quarter)],
                one_in.at[step - 1],
                (fs, peer),
                one_in.at[step - 1],
            )
        )
    for out, back in column:
        out.start()
    weight_grad(1)
    weight_grad(2)
    qkv_sum.to_core()
    out_sum.sideways(0)
    out_sum.sideways(1)
    qkv_sum.diagonal()
    qkv_sum.sideways(0)
    qkv_sum.sideways(1)
    for out, back in column:
        back.wait_recv()
    tokens = tokens_ref[own, :].astype(jnp.float32)
    rstd = lax.rsqrt(jnp.mean(tokens * tokens, axis=1, keepdims=True) + NORM_EPS)
    total = one_parts[own, :].astype(jnp.float32)
    for step in range(1, QUARTERS):
        total = total + one_in[step - 1].astype(jnp.float32)
    mean = jnp.zeros((quarter, 1), jnp.float32)
    sub = lax.broadcasted_iota(jnp.int32, (SMALL, block), 0)
    for b in range(E):
        at = slice(b * block, (b + 1) * block)
        gain = small_ref[b, 0:1, :].astype(jnp.float32)
        normed = tokens[:, at] * rstd
        mean = mean + jnp.sum(total[:, at] * gain * normed, axis=1, keepdims=True)
        gain_grad = jnp.sum(total[:, at] * normed, axis=0, keepdims=True)
        small_parts[b] = jnp.where(sub == 0, gain_grad, small_grad_ref[:, at])
    mean = mean / width
    for b in range(E):
        at = slice(b * block, (b + 1) * block)
        gain = small_ref[b, 0:1, :].astype(jnp.float32)
        normed = tokens[:, at] * rstd
        grad_rows[:, at] = (
            residual_ref[:, at] + rstd * (total[:, at] * gain - normed * mean)
        ).astype(jnp.bfloat16)
    spread = []
    for step in range(1, QUARTERS):
        peer = links.along(step)
        landing = input_grad_ref.at[at_rows(links.along(QUARTERS - step), quarter)]
        spread.append(links.remote(grad_rows, input_grad_ref.at[own], (fs, peer), landing))
    for out, back in spread:
        out.start()
    keep = links.inside(grad_rows, input_grad_ref.at[own])
    keep.start()
    small_copies = []
    for bits in range(1, E):
        peer = links.peer(bits)
        small_copies.append(
            links.remote(
                small_parts.at[peer], small_in.at[bits - 1], (peer, tp), small_in.at[bits - 1]
            )
        )
    for out, back in small_copies:
        out.start()
    out_sum.finish(out_own)
    for out, back in small_copies:
        back.wait_recv()
    small_total = small_parts[fs]
    for bits in range(1, E):
        small_total = small_total + small_in[bits - 1]
    small_column[tp] = small_total
    small_spread = []
    for step in range(1, QUARTERS):
        here = small_column.at[tp]
        landing = small_column.at[links.along(QUARTERS - step)]
        small_spread.append(links.remote(here, here, (fs, links.along(step)), landing))
    for out, back in small_spread:
        out.start()
    qkv_sum.finish(qkv_own)
    for out, back in small_spread:
        back.wait_recv()
    small_own[...] = small_column[0] + small_column[1] + small_column[2] + small_column[3]
    for out, back in spread + slab_copies:
        back.wait_recv()
    slab_own.wait()
    keep.wait()
    for out, back in branch + slab_copies + column + spread + small_copies + small_spread:
        out.wait_send()
    for scatter in (kv_sum, out_sum, qkv_sum):
        scatter.sent()


def backward_call(
    branch_rows,
    residual_grad,
    small_grad,
    attended,
    query_rows,
    hidden_one,
    tokens,
    kv_all,
    qkv_full,
    out_full,
    small_full,
    cosine,
    sine,
    start,
    slabs,
):
    quarter, width = residual_grad.shape
    rows = quarter * QUARTERS
    block = width // E
    local_width = query_rows.shape[1]
    bf, f32 = jnp.bfloat16, jnp.float32
    sds = jax.ShapeDtypeStruct
    vmem = pl.BlockSpec(memory_space=pltpu.VMEM)
    hbm = pl.BlockSpec(memory_space=pl.ANY)
    outs = [
        (sds((rows, width), bf), hbm),
        (sds((3 * block, local_width), f32), vmem),
        (sds((local_width, block), f32), vmem),
        (sds((SMALL, block), f32), vmem),
        (sds(slabs.shape, bf), hbm),
    ]

    def scatter_scratch(count, columns):
        return [
            pltpu.VMEM((E, count, columns), bf),
            pltpu.VMEM((4, count, columns), bf),
            pltpu.VMEM((2, count // 2, columns), bf),
            pltpu.VMEM((2, count, columns), bf),
        ]

    return pl.pallas_call(
        backward_kernel,
        name="attention_backward",
        out_shape=[o[0] for o in outs],
        in_specs=[vmem] * 7 + [hbm] * 3 + [vmem] * 4 + [hbm],
        out_specs=[o[1] for o in outs],
        scratch_shapes=[
            pltpu.VMEM((E, rows, 2 * local_width), bf),
            pltpu.VMEM((3, width, local_width), bf),
            pltpu.VMEM((E, local_width, block), bf),
            pltpu.VMEM((rows, width), bf),
            pltpu.VMEM((rows // SEQ_DEV * local_width // HD, SEQ_DEV, E * SEQ_DEV), f32),
            pltpu.VMEM((rows, local_width), bf),
            pltpu.VMEM((3, rows, local_width), bf),
            pltpu.VMEM((rows, 2 * local_width), f32),
            *scatter_scratch(rows, 2 * local_width),
            *scatter_scratch(3 * block, local_width),
            *scatter_scratch(local_width, block),
            pltpu.VMEM((rows, width), bf),
            pltpu.VMEM((QUARTERS - 1, quarter, width), bf),
            pltpu.VMEM((quarter, width), bf),
            pltpu.VMEM((E, SMALL, block), f32),
            pltpu.VMEM((E - 1, SMALL, block), f32),
            pltpu.VMEM((QUARTERS, SMALL, block), f32),
            pltpu.SemaphoreType.DMA((64,)),
            pltpu.SemaphoreType.DMA((64,)),
            pltpu.SemaphoreType.DMA((16,)),
        ],
        compiler_params=pltpu.CompilerParams(
            collective_id=3, has_side_effects=True, vmem_limit_bytes=62 * 2**20
        ),
    )(
        branch_rows,
        residual_grad,
        small_grad,
        attended,
        query_rows,
        hidden_one,
        tokens,
        kv_all,
        qkv_full,
        out_full,
        small_full,
        cosine,
        sine,
        start,
        slabs,
    )


def shards_units(
    tokens,
    cotangent,
    qkv_weight,
    out_weight,
    norm_gains,
    router_weight,
    shared_gate,
    expert_gate_up,
    expert_down,
    shared_gate_up,
    shared_down,
    routes,
    doc_start,
):
    tok_rows, width = tokens.shape
    seq_count = tok_rows // SEQ_DEV
    local_width = qkv_weight.shape[2]
    quarter = tok_rows // QUARTERS
    fs_index = lax.axis_index("fs")
    tp_index = lax.axis_index("tp")
    fs_size = E
    query_pos = fs_index * SEQ_DEV + jnp.arange(SEQ_DEV, dtype=jnp.int32)
    positions = jnp.tile(query_pos, seq_count)
    half_cos, half_sin = rope_tables(positions)
    cosine = jnp.concatenate([half_cos, half_cos], axis=1)
    sine = jnp.concatenate([-half_sin, half_sin], axis=1)
    small = jnp.concatenate(
        [
            norm_gains,
            router_weight,
            shared_gate[None],
            jnp.zeros((SMALL - 3 - E, shared_gate.shape[0]), jnp.bfloat16),
        ],
        axis=0,
    )
    routed_units = expert_down.shape[1]
    shared_units = shared_down.shape[0] // fs_size
    units = routed_units + shared_units
    block = expert_down.shape[2]
    expert_up_slabs = jnp.transpose(expert_gate_up, (0, 2, 3, 1))
    shared_up_slabs = jnp.transpose(
        shared_gate_up.reshape(block, 2, fs_size, shared_units), (2, 1, 3, 0)
    )
    up_slabs = jnp.concatenate([expert_up_slabs, shared_up_slabs], axis=2)
    down_slabs = jnp.concatenate(
        [expert_down, shared_down.reshape(fs_size, shared_units, block)], axis=1
    )
    slabs = jnp.concatenate([up_slabs, down_slabs[:, None]], axis=1)
    (
        two_rows,
        residual_rows,
        router_rows,
        attended,
        query_rows,
        hidden_one,
        slabs,
        cotangent_all,
        kv_all,
        qkv_full,
        out_full,
        small_full,
    ) = forward_call(
        tokens,
        cotangent,
        qkv_weight,
        out_weight,
        small,
        slabs.reshape(fs_size, 3 * units, block),
        cosine,
        sine,
        doc_start[:, None],
        routes,
    )
    output, branch_rows, residual_grad, small_grad, grad_slabs = expert_call(
        two_rows,
        router_rows,
        residual_rows,
        cotangent,
        cotangent_all,
        slabs,
        small_full,
        width // QUARTERS,
        routed_units,
    )
    input_grad, qkv_own, out_own, small_own, grad_slabs = backward_call(
        branch_rows,
        residual_grad,
        small_grad,
        attended,
        query_rows,
        hidden_one,
        tokens,
        kv_all,
        qkv_full,
        out_full,
        small_full,
        cosine,
        sine,
        doc_start[:, None],
        grad_slabs,
    )
    input_grad = input_grad.astype(jnp.float32)
    grad_slabs = grad_slabs.reshape(fs_size, 3, units, block)
    own = grad_slabs.astype(jnp.float32)
    expert_up_own = jnp.transpose(own[:, :2, :routed_units], (0, 3, 1, 2))
    expert_down_own = own[:, 2, :routed_units]
    shared_up_own = jnp.transpose(own[:, :2, routed_units:], (3, 1, 0, 2)).reshape(
        shared_gate_up.shape
    )
    shared_down_own = own[:, 2, routed_units:].reshape(shared_down.shape)
    return (
        output,
        input_grad,
        qkv_own.reshape(qkv_weight.shape),
        out_own,
        small_own[:2],
        small_own[2 : 2 + E],
        small_own[2 + E],
        expert_up_own,
        expert_down_own,
        shared_up_own,
        shared_down_own,
    )


def solution(mesh):
    return jax.shard_map(
        shards_units if dict(mesh.shape) == {"fs": E, "tp": QUARTERS} else shards_gathered,
        mesh=mesh,
        in_specs=(
            P("fs", None),
            P("fs", None),
            P(None, "fs", "tp"),
            P("tp", "fs"),
            P(None, "fs"),
            P(None, "fs"),
            P("fs"),
            P(None, "fs", None, "tp"),
            P(None, "tp", "fs"),
            P("fs", None, "tp"),
            P("tp", "fs"),
            P("fs", None),
            P("fs"),
        ),
        out_specs=(
            P("fs", "tp"),
            P("fs", None),
            P(None, "fs", "tp"),
            P("tp", "fs"),
            P(None, "fs"),
            P(None, "fs"),
            P("fs"),
            P(None, "fs", None, "tp"),
            P(None, "tp", "fs"),
            P("fs", None, "tp"),
            P("tp", "fs"),
        ),
        check_vma=False,
    )
```

```python
import functools
import math

import jax
import jax.numpy as jnp
from jax import lax
from jax.experimental import pallas as pl
from jax.experimental.pallas import tpu as pltpu
from jax.sharding import PartitionSpec as P

HD = 128
E = 8
SEQ_DEV = 128
SIDE = 128


NORM_EPS = 1e-06
NEG_FILL = -1e30
ROPE_BASE = 1000000.0


def rope_tables(positions):
    half_size = HD // 2
    frequency = ROPE_BASE ** (-(jnp.arange(half_size, dtype=jnp.float32) * 2.0 / HD))
    angles = positions.astype(jnp.float32)[:, None] * frequency[None, :]
    return (jnp.cos(angles), jnp.sin(angles))


def rotate(values, cosine, sine_table):
    shaped = values.reshape(values.shape[0], -1, HD)
    half_size = HD // 2
    first_half = shaped[..., :half_size]
    second_half = shaped[..., half_size:]
    cos_part = cosine[:, None, :]
    sin_part = sine_table[:, None, :]
    turned = jnp.concatenate(
        [
            first_half * cos_part - second_half * sin_part,
            second_half * cos_part + first_half * sin_part,
        ],
        axis=-1,
    )
    return turned.reshape(values.shape)


def key_mask(query_pos, query_start, first_dev, group_size):
    key_pos = (first_dev + jnp.arange(group_size, dtype=jnp.int32)[:, None]) * SEQ_DEV + jnp.arange(
        SEQ_DEV, dtype=jnp.int32
    )[None, :]
    key_pos = key_pos[None, None, :, :]
    return (key_pos <= query_pos[None, :, None, None]) & (key_pos >= query_start[:, :, None, None])


def shards_gathered(
    tokens,
    cotangent,
    qkv_weight,
    out_weight,
    norm_gains,
    router_weight,
    shared_gate,
    expert_gate_up,
    expert_down,
    shared_gate_up,
    shared_down,
    routes,
    doc_start,
):
    tok_rows = tokens.shape[0]
    seq_count = tok_rows // SEQ_DEV
    local_width = qkv_weight.shape[2]
    head_count = local_width // HD
    out_width = tokens.shape[1] // lax.axis_size("tp")
    score_scale = HD ** (-0.5)
    fs_index = lax.axis_index("fs")
    tp_index = lax.axis_index("tp")
    query_pos = fs_index * SEQ_DEV + jnp.arange(SEQ_DEV, dtype=jnp.int32)
    positions = jnp.tile(query_pos, seq_count)
    query_start = doc_start.reshape(seq_count, SEQ_DEV)
    cosine, sine_table = rope_tables(positions)
    group_limit = max(1, 512 // SEQ_DEV)
    qkv_full, out_full, gains_full, router_full, shared_gate_full = (
        lax.all_gather(qkv_weight, "fs", axis=1, tiled=True),
        lax.all_gather(out_weight, "fs", axis=1, tiled=True),
        lax.all_gather(norm_gains, "fs", axis=1, tiled=True),
        lax.all_gather(router_weight, "fs", axis=1, tiled=True),
        lax.all_gather(shared_gate, "fs", axis=0, tiled=True),
    )
    token_float = tokens.astype(jnp.float32)
    rstd_one = lax.rsqrt(jnp.mean(token_float * token_float, axis=1, keepdims=True) + NORM_EPS)
    normed_one = token_float * rstd_one
    hidden_one = (normed_one * gains_full[0].astype(jnp.float32)[None, :]).astype(jnp.bfloat16)
    projected = jnp.einsum("td,jdf->jtf", hidden_one, qkv_full, preferred_element_type=jnp.float32)
    query_rows = rotate(projected[0], cosine, sine_table).astype(jnp.bfloat16)
    key_own = rotate(projected[1], cosine, sine_table).astype(jnp.bfloat16)
    value_own = projected[2].astype(jnp.bfloat16)
    query_heads = query_rows.reshape(seq_count, SEQ_DEV, head_count, HD)

    def score_block(key_group, first_dev):
        allowed = key_mask(query_pos, query_start, first_dev, key_group.shape[0])[:, None]
        scores = (
            jnp.einsum(
                "pqhd,gpkhd->phqgk", query_heads, key_group, preferred_element_type=jnp.float32
            )
            * score_scale
        )
        return (jnp.where(allowed, scores, NEG_FILL), allowed)

    def forward_update(running, key_group, value_group, first_dev):
        run_max, run_sum, accumulated = running
        scores, allowed = score_block(key_group, first_dev)
        new_max = jnp.maximum(run_max, jnp.max(scores, axis=(3, 4)))
        weights = jnp.where(allowed, jnp.exp(scores - new_max[..., None, None]), 0.0)
        factor = jnp.exp(run_max - new_max)
        new_sum = run_sum * factor + jnp.sum(weights, axis=(3, 4))
        mixed_part = jnp.einsum(
            "phqgk,gpkhd->pqhd",
            weights.astype(jnp.bfloat16),
            value_group,
            preferred_element_type=jnp.float32,
        )
        new_accum = accumulated * jnp.transpose(factor, (0, 2, 1))[..., None] + mixed_part
        return (new_max, new_sum, new_accum)

    initial = (
        jnp.full((seq_count, head_count, SEQ_DEV), NEG_FILL, jnp.float32),
        jnp.zeros((seq_count, head_count, SEQ_DEV), jnp.float32),
        jnp.zeros((seq_count, SEQ_DEV, head_count, HD), jnp.float32),
    )
    running = initial
    key_piece = lax.all_gather(key_own, "fs", axis=0, tiled=True)
    value_piece = lax.all_gather(value_own, "fs", axis=0, tiled=True)
    shard_count = key_piece.shape[0] // tok_rows
    group_size = math.gcd(shard_count, group_limit)
    step_count = shard_count // group_size
    shaped = (step_count, group_size, seq_count, SEQ_DEV, head_count, HD)
    first_dev = jnp.int32(0) // tok_rows

    def one_step(carried, inputs):
        key_group, value_group, group_index = inputs
        start_dev = group_index * group_size
        updated = lax.cond(
            start_dev <= fs_index,
            lambda state_in: forward_update(state_in, key_group, value_group, start_dev),
            lambda state_in: state_in,
            carried,
        )
        return (updated, None)

    running, ignored = lax.scan(
        one_step,
        running,
        (
            key_piece.reshape(shaped),
            value_piece.reshape(shaped),
            jnp.arange(step_count, dtype=jnp.int32),
        ),
    )
    run_max, run_sum, accumulated = running
    attended_heads = (accumulated / jnp.transpose(run_sum, (0, 2, 1))[..., None]).astype(
        jnp.bfloat16
    )
    log_total = run_max + jnp.log(run_sum)
    attended = attended_heads.reshape(tok_rows, local_width)
    branch_part = jnp.dot(attended, out_full, preferred_element_type=jnp.float32)
    branch = lax.psum(branch_part.astype(jnp.bfloat16), "tp").astype(jnp.float32)
    residual = token_float + branch
    rstd_two = lax.rsqrt(jnp.mean(residual * residual, axis=1, keepdims=True) + NORM_EPS)
    normed_two = residual * rstd_two
    hidden_two = (normed_two * gains_full[1].astype(jnp.float32)[None, :]).astype(jnp.bfloat16)
    expert_gate_all, expert_down_all, shared_up_all, shared_down_all = (
        lax.all_gather(expert_gate_up, "fs", axis=1, tiled=True),
        lax.all_gather(expert_down, "fs", axis=2, tiled=True),
        lax.all_gather(shared_gate_up, "fs", axis=0, tiled=True),
        lax.all_gather(shared_down, "fs", axis=1, tiled=True),
    )
    logits = jnp.einsum("td,ed->te", hidden_two, router_full, preferred_element_type=jnp.float32)
    router_probs = jax.nn.softmax(logits, axis=-1)
    chosen = jnp.sum(
        (routes[:, :, None] == jnp.arange(E, dtype=jnp.int32)[None, None, :]).astype(jnp.float32),
        axis=1,
    )
    gate_weights = router_probs * chosen
    gate_up = jnp.einsum(
        "td,edkf->tekf", hidden_two, expert_gate_all, preferred_element_type=jnp.float32
    )
    gate_part = gate_up[:, :, 0]
    up_part = gate_up[:, :, 1]
    gate_sigmoid = jax.nn.sigmoid(gate_part)
    active = gate_part * gate_sigmoid * up_part
    hidden = (gate_weights[:, :, None] * active).astype(jnp.bfloat16)
    shared_in = jnp.einsum(
        "td,dkf->tkf", hidden_two, shared_up_all, preferred_element_type=jnp.float32
    )
    shared_gate_in = shared_in[:, 0]
    shared_up_in = shared_in[:, 1]
    shared_sigmoid = jax.nn.sigmoid(shared_gate_in)
    shared_active = shared_gate_in * shared_sigmoid * shared_up_in
    gate_logit = jnp.einsum(
        "td,d->t", hidden_two, shared_gate_full, preferred_element_type=jnp.float32
    )
    gate_value = jax.nn.sigmoid(gate_logit)
    shared_hidden = (gate_value[:, None] * shared_active).astype(jnp.bfloat16)
    mixture_part = jnp.einsum(
        "tef,efd->td", hidden, expert_down_all, preferred_element_type=jnp.float32
    ) + jnp.dot(shared_hidden, shared_down_all, preferred_element_type=jnp.float32)
    mixture = lax.psum_scatter(
        mixture_part.astype(jnp.bfloat16), "tp", scatter_dimension=1, tiled=True
    ).astype(jnp.float32)
    output = (
        lax.dynamic_slice_in_dim(residual, tp_index * out_width, out_width, 1) + mixture
    ).astype(jnp.bfloat16)
    qkv_back, out_back, gains_back, router_back, shared_gate_back = (
        lax.all_gather(qkv_weight, "fs", axis=1, tiled=True),
        lax.all_gather(out_weight, "fs", axis=1, tiled=True),
        lax.all_gather(norm_gains, "fs", axis=1, tiled=True),
        lax.all_gather(router_weight, "fs", axis=1, tiled=True),
        lax.all_gather(shared_gate, "fs", axis=0, tiled=True),
    )
    expert_gate_back, expert_down_back, shared_up_back, shared_down_back = (
        lax.all_gather(expert_gate_up, "fs", axis=1, tiled=True),
        lax.all_gather(expert_down, "fs", axis=2, tiled=True),
        lax.all_gather(shared_gate_up, "fs", axis=0, tiled=True),
        lax.all_gather(shared_down, "fs", axis=1, tiled=True),
    )
    hidden_grad = jnp.einsum(
        "td,efd->tef", cotangent, expert_down_back, preferred_element_type=jnp.float32
    )
    expert_down_grad = jnp.einsum(
        "tef,td->efd", hidden, cotangent, preferred_element_type=jnp.float32
    )
    shared_grad = jnp.einsum(
        "td,fd->tf", cotangent, shared_down_back, preferred_element_type=jnp.float32
    )
    shared_down_grad = jnp.einsum(
        "tf,td->fd", shared_hidden, cotangent, preferred_element_type=jnp.float32
    )
    gate_dot = jnp.sum(active * hidden_grad, axis=2)
    shared_dot = jnp.sum(shared_active * shared_grad, axis=1)
    active_grad = gate_weights[:, :, None] * hidden_grad
    gate_grad = active_grad * up_part * gate_sigmoid * (1.0 + gate_part * (1.0 - gate_sigmoid))
    up_grad = active_grad * gate_part * gate_sigmoid
    gate_up_grad = jnp.stack([gate_grad, up_grad], axis=2).astype(jnp.bfloat16)
    shared_active_grad = gate_value[:, None] * shared_grad
    shared_gate_grad = (
        shared_active_grad
        * shared_up_in
        * shared_sigmoid
        * (1.0 + shared_gate_in * (1.0 - shared_sigmoid))
    )
    shared_unit_grad = shared_active_grad * shared_gate_in * shared_sigmoid
    shared_up_grad = jnp.stack([shared_gate_grad, shared_unit_grad], axis=1).astype(jnp.bfloat16)
    expert_gate_grad = jnp.einsum(
        "td,tekf->edkf", hidden_two, gate_up_grad, preferred_element_type=jnp.float32
    )
    shared_proj_grad = jnp.einsum(
        "td,tkf->dkf", hidden_two, shared_up_grad, preferred_element_type=jnp.float32
    )
    input_part = jnp.einsum(
        "tekf,edkf->td", gate_up_grad, expert_gate_back, preferred_element_type=jnp.float32
    ) + jnp.einsum(
        "tkf,dkf->td", shared_up_grad, shared_up_back, preferred_element_type=jnp.float32
    )
    input_sum, gate_sum, shared_sum = (
        lax.psum(input_part.astype(jnp.bfloat16), "tp").astype(jnp.float32),
        lax.psum(gate_dot.astype(jnp.bfloat16), "tp").astype(jnp.float32),
        lax.psum(shared_dot.astype(jnp.bfloat16), "tp").astype(jnp.float32),
    )
    chosen_grad = chosen * gate_sum
    logit_grad = (
        router_probs * (chosen_grad - jnp.sum(router_probs * chosen_grad, axis=1, keepdims=True))
    ).astype(jnp.bfloat16)
    gate_logit_grad = (shared_sum * gate_value * (1.0 - gate_value)).astype(jnp.bfloat16)
    router_grad = jnp.einsum(
        "te,td->ed", logit_grad, hidden_two, preferred_element_type=jnp.float32
    )
    shared_vector_grad = jnp.einsum(
        "t,td->d", gate_logit_grad, hidden_two, preferred_element_type=jnp.float32
    )
    two_grad = (
        input_sum
        + jnp.einsum("te,ed->td", logit_grad, router_back, preferred_element_type=jnp.float32)
        + gate_logit_grad.astype(jnp.float32)[:, None]
        * shared_gate_back.astype(jnp.float32)[None, :]
    )
    scaled_two = two_grad * gains_back[1].astype(jnp.float32)[None, :]
    gain_two_grad = jnp.sum(two_grad * normed_two, axis=0)
    residual_grad = cotangent.astype(jnp.float32) + rstd_two * (
        scaled_two - normed_two * jnp.mean(scaled_two * normed_two, axis=1, keepdims=True)
    )
    branch_grad = residual_grad.astype(jnp.bfloat16)
    out_grad = jnp.einsum("tf,td->fd", attended, branch_grad, preferred_element_type=jnp.float32)
    attended_grad = jnp.einsum(
        "td,fd->tf", branch_grad, out_back, preferred_element_type=jnp.float32
    ).astype(jnp.bfloat16)
    grad_heads = attended_grad.reshape(seq_count, SEQ_DEV, head_count, HD)
    delta_rows = jnp.einsum(
        "pqhd,pqhd->phq", grad_heads, attended_heads, preferred_element_type=jnp.float32
    )
    key_all, value_all = (
        lax.all_gather(key_own, "fs", axis=0, tiled=True),
        lax.all_gather(value_own, "fs", axis=0, tiled=True),
    )
    device_count = key_all.shape[0] // tok_rows
    back_group = math.gcd(device_count, group_limit)
    back_steps = device_count // back_group
    back_shape = (back_steps, back_group, seq_count, SEQ_DEV, head_count, HD)

    def backward_update(key_group, value_group, start_dev):
        scores, allowed = score_block(key_group, start_dev)
        probs_block = jnp.where(allowed, jnp.exp(scores - log_total[..., None, None]), 0.0)
        weights_grad = jnp.einsum(
            "pqhd,gpkhd->phqgk", grad_heads, value_group, preferred_element_type=jnp.float32
        )
        score_grad = (probs_block * (weights_grad - delta_rows[..., None, None])).astype(
            jnp.bfloat16
        )
        query_part = (
            jnp.einsum(
                "phqgk,gpkhd->pqhd", score_grad, key_group, preferred_element_type=jnp.float32
            )
            * score_scale
        )
        key_part = (
            jnp.einsum(
                "phqgk,pqhd->gpkhd", score_grad, query_heads, preferred_element_type=jnp.float32
            )
            * score_scale
        )
        value_part = jnp.einsum(
            "phqgk,pqhd->gpkhd",
            probs_block.astype(jnp.bfloat16),
            grad_heads,
            preferred_element_type=jnp.float32,
        )
        return (query_part, key_part, value_part)

    empty_grads = (
        jnp.zeros((seq_count, SEQ_DEV, head_count, HD), jnp.float32),
        jnp.zeros((back_group, seq_count, SEQ_DEV, head_count, HD), jnp.float32),
        jnp.zeros((back_group, seq_count, SEQ_DEV, head_count, HD), jnp.float32),
    )
    scan_inputs = (
        key_all.reshape(back_shape),
        value_all.reshape(back_shape),
        jnp.arange(back_steps, dtype=jnp.int32),
    )

    def back_step(query_acc, inputs):
        key_group, value_group, group_index = inputs
        start_dev = group_index * back_group
        query_part, key_part, value_part = lax.cond(
            start_dev <= fs_index,
            lambda ignored_in: backward_update(key_group, value_group, start_dev),
            lambda ignored_in: empty_grads,
            key_group,
        )
        term_rows = jnp.concatenate(
            [
                key_part.reshape(back_group * tok_rows, local_width),
                value_part.reshape(back_group * tok_rows, local_width),
            ],
            axis=1,
        )
        return (query_acc + query_part, term_rows)

    query_grad, key_value_terms = lax.scan(back_step, empty_grads[0], scan_inputs)
    key_value_sum = lax.psum_scatter(
        key_value_terms.reshape(device_count * tok_rows, 2 * local_width).astype(jnp.bfloat16),
        "fs",
        scatter_dimension=0,
        tiled=True,
    ).astype(jnp.float32)
    key_grad_rows = key_value_sum[:, :local_width]
    value_grad_rows = key_value_sum[:, local_width:]
    projected_grad = jnp.stack(
        [
            rotate(query_grad.reshape(tok_rows, local_width), cosine, -sine_table),
            rotate(key_grad_rows, cosine, -sine_table),
            value_grad_rows,
        ],
        axis=0,
    ).astype(jnp.bfloat16)
    qkv_grad = jnp.einsum(
        "td,jtf->jdf", hidden_one, projected_grad, preferred_element_type=jnp.float32
    )
    one_part = jnp.einsum(
        "jtf,jdf->td", projected_grad, qkv_back, preferred_element_type=jnp.float32
    )
    one_grad = lax.psum(one_part.astype(jnp.bfloat16), "tp").astype(jnp.float32)
    scaled_one = one_grad * gains_back[0].astype(jnp.float32)[None, :]
    gain_one_grad = jnp.sum(one_grad * normed_one, axis=0)
    input_grad = residual_grad + rstd_one * (
        scaled_one - normed_one * jnp.mean(scaled_one * normed_one, axis=1, keepdims=True)
    )
    gains_grad = jnp.stack([gain_one_grad, gain_two_grad], axis=0)
    reduced = (
        lax.psum_scatter(
            qkv_grad.astype(jnp.bfloat16), "fs", scatter_dimension=1, tiled=True
        ).astype(jnp.float32),
        lax.psum_scatter(
            out_grad.astype(jnp.bfloat16), "fs", scatter_dimension=1, tiled=True
        ).astype(jnp.float32),
        lax.psum_scatter(
            gains_grad.astype(jnp.bfloat16), "fs", scatter_dimension=1, tiled=True
        ).astype(jnp.float32),
        lax.psum_scatter(
            router_grad.astype(jnp.bfloat16), "fs", scatter_dimension=1, tiled=True
        ).astype(jnp.float32),
        lax.psum_scatter(
            shared_vector_grad.astype(jnp.bfloat16), "fs", scatter_dimension=0, tiled=True
        ).astype(jnp.float32),
        lax.psum_scatter(
            expert_gate_grad.astype(jnp.bfloat16), "fs", scatter_dimension=1, tiled=True
        ).astype(jnp.float32),
        lax.psum_scatter(
            expert_down_grad.astype(jnp.bfloat16), "fs", scatter_dimension=2, tiled=True
        ).astype(jnp.float32),
        lax.psum_scatter(
            shared_proj_grad.astype(jnp.bfloat16), "fs", scatter_dimension=0, tiled=True
        ).astype(jnp.float32),
        lax.psum_scatter(
            shared_down_grad.astype(jnp.bfloat16), "fs", scatter_dimension=1, tiled=True
        ).astype(jnp.float32),
    )
    return (
        output,
        input_grad,
        reduced[0],
        reduced[1],
        reduced[2],
        reduced[3],
        reduced[4],
        reduced[5],
        reduced[6],
        reduced[7],
        reduced[8],
    )


MESH = pl.DeviceIdType.MESH
X_BIT, Y_BIT, CORE_BIT = 2, 4, 1
QUARTERS = 4
SMALL = 16
CUT = 1536


def flip(index, bit):
    return index + bit - 2 * bit * ((index // bit) % 2)


class Links:
    def __init__(self, send, recv, local):
        self.fs = lax.axis_index("fs")
        self.tp = lax.axis_index("tp")
        self.send, self.recv, self.local = send, recv, local
        self.used = 0
        self.used_local = 0

    def peer(self, bits):
        where = self.fs
        for bit in (X_BIT, Y_BIT, CORE_BIT):
            if bits & bit:
                where = flip(where, bit)
        return where

    def along(self, step):
        return lax.rem(self.tp + step, QUARTERS)

    def remote(self, source, target, device, landing):
        i = self.used
        self.used += 1
        out = pltpu.make_async_remote_copy(
            src_ref=source,
            dst_ref=target,
            send_sem=self.send.at[i],
            recv_sem=self.recv.at[i],
            device_id=device,
            device_id_type=MESH,
        )
        back = pltpu.make_async_remote_copy(
            src_ref=landing,
            dst_ref=landing,
            send_sem=self.send.at[i],
            recv_sem=self.recv.at[i],
            device_id=device,
            device_id_type=MESH,
        )
        return out, back

    def inside(self, source, target):
        i = self.used_local
        self.used_local += 1
        return pltpu.make_async_copy(source, target, self.local.at[i])

    def greet(self, plane, column):
        barrier = pltpu.get_barrier_semaphore()
        for bits in plane:
            pl.semaphore_signal(
                barrier, inc=1, device_id=(self.peer(bits), self.tp), device_id_type=MESH
            )
        for step in column:
            pl.semaphore_signal(
                barrier, inc=1, device_id=(self.fs, self.along(step)), device_id_type=MESH
            )
        pl.semaphore_wait(barrier, len(plane) + len(column))


class Gather:
    def __init__(self, links, source, place, half):
        self.links = links
        fs, tp = links.fs, links.tp

        def to(bits, what, landing, origin=None):
            return links.remote(
                what if origin is None else origin, what, (links.peer(bits), tp), landing
            )

        p = links.peer
        self.keep = None if source is None else links.inside(source, place(fs))
        self.to_x = to(X_BIT, place(fs), place(p(X_BIT)), source)
        self.to_y = to(Y_BIT, place(fs), place(p(Y_BIT)), source)
        self.to_c = to(CORE_BIT, place(fs), place(p(CORE_BIT)), source)
        xy = X_BIT + Y_BIT
        self.x_on = to(Y_BIT, half(p(X_BIT), 0), half(p(xy), 0))
        self.y_on = to(X_BIT, half(p(Y_BIT), 1), half(p(xy), 1))
        self.x_core = to(CORE_BIT, place(p(X_BIT)), place(p(X_BIT + CORE_BIT)))
        self.y_core = to(CORE_BIT, place(p(Y_BIT)), place(p(Y_BIT + CORE_BIT)))
        self.d_core = [
            to(CORE_BIT, half(p(xy), h), half(p(xy + CORE_BIT), h)) for h in range(2)
        ]

    def first(self):
        self.to_x[0].start()
        self.to_y[0].start()
        self.to_c[0].start()
        if self.keep is not None:
            self.keep.start()

    def second(self):
        self.to_x[1].wait_recv()
        self.x_on[0].start()
        self.x_core[0].start()
        self.to_y[1].wait_recv()
        self.y_on[0].start()
        self.y_core[0].start()

    def third(self):
        self.x_on[1].wait_recv()
        self.d_core[0][0].start()
        self.y_on[1].wait_recv()
        self.d_core[1][0].start()

    def last(self):
        if self.keep is not None:
            self.keep.wait()
        for out, back in (self.to_c, self.x_core, self.y_core, *self.d_core):
            back.wait_recv()
        for out, back in (
            self.to_x,
            self.to_y,
            self.to_c,
            self.x_on,
            self.y_on,
            self.x_core,
            self.y_core,
            *self.d_core,
        ):
            out.wait_send()


class CrossGather:
    def __init__(self, links, source, blocks):
        self.links = links
        tp = links.tp
        size = source.shape[0]

        def slot(k, h=None):
            start, count = (3 - k // 2) * size, size
            if h is not None:
                count = size // 2
                start = start + h * count
            return blocks.at[1, pl.ds(start, count)]

        def to(bits, start, there):
            return links.remote(start, there, (links.peer(bits), tp), there)

        x, y, c = X_BIT, Y_BIT, CORE_BIT
        self.keep = links.inside(source, slot(0))
        self.to_x = to(x, source, slot(x))
        self.to_y = to(y, source, slot(y))
        self.x_on = to(y, slot(x, 0), slot(x + y, 0))
        self.y_on = to(x, slot(y, 1), slot(x + y, 1))
        self.along = []
        for step in range(1, QUARTERS):
            there = blocks.at[2 * step + 1]
            self.along.append(
                links.remote(blocks.at[1], there, (links.fs, links.along(step)), there)
            )
        self.core = [
            to(c, blocks.at[2 * s + 1], blocks.at[2 * s]) for s in range(QUARTERS)
        ]

    def first(self):
        self.to_x[0].start()
        self.to_y[0].start()
        self.keep.start()

    def second(self):
        self.to_x[1].wait_recv()
        self.x_on[0].start()
        self.to_y[1].wait_recv()
        self.y_on[0].start()

    def third(self):
        self.keep.wait()
        self.x_on[1].wait_recv()
        self.y_on[1].wait_recv()
        for out, back in self.along:
            out.start()
        self.core[0][0].start()

    def last(self):
        for s, (out, back) in enumerate(self.along):
            back.wait_recv()
            self.core[s + 1][0].start()
        for out, back in self.core:
            back.wait_recv()
        for out, back in (self.to_x, self.to_y, self.x_on, self.y_on, *self.along, *self.core):
            out.wait_send()


def turn(values, cosine, sine_signed):
    parts = []
    for h in range(values.shape[1] // HD):
        v = values[:, h * HD : (h + 1) * HD]
        parts.append(v * cosine + pltpu.roll(v, HD // 2, 1) * sine_signed)
    return jnp.concatenate(parts, axis=1)


def as_column(row):
    size = row.shape[1]
    same = lax.broadcasted_iota(jnp.int32, (size, size), 0) == lax.broadcasted_iota(
        jnp.int32, (size, size), 1
    )
    spread = jnp.where(same, row.astype(jnp.float32), 0.0)
    return jnp.sum(spread, axis=1, keepdims=True).astype(jnp.int32)


def matmul(a, b):
    return jnp.dot(a, b, preferred_element_type=jnp.float32)


def matmul_nt(a, b):
    return lax.dot_general(a, b, (((1,), (1,)), ((), ())), preferred_element_type=jnp.float32)


def matmul_tn(a, b):
    return lax.dot_general(a, b, (((0,), (0,)), ((), ())), preferred_element_type=jnp.float32)


def forward_kernel(
    tokens_ref,
    cotangent_ref,
    qkv_ref,
    out_ref,
    gains_ref,
    router_ref,
    gate_ref,
    up_ref,
    shared_up_ref,
    down_ref,
    shared_down_ref,
    cos_ref,
    sin_ref,
    start_ref,
    routes_ref,
    two_out,
    residual_ref,
    scales_ref,
    attended_ref,
    query_ref,
    hidden_buf,
    slabs_all,
    cotangent_all,
    cotangent_plane,
    kv_out,
    qkv_out,
    out_out,
    small_out,
    qkv_full,
    out_full,
    small_full,
    kv_own,
    kv_full,
    branch_buf,
    branch_in,
    two_ref,
    small_ref,
    send,
    recv,
    local,
):
    links = Links(send, recv, local)
    fs, tp = links.fs, links.tp
    rows, width = tokens_ref.shape
    block = width // E
    local_width = qkv_ref.shape[2]
    heads = local_width // HD
    seqs = rows // SEQ_DEV
    quarter = rows // QUARTERS

    def at_rows(index, size):
        return pl.ds(pl.multiple_of(index * size, size), size)

    f32 = jnp.float32
    small_ref[...] = jnp.concatenate(
        [
            gains_ref[...].astype(f32),
            router_ref[...].astype(f32),
            gate_ref[...].astype(f32),
            jnp.zeros((SMALL - 3 - E, block), f32),
        ],
        axis=0,
    ).astype(jnp.bfloat16)
    links.greet(range(1, 8), range(1, QUARTERS))
    small = Gather(
        links, small_ref, lambda f: small_full.at[f], lambda f, h: small_full.at[f, :, pl.ds(h * 128, 128)]
    )
    qkv = Gather(
        links,
        qkv_ref,
        lambda f: qkv_full.at[:, at_rows(f, block)],
        lambda f, h: qkv_full.at[:, pl.ds(pl.multiple_of(f * block + h * (block // 2), block // 2), block // 2)],
    )
    outs = Gather(
        links,
        out_ref,
        lambda f: out_full.at[f],
        lambda f, h: out_full.at[f, pl.ds(h * (local_width // 2), local_width // 2)],
    )
    cut = cotangent_all.shape[2]
    cot = CrossGather(
        links, cotangent_ref.at[at_rows(tp, quarter), pl.ds(0, cut)], cotangent_all
    )
    cot_plane = Gather(
        links,
        cotangent_ref.at[:, pl.ds(cut, width - cut)],
        lambda f: cotangent_plane.at[f],
        lambda f, h: cotangent_plane.at[f, pl.ds(h * SEQ_DEV, SEQ_DEV)],
    )
    small.first()
    cot.first()
    qkv.first()
    small.second()
    small.third()
    small.last()
    cot.second()
    tokens = tokens_ref[...].astype(jnp.float32)
    rstd_one = lax.rsqrt(jnp.mean(tokens * tokens, axis=1, keepdims=True) + NORM_EPS)
    for b in range(E):
        cols = slice(b * block, (b + 1) * block)
        gain = small_full[b, 0:1, :].astype(jnp.float32)
        hidden_buf[:, cols] = (tokens[:, cols] * rstd_one * gain).astype(jnp.bfloat16)
    cot.third()
    qkv.second()
    qkv.third()
    outs.first()
    cot_plane.first()
    qkv.last()
    hidden = hidden_buf[...]
    cosine, sine = cos_ref[...], sin_ref[...]
    kv_own[:, :local_width] = turn(matmul(hidden, qkv_full[1]), cosine, sine).astype(jnp.bfloat16)
    kv_own[:, local_width:] = matmul(hidden, qkv_full[2]).astype(jnp.bfloat16)
    kv = Gather(
        links,
        kv_own,
        lambda f: kv_full.at[f],
        lambda f, h: kv_full.at[f, pl.ds(h * SEQ_DEV, SEQ_DEV)],
    )
    kv.first()
    qkv_keep = links.inside(qkv_full, qkv_out)
    qkv_keep.start()
    query_ref[...] = turn(matmul(hidden, qkv_full[0]), cosine, sine).astype(jnp.bfloat16)
    outs.second()
    kv.second()
    outs.third()
    kv.third()
    cot_plane.second()
    routed, shared = down_ref.shape[1], shared_down_ref.shape[0] // E

    def slab(peer, where):
        units = pl.ds(pl.multiple_of(peer * shared, 16), shared)
        pieces = [
            up_ref.at[peer],
            shared_up_ref.at[0, units],
            shared_up_ref.at[1, units],
            down_ref.at[peer],
            shared_down_ref.at[units],
        ]
        placed, at = [], 0
        for piece, size in zip(pieces, (2 * routed, shared, shared, routed, shared), strict=True):
            placed.append((piece, slabs_all.at[where, pl.ds(at, size)]))
            at += size
        return placed

    slab_copies = []
    for bits in (6, 7, 2, 3, 4, 5, 1):
        peer = links.peer(bits)
        for (piece, place), (_, landing) in zip(slab(peer, fs), slab(peer, peer), strict=True):
            slab_copies.append(links.remote(piece, place, (peer, tp), landing))
    for out, back in slab_copies:
        out.start()
    slab_own = [links.inside(piece, place) for piece, place in slab(fs, fs)]
    for copy in slab_own:
        copy.start()
    kv.last()
    kv_keep = links.inside(kv_full, kv_out)
    kv_keep.start()
    length = E * SEQ_DEV
    key_pos = lax.broadcasted_iota(jnp.int32, (SEQ_DEV, length), 1)
    query_pos = fs * SEQ_DEV + lax.broadcasted_iota(jnp.int32, (SEQ_DEV, length), 0)
    for s in range(seqs):
        here = slice(s * SEQ_DEV, (s + 1) * SEQ_DEV)
        allowed = (key_pos <= query_pos) & (key_pos >= as_column(start_ref[s : s + 1, :]))
        for h in range(heads):
            cols = slice(h * HD, (h + 1) * HD)
            vcols = slice(local_width + h * HD, local_width + (h + 1) * HD)
            keys = kv_full[:, here, cols].reshape(length, HD)
            values = kv_full[:, here, vcols].reshape(length, HD)
            scores = matmul_nt(query_ref[here, cols], keys) * (HD ** (-0.5))
            scores = jnp.where(allowed, scores, NEG_FILL)
            top = jnp.max(scores, axis=1, keepdims=True)
            weights = jnp.exp(scores - top)
            weights = weights / jnp.sum(weights, axis=1, keepdims=True)
            attended_ref[here, cols] = matmul(weights.astype(jnp.bfloat16), values).astype(
                jnp.bfloat16
            )
    outs.last()
    cot_plane.third()
    out_keep = links.inside(out_full, out_out)
    out_keep.start()
    small_keep = links.inside(small_full, small_out)
    small_keep.start()
    attended = attended_ref[...]
    for b in range(E):
        branch_buf[:, b * block : (b + 1) * block] = matmul(attended, out_full[b]).astype(
            jnp.bfloat16
        )
    branch = []
    for step in range(1, QUARTERS):
        peer = links.along(step)
        branch.append(
            links.remote(
                branch_buf.at[at_rows(peer, quarter)],
                branch_in.at[step - 1],
                (fs, peer),
                branch_in.at[step - 1],
            )
        )
    for out, back in branch:
        out.start()
    for out, back in branch:
        back.wait_recv()
    mine = at_rows(tp, quarter)
    total = branch_buf[mine, :].astype(jnp.float32)
    for step in range(1, QUARTERS):
        total = total + branch_in[step - 1].astype(jnp.float32)
    residual = tokens_ref[mine, :].astype(jnp.float32) + total
    residual_ref[...] = residual
    rstd_two = lax.rsqrt(jnp.mean(residual * residual, axis=1, keepdims=True) + NORM_EPS)
    logits = jnp.zeros((quarter, SMALL), jnp.float32)
    for b in range(E):
        cols = slice(b * block, (b + 1) * block)
        gain = small_full[b, 1:2, :].astype(jnp.float32)
        part = (residual[:, cols] * rstd_two * gain).astype(jnp.bfloat16)
        two_ref[:, cols] = part
        logits = logits + matmul_nt(part, small_full[b])
    lane = lax.broadcasted_iota(jnp.int32, (quarter, SMALL), 1)
    routed = (lane >= 2) & (lane < 2 + E)
    masked = jnp.where(routed, logits, NEG_FILL)
    odds = jnp.exp(masked - jnp.max(masked, axis=1, keepdims=True))
    odds = jnp.where(routed, odds, 0.0)
    probs = odds / jnp.sum(odds, axis=1, keepdims=True)
    expert = lax.broadcasted_iota(jnp.int32, (SMALL, rows), 0) - 2
    named = jnp.zeros((SMALL, rows), jnp.float32)
    for k in range(routes_ref.shape[0]):
        named = named + (routes_ref[k : k + 1, :] == expert).astype(jnp.float32)
    pick = lax.broadcasted_iota(jnp.int32, (quarter, rows), 1) == (
        tp * quarter + lax.broadcasted_iota(jnp.int32, (quarter, rows), 0)
    )
    chosen = matmul_nt(pick.astype(jnp.bfloat16), named.astype(jnp.bfloat16))
    gate_value = 1.0 / (1.0 + jnp.exp(-logits))
    scales = jnp.where(lane == 2 + E, gate_value, probs * chosen)
    scales_ref[...] = jnp.concatenate([scales, probs, chosen], axis=1)
    high = scales.astype(jnp.bfloat16)
    low = (scales - high.astype(jnp.float32)).astype(jnp.bfloat16)
    two_ref[:, width:] = jnp.concatenate(
        [high, low, jnp.zeros((quarter, SIDE - 2 * SMALL), jnp.bfloat16)], axis=1
    )
    two_keep = links.inside(two_ref, two_out.at[0])
    two_keep.start()
    two_along = []
    for step in range(1, QUARTERS):
        there = two_out.at[step]
        two_along.append(links.remote(two_ref, there, (fs, links.along(step)), there))
    for out, back in two_along:
        out.start()
    cot_plane.last()
    cot.last()
    for out, back in slab_copies + two_along:
        back.wait_recv()
    for out, back in slab_copies + branch + two_along:
        out.wait_send()
    for copy in (*slab_own, two_keep, qkv_keep, kv_keep, out_keep, small_keep):
        copy.wait()


def forward_call(
    tokens,
    cotangent,
    qkv_weight,
    out_weight,
    norm_gains,
    router_weight,
    shared_gate,
    up,
    shared_up,
    down,
    shared_down,
    cosine,
    sine,
    start,
    routes,
):
    rows, width = tokens.shape
    block = width // E
    local_width = qkv_weight.shape[2]
    quarter = rows // QUARTERS
    bf, f32 = jnp.bfloat16, jnp.float32
    sds = jax.ShapeDtypeStruct
    vmem = pl.BlockSpec(memory_space=pltpu.VMEM)
    hbm = pl.BlockSpec(memory_space=pl.ANY)
    outs = [
        (sds((QUARTERS, quarter, width + SIDE), bf), hbm),
        (sds((quarter, width), f32), vmem),
        (sds((quarter, 3 * SMALL), f32), vmem),
        (sds((rows, local_width), bf), vmem),
        (sds((rows, local_width), bf), vmem),
        (sds((rows, width), bf), vmem),
        (sds((E, 3 * (down.shape[1] + shared_down.shape[0] // E), block), bf), hbm),
        (sds((E, rows, CUT), bf), hbm),
        (sds((E, rows, width - CUT), bf), hbm),
        (sds((E, rows, 2 * local_width), bf), hbm),
        (sds((3, width, local_width), bf), hbm),
        (sds((E, local_width, block), bf), hbm),
        (sds((E, SMALL, block), bf), hbm),
    ]
    return pl.pallas_call(
        forward_kernel,
        name="attention_forward",
        out_shape=[o[0] for o in outs],
        in_specs=[vmem, hbm, hbm, hbm, vmem, vmem, vmem, hbm, hbm, hbm, hbm, vmem, vmem, vmem, vmem],
        out_specs=[o[1] for o in outs],
        scratch_shapes=[
            pltpu.VMEM((3, width, local_width), bf),
            pltpu.VMEM((E, local_width, block), bf),
            pltpu.VMEM((E, SMALL, block), bf),
            pltpu.VMEM((rows, 2 * local_width), bf),
            pltpu.VMEM((E, rows, 2 * local_width), bf),
            pltpu.VMEM((rows, width), bf),
            pltpu.VMEM((QUARTERS - 1, quarter, width), bf),
            pltpu.VMEM((quarter, width + SIDE), bf),
            pltpu.VMEM((SMALL, block), bf),
            pltpu.SemaphoreType.DMA((128,)),
            pltpu.SemaphoreType.DMA((128,)),
            pltpu.SemaphoreType.DMA((32,)),
        ],
        compiler_params=pltpu.CompilerParams(
            collective_id=1, has_side_effects=True, vmem_limit_bytes=56 * 2**20
        ),
    )(
        tokens,
        cotangent,
        qkv_weight,
        out_weight,
        norm_gains,
        router_weight,
        shared_gate,
        up,
        shared_up,
        down,
        shared_down,
        cosine,
        sine,
        start,
        routes,
    )


class RowGather:
    def __init__(self, links, source, slot, half):
        self.links = links

        def to(bits, owner, h=None):
            view = slot if h is None else lambda k: half(k, h)
            start = source if owner == 0 and source is not None else view(owner)
            return links.remote(
                start, view(owner ^ bits), (links.peer(bits), links.tp), view(owner ^ bits)
            )

        x, y, c = X_BIT, Y_BIT, CORE_BIT
        self.keep = None if source is None else links.inside(source, slot(0))
        self.own = [to(x, 0), to(y, 0), to(c, 0)]
        self.x_on = [to(y, x, 0), to(c, x)]
        self.y_on = [to(x, y, 1), to(c, y)]
        self.d_on = [to(c, x + y, 0), to(c, x + y, 1)]

    def first(self):
        for out, back in self.own:
            out.start()
        if self.keep is not None:
            self.keep.start()

    def second(self):
        self.own[0][1].wait_recv()
        for out, back in self.x_on:
            out.start()
        self.own[1][1].wait_recv()
        for out, back in self.y_on:
            out.start()

    def third(self):
        self.x_on[0][1].wait_recv()
        self.d_on[0][0].start()
        self.y_on[0][1].wait_recv()
        self.d_on[1][0].start()

    def last(self):
        if self.keep is not None:
            self.keep.wait()
        for out, back in (self.own[2], self.x_on[1], self.y_on[1], *self.d_on):
            back.wait_recv()

    def sent(self):
        for out, back in self.own + self.x_on + self.y_on + self.d_on:
            out.wait_send()


def expert_kernel(
    routed,
    two_ref,
    router_ref,
    residual_ref,
    cotangent_ref,
    cotangent_all,
    cotangent_plane,
    slabs_ref,
    small_ref,
    output_ref,
    branch_ref,
    back_ref,
    small_grad_ref,
    grads_out,
    two_all,
    cot_all,
    weights,
    units,
    first,
    parts,
    core_in,
    diag_in,
    side_in,
    rows_in,
    cols_in,
    own_rows,
    own_cols,
    staged,
    send,
    recv,
    local,
    credit,
):
    links = Links(send, recv, local)
    fs, tp = links.fs, links.tp
    quarter, width = residual_ref.shape
    rows = quarter * QUARTERS
    block = width // E
    count = weights.shape[0] // 3
    out_width = output_ref.shape[1]
    back_width = width + SIDE

    def at_rows(index, size):
        return pl.ds(pl.multiple_of(index * size, size), size)

    links.greet(range(1, 8), range(1, QUARTERS))

    def slot(s, k, h=None):
        start = (3 - k // 2) * quarter
        size = quarter
        if h is not None:
            size = quarter // 2
            start = start + h * size
        return two_all.at[2 * s + 1 - k % 2, pl.ds(start, size)]

    gathers = []
    for s in range(QUARTERS):
        gathers.append(
            RowGather(
                links,
                two_ref.at[s],
                lambda k, s=s: slot(s, k),
                lambda k, h, s=s: slot(s, k, h),
            )
        )
    gathers[0].first()
    gathers[1].first()
    loads = [
        links.inside(slabs_ref.at[g], weights.at[:, pl.ds(g * block, block)]) for g in range(E)
    ]
    cut = cotangent_all.shape[2]
    loads.append(links.inside(cotangent_all, cot_all.at[:, :, pl.ds(0, cut)]))
    for s in range(QUARTERS):
        q = links.along(QUARTERS - s)
        for k in range(E):
            there = cot_all.at[
                2 * s + 1 - k % 2, pl.ds((3 - k // 2) * quarter, quarter), pl.ds(cut, width - cut)
            ]
            loads.append(
                links.inside(cotangent_plane.at[links.peer(k), at_rows(q, quarter)], there)
            )
    for load in loads:
        load.start()

    core = [
        links.remote(
            parts.at[s % 2], core_in.at[s % 2], (links.peer(CORE_BIT), tp), core_in.at[s % 2]
        )
        for s in range(QUARTERS)
    ]
    diag, side, rows_along, cols_along = [], [], [], []
    for s in range(QUARTERS):
        held = parts.at[2 + s % 3]
        diag.append(
            [
                links.remote(
                    held.at[pl.ds(h * (quarter // 2), quarter // 2)],
                    diag_in.at[s, h],
                    (links.peer(bits), tp),
                    diag_in.at[s, h],
                )
                for h, bits in enumerate((Y_BIT, X_BIT))
            ]
        )
        side.append(
            [
                links.remote(
                    held.at[pl.ds((3 - bits // 2) * quarter, quarter)],
                    side_in.at[s, i],
                    (links.peer(bits), tp),
                    side_in.at[s, i],
                )
                for i, bits in enumerate((X_BIT, Y_BIT))
            ]
        )
        last = pl.ds(3 * quarter, quarter)
        if s:
            rows_along.append(
                links.remote(
                    held.at[last, pl.ds(0, back_width)],
                    rows_in.at[s - 1],
                    (fs, links.along(QUARTERS - s)),
                    rows_in.at[s - 1],
                )
            )
        q = links.along(QUARTERS - s)
        for step in range(1, QUARTERS):
            peer = links.along(step)
            start = pl.multiple_of(back_width + peer * out_width, 128)
            q_there = links.along(2 * QUARTERS - s - step)
            cols_along.append(
                links.remote(
                    held.at[last, pl.ds(start, out_width)],
                    cols_in.at[step - 1, at_rows(q, quarter)],
                    (fs, peer),
                    cols_in.at[step - 1, at_rows(q_there, quarter)],
                )
            )

    sub = lax.broadcasted_iota(jnp.int32, (8, SIDE), 0)
    lane = lax.broadcasted_iota(jnp.int32, (8, SIDE), 1)
    mine, common = 2 + fs, 2 + E
    pick_in = (
        ((sub == 0) & ((lane == mine) | (lane == mine + SMALL)))
        | ((sub == 1) & ((lane == common) | (lane == common + SMALL)))
    ).astype(jnp.bfloat16)
    pick_out = (((sub == 0) & (lane == mine)) | ((sub == 1) & (lane == common))).astype(
        jnp.bfloat16
    )

    def one_block(t, slot_out, pause):
        first[: 2 * count] = matmul_nt(weights[: 2 * count], two_all[t, :, :width])
        pause(0)
        first[2 * count :] = matmul_nt(weights[2 * count :], cot_all[t])
        scale = matmul_nt(pick_in, two_all[t, :, width:])
        cols = pl.ds(pl.multiple_of(t * rows, rows), rows)
        dots = []
        shared = count - routed
        groups = ((0, 2 * count, routed), (2 * routed, 2 * count + routed, shared))
        for group, (low, last, size) in enumerate(groups):
            gate = first[low : low + size]
            up = first[low + size : low + 2 * size]
            grad = first[last : last + size]
            by = scale[group : group + 1]
            sigmoid = 1.0 / (1.0 + jnp.exp(-gate))
            silu = gate * sigmoid
            active = silu * up
            units[last : last + size, cols] = (by * active).astype(jnp.bfloat16)
            dots.append(jnp.sum(active * grad, axis=0, keepdims=True))
            active_grad = by * grad
            units[low : low + size, cols] = (
                active_grad * up * sigmoid * (1.0 + gate * (1.0 - sigmoid))
            ).astype(jnp.bfloat16)
            units[low + size : low + 2 * size, cols] = (active_grad * silu).astype(jnp.bfloat16)
        both = jnp.concatenate([*dots, jnp.zeros((6, rows), jnp.float32)], axis=0)
        parts[slot_out, :, width:back_width] = matmul_tn(
            both.astype(jnp.bfloat16), pick_out
        ).astype(jnp.bfloat16)
        pause(1)
        tile = 512
        for n in range(width // tile):
            at = slice(n * tile, (n + 1) * tile)
            parts[slot_out, :, at] = matmul_tn(
                units[: 2 * count, cols], weights[: 2 * count, at]
            ).astype(jnp.bfloat16)
            if n == 1:
                pause(2)
        for n in range(width // tile):
            at = slice(n * tile, (n + 1) * tile)
            beyond = slice(back_width + n * tile, back_width + (n + 1) * tile)
            parts[slot_out, :, beyond] = matmul_tn(
                units[2 * count :, cols], weights[2 * count :, at]
            ).astype(jnp.bfloat16)
        pause(3)

    def add_in(held, start, size, others):
        chunk = 32

        @pl.loop(0, size // chunk)
        def _(r):
            at = pl.ds(pl.multiple_of(start + r * chunk, chunk), chunk)
            there = pl.ds(pl.multiple_of(r * chunk, chunk), chunk)
            total = parts[held, at, :].astype(jnp.float32)
            for ref in others:
                total = total + ref[there, :].astype(jnp.float32)
            parts[held, at, :] = total.astype(jnp.bfloat16)

    def to_core(s):
        if s >= 2:
            pl.semaphore_wait(credit, 1)
        core[s][0].start()

    def diagonal(s):
        core[s][1].wait_recv()
        add_in(2 + s % 3, 0, rows, [core_in.at[s % 2]])
        if s < 2:
            pl.semaphore_signal(
                credit, inc=1, device_id=(links.peer(CORE_BIT), tp), device_id_type=MESH
            )
        for out, back in diag[s]:
            out.start()

    def sideways(s):
        for h, (out, back) in enumerate(diag[s]):
            back.wait_recv()
            start = (2 - h) * quarter + h * (quarter // 2)
            add_in(2 + s % 3, start, quarter // 2, [diag_in.at[s, h]])
            side[s][h][0].start()

    def finish(s):
        held = 2 + s % 3
        for out, back in side[s]:
            back.wait_recv()
        last = slice(3 * quarter, rows)
        add_in(held, 3 * quarter, quarter, [side_in.at[s, 0], side_in.at[s, 1]])
        if s == 0:
            own_rows[...] = parts[held, last, :back_width].astype(jnp.float32)
            parts[held, last, back_width:] = (
                parts[held, last, back_width:].astype(jnp.float32) + residual_ref[...]
            ).astype(jnp.bfloat16)
        else:
            rows_along[s - 1][0].start()
        for out, back in cols_along[3 * s : 3 * s + 3]:
            out.start()
        start = pl.multiple_of(back_width + tp * out_width, 128)
        own_cols[at_rows(links.along(QUARTERS - s), quarter), :] = parts[
            held, last, pl.ds(start, out_width)
        ].astype(jnp.float32)

    def before_last():
        core[1][0].wait_send()

    def slot_free():
        for out, back in diag[0] + side[0] + cols_along[:3]:
            out.wait_send()

    plan = {
        (0, 0): [gathers[1].third, gathers[2].second],
        (0, 1): [gathers[2].third],
        (0, 2): [gathers[3].second],
        (0, 3): [lambda: to_core(0), gathers[1].last],
        (1, 0): [gathers[3].third],
        (1, 3): [lambda: diagonal(0), gathers[2].last],
        (2, 2): [lambda: sideways(0)],
        (2, 3): [lambda: to_core(1)],
        (3, 3): [lambda: diagonal(1), gathers[3].last],
        (4, 2): [lambda: sideways(1)],
        (4, 3): [lambda: to_core(2)],
        (5, 0): [lambda: finish(0)],
        (5, 3): [lambda: diagonal(2)],
        (6, 2): [lambda: sideways(2)],
        (6, 3): [lambda: to_core(3)],
        (7, 0): [lambda: finish(1)],
        (7, 3): [lambda: diagonal(3)],
    }
    before = {4: [core[0][0].wait_send], 6: [before_last], 7: [slot_free]}

    gathers[0].second()
    gathers[2].first()
    gathers[0].third()
    gathers[1].second()
    gathers[3].first()
    for load in loads:
        load.wait()
    gathers[0].last()

    @pl.loop(0, 8)
    def _(t):
        s = t // 2
        slot_out = (1 - t % 2) * (s % 2) + (t % 2) * (2 + s % 3)
        for at, steps in before.items():

            @pl.when(t == at)
            def _(steps=steps):
                for step in steps:
                    step()

        def pause(point):
            for (at, where), steps in plan.items():
                if where == point:

                    @pl.when(t == at)
                    def _(steps=steps):
                        for step in steps:
                            step()

        one_block(t, slot_out, pause)

    keeps = []

    def weight_grads(g):
        at = pl.ds(g * block, block)
        if g >= 2:
            keeps[g - 2].wait()
        hidden_cols = two_all[:, :, at].reshape(E * rows, block)
        staged[g % 2, : 2 * count] = matmul(units[: 2 * count], hidden_cols).astype(jnp.bfloat16)
        cot_cols = cot_all[:, :, at].reshape(E * rows, block)
        staged[g % 2, 2 * count :] = matmul(units[2 * count :], cot_cols).astype(jnp.bfloat16)
        keep = links.inside(staged.at[g % 2], grads_out.at[g])
        keep.start()
        keeps.append(keep)

    for g in range(3):
        weight_grads(g)
    sideways(3)
    finish(2)
    for g in range(3, E):
        weight_grads(g)
    finish(3)
    for out, back in rows_along:
        back.wait_recv()
    total = own_rows[...]
    for step in range(1, QUARTERS):
        total = total + rows_in[step - 1].astype(jnp.float32)
    dots = total[:, width : width + SMALL]
    scales = router_ref[:, :SMALL]
    probs = router_ref[:, SMALL : 2 * SMALL]
    chosen = router_ref[:, 2 * SMALL :]
    chosen_grad = chosen * dots
    logit_grad = probs * (chosen_grad - jnp.sum(probs * chosen_grad, axis=1, keepdims=True))
    gate_lane = lax.broadcasted_iota(jnp.int32, (quarter, SMALL), 1) == 2 + E
    logit_grad = jnp.where(gate_lane, dots * scales * (1.0 - scales), logit_grad).astype(
        jnp.bfloat16
    )
    residual = residual_ref[...]
    rstd = lax.rsqrt(jnp.mean(residual * residual, axis=1, keepdims=True) + NORM_EPS)
    mean = jnp.zeros((quarter, 1), jnp.float32)
    for b in range(E):
        at = slice(b * block, (b + 1) * block)
        two_grad = total[:, at] + matmul(logit_grad, small_ref[b])
        normed = residual[:, at] * rstd
        gain = small_ref[b, 1:2, :].astype(jnp.float32)
        back_ref[:, at] = two_grad
        mean = mean + jnp.sum(two_grad * gain * normed, axis=1, keepdims=True)
        grads = matmul_tn(logit_grad, two_all[1, 3 * quarter :, at])
        line = lax.broadcasted_iota(jnp.int32, (SMALL, block), 0)
        gain_grad = jnp.sum(two_grad * normed, axis=0, keepdims=True)
        small_grad_ref[:, at] = jnp.where(line == 1, gain_grad, grads)
    mean = mean / width
    own = at_rows(tp, quarter)
    for b in range(E):
        at = slice(b * block, (b + 1) * block)
        gain = small_ref[b, 1:2, :].astype(jnp.float32)
        normed = residual[:, at] * rstd
        grad = cotangent_ref[own, at].astype(jnp.float32) + rstd * (
            back_ref[:, at] * gain - normed * mean
        )
        back_ref[:, at] = grad
        branch_ref[:, at] = grad.astype(jnp.bfloat16)
    for out, back in cols_along:
        back.wait_recv()
    total = own_cols[...]
    for step in range(1, QUARTERS):
        total = total + cols_in[step - 1].astype(jnp.float32)
    output_ref[...] = total.astype(jnp.bfloat16)
    for out, back in core[2:] + rows_along + cols_along[3:]:
        out.wait_send()
    for s in range(1, QUARTERS):
        for out, back in diag[s] + side[s]:
            out.wait_send()
    for gather in gathers:
        gather.sent()
    for keep in keeps[-2:]:
        keep.wait()


def expert_call(
    two_rows, router_rows, residual_rows, cotangent, cotangent_all, cotangent_plane, slabs, small_full, out_width, routed
):
    quarter, width = residual_rows.shape
    rows = quarter * QUARTERS
    back_width = width + SIDE
    whole = back_width + width
    block = width // E
    bf, f32 = jnp.bfloat16, jnp.float32
    sds = jax.ShapeDtypeStruct
    vmem = pl.BlockSpec(memory_space=pltpu.VMEM)
    hbm = pl.BlockSpec(memory_space=pl.ANY)
    outs = [
        (sds((rows, out_width), bf), vmem),
        (sds((quarter, width), bf), vmem),
        (sds((quarter, width), f32), vmem),
        (sds((SMALL, width), f32), vmem),
        (sds(slabs.shape, bf), hbm),
    ]
    units = slabs.shape[1]
    return pl.pallas_call(
        functools.partial(expert_kernel, routed),
        name="experts",
        out_shape=[o[0] for o in outs],
        in_specs=[hbm, vmem, vmem, vmem, hbm, hbm, hbm, vmem],
        out_specs=[o[1] for o in outs],
        scratch_shapes=[
            pltpu.VMEM((E, rows, back_width), bf),
            pltpu.VMEM((E, rows, width), bf),
            pltpu.VMEM((units, width), bf),
            pltpu.VMEM((units, E * rows), bf),
            pltpu.VMEM((units, rows), f32),
            pltpu.VMEM((5, rows, whole), bf),
            pltpu.VMEM((2, rows, whole), bf),
            pltpu.VMEM((QUARTERS, 2, quarter // 2, whole), bf),
            pltpu.VMEM((QUARTERS, 2, quarter, whole), bf),
            pltpu.VMEM((QUARTERS - 1, quarter, back_width), bf),
            pltpu.VMEM((QUARTERS - 1, rows, out_width), bf),
            pltpu.VMEM((quarter, back_width), f32),
            pltpu.VMEM((rows, out_width), f32),
            pltpu.VMEM((2, units, block), bf),
            pltpu.SemaphoreType.DMA((80,)),
            pltpu.SemaphoreType.DMA((80,)),
            pltpu.SemaphoreType.DMA((56,)),
            pltpu.SemaphoreType.REGULAR,
        ],
        compiler_params=pltpu.CompilerParams(
            collective_id=2, has_side_effects=True, vmem_limit_bytes=63 * 2**20
        ),
    )(
        two_rows,
        router_rows,
        residual_rows,
        cotangent,
        cotangent_all,
        cotangent_plane,
        slabs,
        small_full,
    )


class Scatter:
    def __init__(self, links, parts, core_in, diag_in, side_in):
        self.links, self.parts = links, parts
        self.core_in, self.diag_in, self.side_in = core_in, diag_in, side_in
        self.rows = parts.shape[1]
        p, tp = links.peer, links.tp
        half = self.rows // 2
        self.core = [
            links.remote(
                parts.at[p(bits + CORE_BIT)], core_in.at[i], (p(CORE_BIT), tp), core_in.at[i]
            )
            for i, bits in enumerate((6, 2, 4, 0))
        ]
        self.diag = [
            links.remote(
                parts.at[p(6), pl.ds(h * half, half)], diag_in.at[h], (p(bits), tp), diag_in.at[h]
            )
            for h, bits in enumerate((Y_BIT, X_BIT))
        ]
        self.side = [
            links.remote(parts.at[p(bits)], side_in.at[i], (p(bits), tp), side_in.at[i])
            for i, bits in enumerate((X_BIT, Y_BIT))
        ]

    def add(self, index, first, count, refs, target=None):
        chunk = 32

        @pl.loop(0, count // chunk)
        def _(r):
            here = pl.ds(pl.multiple_of(first + r * chunk, chunk), chunk)
            there = pl.ds(pl.multiple_of(r * chunk, chunk), chunk)
            total = self.parts[index, here, :].astype(jnp.float32)
            for ref in refs:
                total = total + ref[there, :].astype(jnp.float32)
            if target is None:
                self.parts[index, here, :] = total.astype(jnp.bfloat16)
            else:
                target[here, :] = total

    def to_core(self):
        for out, back in self.core:
            out.start()

    def diagonal(self):
        self.core[0][1].wait_recv()
        self.add(self.links.peer(6), 0, self.rows, [self.core_in.at[0]])
        for out, back in self.diag:
            out.start()

    def sideways(self, i):
        index = self.links.peer((X_BIT, Y_BIT)[i])
        self.core[1 + i][1].wait_recv()
        self.add(index, 0, self.rows, [self.core_in.at[1 + i]])
        self.diag[i][1].wait_recv()
        self.add(index, i * (self.rows // 2), self.rows // 2, [self.diag_in.at[i]])
        self.side[i][0].start()

    def finish(self, target):
        self.core[3][1].wait_recv()
        for out, back in self.side:
            back.wait_recv()
        self.add(
            self.links.fs,
            0,
            self.rows,
            [self.core_in.at[3], self.side_in.at[0], self.side_in.at[1]],
            target,
        )

    def sent(self):
        for out, back in self.core + self.diag + self.side:
            out.wait_send()


def backward_kernel(
    branch_ref,
    residual_ref,
    small_grad_ref,
    attended_ref,
    query_ref,
    hidden_ref,
    tokens_ref,
    kv_ref,
    qkv_ref,
    out_ref,
    small_ref,
    cos_ref,
    sin_ref,
    start_ref,
    slabs_ref,
    input_grad_ref,
    qkv_own,
    out_own,
    small_own,
    up_all,
    shared_up_all,
    down_all,
    shared_down_all,
    kv_full,
    qkv_full,
    out_full,
    branch_all,
    odds,
    query_grad,
    projected,
    kv_total,
    kv_parts,
    kv_core,
    kv_diag,
    kv_side,
    qkv_parts,
    qkv_core,
    qkv_diag,
    qkv_side,
    out_parts,
    out_core,
    out_diag,
    out_side,
    one_parts,
    one_in,
    grad_rows,
    small_parts,
    small_in,
    small_column,
    send,
    recv,
    local,
):
    links = Links(send, recv, local)
    fs, tp = links.fs, links.tp
    quarter, width = residual_ref.shape
    rows = quarter * QUARTERS
    block = width // E
    local_width = query_ref.shape[1]
    heads = local_width // HD
    seqs = rows // SEQ_DEV
    length = E * SEQ_DEV
    scale = HD ** (-0.5)

    def at_rows(index, size):
        return pl.ds(pl.multiple_of(index * size, size), size)

    own = at_rows(tp, quarter)
    links.greet(range(1, 8), range(1, QUARTERS))
    branch = []
    for step in range(1, QUARTERS):
        here = branch_all.at[own]
        landing = branch_all.at[at_rows(links.along(QUARTERS - step), quarter)]
        branch.append(links.remote(branch_ref, here, (fs, links.along(step)), landing))
    for out, back in branch:
        out.start()
    branch_all[own, :] = branch_ref[...]
    routed, shared = down_all.shape[1], shared_down_all.shape[0] // E

    def slab(block_index, source):
        units = pl.ds(pl.multiple_of(source * shared, 16), shared)
        places = [
            up_all.at[source],
            shared_up_all.at[0, units],
            shared_up_all.at[1, units],
            down_all.at[source],
            shared_down_all.at[units],
        ]
        placed, at = [], 0
        for place, size in zip(places, (2 * routed, shared, shared, routed, shared), strict=True):
            placed.append((slabs_ref.at[block_index, pl.ds(at, size)], place))
            at += size
        return placed

    slab_copies = []
    for bits in (1, 6, 7, 2, 4, 3, 5):
        peer = links.peer(bits)
        for (piece, place), (_, landing) in zip(slab(peer, fs), slab(peer, peer), strict=True):
            slab_copies.append(links.remote(piece, place, (peer, tp), landing))
    for out, back in slab_copies[:25]:
        out.start()
    slab_own = [links.inside(piece, place) for piece, place in slab(fs, fs)]
    for copy in slab_own:
        copy.start()
    kv_load = links.inside(kv_ref, kv_full)
    kv_load.start()
    out_load = links.inside(out_ref, out_full)
    out_load.start()
    qkv_load = links.inside(qkv_ref, qkv_full)
    qkv_load.start()
    kv_sum = Scatter(links, kv_parts, kv_core, kv_diag, kv_side)
    qkv_sum = Scatter(links, qkv_parts, qkv_core, qkv_diag, qkv_side)
    out_sum = Scatter(links, out_parts, out_core, out_diag, out_side)

    kv_load.wait()
    key_pos = lax.broadcasted_iota(jnp.int32, (SEQ_DEV, length), 1)
    query_pos = fs * SEQ_DEV + lax.broadcasted_iota(jnp.int32, (SEQ_DEV, length), 0)
    for s in range(seqs):
        here = slice(s * SEQ_DEV, (s + 1) * SEQ_DEV)
        allowed = (key_pos <= query_pos) & (key_pos >= as_column(start_ref[s : s + 1, :]))
        for h in range(heads):
            cols = slice(h * HD, (h + 1) * HD)
            keys = kv_full[:, here, cols].reshape(length, HD)
            scores = matmul_nt(query_ref[here, cols], keys) * scale
            scores = jnp.where(allowed, scores, NEG_FILL)
            top = jnp.max(scores, axis=1, keepdims=True)
            weights = jnp.exp(scores - top)
            odds[s * heads + h] = weights / jnp.sum(weights, axis=1, keepdims=True)
    out_load.wait()
    for out, back in branch:
        back.wait_recv()
    attended_grad = jnp.zeros((rows, local_width), jnp.float32)
    for b in range(E):
        attended_grad = attended_grad + matmul_nt(
            branch_all[:, b * block : (b + 1) * block], out_full[b]
        )
    query_grad[...] = attended_grad.astype(jnp.bfloat16)
    for s in range(seqs):
        here = slice(s * SEQ_DEV, (s + 1) * SEQ_DEV)
        for h in range(heads):
            cols = slice(h * HD, (h + 1) * HD)
            vcols = slice(local_width + h * HD, local_width + (h + 1) * HD)
            keys = kv_full[:, here, cols].reshape(length, HD)
            values = kv_full[:, here, vcols].reshape(length, HD)
            grad = query_grad[here, cols]
            probs = odds[s * heads + h]
            weights_grad = matmul_nt(grad, values)
            delta = jnp.sum(probs * weights_grad, axis=1, keepdims=True)
            score_grad = (probs * (weights_grad - delta)).astype(jnp.bfloat16)
            key_grad = matmul_tn(score_grad, query_ref[here, cols]) * scale
            value_grad = matmul_tn(probs.astype(jnp.bfloat16), grad)
            kv_parts[:, here, cols] = key_grad.astype(jnp.bfloat16).reshape(E, SEQ_DEV, HD)
            kv_parts[:, here, vcols] = value_grad.astype(jnp.bfloat16).reshape(E, SEQ_DEV, HD)
            projected[0, here, cols] = turn(
                matmul(score_grad, keys) * scale, cos_ref[here, :], -sin_ref[here, :]
            ).astype(jnp.bfloat16)
    kv_sum.to_core()
    attended = attended_ref[...]
    for b in range(E):
        cols = slice(b * block, (b + 1) * block)
        out_parts[b] = matmul_tn(attended, branch_all[:, cols]).astype(jnp.bfloat16)
    kv_sum.diagonal()
    out_sum.to_core()

    def weight_grad(j):
        for b in range(E):
            cols = slice(b * block, (b + 1) * block)
            qkv_parts[b, j * block : (j + 1) * block] = matmul_tn(
                hidden_ref[:, cols], projected[j]
            ).astype(jnp.bfloat16)

    weight_grad(0)
    kv_sum.sideways(0)
    kv_sum.sideways(1)
    out_sum.diagonal()
    qkv_load.wait()
    kv_sum.finish(kv_total)
    for out, back in slab_copies[25:]:
        out.start()
    projected[1] = turn(kv_total[:, :local_width], cos_ref[...], -sin_ref[...]).astype(jnp.bfloat16)
    projected[2] = kv_total[:, local_width:].astype(jnp.bfloat16)
    for b in range(E):
        cols = slice(b * block, (b + 1) * block)
        part = jnp.zeros((rows, block), jnp.float32)
        for j in range(3):
            part = part + matmul_nt(projected[j], qkv_full[j, cols])
        one_parts[:, cols] = part.astype(jnp.bfloat16)
    column = []
    for step in range(1, QUARTERS):
        peer = links.along(step)
        column.append(
            links.remote(
                one_parts.at[at_rows(peer, quarter)],
                one_in.at[step - 1],
                (fs, peer),
                one_in.at[step - 1],
            )
        )
    for out, back in column:
        out.start()
    weight_grad(1)
    weight_grad(2)
    qkv_sum.to_core()
    out_sum.sideways(0)
    out_sum.sideways(1)
    qkv_sum.diagonal()
    qkv_sum.sideways(0)
    qkv_sum.sideways(1)
    for out, back in column:
        back.wait_recv()
    tokens = tokens_ref[own, :].astype(jnp.float32)
    rstd = lax.rsqrt(jnp.mean(tokens * tokens, axis=1, keepdims=True) + NORM_EPS)
    total = one_parts[own, :].astype(jnp.float32)
    for step in range(1, QUARTERS):
        total = total + one_in[step - 1].astype(jnp.float32)
    mean = jnp.zeros((quarter, 1), jnp.float32)
    sub = lax.broadcasted_iota(jnp.int32, (SMALL, block), 0)
    for b in range(E):
        at = slice(b * block, (b + 1) * block)
        gain = small_ref[b, 0:1, :].astype(jnp.float32)
        normed = tokens[:, at] * rstd
        mean = mean + jnp.sum(total[:, at] * gain * normed, axis=1, keepdims=True)
        gain_grad = jnp.sum(total[:, at] * normed, axis=0, keepdims=True)
        small_parts[b] = jnp.where(sub == 0, gain_grad, small_grad_ref[:, at])
    mean = mean / width
    for b in range(E):
        at = slice(b * block, (b + 1) * block)
        gain = small_ref[b, 0:1, :].astype(jnp.float32)
        normed = tokens[:, at] * rstd
        grad_rows[:, at] = (
            residual_ref[:, at] + rstd * (total[:, at] * gain - normed * mean)
        ).astype(jnp.bfloat16)
    spread = []
    for step in range(1, QUARTERS):
        peer = links.along(step)
        landing = input_grad_ref.at[at_rows(links.along(QUARTERS - step), quarter)]
        spread.append(links.remote(grad_rows, input_grad_ref.at[own], (fs, peer), landing))
    for out, back in spread:
        out.start()
    keep = links.inside(grad_rows, input_grad_ref.at[own])
    keep.start()
    small_copies = []
    for bits in range(1, E):
        peer = links.peer(bits)
        small_copies.append(
            links.remote(
                small_parts.at[peer], small_in.at[bits - 1], (peer, tp), small_in.at[bits - 1]
            )
        )
    for out, back in small_copies:
        out.start()
    out_sum.finish(out_own)
    for out, back in small_copies:
        back.wait_recv()
    small_total = small_parts[fs]
    for bits in range(1, E):
        small_total = small_total + small_in[bits - 1]
    small_column[tp] = small_total
    small_spread = []
    for step in range(1, QUARTERS):
        here = small_column.at[tp]
        landing = small_column.at[links.along(QUARTERS - step)]
        small_spread.append(links.remote(here, here, (fs, links.along(step)), landing))
    for out, back in small_spread:
        out.start()
    qkv_sum.finish(qkv_own)
    for out, back in small_spread:
        back.wait_recv()
    small_own[...] = small_column[0] + small_column[1] + small_column[2] + small_column[3]
    for out, back in spread + slab_copies:
        back.wait_recv()
    for copy in (*slab_own, keep):
        copy.wait()
    for out, back in branch + slab_copies + column + spread + small_copies + small_spread:
        out.wait_send()
    for scatter in (kv_sum, out_sum, qkv_sum):
        scatter.sent()


def backward_call(
    branch_rows,
    residual_grad,
    small_grad,
    attended,
    query_rows,
    hidden_one,
    tokens,
    kv_all,
    qkv_full,
    out_full,
    small_full,
    cosine,
    sine,
    start,
    slabs,
    routed,
):
    quarter, width = residual_grad.shape
    rows = quarter * QUARTERS
    block = width // E
    local_width = query_rows.shape[1]
    shared = slabs.shape[1] // 3 - routed
    bf, f32 = jnp.bfloat16, jnp.float32
    sds = jax.ShapeDtypeStruct
    vmem = pl.BlockSpec(memory_space=pltpu.VMEM)
    hbm = pl.BlockSpec(memory_space=pl.ANY)
    outs = [
        (sds((rows, width), bf), hbm),
        (sds((3 * block, local_width), f32), vmem),
        (sds((local_width, block), f32), vmem),
        (sds((SMALL, block), f32), vmem),
        (sds((E, 2 * routed, block), bf), hbm),
        (sds((2, E * shared, block), bf), hbm),
        (sds((E, routed, block), bf), hbm),
        (sds((E * shared, block), bf), hbm),
    ]

    def scatter_scratch(count, columns):
        return [
            pltpu.VMEM((E, count, columns), bf),
            pltpu.VMEM((4, count, columns), bf),
            pltpu.VMEM((2, count // 2, columns), bf),
            pltpu.VMEM((2, count, columns), bf),
        ]

    return pl.pallas_call(
        backward_kernel,
        name="attention_backward",
        out_shape=[o[0] for o in outs],
        in_specs=[vmem] * 7 + [hbm] * 3 + [vmem] * 4 + [hbm],
        out_specs=[o[1] for o in outs],
        scratch_shapes=[
            pltpu.VMEM((E, rows, 2 * local_width), bf),
            pltpu.VMEM((3, width, local_width), bf),
            pltpu.VMEM((E, local_width, block), bf),
            pltpu.VMEM((rows, width), bf),
            pltpu.VMEM((rows // SEQ_DEV * local_width // HD, SEQ_DEV, E * SEQ_DEV), f32),
            pltpu.VMEM((rows, local_width), bf),
            pltpu.VMEM((3, rows, local_width), bf),
            pltpu.VMEM((rows, 2 * local_width), f32),
            *scatter_scratch(rows, 2 * local_width),
            *scatter_scratch(3 * block, local_width),
            *scatter_scratch(local_width, block),
            pltpu.VMEM((rows, width), bf),
            pltpu.VMEM((QUARTERS - 1, quarter, width), bf),
            pltpu.VMEM((quarter, width), bf),
            pltpu.VMEM((E, SMALL, block), f32),
            pltpu.VMEM((E - 1, SMALL, block), f32),
            pltpu.VMEM((QUARTERS, SMALL, block), f32),
            pltpu.SemaphoreType.DMA((96,)),
            pltpu.SemaphoreType.DMA((96,)),
            pltpu.SemaphoreType.DMA((16,)),
        ],
        compiler_params=pltpu.CompilerParams(
            collective_id=3, has_side_effects=True, vmem_limit_bytes=62 * 2**20
        ),
    )(
        branch_rows,
        residual_grad,
        small_grad,
        attended,
        query_rows,
        hidden_one,
        tokens,
        kv_all,
        qkv_full,
        out_full,
        small_full,
        cosine,
        sine,
        start,
        slabs,
    )


def shards_units(
    tokens,
    cotangent,
    qkv_weight,
    out_weight,
    norm_gains,
    router_weight,
    shared_gate,
    expert_gate_up,
    expert_down,
    shared_gate_up,
    shared_down,
    routes,
    doc_start,
):
    tok_rows, width = tokens.shape
    seq_count = tok_rows // SEQ_DEV
    fs_index = lax.axis_index("fs")
    query_pos = fs_index * SEQ_DEV + jnp.arange(SEQ_DEV, dtype=jnp.int32)
    positions = jnp.tile(query_pos, seq_count)
    half_cos, half_sin = rope_tables(positions)
    cosine = jnp.concatenate([half_cos, half_cos], axis=1)
    sine = jnp.concatenate([-half_sin, half_sin], axis=1)
    routed_units = expert_down.shape[1]
    (
        two_rows,
        residual_rows,
        router_rows,
        attended,
        query_rows,
        hidden_one,
        slabs,
        cotangent_all,
        cotangent_plane,
        kv_all,
        qkv_full,
        out_full,
        small_full,
    ) = forward_call(
        tokens,
        cotangent,
        qkv_weight,
        out_weight,
        norm_gains,
        router_weight,
        shared_gate[None],
        jnp.transpose(expert_gate_up, (0, 2, 3, 1)).reshape(E, 2 * routed_units, -1),
        jnp.transpose(shared_gate_up, (1, 2, 0)),
        expert_down,
        shared_down,
        cosine,
        sine,
        doc_start.reshape(seq_count, SEQ_DEV),
        routes.T,
    )
    output, branch_rows, residual_grad, small_grad, grad_slabs = expert_call(
        two_rows,
        router_rows,
        residual_rows,
        cotangent,
        cotangent_all,
        cotangent_plane,
        slabs,
        small_full,
        width // QUARTERS,
        routed_units,
    )
    input_grad, qkv_own, out_own, small_own, up_own, shared_up_own, down_own, shared_down_own = (
        backward_call(
            branch_rows,
            residual_grad,
            small_grad,
            attended,
            query_rows,
            hidden_one,
            tokens,
            kv_all,
            qkv_full,
            out_full,
            small_full,
            cosine,
            sine,
            doc_start.reshape(seq_count, SEQ_DEV),
            grad_slabs,
            routed_units,
        )
    )
    f32 = jnp.float32
    up_own = up_own.reshape(E, 2, routed_units, -1)
    return (
        output,
        input_grad.astype(f32),
        qkv_own.reshape(qkv_weight.shape),
        out_own,
        small_own[:2],
        small_own[2 : 2 + E],
        small_own[2 + E],
        jnp.transpose(up_own, (0, 3, 1, 2)).astype(f32),
        down_own.astype(f32),
        jnp.transpose(shared_up_own, (2, 0, 1)).astype(f32),
        shared_down_own.astype(f32),
    )


def solution(mesh):
    return jax.shard_map(
        shards_units if dict(mesh.shape) == {"fs": E, "tp": QUARTERS} else shards_gathered,
        mesh=mesh,
        in_specs=(
            P("fs", None),
            P("fs", None),
            P(None, "fs", "tp"),
            P("tp", "fs"),
            P(None, "fs"),
            P(None, "fs"),
            P("fs"),
            P(None, "fs", None, "tp"),
            P(None, "tp", "fs"),
            P("fs", None, "tp"),
            P("tp", "fs"),
            P("fs", None),
            P("fs"),
        ),
        out_specs=(
            P("fs", "tp"),
            P("fs", None),
            P(None, "fs", "tp"),
            P("tp", "fs"),
            P(None, "fs"),
            P(None, "fs"),
            P("fs"),
            P(None, "fs", None, "tp"),
            P(None, "tp", "fs"),
            P("fs", None, "tp"),
            P("tp", "fs"),
        ),
        check_vma=False,
    )
```

```python
import functools
import math

import jax
import jax.numpy as jnp
from jax import lax
from jax.experimental import pallas as pl
from jax.experimental.pallas import tpu as pltpu
from jax.sharding import PartitionSpec as P

HD = 128
E = 8
SEQ_DEV = 128
SIDE = 128


NORM_EPS = 1e-06
NEG_FILL = -1e30
ROPE_BASE = 1000000.0


def rope_tables(positions):
    half_size = HD // 2
    frequency = ROPE_BASE ** (-(jnp.arange(half_size, dtype=jnp.float32) * 2.0 / HD))
    angles = positions.astype(jnp.float32)[:, None] * frequency[None, :]
    return (jnp.cos(angles), jnp.sin(angles))


def rotate(values, cosine, sine_table):
    shaped = values.reshape(values.shape[0], -1, HD)
    half_size = HD // 2
    first_half = shaped[..., :half_size]
    second_half = shaped[..., half_size:]
    cos_part = cosine[:, None, :]
    sin_part = sine_table[:, None, :]
    turned = jnp.concatenate(
        [
            first_half * cos_part - second_half * sin_part,
            second_half * cos_part + first_half * sin_part,
        ],
        axis=-1,
    )
    return turned.reshape(values.shape)


def key_mask(query_pos, query_start, first_dev, group_size):
    key_pos = (first_dev + jnp.arange(group_size, dtype=jnp.int32)[:, None]) * SEQ_DEV + jnp.arange(
        SEQ_DEV, dtype=jnp.int32
    )[None, :]
    key_pos = key_pos[None, None, :, :]
    return (key_pos <= query_pos[None, :, None, None]) & (key_pos >= query_start[:, :, None, None])


def shards_gathered(
    tokens,
    cotangent,
    qkv_weight,
    out_weight,
    norm_gains,
    router_weight,
    shared_gate,
    expert_gate_up,
    expert_down,
    shared_gate_up,
    shared_down,
    routes,
    doc_start,
):
    tok_rows = tokens.shape[0]
    seq_count = tok_rows // SEQ_DEV
    local_width = qkv_weight.shape[2]
    head_count = local_width // HD
    out_width = tokens.shape[1] // lax.axis_size("tp")
    score_scale = HD ** (-0.5)
    fs_index = lax.axis_index("fs")
    tp_index = lax.axis_index("tp")
    query_pos = fs_index * SEQ_DEV + jnp.arange(SEQ_DEV, dtype=jnp.int32)
    positions = jnp.tile(query_pos, seq_count)
    query_start = doc_start.reshape(seq_count, SEQ_DEV)
    cosine, sine_table = rope_tables(positions)
    group_limit = max(1, 512 // SEQ_DEV)
    qkv_full, out_full, gains_full, router_full, shared_gate_full = (
        lax.all_gather(qkv_weight, "fs", axis=1, tiled=True),
        lax.all_gather(out_weight, "fs", axis=1, tiled=True),
        lax.all_gather(norm_gains, "fs", axis=1, tiled=True),
        lax.all_gather(router_weight, "fs", axis=1, tiled=True),
        lax.all_gather(shared_gate, "fs", axis=0, tiled=True),
    )
    token_float = tokens.astype(jnp.float32)
    rstd_one = lax.rsqrt(jnp.mean(token_float * token_float, axis=1, keepdims=True) + NORM_EPS)
    normed_one = token_float * rstd_one
    hidden_one = (normed_one * gains_full[0].astype(jnp.float32)[None, :]).astype(jnp.bfloat16)
    projected = jnp.einsum("td,jdf->jtf", hidden_one, qkv_full, preferred_element_type=jnp.float32)
    query_rows = rotate(projected[0], cosine, sine_table).astype(jnp.bfloat16)
    key_own = rotate(projected[1], cosine, sine_table).astype(jnp.bfloat16)
    value_own = projected[2].astype(jnp.bfloat16)
    query_heads = query_rows.reshape(seq_count, SEQ_DEV, head_count, HD)

    def score_block(key_group, first_dev):
        allowed = key_mask(query_pos, query_start, first_dev, key_group.shape[0])[:, None]
        scores = (
            jnp.einsum(
                "pqhd,gpkhd->phqgk", query_heads, key_group, preferred_element_type=jnp.float32
            )
            * score_scale
        )
        return (jnp.where(allowed, scores, NEG_FILL), allowed)

    def forward_update(running, key_group, value_group, first_dev):
        run_max, run_sum, accumulated = running
        scores, allowed = score_block(key_group, first_dev)
        new_max = jnp.maximum(run_max, jnp.max(scores, axis=(3, 4)))
        weights = jnp.where(allowed, jnp.exp(scores - new_max[..., None, None]), 0.0)
        factor = jnp.exp(run_max - new_max)
        new_sum = run_sum * factor + jnp.sum(weights, axis=(3, 4))
        mixed_part = jnp.einsum(
            "phqgk,gpkhd->pqhd",
            weights.astype(jnp.bfloat16),
            value_group,
            preferred_element_type=jnp.float32,
        )
        new_accum = accumulated * jnp.transpose(factor, (0, 2, 1))[..., None] + mixed_part
        return (new_max, new_sum, new_accum)

    initial = (
        jnp.full((seq_count, head_count, SEQ_DEV), NEG_FILL, jnp.float32),
        jnp.zeros((seq_count, head_count, SEQ_DEV), jnp.float32),
        jnp.zeros((seq_count, SEQ_DEV, head_count, HD), jnp.float32),
    )
    running = initial
    key_piece = lax.all_gather(key_own, "fs", axis=0, tiled=True)
    value_piece = lax.all_gather(value_own, "fs", axis=0, tiled=True)
    shard_count = key_piece.shape[0] // tok_rows
    group_size = math.gcd(shard_count, group_limit)
    step_count = shard_count // group_size
    shaped = (step_count, group_size, seq_count, SEQ_DEV, head_count, HD)
    first_dev = jnp.int32(0) // tok_rows

    def one_step(carried, inputs):
        key_group, value_group, group_index = inputs
        start_dev = group_index * group_size
        updated = lax.cond(
            start_dev <= fs_index,
            lambda state_in: forward_update(state_in, key_group, value_group, start_dev),
            lambda state_in: state_in,
            carried,
        )
        return (updated, None)

    running, ignored = lax.scan(
        one_step,
        running,
        (
            key_piece.reshape(shaped),
            value_piece.reshape(shaped),
            jnp.arange(step_count, dtype=jnp.int32),
        ),
    )
    run_max, run_sum, accumulated = running
    attended_heads = (accumulated / jnp.transpose(run_sum, (0, 2, 1))[..., None]).astype(
        jnp.bfloat16
    )
    log_total = run_max + jnp.log(run_sum)
    attended = attended_heads.reshape(tok_rows, local_width)
    branch_part = jnp.dot(attended, out_full, preferred_element_type=jnp.float32)
    branch = lax.psum(branch_part.astype(jnp.bfloat16), "tp").astype(jnp.float32)
    residual = token_float + branch
    rstd_two = lax.rsqrt(jnp.mean(residual * residual, axis=1, keepdims=True) + NORM_EPS)
    normed_two = residual * rstd_two
    hidden_two = (normed_two * gains_full[1].astype(jnp.float32)[None, :]).astype(jnp.bfloat16)
    expert_gate_all, expert_down_all, shared_up_all, shared_down_all = (
        lax.all_gather(expert_gate_up, "fs", axis=1, tiled=True),
        lax.all_gather(expert_down, "fs", axis=2, tiled=True),
        lax.all_gather(shared_gate_up, "fs", axis=0, tiled=True),
        lax.all_gather(shared_down, "fs", axis=1, tiled=True),
    )
    logits = jnp.einsum("td,ed->te", hidden_two, router_full, preferred_element_type=jnp.float32)
    router_probs = jax.nn.softmax(logits, axis=-1)
    chosen = jnp.sum(
        (routes[:, :, None] == jnp.arange(E, dtype=jnp.int32)[None, None, :]).astype(jnp.float32),
        axis=1,
    )
    gate_weights = router_probs * chosen
    gate_up = jnp.einsum(
        "td,edkf->tekf", hidden_two, expert_gate_all, preferred_element_type=jnp.float32
    )
    gate_part = gate_up[:, :, 0]
    up_part = gate_up[:, :, 1]
    gate_sigmoid = jax.nn.sigmoid(gate_part)
    active = gate_part * gate_sigmoid * up_part
    hidden = (gate_weights[:, :, None] * active).astype(jnp.bfloat16)
    shared_in = jnp.einsum(
        "td,dkf->tkf", hidden_two, shared_up_all, preferred_element_type=jnp.float32
    )
    shared_gate_in = shared_in[:, 0]
    shared_up_in = shared_in[:, 1]
    shared_sigmoid = jax.nn.sigmoid(shared_gate_in)
    shared_active = shared_gate_in * shared_sigmoid * shared_up_in
    gate_logit = jnp.einsum(
        "td,d->t", hidden_two, shared_gate_full, preferred_element_type=jnp.float32
    )
    gate_value = jax.nn.sigmoid(gate_logit)
    shared_hidden = (gate_value[:, None] * shared_active).astype(jnp.bfloat16)
    mixture_part = jnp.einsum(
        "tef,efd->td", hidden, expert_down_all, preferred_element_type=jnp.float32
    ) + jnp.dot(shared_hidden, shared_down_all, preferred_element_type=jnp.float32)
    mixture = lax.psum_scatter(
        mixture_part.astype(jnp.bfloat16), "tp", scatter_dimension=1, tiled=True
    ).astype(jnp.float32)
    output = (
        lax.dynamic_slice_in_dim(residual, tp_index * out_width, out_width, 1) + mixture
    ).astype(jnp.bfloat16)
    qkv_back, out_back, gains_back, router_back, shared_gate_back = (
        lax.all_gather(qkv_weight, "fs", axis=1, tiled=True),
        lax.all_gather(out_weight, "fs", axis=1, tiled=True),
        lax.all_gather(norm_gains, "fs", axis=1, tiled=True),
        lax.all_gather(router_weight, "fs", axis=1, tiled=True),
        lax.all_gather(shared_gate, "fs", axis=0, tiled=True),
    )
    expert_gate_back, expert_down_back, shared_up_back, shared_down_back = (
        lax.all_gather(expert_gate_up, "fs", axis=1, tiled=True),
        lax.all_gather(expert_down, "fs", axis=2, tiled=True),
        lax.all_gather(shared_gate_up, "fs", axis=0, tiled=True),
        lax.all_gather(shared_down, "fs", axis=1, tiled=True),
    )
    hidden_grad = jnp.einsum(
        "td,efd->tef", cotangent, expert_down_back, preferred_element_type=jnp.float32
    )
    expert_down_grad = jnp.einsum(
        "tef,td->efd", hidden, cotangent, preferred_element_type=jnp.float32
    )
    shared_grad = jnp.einsum(
        "td,fd->tf", cotangent, shared_down_back, preferred_element_type=jnp.float32
    )
    shared_down_grad = jnp.einsum(
        "tf,td->fd", shared_hidden, cotangent, preferred_element_type=jnp.float32
    )
    gate_dot = jnp.sum(active * hidden_grad, axis=2)
    shared_dot = jnp.sum(shared_active * shared_grad, axis=1)
    active_grad = gate_weights[:, :, None] * hidden_grad
    gate_grad = active_grad * up_part * gate_sigmoid * (1.0 + gate_part * (1.0 - gate_sigmoid))
    up_grad = active_grad * gate_part * gate_sigmoid
    gate_up_grad = jnp.stack([gate_grad, up_grad], axis=2).astype(jnp.bfloat16)
    shared_active_grad = gate_value[:, None] * shared_grad
    shared_gate_grad = (
        shared_active_grad
        * shared_up_in
        * shared_sigmoid
        * (1.0 + shared_gate_in * (1.0 - shared_sigmoid))
    )
    shared_unit_grad = shared_active_grad * shared_gate_in * shared_sigmoid
    shared_up_grad = jnp.stack([shared_gate_grad, shared_unit_grad], axis=1).astype(jnp.bfloat16)
    expert_gate_grad = jnp.einsum(
        "td,tekf->edkf", hidden_two, gate_up_grad, preferred_element_type=jnp.float32
    )
    shared_proj_grad = jnp.einsum(
        "td,tkf->dkf", hidden_two, shared_up_grad, preferred_element_type=jnp.float32
    )
    input_part = jnp.einsum(
        "tekf,edkf->td", gate_up_grad, expert_gate_back, preferred_element_type=jnp.float32
    ) + jnp.einsum(
        "tkf,dkf->td", shared_up_grad, shared_up_back, preferred_element_type=jnp.float32
    )
    input_sum, gate_sum, shared_sum = (
        lax.psum(input_part.astype(jnp.bfloat16), "tp").astype(jnp.float32),
        lax.psum(gate_dot.astype(jnp.bfloat16), "tp").astype(jnp.float32),
        lax.psum(shared_dot.astype(jnp.bfloat16), "tp").astype(jnp.float32),
    )
    chosen_grad = chosen * gate_sum
    logit_grad = (
        router_probs * (chosen_grad - jnp.sum(router_probs * chosen_grad, axis=1, keepdims=True))
    ).astype(jnp.bfloat16)
    gate_logit_grad = (shared_sum * gate_value * (1.0 - gate_value)).astype(jnp.bfloat16)
    router_grad = jnp.einsum(
        "te,td->ed", logit_grad, hidden_two, preferred_element_type=jnp.float32
    )
    shared_vector_grad = jnp.einsum(
        "t,td->d", gate_logit_grad, hidden_two, preferred_element_type=jnp.float32
    )
    two_grad = (
        input_sum
        + jnp.einsum("te,ed->td", logit_grad, router_back, preferred_element_type=jnp.float32)
        + gate_logit_grad.astype(jnp.float32)[:, None]
        * shared_gate_back.astype(jnp.float32)[None, :]
    )
    scaled_two = two_grad * gains_back[1].astype(jnp.float32)[None, :]
    gain_two_grad = jnp.sum(two_grad * normed_two, axis=0)
    residual_grad = cotangent.astype(jnp.float32) + rstd_two * (
        scaled_two - normed_two * jnp.mean(scaled_two * normed_two, axis=1, keepdims=True)
    )
    branch_grad = residual_grad.astype(jnp.bfloat16)
    out_grad = jnp.einsum("tf,td->fd", attended, branch_grad, preferred_element_type=jnp.float32)
    attended_grad = jnp.einsum(
        "td,fd->tf", branch_grad, out_back, preferred_element_type=jnp.float32
    ).astype(jnp.bfloat16)
    grad_heads = attended_grad.reshape(seq_count, SEQ_DEV, head_count, HD)
    delta_rows = jnp.einsum(
        "pqhd,pqhd->phq", grad_heads, attended_heads, preferred_element_type=jnp.float32
    )
    key_all, value_all = (
        lax.all_gather(key_own, "fs", axis=0, tiled=True),
        lax.all_gather(value_own, "fs", axis=0, tiled=True),
    )
    device_count = key_all.shape[0] // tok_rows
    back_group = math.gcd(device_count, group_limit)
    back_steps = device_count // back_group
    back_shape = (back_steps, back_group, seq_count, SEQ_DEV, head_count, HD)

    def backward_update(key_group, value_group, start_dev):
        scores, allowed = score_block(key_group, start_dev)
        probs_block = jnp.where(allowed, jnp.exp(scores - log_total[..., None, None]), 0.0)
        weights_grad = jnp.einsum(
            "pqhd,gpkhd->phqgk", grad_heads, value_group, preferred_element_type=jnp.float32
        )
        score_grad = (probs_block * (weights_grad - delta_rows[..., None, None])).astype(
            jnp.bfloat16
        )
        query_part = (
            jnp.einsum(
                "phqgk,gpkhd->pqhd", score_grad, key_group, preferred_element_type=jnp.float32
            )
            * score_scale
        )
        key_part = (
            jnp.einsum(
                "phqgk,pqhd->gpkhd", score_grad, query_heads, preferred_element_type=jnp.float32
            )
            * score_scale
        )
        value_part = jnp.einsum(
            "phqgk,pqhd->gpkhd",
            probs_block.astype(jnp.bfloat16),
            grad_heads,
            preferred_element_type=jnp.float32,
        )
        return (query_part, key_part, value_part)

    empty_grads = (
        jnp.zeros((seq_count, SEQ_DEV, head_count, HD), jnp.float32),
        jnp.zeros((back_group, seq_count, SEQ_DEV, head_count, HD), jnp.float32),
        jnp.zeros((back_group, seq_count, SEQ_DEV, head_count, HD), jnp.float32),
    )
    scan_inputs = (
        key_all.reshape(back_shape),
        value_all.reshape(back_shape),
        jnp.arange(back_steps, dtype=jnp.int32),
    )

    def back_step(query_acc, inputs):
        key_group, value_group, group_index = inputs
        start_dev = group_index * back_group
        query_part, key_part, value_part = lax.cond(
            start_dev <= fs_index,
            lambda ignored_in: backward_update(key_group, value_group, start_dev),
            lambda ignored_in: empty_grads,
            key_group,
        )
        term_rows = jnp.concatenate(
            [
                key_part.reshape(back_group * tok_rows, local_width),
                value_part.reshape(back_group * tok_rows, local_width),
            ],
            axis=1,
        )
        return (query_acc + query_part, term_rows)

    query_grad, key_value_terms = lax.scan(back_step, empty_grads[0], scan_inputs)
    key_value_sum = lax.psum_scatter(
        key_value_terms.reshape(device_count * tok_rows, 2 * local_width).astype(jnp.bfloat16),
        "fs",
        scatter_dimension=0,
        tiled=True,
    ).astype(jnp.float32)
    key_grad_rows = key_value_sum[:, :local_width]
    value_grad_rows = key_value_sum[:, local_width:]
    projected_grad = jnp.stack(
        [
            rotate(query_grad.reshape(tok_rows, local_width), cosine, -sine_table),
            rotate(key_grad_rows, cosine, -sine_table),
            value_grad_rows,
        ],
        axis=0,
    ).astype(jnp.bfloat16)
    qkv_grad = jnp.einsum(
        "td,jtf->jdf", hidden_one, projected_grad, preferred_element_type=jnp.float32
    )
    one_part = jnp.einsum(
        "jtf,jdf->td", projected_grad, qkv_back, preferred_element_type=jnp.float32
    )
    one_grad = lax.psum(one_part.astype(jnp.bfloat16), "tp").astype(jnp.float32)
    scaled_one = one_grad * gains_back[0].astype(jnp.float32)[None, :]
    gain_one_grad = jnp.sum(one_grad * normed_one, axis=0)
    input_grad = residual_grad + rstd_one * (
        scaled_one - normed_one * jnp.mean(scaled_one * normed_one, axis=1, keepdims=True)
    )
    gains_grad = jnp.stack([gain_one_grad, gain_two_grad], axis=0)
    reduced = (
        lax.psum_scatter(
            qkv_grad.astype(jnp.bfloat16), "fs", scatter_dimension=1, tiled=True
        ).astype(jnp.float32),
        lax.psum_scatter(
            out_grad.astype(jnp.bfloat16), "fs", scatter_dimension=1, tiled=True
        ).astype(jnp.float32),
        lax.psum_scatter(
            gains_grad.astype(jnp.bfloat16), "fs", scatter_dimension=1, tiled=True
        ).astype(jnp.float32),
        lax.psum_scatter(
            router_grad.astype(jnp.bfloat16), "fs", scatter_dimension=1, tiled=True
        ).astype(jnp.float32),
        lax.psum_scatter(
            shared_vector_grad.astype(jnp.bfloat16), "fs", scatter_dimension=0, tiled=True
        ).astype(jnp.float32),
        lax.psum_scatter(
            expert_gate_grad.astype(jnp.bfloat16), "fs", scatter_dimension=1, tiled=True
        ).astype(jnp.float32),
        lax.psum_scatter(
            expert_down_grad.astype(jnp.bfloat16), "fs", scatter_dimension=2, tiled=True
        ).astype(jnp.float32),
        lax.psum_scatter(
            shared_proj_grad.astype(jnp.bfloat16), "fs", scatter_dimension=0, tiled=True
        ).astype(jnp.float32),
        lax.psum_scatter(
            shared_down_grad.astype(jnp.bfloat16), "fs", scatter_dimension=1, tiled=True
        ).astype(jnp.float32),
    )
    return (
        output,
        input_grad,
        reduced[0],
        reduced[1],
        reduced[2],
        reduced[3],
        reduced[4],
        reduced[5],
        reduced[6],
        reduced[7],
        reduced[8],
    )


MESH = pl.DeviceIdType.MESH
X_BIT, Y_BIT, CORE_BIT = 2, 4, 1
QUARTERS = 4
SMALL = 16
EARLY = (2, 4)
CUT = 1536


def flip(index, bit):
    return index + bit - 2 * bit * ((index // bit) % 2)


class Links:
    def __init__(self, send, recv, local):
        self.fs = lax.axis_index("fs")
        self.tp = lax.axis_index("tp")
        self.send, self.recv, self.local = send, recv, local
        self.used = 0
        self.used_local = 0

    def peer(self, bits):
        where = self.fs
        for bit in (X_BIT, Y_BIT, CORE_BIT):
            if bits & bit:
                where = flip(where, bit)
        return where

    def along(self, step):
        return lax.rem(self.tp + step, QUARTERS)

    def remote(self, source, target, device, landing):
        i = self.used
        self.used += 1
        out = pltpu.make_async_remote_copy(
            src_ref=source,
            dst_ref=target,
            send_sem=self.send.at[i],
            recv_sem=self.recv.at[i],
            device_id=device,
            device_id_type=MESH,
        )
        back = pltpu.make_async_remote_copy(
            src_ref=landing,
            dst_ref=landing,
            send_sem=self.send.at[i],
            recv_sem=self.recv.at[i],
            device_id=device,
            device_id_type=MESH,
        )
        return out, back

    def inside(self, source, target):
        i = self.used_local
        self.used_local += 1
        return pltpu.make_async_copy(source, target, self.local.at[i])

    def greet(self, plane, column):
        barrier = pltpu.get_barrier_semaphore()
        for bits in plane:
            pl.semaphore_signal(
                barrier, inc=1, device_id=(self.peer(bits), self.tp), device_id_type=MESH
            )
        for step in column:
            pl.semaphore_signal(
                barrier, inc=1, device_id=(self.fs, self.along(step)), device_id_type=MESH
            )
        pl.semaphore_wait(barrier, len(plane) + len(column))


class Gather:
    def __init__(self, links, source, place, half):
        self.links = links
        fs, tp = links.fs, links.tp

        def to(bits, what, landing, origin=None):
            return links.remote(
                what if origin is None else origin, what, (links.peer(bits), tp), landing
            )

        p = links.peer
        self.keep = None if source is None else links.inside(source, place(fs))
        self.to_x = to(X_BIT, place(fs), place(p(X_BIT)), source)
        self.to_y = to(Y_BIT, place(fs), place(p(Y_BIT)), source)
        self.to_c = to(CORE_BIT, place(fs), place(p(CORE_BIT)), source)
        xy = X_BIT + Y_BIT
        self.x_on = to(Y_BIT, half(p(X_BIT), 0), half(p(xy), 0))
        self.y_on = to(X_BIT, half(p(Y_BIT), 1), half(p(xy), 1))
        self.x_core = to(CORE_BIT, place(p(X_BIT)), place(p(X_BIT + CORE_BIT)))
        self.y_core = to(CORE_BIT, place(p(Y_BIT)), place(p(Y_BIT + CORE_BIT)))
        self.d_core = [
            to(CORE_BIT, half(p(xy), h), half(p(xy + CORE_BIT), h)) for h in range(2)
        ]

    def first(self):
        self.to_x[0].start()
        self.to_y[0].start()
        self.to_c[0].start()
        if self.keep is not None:
            self.keep.start()

    def second(self):
        self.to_x[1].wait_recv()
        self.x_on[0].start()
        self.x_core[0].start()
        self.to_y[1].wait_recv()
        self.y_on[0].start()
        self.y_core[0].start()

    def third(self):
        self.x_on[1].wait_recv()
        self.d_core[0][0].start()
        self.y_on[1].wait_recv()
        self.d_core[1][0].start()

    def last(self):
        if self.keep is not None:
            self.keep.wait()
        for out, back in (self.to_c, self.x_core, self.y_core, *self.d_core):
            back.wait_recv()
        for out, back in (
            self.to_x,
            self.to_y,
            self.to_c,
            self.x_on,
            self.y_on,
            self.x_core,
            self.y_core,
            *self.d_core,
        ):
            out.wait_send()


class CrossGather:
    def __init__(self, links, source, blocks):
        self.links = links
        tp = links.tp
        size = source.shape[0]

        def slot(k, h=None):
            start, count = (3 - k // 2) * size, size
            if h is not None:
                count = size // 2
                start = start + h * count
            return blocks.at[1, pl.ds(start, count)]

        def to(bits, start, there):
            return links.remote(start, there, (links.peer(bits), tp), there)

        x, y, c = X_BIT, Y_BIT, CORE_BIT
        self.keep = links.inside(source, slot(0))
        self.to_x = to(x, source, slot(x))
        self.to_y = to(y, source, slot(y))
        self.x_on = to(y, slot(x, 0), slot(x + y, 0))
        self.y_on = to(x, slot(y, 1), slot(x + y, 1))
        self.along = []
        for step in range(1, QUARTERS):
            there = blocks.at[2 * step + 1]
            self.along.append(
                links.remote(blocks.at[1], there, (links.fs, links.along(step)), there)
            )
        self.core = [
            to(c, blocks.at[2 * s + 1], blocks.at[2 * s]) for s in range(QUARTERS)
        ]

    def first(self):
        self.to_x[0].start()
        self.to_y[0].start()
        self.keep.start()

    def second(self):
        self.to_x[1].wait_recv()
        self.x_on[0].start()
        self.to_y[1].wait_recv()
        self.y_on[0].start()

    def third(self):
        self.keep.wait()
        self.x_on[1].wait_recv()
        self.y_on[1].wait_recv()
        for out, back in self.along:
            out.start()
        self.core[0][0].start()

    def last(self):
        for s, (out, back) in enumerate(self.along):
            back.wait_recv()
            self.core[s + 1][0].start()
        for out, back in self.core:
            back.wait_recv()
        for out, back in (self.to_x, self.to_y, self.x_on, self.y_on, *self.along, *self.core):
            out.wait_send()


def grad_shapes(routed, shared, block):
    return (
        (E, 2 * routed, block),
        (2, E * shared, block),
        (E, routed, block),
        (E * shared, block),
    )


def grad_pieces(grads, results, index, source):
    up_all, shared_up_all, down_all, shared_down_all = results
    routed, shared = down_all.shape[1], shared_down_all.shape[0] // E
    units = pl.ds(pl.multiple_of(source * shared, 16), shared)
    places = [
        up_all.at[source],
        shared_up_all.at[0, units],
        shared_up_all.at[1, units],
        down_all.at[source],
        shared_down_all.at[units],
    ]
    placed, at = [], 0
    for place, size in zip(places, (2 * routed, shared, shared, routed, shared), strict=True):
        placed.append((grads.at[index, pl.ds(at, size)], place))
        at += size
    return placed


def grad_copies(links, grads, results, bits):
    peer = links.peer(bits)
    pairs = zip(
        grad_pieces(grads, results, peer, links.fs),
        grad_pieces(grads, results, peer, peer),
        strict=True,
    )
    return [
        links.remote(piece, place, (peer, links.tp), landing)
        for (piece, place), (_, landing) in pairs
    ]


def turn(values, cosine, sine_signed):
    parts = []
    for h in range(values.shape[1] // HD):
        v = values[:, h * HD : (h + 1) * HD]
        parts.append(v * cosine + pltpu.roll(v, HD // 2, 1) * sine_signed)
    return jnp.concatenate(parts, axis=1)


def as_column(row):
    size = row.shape[1]
    same = lax.broadcasted_iota(jnp.int32, (size, size), 0) == lax.broadcasted_iota(
        jnp.int32, (size, size), 1
    )
    spread = jnp.where(same, row.astype(jnp.float32), 0.0)
    return jnp.sum(spread, axis=1, keepdims=True).astype(jnp.int32)


def matmul(a, b):
    return jnp.dot(a, b, preferred_element_type=jnp.float32)


def matmul_nt(a, b):
    return lax.dot_general(a, b, (((1,), (1,)), ((), ())), preferred_element_type=jnp.float32)


def matmul_tn(a, b):
    return lax.dot_general(a, b, (((0,), (0,)), ((), ())), preferred_element_type=jnp.float32)


class RowGather:
    def __init__(self, links, source, slot, half):
        self.links = links

        def to(bits, owner, h=None):
            view = slot if h is None else lambda k: half(k, h)
            start = source if owner == 0 and source is not None else view(owner)
            return links.remote(
                start, view(owner ^ bits), (links.peer(bits), links.tp), view(owner ^ bits)
            )

        x, y, c = X_BIT, Y_BIT, CORE_BIT
        self.keep = None if source is None else links.inside(source, slot(0))
        self.own = [to(x, 0), to(y, 0), to(c, 0)]
        self.x_on = [to(y, x, 0), to(c, x)]
        self.y_on = [to(x, y, 1), to(c, y)]
        self.d_on = [to(c, x + y, 0), to(c, x + y, 1)]

    def first(self):
        for out, back in self.own:
            out.start()
        if self.keep is not None:
            self.keep.start()

    def second(self):
        self.own[0][1].wait_recv()
        for out, back in self.x_on:
            out.start()
        self.own[1][1].wait_recv()
        for out, back in self.y_on:
            out.start()

    def third(self):
        self.x_on[0][1].wait_recv()
        self.d_on[0][0].start()
        self.y_on[0][1].wait_recv()
        self.d_on[1][0].start()

    def last(self):
        if self.keep is not None:
            self.keep.wait()
        for out, back in (self.own[2], self.x_on[1], self.y_on[1], *self.d_on):
            back.wait_recv()

    def sent(self):
        for out, back in self.own + self.x_on + self.y_on + self.d_on:
            out.wait_send()


def layer_kernel(
    routed,
    tokens_hbm,
    cotangent_ref,
    qkv_ref,
    out_ref,
    gains_ref,
    router_ref,
    gate_ref,
    up_ref,
    shared_up_ref,
    down_ref,
    shared_down_ref,
    cos_ref,
    sin_ref,
    start_ref,
    routes_ref,
    output_ref,
    branch_ref,
    back_ref,
    small_grad_ref,
    grads_out,
    up_all,
    shared_up_all,
    down_all,
    shared_down_all,
    attended_out,
    query_out,
    hidden_out,
    slabs_all,
    cotangent_all,
    cotangent_plane,
    kv_out,
    qkv_out,
    out_out,
    small_out,
    small_full,
    branch_in,
    two_ref,
    small_ref,
    scales_ref,
    residual_ref,
    two_all,
    core_in,
    diag_in,
    side_in,
    rows_in,
    cols_in,
    send,
    recv,
    local,
    credit,
):
    links = Links(send, recv, local)
    fs, tp = links.fs, links.tp
    rows, width = tokens_hbm.shape
    block = width // E
    local_width = qkv_ref.shape[2]
    heads = local_width // HD
    seqs = rows // SEQ_DEV
    quarter = rows // QUARTERS
    out_width = output_ref.shape[1]
    back_width = width + SIDE
    whole = back_width + width
    slab_rows = slabs_all.shape[1]
    count = slab_rows // 3
    bf, f32 = jnp.bfloat16, jnp.float32

    def at_rows(index, size):
        return pl.ds(pl.multiple_of(index * size, size), size)

    small_ref[...] = jnp.concatenate(
        [
            gains_ref[...].astype(f32),
            router_ref[...].astype(f32),
            gate_ref[...].astype(f32),
            jnp.zeros((SMALL - 3 - E, block), f32),
        ],
        axis=0,
    ).astype(jnp.bfloat16)
    links.greet(range(1, 8), range(1, QUARTERS))
    cut = cotangent_all.shape[2]
    cot = CrossGather(
        links, cotangent_ref.at[at_rows(tp, quarter), pl.ds(0, cut)], cotangent_all
    )
    cot_plane = Gather(
        links,
        cotangent_ref.at[:, pl.ds(cut, width - cut)],
        lambda f: cotangent_plane.at[f],
        lambda f, h: cotangent_plane.at[f, pl.ds(h * SEQ_DEV, SEQ_DEV)],
    )
    shared = shared_down_ref.shape[0] // E

    def slab(peer, where):
        units = pl.ds(pl.multiple_of(peer * shared, 16), shared)
        pieces = [
            up_ref.at[peer],
            shared_up_ref.at[0, units],
            shared_up_ref.at[1, units],
            down_ref.at[peer],
            shared_down_ref.at[units],
        ]
        placed, at = [], 0
        for piece, size in zip(pieces, (2 * routed, shared, shared, routed, shared), strict=True):
            placed.append((piece, slabs_all.at[where, pl.ds(at, size)]))
            at += size
        return placed

    slab_copies = []
    for bits in (6, 7, 2, 3, 4, 5, 1):
        peer = links.peer(bits)
        for (piece, place), (_, landing) in zip(slab(peer, fs), slab(peer, peer), strict=True):
            slab_copies.append(links.remote(piece, place, (peer, tp), landing))
    slab_own = [links.inside(piece, place) for piece, place in slab(fs, fs)]
    def slot(s, k, h=None):
        start = (3 - k // 2) * quarter
        size = quarter
        if h is not None:
            size = quarter // 2
            start = start + h * size
        return two_all.at[2 * s + 1 - k % 2, pl.ds(start, size)]

    along = []
    for step in range(1, QUARTERS):
        along.append(
            links.remote(two_ref, slot(step, 0), (fs, links.along(step)), slot(step, 0))
        )
    gathers = []
    for s in range(QUARTERS):
        gathers.append(
            RowGather(
                links,
                two_ref if s == 0 else None,
                lambda k, s=s: slot(s, k),
                lambda k, h, s=s: slot(s, k, h),
            )
        )

    def attention(
        tokens_ref,
        hidden_buf,
        attended_ref,
        query_ref,
        qkv_full,
        out_full,
        kv_own,
        kv_full,
        branch_buf,
    ):
        load = links.inside(tokens_hbm, tokens_ref)
        load.start()
        small = Gather(
            links, small_ref, lambda f: small_full.at[f], lambda f, h: small_full.at[f, :, pl.ds(h * 128, 128)]
        )
        qkv = Gather(
            links,
            qkv_ref,
            lambda f: qkv_out.at[:, at_rows(f, block)],
            lambda f, h: qkv_out.at[:, pl.ds(pl.multiple_of(f * block + h * (block // 2), block // 2), block // 2)],
        )
        outs = Gather(
            links,
            out_ref,
            lambda f: out_out.at[f],
            lambda f, h: out_out.at[f, pl.ds(h * (local_width // 2), local_width // 2)],
        )
        small.first()
        cot.first()
        qkv.first()
        small.second()
        small.third()
        small.last()
        cot.second()
        load.wait()
        tokens = tokens_ref[...].astype(jnp.float32)
        rstd_one = lax.rsqrt(jnp.mean(tokens * tokens, axis=1, keepdims=True) + NORM_EPS)
        for b in range(E):
            cols = slice(b * block, (b + 1) * block)
            gain = small_full[b, 0:1, :].astype(jnp.float32)
            hidden_buf[:, cols] = (tokens[:, cols] * rstd_one * gain).astype(jnp.bfloat16)
        cot.third()
        qkv.second()
        qkv.third()
        outs.first()
        cot_plane.first()
        qkv.last()
        qkv_load = links.inside(qkv_out, qkv_full)
        qkv_load.start()
        qkv_load.wait()
        hidden = hidden_buf[...]
        cosine, sine = cos_ref[...], sin_ref[...]
        kv_own[:, :local_width] = turn(matmul(hidden, qkv_full[1]), cosine, sine).astype(jnp.bfloat16)
        kv_own[:, local_width:] = matmul(hidden, qkv_full[2]).astype(jnp.bfloat16)
        kv = Gather(
            links,
            kv_own,
            lambda f: kv_out.at[f],
            lambda f, h: kv_out.at[f, pl.ds(h * SEQ_DEV, SEQ_DEV)],
        )
        kv.first()
        query_ref[...] = turn(matmul(hidden, qkv_full[0]), cosine, sine).astype(jnp.bfloat16)
        outs.second()
        kv.second()
        outs.third()
        kv.third()
        cot_plane.second()
        for out, back in slab_copies:
            out.start()
        for copy in slab_own:
            copy.start()
        kv.last()
        kv_load = links.inside(kv_out, kv_full)
        kv_load.start()
        kv_load.wait()
        length = E * SEQ_DEV
        key_pos = lax.broadcasted_iota(jnp.int32, (SEQ_DEV, length), 1)
        query_pos = fs * SEQ_DEV + lax.broadcasted_iota(jnp.int32, (SEQ_DEV, length), 0)
        for s in range(seqs):
            here = slice(s * SEQ_DEV, (s + 1) * SEQ_DEV)
            allowed = (key_pos <= query_pos) & (key_pos >= as_column(start_ref[s : s + 1, :]))
            for h in range(heads):
                cols = slice(h * HD, (h + 1) * HD)
                vcols = slice(local_width + h * HD, local_width + (h + 1) * HD)
                keys = kv_full[:, here, cols].reshape(length, HD)
                values = kv_full[:, here, vcols].reshape(length, HD)
                scores = matmul_nt(query_ref[here, cols], keys) * (HD ** (-0.5))
                scores = jnp.where(allowed, scores, NEG_FILL)
                top = jnp.max(scores, axis=1, keepdims=True)
                weights = jnp.exp(scores - top)
                weights = weights / jnp.sum(weights, axis=1, keepdims=True)
                attended_ref[here, cols] = matmul(weights.astype(jnp.bfloat16), values).astype(
                    jnp.bfloat16
                )
        outs.last()
        cot_plane.third()
        out_load = links.inside(out_out, out_full)
        out_load.start()
        small_keep = links.inside(small_full, small_out)
        small_keep.start()
        out_load.wait()
        attended = attended_ref[...]
        for b in range(E):
            branch_buf[:, b * block : (b + 1) * block] = matmul(attended, out_full[b]).astype(
                jnp.bfloat16
            )
        branch = []
        for step in range(1, QUARTERS):
            peer = links.along(step)
            branch.append(
                links.remote(
                    branch_buf.at[at_rows(peer, quarter)],
                    branch_in.at[step - 1],
                    (fs, peer),
                    branch_in.at[step - 1],
                )
            )
        for out, back in branch:
            out.start()
        for out, back in branch:
            back.wait_recv()
        mine = at_rows(tp, quarter)
        total = branch_buf[mine, :].astype(jnp.float32)
        for step in range(1, QUARTERS):
            total = total + branch_in[step - 1].astype(jnp.float32)
        residual = tokens_ref[mine, :].astype(jnp.float32) + total
        residual_ref[...] = residual
        rstd_two = lax.rsqrt(jnp.mean(residual * residual, axis=1, keepdims=True) + NORM_EPS)
        logits = jnp.zeros((quarter, SMALL), jnp.float32)
        for b in range(E):
            cols = slice(b * block, (b + 1) * block)
            gain = small_full[b, 1:2, :].astype(jnp.float32)
            part = (residual[:, cols] * rstd_two * gain).astype(jnp.bfloat16)
            two_ref[:, cols] = part
            logits = logits + matmul_nt(part, small_full[b])
        lane = lax.broadcasted_iota(jnp.int32, (quarter, SMALL), 1)
        real = (lane >= 2) & (lane < 2 + E)
        masked = jnp.where(real, logits, NEG_FILL)
        odds = jnp.exp(masked - jnp.max(masked, axis=1, keepdims=True))
        odds = jnp.where(real, odds, 0.0)
        probs = odds / jnp.sum(odds, axis=1, keepdims=True)
        expert = lax.broadcasted_iota(jnp.int32, (SMALL, rows), 0) - 2
        named = jnp.zeros((SMALL, rows), jnp.float32)
        for k in range(routes_ref.shape[0]):
            named = named + (routes_ref[k : k + 1, :] == expert).astype(jnp.float32)
        pick = lax.broadcasted_iota(jnp.int32, (quarter, rows), 1) == (
            tp * quarter + lax.broadcasted_iota(jnp.int32, (quarter, rows), 0)
        )
        chosen = matmul_nt(pick.astype(jnp.bfloat16), named.astype(jnp.bfloat16))
        gate_value = 1.0 / (1.0 + jnp.exp(-logits))
        scales = jnp.where(lane == 2 + E, gate_value, probs * chosen)
        scales_ref[...] = jnp.concatenate([scales, probs, chosen], axis=1)
        high = scales.astype(jnp.bfloat16)
        low = (scales - high.astype(jnp.float32)).astype(jnp.bfloat16)
        two_ref[:, width:] = jnp.concatenate(
            [high, low, jnp.zeros((quarter, SIDE - 2 * SMALL), jnp.bfloat16)], axis=1
        )
        keeps = [
            links.inside(attended_ref, attended_out),
            links.inside(query_ref, query_out),
            links.inside(hidden_buf, hidden_out),
            small_keep,
        ]
        for keep in keeps[:3]:
            keep.start()
        for out, back in along:
            out.start()
        for out, back in branch:
            out.wait_send()
        for keep in keeps:
            keep.wait()

    pl.run_scoped(
        attention,
        pltpu.VMEM((rows, width), bf),
        pltpu.VMEM((rows, width), bf),
        pltpu.VMEM((rows, local_width), bf),
        pltpu.VMEM((rows, local_width), bf),
        pltpu.VMEM((3, width, local_width), bf),
        pltpu.VMEM((E, local_width, block), bf),
        pltpu.VMEM((rows, 2 * local_width), bf),
        pltpu.VMEM((E, rows, 2 * local_width), bf),
        pltpu.VMEM((rows, width), bf),
    )

    def experts(weights, cot_all, units, first, parts, own_rows, own_cols, staged, cot_rows):
        loads = [
            links.inside(slabs_all.at[g], weights.at[:, pl.ds(g * block, block)]) for g in range(E)
        ]
        loads.append(links.inside(cotangent_all, cot_all.at[:, :, pl.ds(0, cut)]))
        for s in range(QUARTERS):
            q = links.along(QUARTERS - s)
            for k in range(E):
                there = cot_all.at[
                    2 * s + 1 - k % 2, pl.ds((3 - k // 2) * quarter, quarter), pl.ds(cut, width - cut)
                ]
                loads.append(
                    links.inside(cotangent_plane.at[links.peer(k), at_rows(q, quarter)], there)
                )
        along[0][1].wait_recv()
        gathers[1].first()
        along[1][1].wait_recv()
        gathers[2].first()
        gathers[1].second()
        along[2][1].wait_recv()
        gathers[3].first()
        gathers[0].first()
        cot.last()
        cot_plane.last()
        for out, back in slab_copies:
            back.wait_recv()
        for copy in slab_own:
            copy.wait()
        for load in loads:
            load.start()

        cot_load = links.inside(cotangent_ref.at[at_rows(tp, quarter)], cot_rows)
        cot_load.start()
        core = [
            links.remote(
                parts.at[s % 2], core_in.at[s % 2], (links.peer(CORE_BIT), tp), core_in.at[s % 2]
            )
            for s in range(QUARTERS)
        ]
        diag, side, rows_along, cols_along = [], [], [], []
        for s in range(QUARTERS):
            held = parts.at[2 + s % 3]
            diag.append(
                [
                    links.remote(
                        held.at[pl.ds(h * (quarter // 2), quarter // 2)],
                        diag_in.at[s, h],
                        (links.peer(bits), tp),
                        diag_in.at[s, h],
                    )
                    for h, bits in enumerate((Y_BIT, X_BIT))
                ]
            )
            side.append(
                [
                    links.remote(
                        held.at[pl.ds((3 - bits // 2) * quarter, quarter)],
                        side_in.at[s, i],
                        (links.peer(bits), tp),
                        side_in.at[s, i],
                    )
                    for i, bits in enumerate((X_BIT, Y_BIT))
                ]
            )
            last = pl.ds(3 * quarter, quarter)
            if s < QUARTERS - 1:
                rows_along.append(
                    links.remote(
                        held.at[last, pl.ds(0, back_width)],
                        rows_in.at[s],
                        (fs, links.along(QUARTERS - 1 - s)),
                        rows_in.at[s],
                    )
                )
            q = links.along(2 * QUARTERS - 1 - s)
            for step in range(1, QUARTERS):
                peer = links.along(step)
                start = pl.multiple_of(back_width + peer * out_width, 128)
                q_there = links.along(2 * QUARTERS - 1 - s - step)
                cols_along.append(
                    links.remote(
                        held.at[last, pl.ds(start, out_width)],
                        cols_in.at[step - 1, at_rows(q, quarter)],
                        (fs, peer),
                        cols_in.at[step - 1, at_rows(q_there, quarter)],
                    )
                )

        sub = lax.broadcasted_iota(jnp.int32, (8, SIDE), 0)
        lane = lax.broadcasted_iota(jnp.int32, (8, SIDE), 1)
        mine, common = 2 + fs, 2 + E
        pick_in = (
            ((sub == 0) & ((lane == mine) | (lane == mine + SMALL)))
            | ((sub == 1) & ((lane == common) | (lane == common + SMALL)))
        ).astype(jnp.bfloat16)
        pick_out = (((sub == 0) & (lane == mine)) | ((sub == 1) & (lane == common))).astype(
            jnp.bfloat16
        )

        def one_block(t, index, slot_out, pause):
            first[: 2 * count] = matmul_nt(weights[: 2 * count], two_all[index, :, :width])
            pause(0)
            first[2 * count :] = matmul_nt(weights[2 * count :], cot_all[index])
            scale = matmul_nt(pick_in, two_all[index, :, width:])
            cols = pl.ds(pl.multiple_of(index * rows, rows), rows)
            dots = []
            shared = count - routed
            groups = ((0, 2 * count, routed), (2 * routed, 2 * count + routed, shared))
            for group, (low, last, size) in enumerate(groups):
                gate = first[low : low + size]
                up = first[low + size : low + 2 * size]
                grad = first[last : last + size]
                by = scale[group : group + 1]
                sigmoid = 1.0 / (1.0 + jnp.exp(-gate))
                silu = gate * sigmoid
                active = silu * up
                units[last : last + size, cols] = (by * active).astype(jnp.bfloat16)
                dots.append(jnp.sum(active * grad, axis=0, keepdims=True))
                active_grad = by * grad
                units[low : low + size, cols] = (
                    active_grad * up * sigmoid * (1.0 + gate * (1.0 - sigmoid))
                ).astype(jnp.bfloat16)
                units[low + size : low + 2 * size, cols] = (active_grad * silu).astype(jnp.bfloat16)
            both = jnp.concatenate([*dots, jnp.zeros((6, rows), jnp.float32)], axis=0)
            pause(1)
            tile = 512

            def put(at, value, other):
                if other is not None:
                    value = value + other[:, at].astype(jnp.float32)
                parts[slot_out, :, at] = value.astype(jnp.bfloat16)

            def products(other):
                put(
                    slice(width, back_width), matmul_tn(both.astype(jnp.bfloat16), pick_out), other
                )
                for n in range(width // tile):
                    at = slice(n * tile, (n + 1) * tile)
                    put(at, matmul_tn(units[: 2 * count, cols], weights[: 2 * count, at]), other)
                    beyond = slice(back_width + n * tile, back_width + (n + 1) * tile)
                    put(beyond, matmul_tn(units[2 * count :, cols], weights[2 * count :, at]), other)

            @pl.when(t % 2 == 0)
            def _():
                products(None)

            @pl.when(t % 2 == 1)
            def _():
                products(core_in.at[(t // 2) % 2])

            pause(3)

        def add_in(held, start, size, others):
            chunk = 32

            @pl.loop(0, size // chunk)
            def _(r):
                at = pl.ds(pl.multiple_of(start + r * chunk, chunk), chunk)
                there = pl.ds(pl.multiple_of(r * chunk, chunk), chunk)
                total = parts[held, at, :].astype(jnp.float32)
                for ref in others:
                    total = total + ref[there, :].astype(jnp.float32)
                parts[held, at, :] = total.astype(jnp.bfloat16)

        def to_core(s):
            if s >= 2:
                pl.semaphore_wait(credit, 1)
            core[s][0].start()

        def diagonal(s):
            if s < 2:
                pl.semaphore_signal(
                    credit, inc=1, device_id=(links.peer(CORE_BIT), tp), device_id_type=MESH
                )
            for out, back in diag[s]:
                out.start()

        def sideways(s):
            for h, (out, back) in enumerate(diag[s]):
                back.wait_recv()
                start = (2 - h) * quarter + h * (quarter // 2)
                add_in(2 + s % 3, start, quarter // 2, [diag_in.at[s, h]])
                side[s][h][0].start()

        def finish(s):
            held = 2 + s % 3
            for out, back in side[s]:
                back.wait_recv()
            last = slice(3 * quarter, rows)
            add_in(held, 3 * quarter, quarter, [side_in.at[s, 0], side_in.at[s, 1]])
            if s == QUARTERS - 1:
                own_rows[...] = parts[held, last, :back_width].astype(jnp.float32)
                parts[held, last, back_width:] = (
                    parts[held, last, back_width:].astype(jnp.float32) + residual_ref[...]
                ).astype(jnp.bfloat16)
            else:
                rows_along[s][0].start()
            for out, back in cols_along[3 * s : 3 * s + 3]:
                out.start()
            start = pl.multiple_of(back_width + tp * out_width, 128)
            own_cols[at_rows(links.along(2 * QUARTERS - 1 - s), quarter), :] = parts[
                held, last, pl.ds(start, out_width)
            ].astype(jnp.float32)

        def before_last():
            core[1][0].wait_send()

        def slot_free():
            for out, back in diag[0] + side[0] + cols_along[:3] + rows_along[:1]:
                out.wait_send()

        plan = {
            (0, 0): [gathers[2].third, gathers[3].second],
            (0, 1): [gathers[0].second, gathers[3].third],
            (0, 3): [lambda: to_core(0), gathers[2].last],
            (1, 0): [gathers[0].third],
            (1, 1): [core[0][1].wait_recv],
            (1, 3): [lambda: diagonal(0), gathers[3].last],
            (2, 1): [lambda: sideways(0)],
            (2, 3): [lambda: to_core(1)],
            (3, 1): [core[1][1].wait_recv],
            (3, 3): [lambda: diagonal(1)],
            (4, 1): [lambda: sideways(1)],
            (4, 3): [lambda: to_core(2)],
            (5, 0): [lambda: finish(0)],
            (5, 1): [core[2][1].wait_recv],
            (5, 3): [lambda: diagonal(2), gathers[0].last],
            (6, 1): [lambda: sideways(2)],
            (6, 3): [lambda: to_core(3)],
            (7, 0): [lambda: finish(1)],
            (7, 1): [core[3][1].wait_recv],
            (7, 3): [lambda: diagonal(3)],
        }
        before = {4: [core[0][0].wait_send], 6: [before_last], 7: [slot_free]}

        gathers[1].third()
        gathers[2].second()
        for load in loads:
            load.wait()
        gathers[1].last()

        @pl.loop(0, 8)
        def _(t):
            s = t // 2
            slot_out = (1 - t % 2) * (s % 2) + (t % 2) * (2 + s % 3)
            for at, steps in before.items():

                @pl.when(t == at)
                def _(steps=steps):
                    for step in steps:
                        step()

            def pause(point):
                for (at, where), steps in plan.items():
                    if where == point:

                        @pl.when(t == at)
                        def _(steps=steps):
                            for step in steps:
                                step()

            one_block(t, 2 * ((s + 1) % QUARTERS) + t % 2, slot_out, pause)

        keeps = []

        pending = [None, None]

        def settle(place):
            if pending[place] is not None:
                pending[place].wait()
            pending[place] = None

        def weight_grads(bits):
            g = links.peer(bits)
            at = pl.ds(pl.multiple_of(g * block, block), block)
            place = len(keeps) % 2
            settle(place)
            hidden_cols = two_all[:, :, at].reshape(E * rows, block)
            staged[place, : 2 * count] = matmul(units[: 2 * count], hidden_cols).astype(
                jnp.bfloat16
            )
            cot_cols = cot_all[:, :, at].reshape(E * rows, block)
            staged[place, 2 * count :] = matmul(units[2 * count :], cot_cols).astype(jnp.bfloat16)
            keep = links.inside(staged.at[place], grads_out.at[g])
            keep.start()
            keeps.append(keep)
            pending[place] = keep

        results = (up_all, shared_up_all, down_all, shared_down_all)
        early = [copy for bits in EARLY for copy in grad_copies(links, grads_out, results, bits)]
        finish(2)
        for bits in EARLY:
            weight_grads(bits)
        sideways(3)
        settle(0)
        settle(1)
        for out, back in early:
            out.start()
        for bits in (6, 7, 3, 5, 1, 0):
            weight_grads(bits)
        finish(3)
        for out, back in rows_along:
            back.wait_recv()
        total = own_rows[...]
        for step in range(1, QUARTERS):
            total = total + rows_in[step - 1].astype(jnp.float32)
        dots = total[:, width : width + SMALL]
        scales = scales_ref[:, :SMALL]
        probs = scales_ref[:, SMALL : 2 * SMALL]
        chosen = scales_ref[:, 2 * SMALL :]
        chosen_grad = chosen * dots
        logit_grad = probs * (chosen_grad - jnp.sum(probs * chosen_grad, axis=1, keepdims=True))
        gate_lane = lax.broadcasted_iota(jnp.int32, (quarter, SMALL), 1) == 2 + E
        logit_grad = jnp.where(gate_lane, dots * scales * (1.0 - scales), logit_grad).astype(
            jnp.bfloat16
        )
        residual = residual_ref[...]
        rstd = lax.rsqrt(jnp.mean(residual * residual, axis=1, keepdims=True) + NORM_EPS)
        mean = jnp.zeros((quarter, 1), jnp.float32)
        for b in range(E):
            at = slice(b * block, (b + 1) * block)
            two_grad = total[:, at] + matmul(logit_grad, small_full[b])
            normed = residual[:, at] * rstd
            gain = small_full[b, 1:2, :].astype(jnp.float32)
            back_ref[:, at] = two_grad
            mean = mean + jnp.sum(two_grad * gain * normed, axis=1, keepdims=True)
            grads = matmul_tn(logit_grad, two_all[1, 3 * quarter :, at])
            line = lax.broadcasted_iota(jnp.int32, (SMALL, block), 0)
            gain_grad = jnp.sum(two_grad * normed, axis=0, keepdims=True)
            small_grad_ref[:, at] = jnp.where(line == 1, gain_grad, grads)
        mean = mean / width
        cot_load.wait()
        for b in range(E):
            at = slice(b * block, (b + 1) * block)
            gain = small_full[b, 1:2, :].astype(jnp.float32)
            normed = residual[:, at] * rstd
            grad = cot_rows[:, at].astype(jnp.float32) + rstd * (
                back_ref[:, at] * gain - normed * mean
            )
            back_ref[:, at] = grad
            branch_ref[:, at] = grad.astype(jnp.bfloat16)
        for out, back in cols_along:
            back.wait_recv()
        total = own_cols[...]
        for step in range(1, QUARTERS):
            total = total + cols_in[step - 1].astype(jnp.float32)
        output_ref[...] = total.astype(jnp.bfloat16)
        for out, back in core[2:] + rows_along[1:] + cols_along[3:]:
            out.wait_send()
        for s in range(1, QUARTERS):
            for out, back in diag[s] + side[s]:
                out.wait_send()
        for gather in gathers:
            gather.sent()
        for out, back in slab_copies + along:
            out.wait_send()
        settle(0)
        settle(1)
        for out, back in early:
            back.wait_recv()
            out.wait_send()

    pl.run_scoped(
        experts,
        pltpu.VMEM((slab_rows, width), bf),
        pltpu.VMEM((E, rows, width), bf),
        pltpu.VMEM((slab_rows, E * rows), bf),
        pltpu.VMEM((slab_rows, rows), f32),
        pltpu.VMEM((5, rows, whole), bf),
        pltpu.VMEM((quarter, back_width), f32),
        pltpu.VMEM((rows, out_width), f32),
        pltpu.VMEM((2, slab_rows, block), bf),
        pltpu.VMEM((quarter, width), bf),
    )


def layer_call(
    tokens,
    cotangent,
    qkv_weight,
    out_weight,
    norm_gains,
    router_weight,
    shared_gate,
    up,
    shared_up,
    down,
    shared_down,
    cosine,
    sine,
    start,
    routes,
):
    rows, width = tokens.shape
    block = width // E
    local_width = qkv_weight.shape[2]
    quarter = rows // QUARTERS
    out_width = width // QUARTERS
    back_width = width + SIDE
    whole = back_width + width
    routed = down.shape[1]
    slabs = (E, 3 * (routed + shared_down.shape[0] // E), block)
    bf, f32 = jnp.bfloat16, jnp.float32
    sds = jax.ShapeDtypeStruct
    vmem = pl.BlockSpec(memory_space=pltpu.VMEM)
    hbm = pl.BlockSpec(memory_space=pl.ANY)
    outs = [
        (sds((rows, out_width), bf), vmem),
        (sds((quarter, width), bf), vmem),
        (sds((quarter, width), f32), vmem),
        (sds((SMALL, width), f32), vmem),
        (sds(slabs, bf), hbm),
        *((sds(shape, bf), hbm) for shape in grad_shapes(routed, shared_down.shape[0] // E, block)),
        (sds((rows, local_width), bf), hbm),
        (sds((rows, local_width), bf), hbm),
        (sds((rows, width), bf), hbm),
        (sds(slabs, bf), hbm),
        (sds((E, rows, CUT), bf), hbm),
        (sds((E, rows, width - CUT), bf), hbm),
        (sds((E, rows, 2 * local_width), bf), hbm),
        (sds((3, width, local_width), bf), hbm),
        (sds((E, local_width, block), bf), hbm),
        (sds((E, SMALL, block), bf), hbm),
    ]
    return pl.pallas_call(
        functools.partial(layer_kernel, routed),
        name="layer",
        out_shape=[o[0] for o in outs],
        in_specs=[hbm] * 4 + [vmem] * 3 + [hbm] * 4 + [vmem] * 4,
        out_specs=[o[1] for o in outs],
        scratch_shapes=[
            pltpu.VMEM((E, SMALL, block), bf),
            pltpu.VMEM((QUARTERS - 1, quarter, width), bf),
            pltpu.VMEM((quarter, back_width), bf),
            pltpu.VMEM((SMALL, block), bf),
            pltpu.VMEM((quarter, 3 * SMALL), f32),
            pltpu.VMEM((quarter, width), f32),
            pltpu.VMEM((E, rows, back_width), bf),
            pltpu.VMEM((2, rows, whole), bf),
            pltpu.VMEM((QUARTERS, 2, quarter // 2, whole), bf),
            pltpu.VMEM((QUARTERS, 2, quarter, whole), bf),
            pltpu.VMEM((QUARTERS - 1, quarter, back_width), bf),
            pltpu.VMEM((QUARTERS - 1, rows, out_width), bf),
            pltpu.SemaphoreType.DMA((192,)),
            pltpu.SemaphoreType.DMA((192,)),
            pltpu.SemaphoreType.DMA((96,)),
            pltpu.SemaphoreType.REGULAR,
        ],
        compiler_params=pltpu.CompilerParams(
            collective_id=1, has_side_effects=True, vmem_limit_bytes=63 * 2**20
        ),
    )(
        tokens,
        cotangent,
        qkv_weight,
        out_weight,
        norm_gains,
        router_weight,
        shared_gate,
        up,
        shared_up,
        down,
        shared_down,
        cosine,
        sine,
        start,
        routes,
    )


LATE = 20


class Scatter:
    def __init__(self, links, parts, core_in, diag_in, side_in):
        self.links, self.parts = links, parts
        self.core_in, self.diag_in, self.side_in = core_in, diag_in, side_in
        self.rows = parts.shape[1]
        p, tp = links.peer, links.tp
        half = self.rows // 2
        self.core = [
            links.remote(
                parts.at[p(bits + CORE_BIT)], core_in.at[i], (p(CORE_BIT), tp), core_in.at[i]
            )
            for i, bits in enumerate((6, 2, 4, 0))
        ]
        self.diag = [
            links.remote(
                parts.at[p(6), pl.ds(h * half, half)], diag_in.at[h], (p(bits), tp), diag_in.at[h]
            )
            for h, bits in enumerate((Y_BIT, X_BIT))
        ]
        self.side = [
            links.remote(parts.at[p(bits)], side_in.at[i], (p(bits), tp), side_in.at[i])
            for i, bits in enumerate((X_BIT, Y_BIT))
        ]

    def add(self, index, first, count, refs, target=None):
        chunk = 32

        @pl.loop(0, count // chunk)
        def _(r):
            here = pl.ds(pl.multiple_of(first + r * chunk, chunk), chunk)
            there = pl.ds(pl.multiple_of(r * chunk, chunk), chunk)
            total = self.parts[index, here, :].astype(jnp.float32)
            for ref in refs:
                total = total + ref[there, :].astype(jnp.float32)
            if target is None:
                self.parts[index, here, :] = total.astype(jnp.bfloat16)
            else:
                target[here, :] = total

    def to_core(self):
        for out, back in self.core:
            out.start()

    def diagonal(self):
        self.core[0][1].wait_recv()
        self.add(self.links.peer(6), 0, self.rows, [self.core_in.at[0]])
        for out, back in self.diag:
            out.start()

    def sideways(self, i):
        index = self.links.peer((X_BIT, Y_BIT)[i])
        self.core[1 + i][1].wait_recv()
        self.add(index, 0, self.rows, [self.core_in.at[1 + i]])
        self.diag[i][1].wait_recv()
        self.add(index, i * (self.rows // 2), self.rows // 2, [self.diag_in.at[i]])
        self.side[i][0].start()

    def finish(self, target):
        self.core[3][1].wait_recv()
        for out, back in self.side:
            back.wait_recv()
        self.add(
            self.links.fs,
            0,
            self.rows,
            [self.core_in.at[3], self.side_in.at[0], self.side_in.at[1]],
            target,
        )

    def sent(self):
        for out, back in self.core + self.diag + self.side:
            out.wait_send()


def backward_kernel(
    branch_ref,
    residual_ref,
    small_grad_ref,
    attended_ref,
    query_ref,
    hidden_ref,
    tokens_ref,
    kv_ref,
    qkv_ref,
    out_ref,
    small_ref,
    cos_ref,
    sin_ref,
    start_ref,
    slabs_ref,
    up_in,
    shared_up_in,
    down_in,
    shared_down_in,
    input_grad_ref,
    qkv_own,
    out_own,
    small_own,
    up_all,
    shared_up_all,
    down_all,
    shared_down_all,
    kv_full,
    qkv_full,
    out_full,
    branch_all,
    odds,
    query_grad,
    projected,
    kv_total,
    kv_parts,
    kv_core,
    kv_diag,
    kv_side,
    qkv_parts,
    qkv_core,
    qkv_diag,
    qkv_side,
    out_parts,
    out_core,
    out_diag,
    out_side,
    one_parts,
    one_in,
    grad_rows,
    small_parts,
    small_in,
    small_column,
    send,
    recv,
    local,
):
    links = Links(send, recv, local)
    fs, tp = links.fs, links.tp
    quarter, width = residual_ref.shape
    rows = quarter * QUARTERS
    block = width // E
    local_width = query_ref.shape[1]
    heads = local_width // HD
    seqs = rows // SEQ_DEV
    length = E * SEQ_DEV
    scale = HD ** (-0.5)

    def at_rows(index, size):
        return pl.ds(pl.multiple_of(index * size, size), size)

    own = at_rows(tp, quarter)
    links.greet(range(1, 8), range(1, QUARTERS))
    branch = []
    for step in range(1, QUARTERS):
        here = branch_all.at[own]
        landing = branch_all.at[at_rows(links.along(QUARTERS - step), quarter)]
        branch.append(links.remote(branch_ref, here, (fs, links.along(step)), landing))
    for out, back in branch:
        out.start()
    branch_all[own, :] = branch_ref[...]
    results = (up_all, shared_up_all, down_all, shared_down_all)
    slab_copies = []
    for bits in (1, 6, 3, 5, 7):
        slab_copies += grad_copies(links, slabs_ref, results, bits)
    for out, back in slab_copies[:LATE]:
        out.start()
    slab_own = [links.inside(*pair) for pair in grad_pieces(slabs_ref, results, fs, fs)]
    for copy in slab_own:
        copy.start()
    kv_load = links.inside(kv_ref, kv_full)
    kv_load.start()
    out_load = links.inside(out_ref, out_full)
    out_load.start()
    qkv_load = links.inside(qkv_ref, qkv_full)
    qkv_load.start()
    kv_sum = Scatter(links, kv_parts, kv_core, kv_diag, kv_side)
    qkv_sum = Scatter(links, qkv_parts, qkv_core, qkv_diag, qkv_side)
    out_sum = Scatter(links, out_parts, out_core, out_diag, out_side)

    kv_load.wait()
    key_pos = lax.broadcasted_iota(jnp.int32, (SEQ_DEV, length), 1)
    query_pos = fs * SEQ_DEV + lax.broadcasted_iota(jnp.int32, (SEQ_DEV, length), 0)
    for s in range(seqs):
        here = slice(s * SEQ_DEV, (s + 1) * SEQ_DEV)
        allowed = (key_pos <= query_pos) & (key_pos >= as_column(start_ref[s : s + 1, :]))
        for h in range(heads):
            cols = slice(h * HD, (h + 1) * HD)
            keys = kv_full[:, here, cols].reshape(length, HD)
            scores = matmul_nt(query_ref[here, cols], keys) * scale
            scores = jnp.where(allowed, scores, NEG_FILL)
            top = jnp.max(scores, axis=1, keepdims=True)
            weights = jnp.exp(scores - top)
            odds[s * heads + h] = weights / jnp.sum(weights, axis=1, keepdims=True)
    out_load.wait()
    for out, back in branch:
        back.wait_recv()
    attended_grad = jnp.zeros((rows, local_width), jnp.float32)
    for b in range(E):
        attended_grad = attended_grad + matmul_nt(
            branch_all[:, b * block : (b + 1) * block], out_full[b]
        )
    query_grad[...] = attended_grad.astype(jnp.bfloat16)
    for s in range(seqs):
        here = slice(s * SEQ_DEV, (s + 1) * SEQ_DEV)
        for h in range(heads):
            cols = slice(h * HD, (h + 1) * HD)
            vcols = slice(local_width + h * HD, local_width + (h + 1) * HD)
            keys = kv_full[:, here, cols].reshape(length, HD)
            values = kv_full[:, here, vcols].reshape(length, HD)
            grad = query_grad[here, cols]
            probs = odds[s * heads + h]
            weights_grad = matmul_nt(grad, values)
            delta = jnp.sum(probs * weights_grad, axis=1, keepdims=True)
            score_grad = (probs * (weights_grad - delta)).astype(jnp.bfloat16)
            key_grad = matmul_tn(score_grad, query_ref[here, cols]) * scale
            value_grad = matmul_tn(probs.astype(jnp.bfloat16), grad)
            kv_parts[:, here, cols] = key_grad.astype(jnp.bfloat16).reshape(E, SEQ_DEV, HD)
            kv_parts[:, here, vcols] = value_grad.astype(jnp.bfloat16).reshape(E, SEQ_DEV, HD)
            projected[0, here, cols] = turn(
                matmul(score_grad, keys) * scale, cos_ref[here, :], -sin_ref[here, :]
            ).astype(jnp.bfloat16)
    kv_sum.to_core()
    attended = attended_ref[...]
    for b in range(E):
        cols = slice(b * block, (b + 1) * block)
        out_parts[b] = matmul_tn(attended, branch_all[:, cols]).astype(jnp.bfloat16)
    kv_sum.diagonal()
    out_sum.to_core()

    def weight_grad(j):
        for b in range(E):
            cols = slice(b * block, (b + 1) * block)
            qkv_parts[b, j * block : (j + 1) * block] = matmul_tn(
                hidden_ref[:, cols], projected[j]
            ).astype(jnp.bfloat16)

    weight_grad(0)
    kv_sum.sideways(0)
    kv_sum.sideways(1)
    out_sum.diagonal()
    qkv_load.wait()
    kv_sum.finish(kv_total)
    for out, back in slab_copies[LATE:]:
        out.start()
    projected[1] = turn(kv_total[:, :local_width], cos_ref[...], -sin_ref[...]).astype(jnp.bfloat16)
    projected[2] = kv_total[:, local_width:].astype(jnp.bfloat16)
    for b in range(E):
        cols = slice(b * block, (b + 1) * block)
        part = jnp.zeros((rows, block), jnp.float32)
        for j in range(3):
            part = part + matmul_nt(projected[j], qkv_full[j, cols])
        one_parts[:, cols] = part.astype(jnp.bfloat16)
    column = []
    for step in range(1, QUARTERS):
        peer = links.along(step)
        column.append(
            links.remote(
                one_parts.at[at_rows(peer, quarter)],
                one_in.at[step - 1],
                (fs, peer),
                one_in.at[step - 1],
            )
        )
    for out, back in column:
        out.start()
    weight_grad(1)
    weight_grad(2)
    qkv_sum.to_core()
    out_sum.sideways(0)
    out_sum.sideways(1)
    qkv_sum.diagonal()
    qkv_sum.sideways(0)
    qkv_sum.sideways(1)
    for out, back in column:
        back.wait_recv()
    tokens = tokens_ref[own, :].astype(jnp.float32)
    rstd = lax.rsqrt(jnp.mean(tokens * tokens, axis=1, keepdims=True) + NORM_EPS)
    total = one_parts[own, :].astype(jnp.float32)
    for step in range(1, QUARTERS):
        total = total + one_in[step - 1].astype(jnp.float32)
    mean = jnp.zeros((quarter, 1), jnp.float32)
    sub = lax.broadcasted_iota(jnp.int32, (SMALL, block), 0)
    for b in range(E):
        at = slice(b * block, (b + 1) * block)
        gain = small_ref[b, 0:1, :].astype(jnp.float32)
        normed = tokens[:, at] * rstd
        mean = mean + jnp.sum(total[:, at] * gain * normed, axis=1, keepdims=True)
        gain_grad = jnp.sum(total[:, at] * normed, axis=0, keepdims=True)
        small_parts[b] = jnp.where(sub == 0, gain_grad, small_grad_ref[:, at])
    mean = mean / width
    for b in range(E):
        at = slice(b * block, (b + 1) * block)
        gain = small_ref[b, 0:1, :].astype(jnp.float32)
        normed = tokens[:, at] * rstd
        grad_rows[:, at] = (
            residual_ref[:, at] + rstd * (total[:, at] * gain - normed * mean)
        ).astype(jnp.bfloat16)
    spread = []
    for step in range(1, QUARTERS):
        peer = links.along(step)
        landing = input_grad_ref.at[at_rows(links.along(QUARTERS - step), quarter)]
        spread.append(links.remote(grad_rows, input_grad_ref.at[own], (fs, peer), landing))
    for out, back in spread:
        out.start()
    keep = links.inside(grad_rows, input_grad_ref.at[own])
    keep.start()
    small_copies = []
    for bits in range(1, E):
        peer = links.peer(bits)
        small_copies.append(
            links.remote(
                small_parts.at[peer], small_in.at[bits - 1], (peer, tp), small_in.at[bits - 1]
            )
        )
    for out, back in small_copies:
        out.start()
    out_sum.finish(out_own)
    for out, back in small_copies:
        back.wait_recv()
    small_total = small_parts[fs]
    for bits in range(1, E):
        small_total = small_total + small_in[bits - 1]
    small_column[tp] = small_total
    small_spread = []
    for step in range(1, QUARTERS):
        here = small_column.at[tp]
        landing = small_column.at[links.along(QUARTERS - step)]
        small_spread.append(links.remote(here, here, (fs, links.along(step)), landing))
    for out, back in small_spread:
        out.start()
    qkv_sum.finish(qkv_own)
    for out, back in small_spread:
        back.wait_recv()
    small_own[...] = small_column[0] + small_column[1] + small_column[2] + small_column[3]
    for out, back in spread + slab_copies:
        back.wait_recv()
    for copy in (*slab_own, keep):
        copy.wait()
    for out, back in branch + slab_copies + column + spread + small_copies + small_spread:
        out.wait_send()
    for scatter in (kv_sum, out_sum, qkv_sum):
        scatter.sent()


def backward_call(
    branch_rows,
    residual_grad,
    small_grad,
    attended,
    query_rows,
    hidden_one,
    tokens,
    kv_all,
    qkv_full,
    out_full,
    small_full,
    cosine,
    sine,
    start,
    slabs,
    *parts,
):
    quarter, width = residual_grad.shape
    rows = quarter * QUARTERS
    block = width // E
    local_width = query_rows.shape[1]
    bf, f32 = jnp.bfloat16, jnp.float32
    sds = jax.ShapeDtypeStruct
    vmem = pl.BlockSpec(memory_space=pltpu.VMEM)
    hbm = pl.BlockSpec(memory_space=pl.ANY)
    outs = [
        (sds((rows, width), bf), hbm),
        (sds((3 * block, local_width), f32), vmem),
        (sds((local_width, block), f32), vmem),
        (sds((SMALL, block), f32), vmem),
        *((sds(part.shape, bf), hbm) for part in parts),
    ]

    def scatter_scratch(count, columns):
        return [
            pltpu.VMEM((E, count, columns), bf),
            pltpu.VMEM((4, count, columns), bf),
            pltpu.VMEM((2, count // 2, columns), bf),
            pltpu.VMEM((2, count, columns), bf),
        ]

    return pl.pallas_call(
        backward_kernel,
        name="attention_backward",
        out_shape=[o[0] for o in outs],
        in_specs=[vmem] * 7 + [hbm] * 3 + [vmem] * 4 + [hbm] * 5,
        out_specs=[o[1] for o in outs],
        input_output_aliases={15 + i: 4 + i for i in range(4)},
        scratch_shapes=[
            pltpu.VMEM((E, rows, 2 * local_width), bf),
            pltpu.VMEM((3, width, local_width), bf),
            pltpu.VMEM((E, local_width, block), bf),
            pltpu.VMEM((rows, width), bf),
            pltpu.VMEM((rows // SEQ_DEV * local_width // HD, SEQ_DEV, E * SEQ_DEV), f32),
            pltpu.VMEM((rows, local_width), bf),
            pltpu.VMEM((3, rows, local_width), bf),
            pltpu.VMEM((rows, 2 * local_width), f32),
            *scatter_scratch(rows, 2 * local_width),
            *scatter_scratch(3 * block, local_width),
            *scatter_scratch(local_width, block),
            pltpu.VMEM((rows, width), bf),
            pltpu.VMEM((QUARTERS - 1, quarter, width), bf),
            pltpu.VMEM((quarter, width), bf),
            pltpu.VMEM((E, SMALL, block), f32),
            pltpu.VMEM((E - 1, SMALL, block), f32),
            pltpu.VMEM((QUARTERS, SMALL, block), f32),
            pltpu.SemaphoreType.DMA((96,)),
            pltpu.SemaphoreType.DMA((96,)),
            pltpu.SemaphoreType.DMA((16,)),
        ],
        compiler_params=pltpu.CompilerParams(
            collective_id=3, has_side_effects=True, vmem_limit_bytes=62 * 2**20
        ),
    )(
        branch_rows,
        residual_grad,
        small_grad,
        attended,
        query_rows,
        hidden_one,
        tokens,
        kv_all,
        qkv_full,
        out_full,
        small_full,
        cosine,
        sine,
        start,
        slabs,
        *parts,
    )


def finish_kernel(
    up_ref, down_ref, shared_ref, grad_ref, qkv_ref, out_ref, output_ref, small_ref,
    up, down, shared, grad, qkv, out, output, gains, router, gate,
):
    up[...] = up_ref[...].astype(jnp.float32)
    down[...] = down_ref[...].astype(jnp.float32)
    shared[...] = shared_ref[...].astype(jnp.float32)
    grad[...] = grad_ref[...].astype(jnp.float32)
    qkv[...] = qkv_ref[...]
    out[...] = out_ref[...]
    output[...] = output_ref[...]
    gains[...] = small_ref[0:2, :]
    router[...] = small_ref[2 : 2 + E, :]
    gate[...] = small_ref[2 + E : 3 + E, :]


def finish_call(up, down, shared, grad, qkv, out, output, small):
    f32 = jnp.float32
    sds = jax.ShapeDtypeStruct
    block = small.shape[1]
    arrays = (up, down, shared, grad, qkv, out, output)

    def split(array):
        shape = (array.shape[0] // E, *array.shape[1:])
        return pl.BlockSpec(shape, lambda i: (i,) + (0,) * (len(shape) - 1))

    def once(shape):
        return pl.BlockSpec(shape, lambda i: (0, 0))

    specs = [split(array) for array in arrays]
    types = (f32, f32, f32, f32, f32, f32, output.dtype)
    return pl.pallas_call(
        finish_kernel,
        name="finish",
        grid=(E,),
        out_shape=[sds(a.shape, t) for a, t in zip(arrays, types, strict=True)]
        + [sds((n, block), f32) for n in (2, E, 1)],
        in_specs=[*specs, once(small.shape)],
        out_specs=[*specs, *(once((n, block)) for n in (2, E, 1))],
    )(*arrays, small)


def shards_units(
    tokens,
    cotangent,
    qkv_weight,
    out_weight,
    norm_gains,
    router_weight,
    shared_gate,
    expert_gate_up,
    expert_down,
    shared_gate_up,
    shared_down,
    routes,
    doc_start,
):
    tok_rows, width = tokens.shape
    seq_count = tok_rows // SEQ_DEV
    fs_index = lax.axis_index("fs")
    query_pos = fs_index * SEQ_DEV + jnp.arange(SEQ_DEV, dtype=jnp.int32)
    positions = jnp.tile(query_pos, seq_count)
    half_cos, half_sin = rope_tables(positions)
    cosine = jnp.concatenate([half_cos, half_cos], axis=1)
    sine = jnp.concatenate([-half_sin, half_sin], axis=1)
    routed_units = expert_down.shape[1]
    (
        output,
        branch_rows,
        residual_grad,
        small_grad,
        grad_slabs,
        up_part,
        shared_up_part,
        down_part,
        shared_down_part,
        attended,
        query_rows,
        hidden_one,
        _,
        _,
        _,
        kv_all,
        qkv_full,
        out_full,
        small_full,
    ) = layer_call(
        tokens,
        cotangent,
        qkv_weight,
        out_weight,
        norm_gains,
        router_weight,
        shared_gate[None],
        jnp.transpose(expert_gate_up, (0, 2, 3, 1)).reshape(E, 2 * routed_units, -1),
        jnp.transpose(shared_gate_up, (1, 2, 0)),
        expert_down,
        shared_down,
        cosine,
        sine,
        doc_start.reshape(seq_count, SEQ_DEV),
        routes.T,
    )
    input_grad, qkv_own, out_own, small_own, up_own, shared_up_own, down_own, shared_down_own = (
        backward_call(
            branch_rows,
            residual_grad,
            small_grad,
            attended,
            query_rows,
            hidden_one,
            tokens,
            kv_all,
            qkv_full,
            out_full,
            small_full,
            cosine,
            sine,
            doc_start.reshape(seq_count, SEQ_DEV),
            grad_slabs,
            up_part,
            shared_up_part,
            down_part,
            shared_down_part,
        )
    )
    up_own, down_own, shared_down_own, input_grad, qkv_own, out_own, output, gains, router, gate = (
        finish_call(
            up_own, down_own, shared_down_own, input_grad, qkv_own, out_own, output, small_own
        )
    )
    up_own = up_own.reshape(E, 2, routed_units, -1)
    return (
        output,
        input_grad,
        qkv_own.reshape(qkv_weight.shape),
        out_own,
        gains,
        router,
        gate[0],
        jnp.transpose(up_own, (0, 3, 1, 2)),
        down_own,
        jnp.transpose(shared_up_own, (2, 0, 1)).astype(jnp.float32),
        shared_down_own,
    )


def solution(mesh):
    return jax.shard_map(
        shards_units if dict(mesh.shape) == {"fs": E, "tp": QUARTERS} else shards_gathered,
        mesh=mesh,
        in_specs=(
            P("fs", None),
            P("fs", None),
            P(None, "fs", "tp"),
            P("tp", "fs"),
            P(None, "fs"),
            P(None, "fs"),
            P("fs"),
            P(None, "fs", None, "tp"),
            P(None, "tp", "fs"),
            P("fs", None, "tp"),
            P("tp", "fs"),
            P("fs", None),
            P("fs"),
        ),
        out_specs=(
            P("fs", "tp"),
            P("fs", None),
            P(None, "fs", "tp"),
            P("tp", "fs"),
            P(None, "fs"),
            P(None, "fs"),
            P("fs"),
            P(None, "fs", None, "tp"),
            P(None, "tp", "fs"),
            P("fs", None, "tp"),
            P("tp", "fs"),
        ),
        check_vma=False,
    )
```

```python
import functools
import math

import jax
import jax.numpy as jnp
from jax import lax
from jax.experimental import pallas as pl
from jax.experimental.pallas import tpu as pltpu
from jax.sharding import PartitionSpec as P

HD = 128
E = 8
SEQ_DEV = 128
SIDE = 128


NORM_EPS = 1e-06
NEG_FILL = -1e30
ROPE_BASE = 1000000.0


def rope_tables(positions):
    half_size = HD // 2
    frequency = ROPE_BASE ** (-(jnp.arange(half_size, dtype=jnp.float32) * 2.0 / HD))
    angles = positions.astype(jnp.float32)[:, None] * frequency[None, :]
    return (jnp.cos(angles), jnp.sin(angles))


def rotate(values, cosine, sine_table):
    shaped = values.reshape(values.shape[0], -1, HD)
    half_size = HD // 2
    first_half = shaped[..., :half_size]
    second_half = shaped[..., half_size:]
    cos_part = cosine[:, None, :]
    sin_part = sine_table[:, None, :]
    turned = jnp.concatenate(
        [
            first_half * cos_part - second_half * sin_part,
            second_half * cos_part + first_half * sin_part,
        ],
        axis=-1,
    )
    return turned.reshape(values.shape)


def key_mask(query_pos, query_start, first_dev, group_size):
    key_pos = (first_dev + jnp.arange(group_size, dtype=jnp.int32)[:, None]) * SEQ_DEV + jnp.arange(
        SEQ_DEV, dtype=jnp.int32
    )[None, :]
    key_pos = key_pos[None, None, :, :]
    return (key_pos <= query_pos[None, :, None, None]) & (key_pos >= query_start[:, :, None, None])


def shards_gathered(
    tokens,
    cotangent,
    qkv_weight,
    out_weight,
    norm_gains,
    router_weight,
    shared_gate,
    expert_gate_up,
    expert_down,
    shared_gate_up,
    shared_down,
    routes,
    doc_start,
):
    tok_rows = tokens.shape[0]
    seq_count = tok_rows // SEQ_DEV
    local_width = qkv_weight.shape[2]
    head_count = local_width // HD
    out_width = tokens.shape[1] // lax.axis_size("tp")
    score_scale = HD ** (-0.5)
    fs_index = lax.axis_index("fs")
    tp_index = lax.axis_index("tp")
    query_pos = fs_index * SEQ_DEV + jnp.arange(SEQ_DEV, dtype=jnp.int32)
    positions = jnp.tile(query_pos, seq_count)
    query_start = doc_start.reshape(seq_count, SEQ_DEV)
    cosine, sine_table = rope_tables(positions)
    group_limit = max(1, 512 // SEQ_DEV)
    qkv_full, out_full, gains_full, router_full, shared_gate_full = (
        lax.all_gather(qkv_weight, "fs", axis=1, tiled=True),
        lax.all_gather(out_weight, "fs", axis=1, tiled=True),
        lax.all_gather(norm_gains, "fs", axis=1, tiled=True),
        lax.all_gather(router_weight, "fs", axis=1, tiled=True),
        lax.all_gather(shared_gate, "fs", axis=0, tiled=True),
    )
    token_float = tokens.astype(jnp.float32)
    rstd_one = lax.rsqrt(jnp.mean(token_float * token_float, axis=1, keepdims=True) + NORM_EPS)
    normed_one = token_float * rstd_one
    hidden_one = (normed_one * gains_full[0].astype(jnp.float32)[None, :]).astype(jnp.bfloat16)
    projected = jnp.einsum("td,jdf->jtf", hidden_one, qkv_full, preferred_element_type=jnp.float32)
    query_rows = rotate(projected[0], cosine, sine_table).astype(jnp.bfloat16)
    key_own = rotate(projected[1], cosine, sine_table).astype(jnp.bfloat16)
    value_own = projected[2].astype(jnp.bfloat16)
    query_heads = query_rows.reshape(seq_count, SEQ_DEV, head_count, HD)

    def score_block(key_group, first_dev):
        allowed = key_mask(query_pos, query_start, first_dev, key_group.shape[0])[:, None]
        scores = (
            jnp.einsum(
                "pqhd,gpkhd->phqgk", query_heads, key_group, preferred_element_type=jnp.float32
            )
            * score_scale
        )
        return (jnp.where(allowed, scores, NEG_FILL), allowed)

    def forward_update(running, key_group, value_group, first_dev):
        run_max, run_sum, accumulated = running
        scores, allowed = score_block(key_group, first_dev)
        new_max = jnp.maximum(run_max, jnp.max(scores, axis=(3, 4)))
        weights = jnp.where(allowed, jnp.exp(scores - new_max[..., None, None]), 0.0)
        factor = jnp.exp(run_max - new_max)
        new_sum = run_sum * factor + jnp.sum(weights, axis=(3, 4))
        mixed_part = jnp.einsum(
            "phqgk,gpkhd->pqhd",
            weights.astype(jnp.bfloat16),
            value_group,
            preferred_element_type=jnp.float32,
        )
        new_accum = accumulated * jnp.transpose(factor, (0, 2, 1))[..., None] + mixed_part
        return (new_max, new_sum, new_accum)

    initial = (
        jnp.full((seq_count, head_count, SEQ_DEV), NEG_FILL, jnp.float32),
        jnp.zeros((seq_count, head_count, SEQ_DEV), jnp.float32),
        jnp.zeros((seq_count, SEQ_DEV, head_count, HD), jnp.float32),
    )
    running = initial
    key_piece = lax.all_gather(key_own, "fs", axis=0, tiled=True)
    value_piece = lax.all_gather(value_own, "fs", axis=0, tiled=True)
    shard_count = key_piece.shape[0] // tok_rows
    group_size = math.gcd(shard_count, group_limit)
    step_count = shard_count // group_size
    shaped = (step_count, group_size, seq_count, SEQ_DEV, head_count, HD)
    first_dev = jnp.int32(0) // tok_rows

    def one_step(carried, inputs):
        key_group, value_group, group_index = inputs
        start_dev = group_index * group_size
        updated = lax.cond(
            start_dev <= fs_index,
            lambda state_in: forward_update(state_in, key_group, value_group, start_dev),
            lambda state_in: state_in,
            carried,
        )
        return (updated, None)

    running, ignored = lax.scan(
        one_step,
        running,
        (
            key_piece.reshape(shaped),
            value_piece.reshape(shaped),
            jnp.arange(step_count, dtype=jnp.int32),
        ),
    )
    run_max, run_sum, accumulated = running
    attended_heads = (accumulated / jnp.transpose(run_sum, (0, 2, 1))[..., None]).astype(
        jnp.bfloat16
    )
    log_total = run_max + jnp.log(run_sum)
    attended = attended_heads.reshape(tok_rows, local_width)
    branch_part = jnp.dot(attended, out_full, preferred_element_type=jnp.float32)
    branch = lax.psum(branch_part.astype(jnp.bfloat16), "tp").astype(jnp.float32)
    residual = token_float + branch
    rstd_two = lax.rsqrt(jnp.mean(residual * residual, axis=1, keepdims=True) + NORM_EPS)
    normed_two = residual * rstd_two
    hidden_two = (normed_two * gains_full[1].astype(jnp.float32)[None, :]).astype(jnp.bfloat16)
    expert_gate_all, expert_down_all, shared_up_all, shared_down_all = (
        lax.all_gather(expert_gate_up, "fs", axis=1, tiled=True),
        lax.all_gather(expert_down, "fs", axis=2, tiled=True),
        lax.all_gather(shared_gate_up, "fs", axis=0, tiled=True),
        lax.all_gather(shared_down, "fs", axis=1, tiled=True),
    )
    logits = jnp.einsum("td,ed->te", hidden_two, router_full, preferred_element_type=jnp.float32)
    router_probs = jax.nn.softmax(logits, axis=-1)
    chosen = jnp.sum(
        (routes[:, :, None] == jnp.arange(E, dtype=jnp.int32)[None, None, :]).astype(jnp.float32),
        axis=1,
    )
    gate_weights = router_probs * chosen
    gate_up = jnp.einsum(
        "td,edkf->tekf", hidden_two, expert_gate_all, preferred_element_type=jnp.float32
    )
    gate_part = gate_up[:, :, 0]
    up_part = gate_up[:, :, 1]
    gate_sigmoid = jax.nn.sigmoid(gate_part)
    active = gate_part * gate_sigmoid * up_part
    hidden = (gate_weights[:, :, None] * active).astype(jnp.bfloat16)
    shared_in = jnp.einsum(
        "td,dkf->tkf", hidden_two, shared_up_all, preferred_element_type=jnp.float32
    )
    shared_gate_in = shared_in[:, 0]
    shared_up_in = shared_in[:, 1]
    shared_sigmoid = jax.nn.sigmoid(shared_gate_in)
    shared_active = shared_gate_in * shared_sigmoid * shared_up_in
    gate_logit = jnp.einsum(
        "td,d->t", hidden_two, shared_gate_full, preferred_element_type=jnp.float32
    )
    gate_value = jax.nn.sigmoid(gate_logit)
    shared_hidden = (gate_value[:, None] * shared_active).astype(jnp.bfloat16)
    mixture_part = jnp.einsum(
        "tef,efd->td", hidden, expert_down_all, preferred_element_type=jnp.float32
    ) + jnp.dot(shared_hidden, shared_down_all, preferred_element_type=jnp.float32)
    mixture = lax.psum_scatter(
        mixture_part.astype(jnp.bfloat16), "tp", scatter_dimension=1, tiled=True
    ).astype(jnp.float32)
    output = (
        lax.dynamic_slice_in_dim(residual, tp_index * out_width, out_width, 1) + mixture
    ).astype(jnp.bfloat16)
    qkv_back, out_back, gains_back, router_back, shared_gate_back = (
        lax.all_gather(qkv_weight, "fs", axis=1, tiled=True),
        lax.all_gather(out_weight, "fs", axis=1, tiled=True),
        lax.all_gather(norm_gains, "fs", axis=1, tiled=True),
        lax.all_gather(router_weight, "fs", axis=1, tiled=True),
        lax.all_gather(shared_gate, "fs", axis=0, tiled=True),
    )
    expert_gate_back, expert_down_back, shared_up_back, shared_down_back = (
        lax.all_gather(expert_gate_up, "fs", axis=1, tiled=True),
        lax.all_gather(expert_down, "fs", axis=2, tiled=True),
        lax.all_gather(shared_gate_up, "fs", axis=0, tiled=True),
        lax.all_gather(shared_down, "fs", axis=1, tiled=True),
    )
    hidden_grad = jnp.einsum(
        "td,efd->tef", cotangent, expert_down_back, preferred_element_type=jnp.float32
    )
    expert_down_grad = jnp.einsum(
        "tef,td->efd", hidden, cotangent, preferred_element_type=jnp.float32
    )
    shared_grad = jnp.einsum(
        "td,fd->tf", cotangent, shared_down_back, preferred_element_type=jnp.float32
    )
    shared_down_grad = jnp.einsum(
        "tf,td->fd", shared_hidden, cotangent, preferred_element_type=jnp.float32
    )
    gate_dot = jnp.sum(active * hidden_grad, axis=2)
    shared_dot = jnp.sum(shared_active * shared_grad, axis=1)
    active_grad = gate_weights[:, :, None] * hidden_grad
    gate_grad = active_grad * up_part * gate_sigmoid * (1.0 + gate_part * (1.0 - gate_sigmoid))
    up_grad = active_grad * gate_part * gate_sigmoid
    gate_up_grad = jnp.stack([gate_grad, up_grad], axis=2).astype(jnp.bfloat16)
    shared_active_grad = gate_value[:, None] * shared_grad
    shared_gate_grad = (
        shared_active_grad
        * shared_up_in
        * shared_sigmoid
        * (1.0 + shared_gate_in * (1.0 - shared_sigmoid))
    )
    shared_unit_grad = shared_active_grad * shared_gate_in * shared_sigmoid
    shared_up_grad = jnp.stack([shared_gate_grad, shared_unit_grad], axis=1).astype(jnp.bfloat16)
    expert_gate_grad = jnp.einsum(
        "td,tekf->edkf", hidden_two, gate_up_grad, preferred_element_type=jnp.float32
    )
    shared_proj_grad = jnp.einsum(
        "td,tkf->dkf", hidden_two, shared_up_grad, preferred_element_type=jnp.float32
    )
    input_part = jnp.einsum(
        "tekf,edkf->td", gate_up_grad, expert_gate_back, preferred_element_type=jnp.float32
    ) + jnp.einsum(
        "tkf,dkf->td", shared_up_grad, shared_up_back, preferred_element_type=jnp.float32
    )
    input_sum, gate_sum, shared_sum = (
        lax.psum(input_part.astype(jnp.bfloat16), "tp").astype(jnp.float32),
        lax.psum(gate_dot.astype(jnp.bfloat16), "tp").astype(jnp.float32),
        lax.psum(shared_dot.astype(jnp.bfloat16), "tp").astype(jnp.float32),
    )
    chosen_grad = chosen * gate_sum
    logit_grad = (
        router_probs * (chosen_grad - jnp.sum(router_probs * chosen_grad, axis=1, keepdims=True))
    ).astype(jnp.bfloat16)
    gate_logit_grad = (shared_sum * gate_value * (1.0 - gate_value)).astype(jnp.bfloat16)
    router_grad = jnp.einsum(
        "te,td->ed", logit_grad, hidden_two, preferred_element_type=jnp.float32
    )
    shared_vector_grad = jnp.einsum(
        "t,td->d", gate_logit_grad, hidden_two, preferred_element_type=jnp.float32
    )
    two_grad = (
        input_sum
        + jnp.einsum("te,ed->td", logit_grad, router_back, preferred_element_type=jnp.float32)
        + gate_logit_grad.astype(jnp.float32)[:, None]
        * shared_gate_back.astype(jnp.float32)[None, :]
    )
    scaled_two = two_grad * gains_back[1].astype(jnp.float32)[None, :]
    gain_two_grad = jnp.sum(two_grad * normed_two, axis=0)
    residual_grad = cotangent.astype(jnp.float32) + rstd_two * (
        scaled_two - normed_two * jnp.mean(scaled_two * normed_two, axis=1, keepdims=True)
    )
    branch_grad = residual_grad.astype(jnp.bfloat16)
    out_grad = jnp.einsum("tf,td->fd", attended, branch_grad, preferred_element_type=jnp.float32)
    attended_grad = jnp.einsum(
        "td,fd->tf", branch_grad, out_back, preferred_element_type=jnp.float32
    ).astype(jnp.bfloat16)
    grad_heads = attended_grad.reshape(seq_count, SEQ_DEV, head_count, HD)
    delta_rows = jnp.einsum(
        "pqhd,pqhd->phq", grad_heads, attended_heads, preferred_element_type=jnp.float32
    )
    key_all, value_all = (
        lax.all_gather(key_own, "fs", axis=0, tiled=True),
        lax.all_gather(value_own, "fs", axis=0, tiled=True),
    )
    device_count = key_all.shape[0] // tok_rows
    back_group = math.gcd(device_count, group_limit)
    back_steps = device_count // back_group
    back_shape = (back_steps, back_group, seq_count, SEQ_DEV, head_count, HD)

    def backward_update(key_group, value_group, start_dev):
        scores, allowed = score_block(key_group, start_dev)
        probs_block = jnp.where(allowed, jnp.exp(scores - log_total[..., None, None]), 0.0)
        weights_grad = jnp.einsum(
            "pqhd,gpkhd->phqgk", grad_heads, value_group, preferred_element_type=jnp.float32
        )
        score_grad = (probs_block * (weights_grad - delta_rows[..., None, None])).astype(
            jnp.bfloat16
        )
        query_part = (
            jnp.einsum(
                "phqgk,gpkhd->pqhd", score_grad, key_group, preferred_element_type=jnp.float32
            )
            * score_scale
        )
        key_part = (
            jnp.einsum(
                "phqgk,pqhd->gpkhd", score_grad, query_heads, preferred_element_type=jnp.float32
            )
            * score_scale
        )
        value_part = jnp.einsum(
            "phqgk,pqhd->gpkhd",
            probs_block.astype(jnp.bfloat16),
            grad_heads,
            preferred_element_type=jnp.float32,
        )
        return (query_part, key_part, value_part)

    empty_grads = (
        jnp.zeros((seq_count, SEQ_DEV, head_count, HD), jnp.float32),
        jnp.zeros((back_group, seq_count, SEQ_DEV, head_count, HD), jnp.float32),
        jnp.zeros((back_group, seq_count, SEQ_DEV, head_count, HD), jnp.float32),
    )
    scan_inputs = (
        key_all.reshape(back_shape),
        value_all.reshape(back_shape),
        jnp.arange(back_steps, dtype=jnp.int32),
    )

    def back_step(query_acc, inputs):
        key_group, value_group, group_index = inputs
        start_dev = group_index * back_group
        query_part, key_part, value_part = lax.cond(
            start_dev <= fs_index,
            lambda ignored_in: backward_update(key_group, value_group, start_dev),
            lambda ignored_in: empty_grads,
            key_group,
        )
        term_rows = jnp.concatenate(
            [
                key_part.reshape(back_group * tok_rows, local_width),
                value_part.reshape(back_group * tok_rows, local_width),
            ],
            axis=1,
        )
        return (query_acc + query_part, term_rows)

    query_grad, key_value_terms = lax.scan(back_step, empty_grads[0], scan_inputs)
    key_value_sum = lax.psum_scatter(
        key_value_terms.reshape(device_count * tok_rows, 2 * local_width).astype(jnp.bfloat16),
        "fs",
        scatter_dimension=0,
        tiled=True,
    ).astype(jnp.float32)
    key_grad_rows = key_value_sum[:, :local_width]
    value_grad_rows = key_value_sum[:, local_width:]
    projected_grad = jnp.stack(
        [
            rotate(query_grad.reshape(tok_rows, local_width), cosine, -sine_table),
            rotate(key_grad_rows, cosine, -sine_table),
            value_grad_rows,
        ],
        axis=0,
    ).astype(jnp.bfloat16)
    qkv_grad = jnp.einsum(
        "td,jtf->jdf", hidden_one, projected_grad, preferred_element_type=jnp.float32
    )
    one_part = jnp.einsum(
        "jtf,jdf->td", projected_grad, qkv_back, preferred_element_type=jnp.float32
    )
    one_grad = lax.psum(one_part.astype(jnp.bfloat16), "tp").astype(jnp.float32)
    scaled_one = one_grad * gains_back[0].astype(jnp.float32)[None, :]
    gain_one_grad = jnp.sum(one_grad * normed_one, axis=0)
    input_grad = residual_grad + rstd_one * (
        scaled_one - normed_one * jnp.mean(scaled_one * normed_one, axis=1, keepdims=True)
    )
    gains_grad = jnp.stack([gain_one_grad, gain_two_grad], axis=0)
    reduced = (
        lax.psum_scatter(
            qkv_grad.astype(jnp.bfloat16), "fs", scatter_dimension=1, tiled=True
        ).astype(jnp.float32),
        lax.psum_scatter(
            out_grad.astype(jnp.bfloat16), "fs", scatter_dimension=1, tiled=True
        ).astype(jnp.float32),
        lax.psum_scatter(
            gains_grad.astype(jnp.bfloat16), "fs", scatter_dimension=1, tiled=True
        ).astype(jnp.float32),
        lax.psum_scatter(
            router_grad.astype(jnp.bfloat16), "fs", scatter_dimension=1, tiled=True
        ).astype(jnp.float32),
        lax.psum_scatter(
            shared_vector_grad.astype(jnp.bfloat16), "fs", scatter_dimension=0, tiled=True
        ).astype(jnp.float32),
        lax.psum_scatter(
            expert_gate_grad.astype(jnp.bfloat16), "fs", scatter_dimension=1, tiled=True
        ).astype(jnp.float32),
        lax.psum_scatter(
            expert_down_grad.astype(jnp.bfloat16), "fs", scatter_dimension=2, tiled=True
        ).astype(jnp.float32),
        lax.psum_scatter(
            shared_proj_grad.astype(jnp.bfloat16), "fs", scatter_dimension=0, tiled=True
        ).astype(jnp.float32),
        lax.psum_scatter(
            shared_down_grad.astype(jnp.bfloat16), "fs", scatter_dimension=1, tiled=True
        ).astype(jnp.float32),
    )
    return (
        output,
        input_grad,
        reduced[0],
        reduced[1],
        reduced[2],
        reduced[3],
        reduced[4],
        reduced[5],
        reduced[6],
        reduced[7],
        reduced[8],
    )


MESH = pl.DeviceIdType.MESH
X_BIT, Y_BIT, CORE_BIT = 2, 4, 1
QUARTERS = 4
SMALL = 16
EARLY = (2, 4)
CUT = 1536


def flip(index, bit):
    return index + bit - 2 * bit * ((index // bit) % 2)


class Links:
    def __init__(self, send, recv, local):
        self.fs = lax.axis_index("fs")
        self.tp = lax.axis_index("tp")
        self.send, self.recv, self.local = send, recv, local
        self.used = 0
        self.used_local = 0

    def peer(self, bits):
        where = self.fs
        for bit in (X_BIT, Y_BIT, CORE_BIT):
            if bits & bit:
                where = flip(where, bit)
        return where

    def along(self, step):
        return lax.rem(self.tp + step, QUARTERS)

    def remote(self, source, target, device, landing):
        i = self.used
        self.used += 1
        out = pltpu.make_async_remote_copy(
            src_ref=source,
            dst_ref=target,
            send_sem=self.send.at[i],
            recv_sem=self.recv.at[i],
            device_id=device,
            device_id_type=MESH,
        )
        back = pltpu.make_async_remote_copy(
            src_ref=landing,
            dst_ref=landing,
            send_sem=self.send.at[i],
            recv_sem=self.recv.at[i],
            device_id=device,
            device_id_type=MESH,
        )
        return out, back

    def inside(self, source, target):
        i = self.used_local
        self.used_local += 1
        return pltpu.make_async_copy(source, target, self.local.at[i])

    def greet(self, plane, column):
        barrier = pltpu.get_barrier_semaphore()
        for bits in plane:
            pl.semaphore_signal(
                barrier, inc=1, device_id=(self.peer(bits), self.tp), device_id_type=MESH
            )
        for step in column:
            pl.semaphore_signal(
                barrier, inc=1, device_id=(self.fs, self.along(step)), device_id_type=MESH
            )
        pl.semaphore_wait(barrier, len(plane) + len(column))


class Gather:
    def __init__(self, links, source, place, half):
        self.links = links
        fs, tp = links.fs, links.tp

        def to(bits, what, landing, origin=None):
            return links.remote(
                what if origin is None else origin, what, (links.peer(bits), tp), landing
            )

        p = links.peer
        self.keep = None if source is None else links.inside(source, place(fs))
        self.to_x = to(X_BIT, place(fs), place(p(X_BIT)), source)
        self.to_y = to(Y_BIT, place(fs), place(p(Y_BIT)), source)
        self.to_c = to(CORE_BIT, place(fs), place(p(CORE_BIT)), source)
        xy = X_BIT + Y_BIT
        self.x_on = to(Y_BIT, half(p(X_BIT), 0), half(p(xy), 0))
        self.y_on = to(X_BIT, half(p(Y_BIT), 1), half(p(xy), 1))
        self.x_core = to(CORE_BIT, place(p(X_BIT)), place(p(X_BIT + CORE_BIT)))
        self.y_core = to(CORE_BIT, place(p(Y_BIT)), place(p(Y_BIT + CORE_BIT)))
        self.d_core = [
            to(CORE_BIT, half(p(xy), h), half(p(xy + CORE_BIT), h)) for h in range(2)
        ]

    def first(self):
        self.to_x[0].start()
        self.to_y[0].start()
        self.to_c[0].start()
        if self.keep is not None:
            self.keep.start()

    def second(self):
        self.to_x[1].wait_recv()
        self.x_on[0].start()
        self.x_core[0].start()
        self.to_y[1].wait_recv()
        self.y_on[0].start()
        self.y_core[0].start()

    def third(self):
        self.x_on[1].wait_recv()
        self.d_core[0][0].start()
        self.y_on[1].wait_recv()
        self.d_core[1][0].start()

    def last(self):
        if self.keep is not None:
            self.keep.wait()
        for out, back in (self.to_c, self.x_core, self.y_core, *self.d_core):
            back.wait_recv()
        for out, back in (
            self.to_x,
            self.to_y,
            self.to_c,
            self.x_on,
            self.y_on,
            self.x_core,
            self.y_core,
            *self.d_core,
        ):
            out.wait_send()


class CrossGather:
    def __init__(self, links, source, blocks):
        self.links = links
        tp = links.tp
        size = source.shape[0]

        def slot(k, h=None):
            start, count = (3 - k // 2) * size, size
            if h is not None:
                count = size // 2
                start = start + h * count
            return blocks.at[1, pl.ds(start, count)]

        def to(bits, start, there):
            return links.remote(start, there, (links.peer(bits), tp), there)

        x, y, c = X_BIT, Y_BIT, CORE_BIT
        self.keep = links.inside(source, slot(0))
        self.to_x = to(x, source, slot(x))
        self.to_y = to(y, source, slot(y))
        self.x_on = to(y, slot(x, 0), slot(x + y, 0))
        self.y_on = to(x, slot(y, 1), slot(x + y, 1))
        self.along = []
        for step in range(1, QUARTERS):
            there = blocks.at[2 * step + 1]
            self.along.append(
                links.remote(blocks.at[1], there, (links.fs, links.along(step)), there)
            )
        self.core = [
            to(c, blocks.at[2 * s + 1], blocks.at[2 * s]) for s in range(QUARTERS)
        ]

    def first(self):
        self.to_x[0].start()
        self.to_y[0].start()
        self.keep.start()

    def second(self):
        self.to_x[1].wait_recv()
        self.x_on[0].start()
        self.to_y[1].wait_recv()
        self.y_on[0].start()

    def third(self):
        self.keep.wait()
        self.x_on[1].wait_recv()
        self.y_on[1].wait_recv()
        for out, back in self.along:
            out.start()
        self.core[0][0].start()

    def last(self):
        for s, (out, back) in enumerate(self.along):
            back.wait_recv()
            self.core[s + 1][0].start()
        for out, back in self.core:
            back.wait_recv()
        for out, back in (self.to_x, self.to_y, self.x_on, self.y_on, *self.along, *self.core):
            out.wait_send()


def grad_shapes(routed, shared, block):
    return (
        (E, 2 * routed, block),
        (2, E * shared, block),
        (E, routed, block),
        (E * shared, block),
    )


def grad_pieces(grads, results, index, source):
    up_all, shared_up_all, down_all, shared_down_all = results
    routed, shared = down_all.shape[1], shared_down_all.shape[0] // E
    units = pl.ds(pl.multiple_of(source * shared, 16), shared)
    places = [
        up_all.at[source],
        shared_up_all.at[0, units],
        shared_up_all.at[1, units],
        down_all.at[source],
        shared_down_all.at[units],
    ]
    placed, at = [], 0
    for place, size in zip(places, (2 * routed, shared, shared, routed, shared), strict=True):
        placed.append((grads.at[index, pl.ds(at, size)], place))
        at += size
    return placed


def grad_copies(links, grads, results, bits):
    peer = links.peer(bits)
    pairs = zip(
        grad_pieces(grads, results, peer, links.fs),
        grad_pieces(grads, results, peer, peer),
        strict=True,
    )
    return [
        links.remote(piece, place, (peer, links.tp), landing)
        for (piece, place), (_, landing) in pairs
    ]


def turn(values, cosine, sine_signed):
    parts = []
    for h in range(values.shape[1] // HD):
        v = values[:, h * HD : (h + 1) * HD]
        parts.append(v * cosine + pltpu.roll(v, HD // 2, 1) * sine_signed)
    return jnp.concatenate(parts, axis=1)


def as_column(row):
    size = row.shape[1]
    same = lax.broadcasted_iota(jnp.int32, (size, size), 0) == lax.broadcasted_iota(
        jnp.int32, (size, size), 1
    )
    spread = jnp.where(same, row.astype(jnp.float32), 0.0)
    return jnp.sum(spread, axis=1, keepdims=True).astype(jnp.int32)


def matmul(a, b):
    return jnp.dot(a, b, preferred_element_type=jnp.float32)


def matmul_nt(a, b):
    return lax.dot_general(a, b, (((1,), (1,)), ((), ())), preferred_element_type=jnp.float32)


def matmul_tn(a, b):
    return lax.dot_general(a, b, (((0,), (0,)), ((), ())), preferred_element_type=jnp.float32)


class RowGather:
    def __init__(self, links, source, slot, half):
        self.links = links

        def to(bits, owner, h=None):
            view = slot if h is None else lambda k: half(k, h)
            start = source if owner == 0 and source is not None else view(owner)
            return links.remote(
                start, view(owner ^ bits), (links.peer(bits), links.tp), view(owner ^ bits)
            )

        x, y, c = X_BIT, Y_BIT, CORE_BIT
        self.keep = None if source is None else links.inside(source, slot(0))
        self.own = [to(x, 0), to(y, 0), to(c, 0)]
        self.x_on = [to(y, x, 0), to(c, x)]
        self.y_on = [to(x, y, 1), to(c, y)]
        self.d_on = [to(c, x + y, 0), to(c, x + y, 1)]

    def first(self):
        for out, back in self.own:
            out.start()
        if self.keep is not None:
            self.keep.start()

    def second(self):
        self.own[0][1].wait_recv()
        for out, back in self.x_on:
            out.start()
        self.own[1][1].wait_recv()
        for out, back in self.y_on:
            out.start()

    def third(self):
        self.x_on[0][1].wait_recv()
        self.d_on[0][0].start()
        self.y_on[0][1].wait_recv()
        self.d_on[1][0].start()

    def last(self):
        if self.keep is not None:
            self.keep.wait()
        for out, back in (self.own[2], self.x_on[1], self.y_on[1], *self.d_on):
            back.wait_recv()

    def sent(self):
        for out, back in self.own + self.x_on + self.y_on + self.d_on:
            out.wait_send()


def layer_kernel(
    routed,
    tokens_hbm,
    cotangent_ref,
    qkv_ref,
    out_ref,
    gains_ref,
    router_ref,
    gate_ref,
    up_ref,
    shared_raw,
    down_ref,
    shared_down_ref,
    cos_ref,
    sin_ref,
    start_ref,
    routes_ref,
    output_ref,
    branch_ref,
    back_ref,
    small_grad_ref,
    grads_out,
    up_all,
    shared_up_all,
    down_all,
    shared_down_all,
    attended_out,
    query_out,
    hidden_out,
    slabs_all,
    cotangent_all,
    cotangent_plane,
    kv_out,
    qkv_out,
    out_out,
    small_out,
    shared_up_ref,
    small_full,
    branch_in,
    two_ref,
    small_ref,
    scales_ref,
    residual_ref,
    two_all,
    core_in,
    diag_in,
    side_in,
    rows_in,
    cols_in,
    send,
    recv,
    local,
    credit,
):
    links = Links(send, recv, local)
    fs, tp = links.fs, links.tp
    rows, width = tokens_hbm.shape
    block = width // E
    local_width = qkv_ref.shape[2]
    heads = local_width // HD
    seqs = rows // SEQ_DEV
    quarter = rows // QUARTERS
    out_width = output_ref.shape[1]
    back_width = width + SIDE
    whole = back_width + width
    slab_rows = slabs_all.shape[1]
    count = slab_rows // 3
    bf, f32 = jnp.bfloat16, jnp.float32

    def at_rows(index, size):
        return pl.ds(pl.multiple_of(index * size, size), size)

    small_ref[...] = jnp.concatenate(
        [
            gains_ref[...].astype(f32),
            router_ref[...].astype(f32),
            gate_ref[...].astype(f32),
            jnp.zeros((SMALL - 3 - E, block), f32),
        ],
        axis=0,
    ).astype(jnp.bfloat16)
    links.greet(range(1, 8), range(1, QUARTERS))
    cut = cotangent_all.shape[2]
    cot = CrossGather(
        links, cotangent_ref.at[at_rows(tp, quarter), pl.ds(0, cut)], cotangent_all
    )
    cot_plane = Gather(
        links,
        cotangent_ref.at[:, pl.ds(cut, width - cut)],
        lambda f: cotangent_plane.at[f],
        lambda f, h: cotangent_plane.at[f, pl.ds(h * SEQ_DEV, SEQ_DEV)],
    )
    shared = shared_down_ref.shape[0] // E

    def slab(peer, where):
        units = pl.ds(pl.multiple_of(peer * shared, 16), shared)
        pieces = [
            up_ref.at[peer],
            shared_up_ref.at[0, units],
            shared_up_ref.at[1, units],
            down_ref.at[peer],
            shared_down_ref.at[units],
        ]
        placed, at = [], 0
        for piece, size in zip(pieces, (2 * routed, shared, shared, routed, shared), strict=True):
            placed.append((piece, slabs_all.at[where, pl.ds(at, size)]))
            at += size
        return placed

    slab_copies = []
    for bits in (6, 7, 2, 3, 4, 5, 1):
        peer = links.peer(bits)
        for (piece, place), (_, landing) in zip(slab(peer, fs), slab(peer, peer), strict=True):
            slab_copies.append(links.remote(piece, place, (peer, tp), landing))
    slab_own = [links.inside(piece, place) for piece, place in slab(fs, fs)]
    def slot(s, k, h=None):
        start = (3 - k // 2) * quarter
        size = quarter
        if h is not None:
            size = quarter // 2
            start = start + h * size
        return two_all.at[2 * s + 1 - k % 2, pl.ds(start, size)]

    along = []
    for step in range(1, QUARTERS):
        along.append(
            links.remote(two_ref, slot(step, 0), (fs, links.along(step)), slot(step, 0))
        )
    gathers = []
    for s in range(QUARTERS):
        gathers.append(
            RowGather(
                links,
                two_ref if s == 0 else None,
                lambda k, s=s: slot(s, k),
                lambda k, h, s=s: slot(s, k, h),
            )
        )

    def attention(
        tokens_ref,
        hidden_buf,
        attended_ref,
        query_ref,
        qkv_full,
        out_full,
        kv_own,
        kv_full,
        branch_buf,
        raw,
        by_unit,
    ):
        load = links.inside(tokens_hbm, tokens_ref)
        load.start()
        raw_load = links.inside(shared_raw, raw)
        raw_load.start()
        small = Gather(
            links, small_ref, lambda f: small_full.at[f], lambda f, h: small_full.at[f, :, pl.ds(h * 128, 128)]
        )
        qkv = Gather(
            links,
            qkv_ref,
            lambda f: qkv_out.at[:, at_rows(f, block)],
            lambda f, h: qkv_out.at[:, pl.ds(pl.multiple_of(f * block + h * (block // 2), block // 2), block // 2)],
        )
        outs = Gather(
            links,
            out_ref,
            lambda f: out_out.at[f],
            lambda f, h: out_out.at[f, pl.ds(h * (local_width // 2), local_width // 2)],
        )
        small.first()
        cot.first()
        qkv.first()
        small.second()
        small.third()
        small.last()
        cot.second()
        load.wait()
        tokens = tokens_ref[...].astype(jnp.float32)
        rstd_one = lax.rsqrt(jnp.mean(tokens * tokens, axis=1, keepdims=True) + NORM_EPS)
        for b in range(E):
            cols = slice(b * block, (b + 1) * block)
            gain = small_full[b, 0:1, :].astype(jnp.float32)
            hidden_buf[:, cols] = (tokens[:, cols] * rstd_one * gain).astype(jnp.bfloat16)
        raw_load.wait()
        for k in range(2):
            by_unit[k] = raw[:, k, :].astype(f32).T.astype(bf)
        unit_keep = links.inside(by_unit, shared_up_ref)
        unit_keep.start()
        cot.third()
        qkv.second()
        qkv.third()
        outs.first()
        cot_plane.first()
        qkv.last()
        qkv_load = links.inside(qkv_out, qkv_full)
        qkv_load.start()
        qkv_load.wait()
        hidden = hidden_buf[...]
        cosine, sine = cos_ref[...], sin_ref[...]
        kv_own[:, :local_width] = turn(matmul(hidden, qkv_full[1]), cosine, sine).astype(jnp.bfloat16)
        kv_own[:, local_width:] = matmul(hidden, qkv_full[2]).astype(jnp.bfloat16)
        kv = Gather(
            links,
            kv_own,
            lambda f: kv_out.at[f],
            lambda f, h: kv_out.at[f, pl.ds(h * SEQ_DEV, SEQ_DEV)],
        )
        kv.first()
        query_ref[...] = turn(matmul(hidden, qkv_full[0]), cosine, sine).astype(jnp.bfloat16)
        outs.second()
        kv.second()
        outs.third()
        kv.third()
        cot_plane.second()
        unit_keep.wait()
        for out, back in slab_copies:
            out.start()
        for copy in slab_own:
            copy.start()
        kv.last()
        kv_load = links.inside(kv_out, kv_full)
        kv_load.start()
        kv_load.wait()
        length = E * SEQ_DEV
        key_pos = lax.broadcasted_iota(jnp.int32, (SEQ_DEV, length), 1)
        query_pos = fs * SEQ_DEV + lax.broadcasted_iota(jnp.int32, (SEQ_DEV, length), 0)
        for s in range(seqs):
            here = slice(s * SEQ_DEV, (s + 1) * SEQ_DEV)
            allowed = (key_pos <= query_pos) & (key_pos >= as_column(start_ref[s : s + 1, :]))
            for h in range(heads):
                cols = slice(h * HD, (h + 1) * HD)
                vcols = slice(local_width + h * HD, local_width + (h + 1) * HD)
                keys = kv_full[:, here, cols].reshape(length, HD)
                values = kv_full[:, here, vcols].reshape(length, HD)
                scores = matmul_nt(query_ref[here, cols], keys) * (HD ** (-0.5))
                scores = jnp.where(allowed, scores, NEG_FILL)
                top = jnp.max(scores, axis=1, keepdims=True)
                weights = jnp.exp(scores - top)
                weights = weights / jnp.sum(weights, axis=1, keepdims=True)
                attended_ref[here, cols] = matmul(weights.astype(jnp.bfloat16), values).astype(
                    jnp.bfloat16
                )
        outs.last()
        cot_plane.third()
        out_load = links.inside(out_out, out_full)
        out_load.start()
        small_keep = links.inside(small_full, small_out)
        small_keep.start()
        out_load.wait()
        attended = attended_ref[...]
        for b in range(E):
            branch_buf[:, b * block : (b + 1) * block] = matmul(attended, out_full[b]).astype(
                jnp.bfloat16
            )
        branch = []
        for step in range(1, QUARTERS):
            peer = links.along(step)
            branch.append(
                links.remote(
                    branch_buf.at[at_rows(peer, quarter)],
                    branch_in.at[step - 1],
                    (fs, peer),
                    branch_in.at[step - 1],
                )
            )
        for out, back in branch:
            out.start()
        for out, back in branch:
            back.wait_recv()
        mine = at_rows(tp, quarter)
        total = branch_buf[mine, :].astype(jnp.float32)
        for step in range(1, QUARTERS):
            total = total + branch_in[step - 1].astype(jnp.float32)
        residual = tokens_ref[mine, :].astype(jnp.float32) + total
        residual_ref[...] = residual
        rstd_two = lax.rsqrt(jnp.mean(residual * residual, axis=1, keepdims=True) + NORM_EPS)
        logits = jnp.zeros((quarter, SMALL), jnp.float32)
        for b in range(E):
            cols = slice(b * block, (b + 1) * block)
            gain = small_full[b, 1:2, :].astype(jnp.float32)
            part = (residual[:, cols] * rstd_two * gain).astype(jnp.bfloat16)
            two_ref[:, cols] = part
            logits = logits + matmul_nt(part, small_full[b])
        lane = lax.broadcasted_iota(jnp.int32, (quarter, SMALL), 1)
        real = (lane >= 2) & (lane < 2 + E)
        masked = jnp.where(real, logits, NEG_FILL)
        odds = jnp.exp(masked - jnp.max(masked, axis=1, keepdims=True))
        odds = jnp.where(real, odds, 0.0)
        probs = odds / jnp.sum(odds, axis=1, keepdims=True)
        expert = lax.broadcasted_iota(jnp.int32, (SMALL, rows), 0) - 2
        named = jnp.zeros((SMALL, rows), jnp.float32)
        for k in range(routes_ref.shape[0]):
            named = named + (routes_ref[k : k + 1, :] == expert).astype(jnp.float32)
        pick = lax.broadcasted_iota(jnp.int32, (quarter, rows), 1) == (
            tp * quarter + lax.broadcasted_iota(jnp.int32, (quarter, rows), 0)
        )
        chosen = matmul_nt(pick.astype(jnp.bfloat16), named.astype(jnp.bfloat16))
        gate_value = 1.0 / (1.0 + jnp.exp(-logits))
        scales = jnp.where(lane == 2 + E, gate_value, probs * chosen)
        scales_ref[...] = jnp.concatenate([scales, probs, chosen], axis=1)
        high = scales.astype(jnp.bfloat16)
        low = (scales - high.astype(jnp.float32)).astype(jnp.bfloat16)
        two_ref[:, width:] = jnp.concatenate(
            [high, low, jnp.zeros((quarter, SIDE - 2 * SMALL), jnp.bfloat16)], axis=1
        )
        keeps = [
            links.inside(attended_ref, attended_out),
            links.inside(query_ref, query_out),
            links.inside(hidden_buf, hidden_out),
            small_keep,
        ]
        for keep in keeps[:3]:
            keep.start()
        for out, back in along:
            out.start()
        for out, back in branch:
            out.wait_send()
        for keep in keeps:
            keep.wait()

    pl.run_scoped(
        attention,
        pltpu.VMEM((rows, width), bf),
        pltpu.VMEM((rows, width), bf),
        pltpu.VMEM((rows, local_width), bf),
        pltpu.VMEM((rows, local_width), bf),
        pltpu.VMEM((3, width, local_width), bf),
        pltpu.VMEM((E, local_width, block), bf),
        pltpu.VMEM((rows, 2 * local_width), bf),
        pltpu.VMEM((E, rows, 2 * local_width), bf),
        pltpu.VMEM((rows, width), bf),
        pltpu.VMEM(shared_raw.shape, bf),
        pltpu.VMEM(shared_up_ref.shape, bf),
    )

    def experts(weights, cot_all, units, first, parts, own_rows, own_cols, staged, cot_rows):
        loads = [
            links.inside(slabs_all.at[g], weights.at[:, pl.ds(g * block, block)]) for g in range(E)
        ]
        loads.append(links.inside(cotangent_all, cot_all.at[:, :, pl.ds(0, cut)]))
        for s in range(QUARTERS):
            q = links.along(QUARTERS - s)
            for k in range(E):
                there = cot_all.at[
                    2 * s + 1 - k % 2, pl.ds((3 - k // 2) * quarter, quarter), pl.ds(cut, width - cut)
                ]
                loads.append(
                    links.inside(cotangent_plane.at[links.peer(k), at_rows(q, quarter)], there)
                )
        along[0][1].wait_recv()
        gathers[1].first()
        along[1][1].wait_recv()
        gathers[2].first()
        gathers[1].second()
        along[2][1].wait_recv()
        gathers[3].first()
        gathers[0].first()
        cot.last()
        cot_plane.last()
        for out, back in slab_copies:
            back.wait_recv()
        for copy in slab_own:
            copy.wait()
        for load in loads:
            load.start()

        cot_load = links.inside(cotangent_ref.at[at_rows(tp, quarter)], cot_rows)
        cot_load.start()
        core = [
            links.remote(
                parts.at[s % 2], core_in.at[s % 2], (links.peer(CORE_BIT), tp), core_in.at[s % 2]
            )
            for s in range(QUARTERS)
        ]
        diag, side, rows_along, cols_along = [], [], [], []
        for s in range(QUARTERS):
            held = parts.at[2 + s % 3]
            diag.append(
                [
                    links.remote(
                        held.at[pl.ds(h * (quarter // 2), quarter // 2)],
                        diag_in.at[s, h],
                        (links.peer(bits), tp),
                        diag_in.at[s, h],
                    )
                    for h, bits in enumerate((Y_BIT, X_BIT))
                ]
            )
            side.append(
                [
                    links.remote(
                        held.at[pl.ds((3 - bits // 2) * quarter, quarter)],
                        side_in.at[s, i],
                        (links.peer(bits), tp),
                        side_in.at[s, i],
                    )
                    for i, bits in enumerate((X_BIT, Y_BIT))
                ]
            )
            last = pl.ds(3 * quarter, quarter)
            if s < QUARTERS - 1:
                rows_along.append(
                    links.remote(
                        held.at[last, pl.ds(0, back_width)],
                        rows_in.at[s],
                        (fs, links.along(QUARTERS - 1 - s)),
                        rows_in.at[s],
                    )
                )
            q = links.along(2 * QUARTERS - 1 - s)
            for step in range(1, QUARTERS):
                peer = links.along(step)
                start = pl.multiple_of(back_width + peer * out_width, 128)
                q_there = links.along(2 * QUARTERS - 1 - s - step)
                cols_along.append(
                    links.remote(
                        held.at[last, pl.ds(start, out_width)],
                        cols_in.at[step - 1, at_rows(q, quarter)],
                        (fs, peer),
                        cols_in.at[step - 1, at_rows(q_there, quarter)],
                    )
                )

        sub = lax.broadcasted_iota(jnp.int32, (8, SIDE), 0)
        lane = lax.broadcasted_iota(jnp.int32, (8, SIDE), 1)
        mine, common = 2 + fs, 2 + E
        pick_in = (
            ((sub == 0) & ((lane == mine) | (lane == mine + SMALL)))
            | ((sub == 1) & ((lane == common) | (lane == common + SMALL)))
        ).astype(jnp.bfloat16)
        pick_out = (((sub == 0) & (lane == mine)) | ((sub == 1) & (lane == common))).astype(
            jnp.bfloat16
        )

        def one_block(t, index, slot_out, pause):
            first[: 2 * count] = matmul_nt(weights[: 2 * count], two_all[index, :, :width])
            pause(0)
            first[2 * count :] = matmul_nt(weights[2 * count :], cot_all[index])
            scale = matmul_nt(pick_in, two_all[index, :, width:])
            cols = pl.ds(pl.multiple_of(index * rows, rows), rows)
            dots = []
            shared = count - routed
            groups = ((0, 2 * count, routed), (2 * routed, 2 * count + routed, shared))
            for group, (low, last, size) in enumerate(groups):
                gate = first[low : low + size]
                up = first[low + size : low + 2 * size]
                grad = first[last : last + size]
                by = scale[group : group + 1]
                sigmoid = 1.0 / (1.0 + jnp.exp(-gate))
                silu = gate * sigmoid
                active = silu * up
                units[last : last + size, cols] = (by * active).astype(jnp.bfloat16)
                dots.append(jnp.sum(active * grad, axis=0, keepdims=True))
                active_grad = by * grad
                units[low : low + size, cols] = (
                    active_grad * up * sigmoid * (1.0 + gate * (1.0 - sigmoid))
                ).astype(jnp.bfloat16)
                units[low + size : low + 2 * size, cols] = (active_grad * silu).astype(jnp.bfloat16)
            both = jnp.concatenate([*dots, jnp.zeros((6, rows), jnp.float32)], axis=0)
            pause(1)
            tile = 512

            def put(at, value, other):
                if other is not None:
                    value = value + other[:, at].astype(jnp.float32)
                parts[slot_out, :, at] = value.astype(jnp.bfloat16)

            def products(other):
                put(
                    slice(width, back_width), matmul_tn(both.astype(jnp.bfloat16), pick_out), other
                )
                for n in range(width // tile):
                    at = slice(n * tile, (n + 1) * tile)
                    put(at, matmul_tn(units[: 2 * count, cols], weights[: 2 * count, at]), other)
                    beyond = slice(back_width + n * tile, back_width + (n + 1) * tile)
                    put(beyond, matmul_tn(units[2 * count :, cols], weights[2 * count :, at]), other)

            @pl.when(t % 2 == 0)
            def _():
                products(None)

            @pl.when(t % 2 == 1)
            def _():
                products(core_in.at[(t // 2) % 2])

            pause(3)

        def add_in(held, start, size, others):
            chunk = 32

            @pl.loop(0, size // chunk)
            def _(r):
                at = pl.ds(pl.multiple_of(start + r * chunk, chunk), chunk)
                there = pl.ds(pl.multiple_of(r * chunk, chunk), chunk)
                total = parts[held, at, :].astype(jnp.float32)
                for ref in others:
                    total = total + ref[there, :].astype(jnp.float32)
                parts[held, at, :] = total.astype(jnp.bfloat16)

        def to_core(s):
            if s >= 2:
                pl.semaphore_wait(credit, 1)
            core[s][0].start()

        def diagonal(s):
            if s < 2:
                pl.semaphore_signal(
                    credit, inc=1, device_id=(links.peer(CORE_BIT), tp), device_id_type=MESH
                )
            for out, back in diag[s]:
                out.start()

        def sideways(s):
            for h, (out, back) in enumerate(diag[s]):
                back.wait_recv()
                start = (2 - h) * quarter + h * (quarter // 2)
                add_in(2 + s % 3, start, quarter // 2, [diag_in.at[s, h]])
                side[s][h][0].start()

        def finish(s):
            held = 2 + s % 3
            for out, back in side[s]:
                back.wait_recv()
            last = slice(3 * quarter, rows)
            add_in(held, 3 * quarter, quarter, [side_in.at[s, 0], side_in.at[s, 1]])
            if s == QUARTERS - 1:
                own_rows[...] = parts[held, last, :back_width].astype(jnp.float32)
                parts[held, last, back_width:] = (
                    parts[held, last, back_width:].astype(jnp.float32) + residual_ref[...]
                ).astype(jnp.bfloat16)
            else:
                rows_along[s][0].start()
            for out, back in cols_along[3 * s : 3 * s + 3]:
                out.start()
            start = pl.multiple_of(back_width + tp * out_width, 128)
            own_cols[at_rows(links.along(2 * QUARTERS - 1 - s), quarter), :] = parts[
                held, last, pl.ds(start, out_width)
            ].astype(jnp.float32)

        def before_last():
            core[1][0].wait_send()

        def slot_free():
            for out, back in diag[0] + side[0] + cols_along[:3] + rows_along[:1]:
                out.wait_send()

        plan = {
            (0, 0): [gathers[2].third, gathers[3].second],
            (0, 1): [gathers[0].second, gathers[3].third],
            (0, 3): [lambda: to_core(0), gathers[2].last],
            (1, 0): [gathers[0].third],
            (1, 1): [core[0][1].wait_recv],
            (1, 3): [lambda: diagonal(0), gathers[3].last],
            (2, 1): [lambda: sideways(0)],
            (2, 3): [lambda: to_core(1)],
            (3, 1): [core[1][1].wait_recv],
            (3, 3): [lambda: diagonal(1)],
            (4, 1): [lambda: sideways(1)],
            (4, 3): [lambda: to_core(2)],
            (5, 0): [lambda: finish(0)],
            (5, 1): [core[2][1].wait_recv],
            (5, 3): [lambda: diagonal(2), gathers[0].last],
            (6, 1): [lambda: sideways(2)],
            (6, 3): [lambda: to_core(3)],
            (7, 0): [lambda: finish(1)],
            (7, 1): [core[3][1].wait_recv],
            (7, 3): [lambda: diagonal(3)],
        }
        before = {4: [core[0][0].wait_send], 6: [before_last], 7: [slot_free]}

        gathers[1].third()
        gathers[2].second()
        for load in loads:
            load.wait()
        gathers[1].last()

        @pl.loop(0, 8)
        def _(t):
            s = t // 2
            slot_out = (1 - t % 2) * (s % 2) + (t % 2) * (2 + s % 3)
            for at, steps in before.items():

                @pl.when(t == at)
                def _(steps=steps):
                    for step in steps:
                        step()

            def pause(point):
                for (at, where), steps in plan.items():
                    if where == point:

                        @pl.when(t == at)
                        def _(steps=steps):
                            for step in steps:
                                step()

            one_block(t, 2 * ((s + 1) % QUARTERS) + t % 2, slot_out, pause)

        keeps = []

        pending = [None, None]

        def settle(place):
            if pending[place] is not None:
                pending[place].wait()
            pending[place] = None

        def weight_grads(bits):
            g = links.peer(bits)
            at = pl.ds(pl.multiple_of(g * block, block), block)
            place = len(keeps) % 2
            settle(place)
            hidden_cols = two_all[:, :, at].reshape(E * rows, block)
            staged[place, : 2 * count] = matmul(units[: 2 * count], hidden_cols).astype(
                jnp.bfloat16
            )
            cot_cols = cot_all[:, :, at].reshape(E * rows, block)
            staged[place, 2 * count :] = matmul(units[2 * count :], cot_cols).astype(jnp.bfloat16)
            keep = links.inside(staged.at[place], grads_out.at[g])
            keep.start()
            keeps.append(keep)
            pending[place] = keep

        results = (up_all, shared_up_all, down_all, shared_down_all)
        early = [copy for bits in EARLY for copy in grad_copies(links, grads_out, results, bits)]
        finish(2)
        for bits in EARLY:
            weight_grads(bits)
        sideways(3)
        settle(0)
        settle(1)
        for out, back in early:
            out.start()
        for bits in (6, 7, 3, 5, 1, 0):
            weight_grads(bits)
        finish(3)
        for out, back in rows_along:
            back.wait_recv()
        total = own_rows[...]
        for step in range(1, QUARTERS):
            total = total + rows_in[step - 1].astype(jnp.float32)
        dots = total[:, width : width + SMALL]
        scales = scales_ref[:, :SMALL]
        probs = scales_ref[:, SMALL : 2 * SMALL]
        chosen = scales_ref[:, 2 * SMALL :]
        chosen_grad = chosen * dots
        logit_grad = probs * (chosen_grad - jnp.sum(probs * chosen_grad, axis=1, keepdims=True))
        gate_lane = lax.broadcasted_iota(jnp.int32, (quarter, SMALL), 1) == 2 + E
        logit_grad = jnp.where(gate_lane, dots * scales * (1.0 - scales), logit_grad).astype(
            jnp.bfloat16
        )
        residual = residual_ref[...]
        rstd = lax.rsqrt(jnp.mean(residual * residual, axis=1, keepdims=True) + NORM_EPS)
        mean = jnp.zeros((quarter, 1), jnp.float32)
        for b in range(E):
            at = slice(b * block, (b + 1) * block)
            two_grad = total[:, at] + matmul(logit_grad, small_full[b])
            normed = residual[:, at] * rstd
            gain = small_full[b, 1:2, :].astype(jnp.float32)
            back_ref[:, at] = two_grad
            mean = mean + jnp.sum(two_grad * gain * normed, axis=1, keepdims=True)
            grads = matmul_tn(logit_grad, two_all[1, 3 * quarter :, at])
            line = lax.broadcasted_iota(jnp.int32, (SMALL, block), 0)
            gain_grad = jnp.sum(two_grad * normed, axis=0, keepdims=True)
            small_grad_ref[:, at] = jnp.where(line == 1, gain_grad, grads)
        mean = mean / width
        cot_load.wait()
        for b in range(E):
            at = slice(b * block, (b + 1) * block)
            gain = small_full[b, 1:2, :].astype(jnp.float32)
            normed = residual[:, at] * rstd
            grad = cot_rows[:, at].astype(jnp.float32) + rstd * (
                back_ref[:, at] * gain - normed * mean
            )
            back_ref[:, at] = grad
            branch_ref[:, at] = grad.astype(jnp.bfloat16)
        for out, back in cols_along:
            back.wait_recv()
        total = own_cols[...]
        for step in range(1, QUARTERS):
            total = total + cols_in[step - 1].astype(jnp.float32)
        output_ref[...] = total.astype(jnp.bfloat16)
        for out, back in core[2:] + rows_along[1:] + cols_along[3:]:
            out.wait_send()
        for s in range(1, QUARTERS):
            for out, back in diag[s] + side[s]:
                out.wait_send()
        for gather in gathers:
            gather.sent()
        for out, back in slab_copies + along:
            out.wait_send()
        settle(0)
        settle(1)
        for out, back in early:
            back.wait_recv()
            out.wait_send()

    pl.run_scoped(
        experts,
        pltpu.VMEM((slab_rows, width), bf),
        pltpu.VMEM((E, rows, width), bf),
        pltpu.VMEM((slab_rows, E * rows), bf),
        pltpu.VMEM((slab_rows, rows), f32),
        pltpu.VMEM((5, rows, whole), bf),
        pltpu.VMEM((quarter, back_width), f32),
        pltpu.VMEM((rows, out_width), f32),
        pltpu.VMEM((2, slab_rows, block), bf),
        pltpu.VMEM((quarter, width), bf),
    )


def layer_call(
    tokens,
    cotangent,
    qkv_weight,
    out_weight,
    norm_gains,
    router_weight,
    shared_gate,
    up,
    shared_up,
    down,
    shared_down,
    cosine,
    sine,
    start,
    routes,
):
    rows, width = tokens.shape
    block = width // E
    local_width = qkv_weight.shape[2]
    quarter = rows // QUARTERS
    out_width = width // QUARTERS
    back_width = width + SIDE
    whole = back_width + width
    routed = down.shape[1]
    slabs = (E, 3 * (routed + shared_down.shape[0] // E), block)
    bf, f32 = jnp.bfloat16, jnp.float32
    sds = jax.ShapeDtypeStruct
    vmem = pl.BlockSpec(memory_space=pltpu.VMEM)
    hbm = pl.BlockSpec(memory_space=pl.ANY)
    outs = [
        (sds((rows, out_width), bf), vmem),
        (sds((quarter, width), bf), vmem),
        (sds((quarter, width), f32), vmem),
        (sds((SMALL, width), f32), vmem),
        (sds(slabs, bf), hbm),
        *((sds(shape, bf), hbm) for shape in grad_shapes(routed, shared_down.shape[0] // E, block)),
        (sds((rows, local_width), bf), hbm),
        (sds((rows, local_width), bf), hbm),
        (sds((rows, width), bf), hbm),
        (sds(slabs, bf), hbm),
        (sds((E, rows, CUT), bf), hbm),
        (sds((E, rows, width - CUT), bf), hbm),
        (sds((E, rows, 2 * local_width), bf), hbm),
        (sds((3, width, local_width), bf), hbm),
        (sds((E, local_width, block), bf), hbm),
        (sds((E, SMALL, block), bf), hbm),
        (sds((2, shared_down.shape[0], block), bf), hbm),
    ]
    return pl.pallas_call(
        functools.partial(layer_kernel, routed),
        name="layer",
        out_shape=[o[0] for o in outs],
        in_specs=[hbm] * 4 + [vmem] * 3 + [hbm] * 4 + [vmem] * 4,
        out_specs=[o[1] for o in outs],
        scratch_shapes=[
            pltpu.VMEM((E, SMALL, block), bf),
            pltpu.VMEM((QUARTERS - 1, quarter, width), bf),
            pltpu.VMEM((quarter, back_width), bf),
            pltpu.VMEM((SMALL, block), bf),
            pltpu.VMEM((quarter, 3 * SMALL), f32),
            pltpu.VMEM((quarter, width), f32),
            pltpu.VMEM((E, rows, back_width), bf),
            pltpu.VMEM((2, rows, whole), bf),
            pltpu.VMEM((QUARTERS, 2, quarter // 2, whole), bf),
            pltpu.VMEM((QUARTERS, 2, quarter, whole), bf),
            pltpu.VMEM((QUARTERS - 1, quarter, back_width), bf),
            pltpu.VMEM((QUARTERS - 1, rows, out_width), bf),
            pltpu.SemaphoreType.DMA((192,)),
            pltpu.SemaphoreType.DMA((192,)),
            pltpu.SemaphoreType.DMA((96,)),
            pltpu.SemaphoreType.REGULAR,
        ],
        compiler_params=pltpu.CompilerParams(
            collective_id=1, has_side_effects=True, vmem_limit_bytes=63 * 2**20
        ),
    )(
        tokens,
        cotangent,
        qkv_weight,
        out_weight,
        norm_gains,
        router_weight,
        shared_gate,
        up,
        shared_up,
        down,
        shared_down,
        cosine,
        sine,
        start,
        routes,
    )


LATE = 20


class Scatter:
    def __init__(self, links, parts, core_in, diag_in, side_in):
        self.links, self.parts = links, parts
        self.core_in, self.diag_in, self.side_in = core_in, diag_in, side_in
        self.rows = parts.shape[1]
        p, tp = links.peer, links.tp
        half = self.rows // 2
        self.core = [
            links.remote(
                parts.at[p(bits + CORE_BIT)], core_in.at[i], (p(CORE_BIT), tp), core_in.at[i]
            )
            for i, bits in enumerate((6, 2, 4, 0))
        ]
        self.diag = [
            links.remote(
                parts.at[p(6), pl.ds(h * half, half)], diag_in.at[h], (p(bits), tp), diag_in.at[h]
            )
            for h, bits in enumerate((Y_BIT, X_BIT))
        ]
        self.side = [
            links.remote(parts.at[p(bits)], side_in.at[i], (p(bits), tp), side_in.at[i])
            for i, bits in enumerate((X_BIT, Y_BIT))
        ]

    def add(self, index, first, count, refs, target=None):
        chunk = 32

        @pl.loop(0, count // chunk)
        def _(r):
            here = pl.ds(pl.multiple_of(first + r * chunk, chunk), chunk)
            there = pl.ds(pl.multiple_of(r * chunk, chunk), chunk)
            total = self.parts[index, here, :].astype(jnp.float32)
            for ref in refs:
                total = total + ref[there, :].astype(jnp.float32)
            if target is None:
                self.parts[index, here, :] = total.astype(jnp.bfloat16)
            else:
                target[here, :] = total

    def to_core(self):
        for out, back in self.core:
            out.start()

    def diagonal(self):
        self.core[0][1].wait_recv()
        self.add(self.links.peer(6), 0, self.rows, [self.core_in.at[0]])
        for out, back in self.diag:
            out.start()

    def sideways(self, i):
        index = self.links.peer((X_BIT, Y_BIT)[i])
        self.core[1 + i][1].wait_recv()
        self.add(index, 0, self.rows, [self.core_in.at[1 + i]])
        self.diag[i][1].wait_recv()
        self.add(index, i * (self.rows // 2), self.rows // 2, [self.diag_in.at[i]])
        self.side[i][0].start()

    def finish(self, target):
        self.core[3][1].wait_recv()
        for out, back in self.side:
            back.wait_recv()
        self.add(
            self.links.fs,
            0,
            self.rows,
            [self.core_in.at[3], self.side_in.at[0], self.side_in.at[1]],
            target,
        )

    def sent(self):
        for out, back in self.core + self.diag + self.side:
            out.wait_send()


def backward_kernel(
    branch_ref,
    residual_ref,
    small_grad_ref,
    attended_ref,
    query_ref,
    hidden_ref,
    tokens_ref,
    kv_ref,
    qkv_ref,
    out_ref,
    small_ref,
    cos_ref,
    sin_ref,
    start_ref,
    slabs_ref,
    up_in,
    shared_up_in,
    down_in,
    shared_down_in,
    input_grad_ref,
    qkv_own,
    out_own,
    small_own,
    up_all,
    shared_up_all,
    down_all,
    shared_down_all,
    kv_full,
    qkv_full,
    out_full,
    branch_all,
    odds,
    query_grad,
    projected,
    kv_total,
    kv_parts,
    kv_core,
    kv_diag,
    kv_side,
    query_parts,
    query_core,
    query_diag,
    query_side,
    rest_parts,
    rest_core,
    rest_diag,
    rest_side,
    out_parts,
    out_core,
    out_diag,
    out_side,
    one_parts,
    one_in,
    grad_rows,
    small_parts,
    small_in,
    small_column,
    send,
    recv,
    local,
):
    links = Links(send, recv, local)
    fs, tp = links.fs, links.tp
    quarter, width = residual_ref.shape
    rows = quarter * QUARTERS
    block = width // E
    local_width = query_ref.shape[1]
    heads = local_width // HD
    seqs = rows // SEQ_DEV
    length = E * SEQ_DEV
    scale = HD ** (-0.5)

    def at_rows(index, size):
        return pl.ds(pl.multiple_of(index * size, size), size)

    own = at_rows(tp, quarter)
    links.greet(range(1, 8), range(1, QUARTERS))
    branch = []
    for step in range(1, QUARTERS):
        here = branch_all.at[own]
        landing = branch_all.at[at_rows(links.along(QUARTERS - step), quarter)]
        branch.append(links.remote(branch_ref, here, (fs, links.along(step)), landing))
    for out, back in branch:
        out.start()
    branch_all[own, :] = branch_ref[...]
    results = (up_all, shared_up_all, down_all, shared_down_all)
    slab_copies = []
    for bits in (1, 6, 3, 5, 7):
        slab_copies += grad_copies(links, slabs_ref, results, bits)
    for out, back in slab_copies[:LATE]:
        out.start()
    slab_own = [links.inside(*pair) for pair in grad_pieces(slabs_ref, results, fs, fs)]
    for copy in slab_own:
        copy.start()
    kv_load = links.inside(kv_ref, kv_full)
    kv_load.start()
    out_load = links.inside(out_ref, out_full)
    out_load.start()
    qkv_load = links.inside(qkv_ref, qkv_full)
    qkv_load.start()
    kv_sum = Scatter(links, kv_parts, kv_core, kv_diag, kv_side)
    query_sum = Scatter(links, query_parts, query_core, query_diag, query_side)
    rest_sum = Scatter(links, rest_parts, rest_core, rest_diag, rest_side)
    out_sum = Scatter(links, out_parts, out_core, out_diag, out_side)

    kv_load.wait()
    key_pos = lax.broadcasted_iota(jnp.int32, (SEQ_DEV, length), 1)
    query_pos = fs * SEQ_DEV + lax.broadcasted_iota(jnp.int32, (SEQ_DEV, length), 0)
    for s in range(seqs):
        here = slice(s * SEQ_DEV, (s + 1) * SEQ_DEV)
        allowed = (key_pos <= query_pos) & (key_pos >= as_column(start_ref[s : s + 1, :]))
        for h in range(heads):
            cols = slice(h * HD, (h + 1) * HD)
            keys = kv_full[:, here, cols].reshape(length, HD)
            scores = matmul_nt(query_ref[here, cols], keys) * scale
            scores = jnp.where(allowed, scores, NEG_FILL)
            top = jnp.max(scores, axis=1, keepdims=True)
            weights = jnp.exp(scores - top)
            odds[s * heads + h] = weights / jnp.sum(weights, axis=1, keepdims=True)
    out_load.wait()
    for out, back in branch:
        back.wait_recv()
    attended_grad = jnp.zeros((rows, local_width), jnp.float32)
    for b in range(E):
        attended_grad = attended_grad + matmul_nt(
            branch_all[:, b * block : (b + 1) * block], out_full[b]
        )
    query_grad[...] = attended_grad.astype(jnp.bfloat16)
    for s in range(seqs):
        here = slice(s * SEQ_DEV, (s + 1) * SEQ_DEV)
        for h in range(heads):
            cols = slice(h * HD, (h + 1) * HD)
            vcols = slice(local_width + h * HD, local_width + (h + 1) * HD)
            keys = kv_full[:, here, cols].reshape(length, HD)
            values = kv_full[:, here, vcols].reshape(length, HD)
            grad = query_grad[here, cols]
            probs = odds[s * heads + h]
            weights_grad = matmul_nt(grad, values)
            delta = jnp.sum(probs * weights_grad, axis=1, keepdims=True)
            score_grad = (probs * (weights_grad - delta)).astype(jnp.bfloat16)
            key_grad = matmul_tn(score_grad, query_ref[here, cols]) * scale
            value_grad = matmul_tn(probs.astype(jnp.bfloat16), grad)
            kv_parts[:, here, cols] = key_grad.astype(jnp.bfloat16).reshape(E, SEQ_DEV, HD)
            kv_parts[:, here, vcols] = value_grad.astype(jnp.bfloat16).reshape(E, SEQ_DEV, HD)
            projected[0, here, cols] = turn(
                matmul(score_grad, keys) * scale, cos_ref[here, :], -sin_ref[here, :]
            ).astype(jnp.bfloat16)
    kv_sum.to_core()
    attended = attended_ref[...]
    for b in range(E):
        cols = slice(b * block, (b + 1) * block)
        out_parts[b] = matmul_tn(attended, branch_all[:, cols]).astype(jnp.bfloat16)
    def weight_grad(j):
        for b in range(E):
            cols = slice(b * block, (b + 1) * block)
            part = matmul_tn(hidden_ref[:, cols], projected[j]).astype(jnp.bfloat16)
            if j == 0:
                query_parts[b] = part
            else:
                rest_parts[b, (j - 1) * block : j * block] = part

    kv_sum.diagonal()
    out_sum.to_core()
    weight_grad(0)
    query_sum.to_core()
    kv_sum.sideways(0)
    kv_sum.sideways(1)
    out_sum.diagonal()
    query_sum.diagonal()
    qkv_load.wait()
    kv_sum.finish(kv_total)
    for out, back in slab_copies[LATE:]:
        out.start()
    projected[1] = turn(kv_total[:, :local_width], cos_ref[...], -sin_ref[...]).astype(jnp.bfloat16)
    projected[2] = kv_total[:, local_width:].astype(jnp.bfloat16)
    for b in range(E):
        cols = slice(b * block, (b + 1) * block)
        part = jnp.zeros((rows, block), jnp.float32)
        for j in range(3):
            part = part + matmul_nt(projected[j], qkv_full[j, cols])
        one_parts[:, cols] = part.astype(jnp.bfloat16)
    column = []
    for step in range(1, QUARTERS):
        peer = links.along(step)
        column.append(
            links.remote(
                one_parts.at[at_rows(peer, quarter)],
                one_in.at[step - 1],
                (fs, peer),
                one_in.at[step - 1],
            )
        )
    for out, back in column:
        out.start()
    weight_grad(1)
    weight_grad(2)
    rest_sum.to_core()
    out_sum.sideways(0)
    out_sum.sideways(1)
    query_sum.sideways(0)
    query_sum.sideways(1)
    rest_sum.diagonal()
    for out, back in column:
        back.wait_recv()
    tokens = tokens_ref[own, :].astype(jnp.float32)
    rstd = lax.rsqrt(jnp.mean(tokens * tokens, axis=1, keepdims=True) + NORM_EPS)
    total = one_parts[own, :].astype(jnp.float32)
    for step in range(1, QUARTERS):
        total = total + one_in[step - 1].astype(jnp.float32)
    mean = jnp.zeros((quarter, 1), jnp.float32)
    sub = lax.broadcasted_iota(jnp.int32, (SMALL, block), 0)
    for b in range(E):
        at = slice(b * block, (b + 1) * block)
        gain = small_ref[b, 0:1, :].astype(jnp.float32)
        normed = tokens[:, at] * rstd
        mean = mean + jnp.sum(total[:, at] * gain * normed, axis=1, keepdims=True)
        gain_grad = jnp.sum(total[:, at] * normed, axis=0, keepdims=True)
        small_parts[b] = jnp.where(sub == 0, gain_grad, small_grad_ref[:, at])
    mean = mean / width
    for b in range(E):
        at = slice(b * block, (b + 1) * block)
        gain = small_ref[b, 0:1, :].astype(jnp.float32)
        normed = tokens[:, at] * rstd
        grad_rows[:, at] = (
            residual_ref[:, at] + rstd * (total[:, at] * gain - normed * mean)
        ).astype(jnp.bfloat16)
    spread = []
    for step in range(1, QUARTERS):
        peer = links.along(step)
        landing = input_grad_ref.at[at_rows(links.along(QUARTERS - step), quarter)]
        spread.append(links.remote(grad_rows, input_grad_ref.at[own], (fs, peer), landing))
    for out, back in spread:
        out.start()
    keep = links.inside(grad_rows, input_grad_ref.at[own])
    keep.start()
    small_copies = []
    for bits in range(1, E):
        peer = links.peer(bits)
        small_copies.append(
            links.remote(
                small_parts.at[peer], small_in.at[bits - 1], (peer, tp), small_in.at[bits - 1]
            )
        )
    for out, back in small_copies:
        out.start()
    rest_sum.sideways(0)
    rest_sum.sideways(1)
    out_sum.finish(out_own)
    query_sum.finish(qkv_own.at[pl.ds(0, block)])
    for out, back in small_copies:
        back.wait_recv()
    small_total = small_parts[fs]
    for bits in range(1, E):
        small_total = small_total + small_in[bits - 1]
    small_column[tp] = small_total
    small_spread = []
    for step in range(1, QUARTERS):
        here = small_column.at[tp]
        landing = small_column.at[links.along(QUARTERS - step)]
        small_spread.append(links.remote(here, here, (fs, links.along(step)), landing))
    for out, back in small_spread:
        out.start()
    rest_sum.finish(qkv_own.at[pl.ds(block, 2 * block)])
    for out, back in small_spread:
        back.wait_recv()
    small_own[...] = small_column[0] + small_column[1] + small_column[2] + small_column[3]
    for out, back in spread + slab_copies:
        back.wait_recv()
    for copy in (*slab_own, keep):
        copy.wait()
    for out, back in branch + slab_copies + column + spread + small_copies + small_spread:
        out.wait_send()
    for scatter in (kv_sum, out_sum, query_sum, rest_sum):
        scatter.sent()


def backward_call(
    branch_rows,
    residual_grad,
    small_grad,
    attended,
    query_rows,
    hidden_one,
    tokens,
    kv_all,
    qkv_full,
    out_full,
    small_full,
    cosine,
    sine,
    start,
    slabs,
    *parts,
):
    quarter, width = residual_grad.shape
    rows = quarter * QUARTERS
    block = width // E
    local_width = query_rows.shape[1]
    bf, f32 = jnp.bfloat16, jnp.float32
    sds = jax.ShapeDtypeStruct
    vmem = pl.BlockSpec(memory_space=pltpu.VMEM)
    hbm = pl.BlockSpec(memory_space=pl.ANY)
    outs = [
        (sds((rows, width), bf), hbm),
        (sds((3 * block, local_width), f32), vmem),
        (sds((local_width, block), f32), vmem),
        (sds((SMALL, block), f32), vmem),
        *((sds(part.shape, bf), hbm) for part in parts),
    ]

    def scatter_scratch(count, columns):
        return [
            pltpu.VMEM((E, count, columns), bf),
            pltpu.VMEM((4, count, columns), bf),
            pltpu.VMEM((2, count // 2, columns), bf),
            pltpu.VMEM((2, count, columns), bf),
        ]

    return pl.pallas_call(
        backward_kernel,
        name="attention_backward",
        out_shape=[o[0] for o in outs],
        in_specs=[vmem] * 7 + [hbm] * 3 + [vmem] * 4 + [hbm] * 5,
        out_specs=[o[1] for o in outs],
        input_output_aliases={15 + i: 4 + i for i in range(4)},
        scratch_shapes=[
            pltpu.VMEM((E, rows, 2 * local_width), bf),
            pltpu.VMEM((3, width, local_width), bf),
            pltpu.VMEM((E, local_width, block), bf),
            pltpu.VMEM((rows, width), bf),
            pltpu.VMEM((rows // SEQ_DEV * local_width // HD, SEQ_DEV, E * SEQ_DEV), f32),
            pltpu.VMEM((rows, local_width), bf),
            pltpu.VMEM((3, rows, local_width), bf),
            pltpu.VMEM((rows, 2 * local_width), f32),
            *scatter_scratch(rows, 2 * local_width),
            *scatter_scratch(block, local_width),
            *scatter_scratch(2 * block, local_width),
            *scatter_scratch(local_width, block),
            pltpu.VMEM((rows, width), bf),
            pltpu.VMEM((QUARTERS - 1, quarter, width), bf),
            pltpu.VMEM((quarter, width), bf),
            pltpu.VMEM((E, SMALL, block), f32),
            pltpu.VMEM((E - 1, SMALL, block), f32),
            pltpu.VMEM((QUARTERS, SMALL, block), f32),
            pltpu.SemaphoreType.DMA((96,)),
            pltpu.SemaphoreType.DMA((96,)),
            pltpu.SemaphoreType.DMA((16,)),
        ],
        compiler_params=pltpu.CompilerParams(
            collective_id=3, has_side_effects=True, vmem_limit_bytes=62 * 2**20
        ),
    )(
        branch_rows,
        residual_grad,
        small_grad,
        attended,
        query_rows,
        hidden_one,
        tokens,
        kv_all,
        qkv_full,
        out_full,
        small_full,
        cosine,
        sine,
        start,
        slabs,
        *parts,
    )


def finish_kernel(
    up_ref,
    down_ref,
    shared_ref,
    grad_ref,
    qkv_ref,
    out_ref,
    output_ref,
    shared_up_ref,
    small_ref,
    up,
    down,
    shared,
    grad,
    qkv,
    out,
    output,
    shared_up,
    gains,
    router,
    gate,
):
    up[...] = up_ref[...].astype(jnp.float32)
    down[...] = down_ref[...].astype(jnp.float32)
    shared[...] = shared_ref[...].astype(jnp.float32)
    grad[...] = grad_ref[...].astype(jnp.float32)
    qkv[...] = qkv_ref[...]
    out[...] = out_ref[...]
    output[...] = output_ref[...]
    for k in range(2):
        shared_up[:, k, :] = shared_up_ref[k].astype(jnp.float32).T
    gains[...] = small_ref[0:2, :]
    router[...] = small_ref[2 : 2 + E, :]
    gate[...] = small_ref[2 + E : 3 + E, :]


def finish_call(up, down, shared, grad, qkv, out, output, shared_up, small):
    steps = 2
    f32 = jnp.float32
    sds = jax.ShapeDtypeStruct
    block = small.shape[1]
    arrays = (up, down, shared, grad, qkv, out, output)
    shared_shape = (block, 2, shared_up.shape[1])

    def split(shape):
        part = (shape[0] // steps, *shape[1:])
        return pl.BlockSpec(part, lambda i: (i,) + (0,) * (len(part) - 1))

    def once(shape):
        return pl.BlockSpec(shape, lambda i: (0, 0))

    specs = [split(array.shape) for array in arrays]
    turned = pl.BlockSpec((*shared_up.shape[:2], block // steps), lambda i: (0, 0, i))
    types = (f32, f32, f32, f32, f32, f32, output.dtype)
    return pl.pallas_call(
        finish_kernel,
        name="finish",
        grid=(steps,),
        out_shape=[sds(a.shape, t) for a, t in zip(arrays, types, strict=True)]
        + [sds(shared_shape, f32)]
        + [sds((n, block), f32) for n in (2, E, 1)],
        in_specs=[*specs, turned, once(small.shape)],
        out_specs=[*specs, split(shared_shape), *(once((n, block)) for n in (2, E, 1))],
        compiler_params=pltpu.CompilerParams(vmem_limit_bytes=60 * 2**20),
    )(*arrays, shared_up, small)


def shards_units(
    tokens,
    cotangent,
    qkv_weight,
    out_weight,
    norm_gains,
    router_weight,
    shared_gate,
    expert_gate_up,
    expert_down,
    shared_gate_up,
    shared_down,
    routes,
    doc_start,
):
    tok_rows, width = tokens.shape
    seq_count = tok_rows // SEQ_DEV
    fs_index = lax.axis_index("fs")
    query_pos = fs_index * SEQ_DEV + jnp.arange(SEQ_DEV, dtype=jnp.int32)
    positions = jnp.tile(query_pos, seq_count)
    half_cos, half_sin = rope_tables(positions)
    cosine = jnp.concatenate([half_cos, half_cos], axis=1)
    sine = jnp.concatenate([-half_sin, half_sin], axis=1)
    routed_units = expert_down.shape[1]
    (
        output,
        branch_rows,
        residual_grad,
        small_grad,
        grad_slabs,
        up_part,
        shared_up_part,
        down_part,
        shared_down_part,
        attended,
        query_rows,
        hidden_one,
        _,
        _,
        _,
        kv_all,
        qkv_full,
        out_full,
        small_full,
        _,
    ) = layer_call(
        tokens,
        cotangent,
        qkv_weight,
        out_weight,
        norm_gains,
        router_weight,
        shared_gate[None],
        jnp.transpose(expert_gate_up, (0, 2, 3, 1)).reshape(E, 2 * routed_units, -1),
        shared_gate_up,
        expert_down,
        shared_down,
        cosine,
        sine,
        doc_start.reshape(seq_count, SEQ_DEV),
        routes.T,
    )
    input_grad, qkv_own, out_own, small_own, up_own, shared_up_own, down_own, shared_down_own = (
        backward_call(
            branch_rows,
            residual_grad,
            small_grad,
            attended,
            query_rows,
            hidden_one,
            tokens,
            kv_all,
            qkv_full,
            out_full,
            small_full,
            cosine,
            sine,
            doc_start.reshape(seq_count, SEQ_DEV),
            grad_slabs,
            up_part,
            shared_up_part,
            down_part,
            shared_down_part,
        )
    )
    (
        up_own,
        down_own,
        shared_down_own,
        input_grad,
        qkv_own,
        out_own,
        output,
        shared_up_own,
        gains,
        router,
        gate,
    ) = finish_call(
        up_own,
        down_own,
        shared_down_own,
        input_grad,
        qkv_own,
        out_own,
        output,
        shared_up_own,
        small_own,
    )
    up_own = up_own.reshape(E, 2, routed_units, -1)
    return (
        output,
        input_grad,
        qkv_own.reshape(qkv_weight.shape),
        out_own,
        gains,
        router,
        gate[0],
        jnp.transpose(up_own, (0, 3, 1, 2)),
        down_own,
        shared_up_own,
        shared_down_own,
    )


def solution(mesh):
    return jax.shard_map(
        shards_units if dict(mesh.shape) == {"fs": E, "tp": QUARTERS} else shards_gathered,
        mesh=mesh,
        in_specs=(
            P("fs", None),
            P("fs", None),
            P(None, "fs", "tp"),
            P("tp", "fs"),
            P(None, "fs"),
            P(None, "fs"),
            P("fs"),
            P(None, "fs", None, "tp"),
            P(None, "tp", "fs"),
            P("fs", None, "tp"),
            P("tp", "fs"),
            P("fs", None),
            P("fs"),
        ),
        out_specs=(
            P("fs", "tp"),
            P("fs", None),
            P(None, "fs", "tp"),
            P("tp", "fs"),
            P(None, "fs"),
            P(None, "fs"),
            P("fs"),
            P(None, "fs", None, "tp"),
            P(None, "tp", "fs"),
            P("fs", None, "tp"),
            P("tp", "fs"),
        ),
        check_vma=False,
    )
```

```python
import functools
import math

import jax
import jax.numpy as jnp
from jax import lax
from jax.experimental import pallas as pl
from jax.experimental.pallas import tpu as pltpu
from jax.sharding import PartitionSpec as P

HD = 128
E = 8
SEQ_DEV = 128
SIDE = 128


NORM_EPS = 1e-06
NEG_FILL = -1e30
ROPE_BASE = 1000000.0


def rope_tables(positions):
    half_size = HD // 2
    frequency = ROPE_BASE ** (-(jnp.arange(half_size, dtype=jnp.float32) * 2.0 / HD))
    angles = positions.astype(jnp.float32)[:, None] * frequency[None, :]
    return (jnp.cos(angles), jnp.sin(angles))


def rotate(values, cosine, sine_table):
    shaped = values.reshape(values.shape[0], -1, HD)
    half_size = HD // 2
    first_half = shaped[..., :half_size]
    second_half = shaped[..., half_size:]
    cos_part = cosine[:, None, :]
    sin_part = sine_table[:, None, :]
    turned = jnp.concatenate(
        [
            first_half * cos_part - second_half * sin_part,
            second_half * cos_part + first_half * sin_part,
        ],
        axis=-1,
    )
    return turned.reshape(values.shape)


def key_mask(query_pos, query_start, first_dev, group_size):
    key_pos = (first_dev + jnp.arange(group_size, dtype=jnp.int32)[:, None]) * SEQ_DEV + jnp.arange(
        SEQ_DEV, dtype=jnp.int32
    )[None, :]
    key_pos = key_pos[None, None, :, :]
    return (key_pos <= query_pos[None, :, None, None]) & (key_pos >= query_start[:, :, None, None])


def shards_gathered(
    tokens,
    cotangent,
    qkv_weight,
    out_weight,
    norm_gains,
    router_weight,
    shared_gate,
    expert_gate_up,
    expert_down,
    shared_gate_up,
    shared_down,
    routes,
    doc_start,
):
    tok_rows = tokens.shape[0]
    seq_count = tok_rows // SEQ_DEV
    local_width = qkv_weight.shape[2]
    head_count = local_width // HD
    out_width = tokens.shape[1] // lax.axis_size("tp")
    score_scale = HD ** (-0.5)
    fs_index = lax.axis_index("fs")
    tp_index = lax.axis_index("tp")
    query_pos = fs_index * SEQ_DEV + jnp.arange(SEQ_DEV, dtype=jnp.int32)
    positions = jnp.tile(query_pos, seq_count)
    query_start = doc_start.reshape(seq_count, SEQ_DEV)
    cosine, sine_table = rope_tables(positions)
    group_limit = max(1, 512 // SEQ_DEV)
    qkv_full, out_full, gains_full, router_full, shared_gate_full = (
        lax.all_gather(qkv_weight, "fs", axis=1, tiled=True),
        lax.all_gather(out_weight, "fs", axis=1, tiled=True),
        lax.all_gather(norm_gains, "fs", axis=1, tiled=True),
        lax.all_gather(router_weight, "fs", axis=1, tiled=True),
        lax.all_gather(shared_gate, "fs", axis=0, tiled=True),
    )
    token_float = tokens.astype(jnp.float32)
    rstd_one = lax.rsqrt(jnp.mean(token_float * token_float, axis=1, keepdims=True) + NORM_EPS)
    normed_one = token_float * rstd_one
    hidden_one = (normed_one * gains_full[0].astype(jnp.float32)[None, :]).astype(jnp.bfloat16)
    projected = jnp.einsum("td,jdf->jtf", hidden_one, qkv_full, preferred_element_type=jnp.float32)
    query_rows = rotate(projected[0], cosine, sine_table).astype(jnp.bfloat16)
    key_own = rotate(projected[1], cosine, sine_table).astype(jnp.bfloat16)
    value_own = projected[2].astype(jnp.bfloat16)
    query_heads = query_rows.reshape(seq_count, SEQ_DEV, head_count, HD)

    def score_block(key_group, first_dev):
        allowed = key_mask(query_pos, query_start, first_dev, key_group.shape[0])[:, None]
        scores = (
            jnp.einsum(
                "pqhd,gpkhd->phqgk", query_heads, key_group, preferred_element_type=jnp.float32
            )
            * score_scale
        )
        return (jnp.where(allowed, scores, NEG_FILL), allowed)

    def forward_update(running, key_group, value_group, first_dev):
        run_max, run_sum, accumulated = running
        scores, allowed = score_block(key_group, first_dev)
        new_max = jnp.maximum(run_max, jnp.max(scores, axis=(3, 4)))
        weights = jnp.where(allowed, jnp.exp(scores - new_max[..., None, None]), 0.0)
        factor = jnp.exp(run_max - new_max)
        new_sum = run_sum * factor + jnp.sum(weights, axis=(3, 4))
        mixed_part = jnp.einsum(
            "phqgk,gpkhd->pqhd",
            weights.astype(jnp.bfloat16),
            value_group,
            preferred_element_type=jnp.float32,
        )
        new_accum = accumulated * jnp.transpose(factor, (0, 2, 1))[..., None] + mixed_part
        return (new_max, new_sum, new_accum)

    initial = (
        jnp.full((seq_count, head_count, SEQ_DEV), NEG_FILL, jnp.float32),
        jnp.zeros((seq_count, head_count, SEQ_DEV), jnp.float32),
        jnp.zeros((seq_count, SEQ_DEV, head_count, HD), jnp.float32),
    )
    running = initial
    key_piece = lax.all_gather(key_own, "fs", axis=0, tiled=True)
    value_piece = lax.all_gather(value_own, "fs", axis=0, tiled=True)
    shard_count = key_piece.shape[0] // tok_rows
    group_size = math.gcd(shard_count, group_limit)
    step_count = shard_count // group_size
    shaped = (step_count, group_size, seq_count, SEQ_DEV, head_count, HD)
    first_dev = jnp.int32(0) // tok_rows

    def one_step(carried, inputs):
        key_group, value_group, group_index = inputs
        start_dev = group_index * group_size
        updated = lax.cond(
            start_dev <= fs_index,
            lambda state_in: forward_update(state_in, key_group, value_group, start_dev),
            lambda state_in: state_in,
            carried,
        )
        return (updated, None)

    running, ignored = lax.scan(
        one_step,
        running,
        (
            key_piece.reshape(shaped),
            value_piece.reshape(shaped),
            jnp.arange(step_count, dtype=jnp.int32),
        ),
    )
    run_max, run_sum, accumulated = running
    attended_heads = (accumulated / jnp.transpose(run_sum, (0, 2, 1))[..., None]).astype(
        jnp.bfloat16
    )
    log_total = run_max + jnp.log(run_sum)
    attended = attended_heads.reshape(tok_rows, local_width)
    branch_part = jnp.dot(attended, out_full, preferred_element_type=jnp.float32)
    branch = lax.psum(branch_part.astype(jnp.bfloat16), "tp").astype(jnp.float32)
    residual = token_float + branch
    rstd_two = lax.rsqrt(jnp.mean(residual * residual, axis=1, keepdims=True) + NORM_EPS)
    normed_two = residual * rstd_two
    hidden_two = (normed_two * gains_full[1].astype(jnp.float32)[None, :]).astype(jnp.bfloat16)
    expert_gate_all, expert_down_all, shared_up_all, shared_down_all = (
        lax.all_gather(expert_gate_up, "fs", axis=1, tiled=True),
        lax.all_gather(expert_down, "fs", axis=2, tiled=True),
        lax.all_gather(shared_gate_up, "fs", axis=0, tiled=True),
        lax.all_gather(shared_down, "fs", axis=1, tiled=True),
    )
    logits = jnp.einsum("td,ed->te", hidden_two, router_full, preferred_element_type=jnp.float32)
    router_probs = jax.nn.softmax(logits, axis=-1)
    chosen = jnp.sum(
        (routes[:, :, None] == jnp.arange(E, dtype=jnp.int32)[None, None, :]).astype(jnp.float32),
        axis=1,
    )
    gate_weights = router_probs * chosen
    gate_up = jnp.einsum(
        "td,edkf->tekf", hidden_two, expert_gate_all, preferred_element_type=jnp.float32
    )
    gate_part = gate_up[:, :, 0]
    up_part = gate_up[:, :, 1]
    gate_sigmoid = jax.nn.sigmoid(gate_part)
    active = gate_part * gate_sigmoid * up_part
    hidden = (gate_weights[:, :, None] * active).astype(jnp.bfloat16)
    shared_in = jnp.einsum(
        "td,dkf->tkf", hidden_two, shared_up_all, preferred_element_type=jnp.float32
    )
    shared_gate_in = shared_in[:, 0]
    shared_up_in = shared_in[:, 1]
    shared_sigmoid = jax.nn.sigmoid(shared_gate_in)
    shared_active = shared_gate_in * shared_sigmoid * shared_up_in
    gate_logit = jnp.einsum(
        "td,d->t", hidden_two, shared_gate_full, preferred_element_type=jnp.float32
    )
    gate_value = jax.nn.sigmoid(gate_logit)
    shared_hidden = (gate_value[:, None] * shared_active).astype(jnp.bfloat16)
    mixture_part = jnp.einsum(
        "tef,efd->td", hidden, expert_down_all, preferred_element_type=jnp.float32
    ) + jnp.dot(shared_hidden, shared_down_all, preferred_element_type=jnp.float32)
    mixture = lax.psum_scatter(
        mixture_part.astype(jnp.bfloat16), "tp", scatter_dimension=1, tiled=True
    ).astype(jnp.float32)
    output = (
        lax.dynamic_slice_in_dim(residual, tp_index * out_width, out_width, 1) + mixture
    ).astype(jnp.bfloat16)
    qkv_back, out_back, gains_back, router_back, shared_gate_back = (
        lax.all_gather(qkv_weight, "fs", axis=1, tiled=True),
        lax.all_gather(out_weight, "fs", axis=1, tiled=True),
        lax.all_gather(norm_gains, "fs", axis=1, tiled=True),
        lax.all_gather(router_weight, "fs", axis=1, tiled=True),
        lax.all_gather(shared_gate, "fs", axis=0, tiled=True),
    )
    expert_gate_back, expert_down_back, shared_up_back, shared_down_back = (
        lax.all_gather(expert_gate_up, "fs", axis=1, tiled=True),
        lax.all_gather(expert_down, "fs", axis=2, tiled=True),
        lax.all_gather(shared_gate_up, "fs", axis=0, tiled=True),
        lax.all_gather(shared_down, "fs", axis=1, tiled=True),
    )
    hidden_grad = jnp.einsum(
        "td,efd->tef", cotangent, expert_down_back, preferred_element_type=jnp.float32
    )
    expert_down_grad = jnp.einsum(
        "tef,td->efd", hidden, cotangent, preferred_element_type=jnp.float32
    )
    shared_grad = jnp.einsum(
        "td,fd->tf", cotangent, shared_down_back, preferred_element_type=jnp.float32
    )
    shared_down_grad = jnp.einsum(
        "tf,td->fd", shared_hidden, cotangent, preferred_element_type=jnp.float32
    )
    gate_dot = jnp.sum(active * hidden_grad, axis=2)
    shared_dot = jnp.sum(shared_active * shared_grad, axis=1)
    active_grad = gate_weights[:, :, None] * hidden_grad
    gate_grad = active_grad * up_part * gate_sigmoid * (1.0 + gate_part * (1.0 - gate_sigmoid))
    up_grad = active_grad * gate_part * gate_sigmoid
    gate_up_grad = jnp.stack([gate_grad, up_grad], axis=2).astype(jnp.bfloat16)
    shared_active_grad = gate_value[:, None] * shared_grad
    shared_gate_grad = (
        shared_active_grad
        * shared_up_in
        * shared_sigmoid
        * (1.0 + shared_gate_in * (1.0 - shared_sigmoid))
    )
    shared_unit_grad = shared_active_grad * shared_gate_in * shared_sigmoid
    shared_up_grad = jnp.stack([shared_gate_grad, shared_unit_grad], axis=1).astype(jnp.bfloat16)
    expert_gate_grad = jnp.einsum(
        "td,tekf->edkf", hidden_two, gate_up_grad, preferred_element_type=jnp.float32
    )
    shared_proj_grad = jnp.einsum(
        "td,tkf->dkf", hidden_two, shared_up_grad, preferred_element_type=jnp.float32
    )
    input_part = jnp.einsum(
        "tekf,edkf->td", gate_up_grad, expert_gate_back, preferred_element_type=jnp.float32
    ) + jnp.einsum(
        "tkf,dkf->td", shared_up_grad, shared_up_back, preferred_element_type=jnp.float32
    )
    input_sum, gate_sum, shared_sum = (
        lax.psum(input_part.astype(jnp.bfloat16), "tp").astype(jnp.float32),
        lax.psum(gate_dot.astype(jnp.bfloat16), "tp").astype(jnp.float32),
        lax.psum(shared_dot.astype(jnp.bfloat16), "tp").astype(jnp.float32),
    )
    chosen_grad = chosen * gate_sum
    logit_grad = (
        router_probs * (chosen_grad - jnp.sum(router_probs * chosen_grad, axis=1, keepdims=True))
    ).astype(jnp.bfloat16)
    gate_logit_grad = (shared_sum * gate_value * (1.0 - gate_value)).astype(jnp.bfloat16)
    router_grad = jnp.einsum(
        "te,td->ed", logit_grad, hidden_two, preferred_element_type=jnp.float32
    )
    shared_vector_grad = jnp.einsum(
        "t,td->d", gate_logit_grad, hidden_two, preferred_element_type=jnp.float32
    )
    two_grad = (
        input_sum
        + jnp.einsum("te,ed->td", logit_grad, router_back, preferred_element_type=jnp.float32)
        + gate_logit_grad.astype(jnp.float32)[:, None]
        * shared_gate_back.astype(jnp.float32)[None, :]
    )
    scaled_two = two_grad * gains_back[1].astype(jnp.float32)[None, :]
    gain_two_grad = jnp.sum(two_grad * normed_two, axis=0)
    residual_grad = cotangent.astype(jnp.float32) + rstd_two * (
        scaled_two - normed_two * jnp.mean(scaled_two * normed_two, axis=1, keepdims=True)
    )
    branch_grad = residual_grad.astype(jnp.bfloat16)
    out_grad = jnp.einsum("tf,td->fd", attended, branch_grad, preferred_element_type=jnp.float32)
    attended_grad = jnp.einsum(
        "td,fd->tf", branch_grad, out_back, preferred_element_type=jnp.float32
    ).astype(jnp.bfloat16)
    grad_heads = attended_grad.reshape(seq_count, SEQ_DEV, head_count, HD)
    delta_rows = jnp.einsum(
        "pqhd,pqhd->phq", grad_heads, attended_heads, preferred_element_type=jnp.float32
    )
    key_all, value_all = (
        lax.all_gather(key_own, "fs", axis=0, tiled=True),
        lax.all_gather(value_own, "fs", axis=0, tiled=True),
    )
    device_count = key_all.shape[0] // tok_rows
    back_group = math.gcd(device_count, group_limit)
    back_steps = device_count // back_group
    back_shape = (back_steps, back_group, seq_count, SEQ_DEV, head_count, HD)

    def backward_update(key_group, value_group, start_dev):
        scores, allowed = score_block(key_group, start_dev)
        probs_block = jnp.where(allowed, jnp.exp(scores - log_total[..., None, None]), 0.0)
        weights_grad = jnp.einsum(
            "pqhd,gpkhd->phqgk", grad_heads, value_group, preferred_element_type=jnp.float32
        )
        score_grad = (probs_block * (weights_grad - delta_rows[..., None, None])).astype(
            jnp.bfloat16
        )
        query_part = (
            jnp.einsum(
                "phqgk,gpkhd->pqhd", score_grad, key_group, preferred_element_type=jnp.float32
            )
            * score_scale
        )
        key_part = (
            jnp.einsum(
                "phqgk,pqhd->gpkhd", score_grad, query_heads, preferred_element_type=jnp.float32
            )
            * score_scale
        )
        value_part = jnp.einsum(
            "phqgk,pqhd->gpkhd",
            probs_block.astype(jnp.bfloat16),
            grad_heads,
            preferred_element_type=jnp.float32,
        )
        return (query_part, key_part, value_part)

    empty_grads = (
        jnp.zeros((seq_count, SEQ_DEV, head_count, HD), jnp.float32),
        jnp.zeros((back_group, seq_count, SEQ_DEV, head_count, HD), jnp.float32),
        jnp.zeros((back_group, seq_count, SEQ_DEV, head_count, HD), jnp.float32),
    )
    scan_inputs = (
        key_all.reshape(back_shape),
        value_all.reshape(back_shape),
        jnp.arange(back_steps, dtype=jnp.int32),
    )

    def back_step(query_acc, inputs):
        key_group, value_group, group_index = inputs
        start_dev = group_index * back_group
        query_part, key_part, value_part = lax.cond(
            start_dev <= fs_index,
            lambda ignored_in: backward_update(key_group, value_group, start_dev),
            lambda ignored_in: empty_grads,
            key_group,
        )
        term_rows = jnp.concatenate(
            [
                key_part.reshape(back_group * tok_rows, local_width),
                value_part.reshape(back_group * tok_rows, local_width),
            ],
            axis=1,
        )
        return (query_acc + query_part, term_rows)

    query_grad, key_value_terms = lax.scan(back_step, empty_grads[0], scan_inputs)
    key_value_sum = lax.psum_scatter(
        key_value_terms.reshape(device_count * tok_rows, 2 * local_width).astype(jnp.bfloat16),
        "fs",
        scatter_dimension=0,
        tiled=True,
    ).astype(jnp.float32)
    key_grad_rows = key_value_sum[:, :local_width]
    value_grad_rows = key_value_sum[:, local_width:]
    projected_grad = jnp.stack(
        [
            rotate(query_grad.reshape(tok_rows, local_width), cosine, -sine_table),
            rotate(key_grad_rows, cosine, -sine_table),
            value_grad_rows,
        ],
        axis=0,
    ).astype(jnp.bfloat16)
    qkv_grad = jnp.einsum(
        "td,jtf->jdf", hidden_one, projected_grad, preferred_element_type=jnp.float32
    )
    one_part = jnp.einsum(
        "jtf,jdf->td", projected_grad, qkv_back, preferred_element_type=jnp.float32
    )
    one_grad = lax.psum(one_part.astype(jnp.bfloat16), "tp").astype(jnp.float32)
    scaled_one = one_grad * gains_back[0].astype(jnp.float32)[None, :]
    gain_one_grad = jnp.sum(one_grad * normed_one, axis=0)
    input_grad = residual_grad + rstd_one * (
        scaled_one - normed_one * jnp.mean(scaled_one * normed_one, axis=1, keepdims=True)
    )
    gains_grad = jnp.stack([gain_one_grad, gain_two_grad], axis=0)
    reduced = (
        lax.psum_scatter(
            qkv_grad.astype(jnp.bfloat16), "fs", scatter_dimension=1, tiled=True
        ).astype(jnp.float32),
        lax.psum_scatter(
            out_grad.astype(jnp.bfloat16), "fs", scatter_dimension=1, tiled=True
        ).astype(jnp.float32),
        lax.psum_scatter(
            gains_grad.astype(jnp.bfloat16), "fs", scatter_dimension=1, tiled=True
        ).astype(jnp.float32),
        lax.psum_scatter(
            router_grad.astype(jnp.bfloat16), "fs", scatter_dimension=1, tiled=True
        ).astype(jnp.float32),
        lax.psum_scatter(
            shared_vector_grad.astype(jnp.bfloat16), "fs", scatter_dimension=0, tiled=True
        ).astype(jnp.float32),
        lax.psum_scatter(
            expert_gate_grad.astype(jnp.bfloat16), "fs", scatter_dimension=1, tiled=True
        ).astype(jnp.float32),
        lax.psum_scatter(
            expert_down_grad.astype(jnp.bfloat16), "fs", scatter_dimension=2, tiled=True
        ).astype(jnp.float32),
        lax.psum_scatter(
            shared_proj_grad.astype(jnp.bfloat16), "fs", scatter_dimension=0, tiled=True
        ).astype(jnp.float32),
        lax.psum_scatter(
            shared_down_grad.astype(jnp.bfloat16), "fs", scatter_dimension=1, tiled=True
        ).astype(jnp.float32),
    )
    return (
        output,
        input_grad,
        reduced[0],
        reduced[1],
        reduced[2],
        reduced[3],
        reduced[4],
        reduced[5],
        reduced[6],
        reduced[7],
        reduced[8],
    )


MESH = pl.DeviceIdType.MESH
X_BIT, Y_BIT, CORE_BIT = 2, 4, 1
QUARTERS = 4
SMALL = 16
EARLY = (2, 4)
CUT = 1536


def flip(index, bit):
    return index + bit - 2 * bit * ((index // bit) % 2)


class Links:
    def __init__(self, send, recv, local):
        self.fs = lax.axis_index("fs")
        self.tp = lax.axis_index("tp")
        self.send, self.recv, self.local = send, recv, local
        self.used = 0
        self.used_local = 0

    def peer(self, bits):
        where = self.fs
        for bit in (X_BIT, Y_BIT, CORE_BIT):
            if bits & bit:
                where = flip(where, bit)
        return where

    def along(self, step):
        return lax.rem(self.tp + step, QUARTERS)

    def remote(self, source, target, device, landing):
        i = self.used
        self.used += 1
        out = pltpu.make_async_remote_copy(
            src_ref=source,
            dst_ref=target,
            send_sem=self.send.at[i],
            recv_sem=self.recv.at[i],
            device_id=device,
            device_id_type=MESH,
        )
        back = pltpu.make_async_remote_copy(
            src_ref=landing,
            dst_ref=landing,
            send_sem=self.send.at[i],
            recv_sem=self.recv.at[i],
            device_id=device,
            device_id_type=MESH,
        )
        return out, back

    def inside(self, source, target):
        i = self.used_local
        self.used_local += 1
        return pltpu.make_async_copy(source, target, self.local.at[i])

    def greet(self, plane, column):
        barrier = pltpu.get_barrier_semaphore()
        for bits in plane:
            pl.semaphore_signal(
                barrier, inc=1, device_id=(self.peer(bits), self.tp), device_id_type=MESH
            )
        for step in column:
            pl.semaphore_signal(
                barrier, inc=1, device_id=(self.fs, self.along(step)), device_id_type=MESH
            )
        pl.semaphore_wait(barrier, len(plane) + len(column))


class Gather:
    def __init__(self, links, source, place, half):
        self.links = links
        fs, tp = links.fs, links.tp

        def to(bits, what, landing, origin=None):
            return links.remote(
                what if origin is None else origin, what, (links.peer(bits), tp), landing
            )

        p = links.peer
        self.keep = None if source is None else links.inside(source, place(fs))
        self.to_x = to(X_BIT, place(fs), place(p(X_BIT)), source)
        self.to_y = to(Y_BIT, place(fs), place(p(Y_BIT)), source)
        self.to_c = to(CORE_BIT, place(fs), place(p(CORE_BIT)), source)
        xy = X_BIT + Y_BIT
        self.x_on = to(Y_BIT, half(p(X_BIT), 0), half(p(xy), 0))
        self.y_on = to(X_BIT, half(p(Y_BIT), 1), half(p(xy), 1))
        self.x_core = to(CORE_BIT, place(p(X_BIT)), place(p(X_BIT + CORE_BIT)))
        self.y_core = to(CORE_BIT, place(p(Y_BIT)), place(p(Y_BIT + CORE_BIT)))
        self.d_core = [
            to(CORE_BIT, half(p(xy), h), half(p(xy + CORE_BIT), h)) for h in range(2)
        ]

    def first(self):
        self.to_x[0].start()
        self.to_y[0].start()
        self.to_c[0].start()
        if self.keep is not None:
            self.keep.start()

    def second(self):
        self.to_x[1].wait_recv()
        self.x_on[0].start()
        self.x_core[0].start()
        self.to_y[1].wait_recv()
        self.y_on[0].start()
        self.y_core[0].start()

    def third(self):
        self.x_on[1].wait_recv()
        self.d_core[0][0].start()
        self.y_on[1].wait_recv()
        self.d_core[1][0].start()

    def last(self):
        if self.keep is not None:
            self.keep.wait()
        for out, back in (self.to_c, self.x_core, self.y_core, *self.d_core):
            back.wait_recv()
        for out, back in (
            self.to_x,
            self.to_y,
            self.to_c,
            self.x_on,
            self.y_on,
            self.x_core,
            self.y_core,
            *self.d_core,
        ):
            out.wait_send()


class CrossGather:
    def __init__(self, links, source, blocks):
        self.links = links
        tp = links.tp
        size = source.shape[0]

        def slot(k, h=None):
            start, count = (3 - k // 2) * size, size
            if h is not None:
                count = size // 2
                start = start + h * count
            return blocks.at[1, pl.ds(start, count)]

        def to(bits, start, there):
            return links.remote(start, there, (links.peer(bits), tp), there)

        x, y, c = X_BIT, Y_BIT, CORE_BIT
        self.keep = links.inside(source, slot(0))
        self.to_x = to(x, source, slot(x))
        self.to_y = to(y, source, slot(y))
        self.x_on = to(y, slot(x, 0), slot(x + y, 0))
        self.y_on = to(x, slot(y, 1), slot(x + y, 1))
        self.along = []
        for step in range(1, QUARTERS):
            there = blocks.at[2 * step + 1]
            self.along.append(
                links.remote(blocks.at[1], there, (links.fs, links.along(step)), there)
            )
        self.core = [
            to(c, blocks.at[2 * s + 1], blocks.at[2 * s]) for s in range(QUARTERS)
        ]

    def first(self):
        self.to_x[0].start()
        self.to_y[0].start()
        self.keep.start()

    def second(self):
        self.to_x[1].wait_recv()
        self.x_on[0].start()
        self.to_y[1].wait_recv()
        self.y_on[0].start()

    def third(self):
        self.keep.wait()
        self.x_on[1].wait_recv()
        self.y_on[1].wait_recv()
        for out, back in self.along:
            out.start()
        self.core[0][0].start()

    def last(self):
        for s, (out, back) in enumerate(self.along):
            back.wait_recv()
            self.core[s + 1][0].start()
        for out, back in self.core:
            back.wait_recv()
        for out, back in (self.to_x, self.to_y, self.x_on, self.y_on, *self.along, *self.core):
            out.wait_send()


def grad_shapes(routed, shared, block):
    return (
        (E, 2 * routed, block),
        (2, E * shared, block),
        (E, routed, block),
        (E * shared, block),
    )


def grad_pieces(grads, results, index, source):
    up_all, shared_up_all, down_all, shared_down_all = results
    routed, shared = down_all.shape[1], shared_down_all.shape[0] // E
    units = pl.ds(pl.multiple_of(source * shared, 16), shared)
    places = [
        up_all.at[source],
        shared_up_all.at[0, units],
        shared_up_all.at[1, units],
        down_all.at[source],
        shared_down_all.at[units],
    ]
    placed, at = [], 0
    for place, size in zip(places, (2 * routed, shared, shared, routed, shared), strict=True):
        placed.append((grads.at[index, pl.ds(at, size)], place))
        at += size
    return placed


def grad_copies(links, grads, results, bits):
    peer = links.peer(bits)
    pairs = zip(
        grad_pieces(grads, results, peer, links.fs),
        grad_pieces(grads, results, peer, peer),
        strict=True,
    )
    return [
        links.remote(piece, place, (peer, links.tp), landing)
        for (piece, place), (_, landing) in pairs
    ]


def turn(values, cosine, sine_signed):
    parts = []
    for h in range(values.shape[1] // HD):
        v = values[:, h * HD : (h + 1) * HD]
        parts.append(v * cosine + pltpu.roll(v, HD // 2, 1) * sine_signed)
    return jnp.concatenate(parts, axis=1)


def as_column(row):
    size = row.shape[1]
    same = lax.broadcasted_iota(jnp.int32, (size, size), 0) == lax.broadcasted_iota(
        jnp.int32, (size, size), 1
    )
    spread = jnp.where(same, row.astype(jnp.float32), 0.0)
    return jnp.sum(spread, axis=1, keepdims=True).astype(jnp.int32)


def matmul(a, b):
    return jnp.dot(a, b, preferred_element_type=jnp.float32)


def matmul_nt(a, b):
    return lax.dot_general(a, b, (((1,), (1,)), ((), ())), preferred_element_type=jnp.float32)


def matmul_tn(a, b):
    return lax.dot_general(a, b, (((0,), (0,)), ((), ())), preferred_element_type=jnp.float32)


class RowGather:
    def __init__(self, links, source, slot, half):
        self.links = links

        def to(bits, owner, h=None):
            view = slot if h is None else lambda k: half(k, h)
            start = source if owner == 0 and source is not None else view(owner)
            return links.remote(
                start, view(owner ^ bits), (links.peer(bits), links.tp), view(owner ^ bits)
            )

        x, y, c = X_BIT, Y_BIT, CORE_BIT
        self.keep = None if source is None else links.inside(source, slot(0))
        self.own = [to(x, 0), to(y, 0), to(c, 0)]
        self.x_on = [to(y, x, 0), to(c, x)]
        self.y_on = [to(x, y, 1), to(c, y)]
        self.d_on = [to(c, x + y, 0), to(c, x + y, 1)]

    def first(self):
        for out, back in self.own:
            out.start()
        if self.keep is not None:
            self.keep.start()

    def second(self):
        self.own[0][1].wait_recv()
        for out, back in self.x_on:
            out.start()
        self.own[1][1].wait_recv()
        for out, back in self.y_on:
            out.start()

    def third(self):
        self.x_on[0][1].wait_recv()
        self.d_on[0][0].start()
        self.y_on[0][1].wait_recv()
        self.d_on[1][0].start()

    def last(self):
        if self.keep is not None:
            self.keep.wait()
        for out, back in (self.own[2], self.x_on[1], self.y_on[1], *self.d_on):
            back.wait_recv()

    def sent(self):
        for out, back in self.own + self.x_on + self.y_on + self.d_on:
            out.wait_send()


def layer_kernel(
    routed,
    tokens_hbm,
    cotangent_ref,
    qkv_ref,
    out_ref,
    gains_ref,
    router_ref,
    gate_ref,
    up_ref,
    shared_raw,
    down_ref,
    shared_down_ref,
    cos_ref,
    sin_ref,
    start_ref,
    routes_ref,
    output_ref,
    branch_ref,
    back_ref,
    small_grad_ref,
    grads_out,
    up_all,
    shared_up_all,
    down_all,
    shared_down_all,
    attended_out,
    query_out,
    hidden_out,
    slabs_all,
    cotangent_all,
    cotangent_plane,
    kv_out,
    qkv_out,
    out_out,
    small_out,
    shared_up_ref,
    small_full,
    branch_in,
    two_ref,
    small_ref,
    scales_ref,
    residual_ref,
    two_all,
    core_in,
    diag_in,
    side_in,
    rows_in,
    cols_in,
    send,
    recv,
    local,
    credit,
):
    links = Links(send, recv, local)
    fs, tp = links.fs, links.tp
    rows, width = tokens_hbm.shape
    block = width // E
    local_width = qkv_ref.shape[2]
    heads = local_width // HD
    seqs = rows // SEQ_DEV
    quarter = rows // QUARTERS
    out_width = output_ref.shape[1]
    back_width = width + SIDE
    whole = back_width + width
    slab_rows = slabs_all.shape[1]
    count = slab_rows // 3
    bf, f32 = jnp.bfloat16, jnp.float32

    def at_rows(index, size):
        return pl.ds(pl.multiple_of(index * size, size), size)

    small_ref[...] = jnp.concatenate(
        [
            gains_ref[...].astype(f32),
            router_ref[...].astype(f32),
            jnp.concatenate([gate_ref[0:1], gate_ref[1:2]], axis=1).astype(f32),
            jnp.zeros((SMALL - 3 - E, block), f32),
        ],
        axis=0,
    ).astype(jnp.bfloat16)
    links.greet(range(1, 8), range(1, QUARTERS))
    cut = cotangent_all.shape[2]
    cot = CrossGather(
        links, cotangent_ref.at[at_rows(tp, quarter), pl.ds(0, cut)], cotangent_all
    )
    cot_plane = Gather(
        links,
        cotangent_ref.at[:, pl.ds(cut, width - cut)],
        lambda f: cotangent_plane.at[f],
        lambda f, h: cotangent_plane.at[f, pl.ds(h * SEQ_DEV, SEQ_DEV)],
    )
    shared = shared_down_ref.shape[0] // E

    def slab(peer, where):
        units = pl.ds(pl.multiple_of(peer * shared, 16), shared)
        pieces = [
            up_ref.at[peer],
            shared_up_ref.at[0, units],
            shared_up_ref.at[1, units],
            down_ref.at[peer],
            shared_down_ref.at[units],
        ]
        placed, at = [], 0
        for piece, size in zip(pieces, (2 * routed, shared, shared, routed, shared), strict=True):
            placed.append((piece, slabs_all.at[where, pl.ds(at, size)]))
            at += size
        return placed

    slab_copies = []
    for bits in (6, 7, 2, 3, 4, 5, 1):
        peer = links.peer(bits)
        for (piece, place), (_, landing) in zip(slab(peer, fs), slab(peer, peer), strict=True):
            slab_copies.append(links.remote(piece, place, (peer, tp), landing))
    slab_own = [links.inside(piece, place) for piece, place in slab(fs, fs)]
    def slot(s, k, h=None):
        start = (3 - k // 2) * quarter
        size = quarter
        if h is not None:
            size = quarter // 2
            start = start + h * size
        return two_all.at[2 * s + 1 - k % 2, pl.ds(start, size)]

    along = []
    for step in range(1, QUARTERS):
        along.append(
            links.remote(two_ref, slot(step, 0), (fs, links.along(step)), slot(step, 0))
        )
    gathers = []
    for s in range(QUARTERS):
        gathers.append(
            RowGather(
                links,
                two_ref if s == 0 else None,
                lambda k, s=s: slot(s, k),
                lambda k, h, s=s: slot(s, k, h),
            )
        )

    def attention(
        tokens_ref,
        hidden_buf,
        attended_ref,
        query_ref,
        qkv_full,
        out_full,
        kv_own,
        kv_full,
        branch_buf,
        raw,
        by_unit,
    ):
        load = links.inside(tokens_hbm, tokens_ref)
        load.start()
        raw_load = links.inside(shared_raw, raw)
        raw_load.start()
        small = Gather(
            links, small_ref, lambda f: small_full.at[f], lambda f, h: small_full.at[f, :, pl.ds(h * 128, 128)]
        )
        qkv = Gather(
            links,
            qkv_ref,
            lambda f: qkv_out.at[:, at_rows(f, block)],
            lambda f, h: qkv_out.at[:, pl.ds(pl.multiple_of(f * block + h * (block // 2), block // 2), block // 2)],
        )
        outs = Gather(
            links,
            out_ref,
            lambda f: out_out.at[f],
            lambda f, h: out_out.at[f, pl.ds(h * (local_width // 2), local_width // 2)],
        )
        small.first()
        cot.first()
        qkv.first()
        small.second()
        small.third()
        small.last()
        cot.second()
        load.wait()
        tokens = tokens_ref[...].astype(jnp.float32)
        rstd_one = lax.rsqrt(jnp.mean(tokens * tokens, axis=1, keepdims=True) + NORM_EPS)
        for b in range(E):
            cols = slice(b * block, (b + 1) * block)
            gain = small_full[b, 0:1, :].astype(jnp.float32)
            hidden_buf[:, cols] = (tokens[:, cols] * rstd_one * gain).astype(jnp.bfloat16)
        raw_load.wait()
        for k in range(2):
            by_unit[k] = raw[:, k, :].astype(f32).T.astype(bf)
        unit_keep = links.inside(by_unit, shared_up_ref)
        unit_keep.start()
        cot.third()
        qkv.second()
        qkv.third()
        outs.first()
        cot_plane.first()
        qkv.last()
        qkv_load = links.inside(qkv_out, qkv_full)
        qkv_load.start()
        qkv_load.wait()
        hidden = hidden_buf[...]
        cosine, sine = cos_ref[...], sin_ref[...]
        kv_own[:, :local_width] = turn(matmul(hidden, qkv_full[1]), cosine, sine).astype(jnp.bfloat16)
        kv_own[:, local_width:] = matmul(hidden, qkv_full[2]).astype(jnp.bfloat16)
        kv = Gather(
            links,
            kv_own,
            lambda f: kv_out.at[f],
            lambda f, h: kv_out.at[f, pl.ds(h * SEQ_DEV, SEQ_DEV)],
        )
        kv.first()
        query_ref[...] = turn(matmul(hidden, qkv_full[0]), cosine, sine).astype(jnp.bfloat16)
        outs.second()
        kv.second()
        outs.third()
        kv.third()
        cot_plane.second()
        unit_keep.wait()
        for out, back in slab_copies:
            out.start()
        for copy in slab_own:
            copy.start()
        kv.last()
        kv_load = links.inside(kv_out, kv_full)
        kv_load.start()
        kv_load.wait()
        length = E * SEQ_DEV
        key_pos = lax.broadcasted_iota(jnp.int32, (SEQ_DEV, length), 1)
        query_pos = fs * SEQ_DEV + lax.broadcasted_iota(jnp.int32, (SEQ_DEV, length), 0)
        for s in range(seqs):
            here = slice(s * SEQ_DEV, (s + 1) * SEQ_DEV)
            allowed = (key_pos <= query_pos) & (key_pos >= as_column(start_ref[s : s + 1, :]))
            for h in range(heads):
                cols = slice(h * HD, (h + 1) * HD)
                vcols = slice(local_width + h * HD, local_width + (h + 1) * HD)
                keys = kv_full[:, here, cols].reshape(length, HD)
                values = kv_full[:, here, vcols].reshape(length, HD)
                scores = matmul_nt(query_ref[here, cols], keys) * (HD ** (-0.5))
                scores = jnp.where(allowed, scores, NEG_FILL)
                top = jnp.max(scores, axis=1, keepdims=True)
                weights = jnp.exp(scores - top)
                weights = weights / jnp.sum(weights, axis=1, keepdims=True)
                attended_ref[here, cols] = matmul(weights.astype(jnp.bfloat16), values).astype(
                    jnp.bfloat16
                )
        outs.last()
        cot_plane.third()
        out_load = links.inside(out_out, out_full)
        out_load.start()
        small_keep = links.inside(small_full, small_out)
        small_keep.start()
        out_load.wait()
        attended = attended_ref[...]
        for b in range(E):
            branch_buf[:, b * block : (b + 1) * block] = matmul(attended, out_full[b]).astype(
                jnp.bfloat16
            )
        branch = []
        for step in range(1, QUARTERS):
            peer = links.along(step)
            branch.append(
                links.remote(
                    branch_buf.at[at_rows(peer, quarter)],
                    branch_in.at[step - 1],
                    (fs, peer),
                    branch_in.at[step - 1],
                )
            )
        for out, back in branch:
            out.start()
        for out, back in branch:
            back.wait_recv()
        mine = at_rows(tp, quarter)
        total = branch_buf[mine, :].astype(jnp.float32)
        for step in range(1, QUARTERS):
            total = total + branch_in[step - 1].astype(jnp.float32)
        residual = tokens_ref[mine, :].astype(jnp.float32) + total
        residual_ref[...] = residual
        rstd_two = lax.rsqrt(jnp.mean(residual * residual, axis=1, keepdims=True) + NORM_EPS)
        logits = jnp.zeros((quarter, SMALL), jnp.float32)
        for b in range(E):
            cols = slice(b * block, (b + 1) * block)
            gain = small_full[b, 1:2, :].astype(jnp.float32)
            part = (residual[:, cols] * rstd_two * gain).astype(jnp.bfloat16)
            two_ref[:, cols] = part
            logits = logits + matmul_nt(part, small_full[b])
        lane = lax.broadcasted_iota(jnp.int32, (quarter, SMALL), 1)
        real = (lane >= 2) & (lane < 2 + E)
        masked = jnp.where(real, logits, NEG_FILL)
        odds = jnp.exp(masked - jnp.max(masked, axis=1, keepdims=True))
        odds = jnp.where(real, odds, 0.0)
        probs = odds / jnp.sum(odds, axis=1, keepdims=True)
        expert = lax.broadcasted_iota(jnp.int32, (SMALL, rows), 0) - 2
        named = jnp.zeros((SMALL, rows), jnp.float32)
        for k in range(routes_ref.shape[0]):
            named = named + (routes_ref[k : k + 1, :] == expert).astype(jnp.float32)
        pick = lax.broadcasted_iota(jnp.int32, (quarter, rows), 1) == (
            tp * quarter + lax.broadcasted_iota(jnp.int32, (quarter, rows), 0)
        )
        chosen = matmul_nt(pick.astype(jnp.bfloat16), named.astype(jnp.bfloat16))
        gate_value = 1.0 / (1.0 + jnp.exp(-logits))
        scales = jnp.where(lane == 2 + E, gate_value, probs * chosen)
        scales_ref[...] = jnp.concatenate([scales, probs, chosen], axis=1)
        high = scales.astype(jnp.bfloat16)
        low = (scales - high.astype(jnp.float32)).astype(jnp.bfloat16)
        two_ref[:, width:] = jnp.concatenate(
            [high, low, jnp.zeros((quarter, SIDE - 2 * SMALL), jnp.bfloat16)], axis=1
        )
        keeps = [
            links.inside(attended_ref, attended_out),
            links.inside(query_ref, query_out),
            links.inside(hidden_buf, hidden_out),
            small_keep,
        ]
        for keep in keeps[:3]:
            keep.start()
        for out, back in along:
            out.start()
        for out, back in branch:
            out.wait_send()
        for keep in keeps:
            keep.wait()

    pl.run_scoped(
        attention,
        pltpu.VMEM((rows, width), bf),
        pltpu.VMEM((rows, width), bf),
        pltpu.VMEM((rows, local_width), bf),
        pltpu.VMEM((rows, local_width), bf),
        pltpu.VMEM((3, width, local_width), bf),
        pltpu.VMEM((E, local_width, block), bf),
        pltpu.VMEM((rows, 2 * local_width), bf),
        pltpu.VMEM((E, rows, 2 * local_width), bf),
        pltpu.VMEM((rows, width), bf),
        pltpu.VMEM(shared_raw.shape, bf),
        pltpu.VMEM(shared_up_ref.shape, bf),
    )

    def experts(weights, cot_all, units, first, parts, own_rows, own_cols, staged, cot_rows):
        loads = [
            links.inside(slabs_all.at[g], weights.at[:, pl.ds(g * block, block)]) for g in range(E)
        ]
        loads.append(links.inside(cotangent_all, cot_all.at[:, :, pl.ds(0, cut)]))
        for s in range(QUARTERS):
            q = links.along(QUARTERS - s)
            for k in range(E):
                there = cot_all.at[
                    2 * s + 1 - k % 2, pl.ds((3 - k // 2) * quarter, quarter), pl.ds(cut, width - cut)
                ]
                loads.append(
                    links.inside(cotangent_plane.at[links.peer(k), at_rows(q, quarter)], there)
                )
        along[0][1].wait_recv()
        gathers[1].first()
        along[1][1].wait_recv()
        gathers[2].first()
        gathers[1].second()
        along[2][1].wait_recv()
        gathers[3].first()
        cot.last()
        cot_plane.last()
        for out, back in slab_copies:
            back.wait_recv()
        for copy in slab_own:
            copy.wait()
        for load in loads:
            load.start()

        cot_load = links.inside(cotangent_ref.at[at_rows(tp, quarter)], cot_rows)
        cot_load.start()
        core = [
            links.remote(
                parts.at[s % 2], core_in.at[s % 2], (links.peer(CORE_BIT), tp), core_in.at[s % 2]
            )
            for s in range(QUARTERS)
        ]
        diag, side, rows_along, cols_along = [], [], [], []
        for s in range(QUARTERS):
            held = parts.at[2 + s % 3]
            diag.append(
                [
                    links.remote(
                        held.at[pl.ds(h * (quarter // 2), quarter // 2)],
                        diag_in.at[s, h],
                        (links.peer(bits), tp),
                        diag_in.at[s, h],
                    )
                    for h, bits in enumerate((Y_BIT, X_BIT))
                ]
            )
            side.append(
                [
                    links.remote(
                        held.at[pl.ds((3 - bits // 2) * quarter, quarter)],
                        side_in.at[s, i],
                        (links.peer(bits), tp),
                        side_in.at[s, i],
                    )
                    for i, bits in enumerate((X_BIT, Y_BIT))
                ]
            )
            last = pl.ds(3 * quarter, quarter)
            if s < QUARTERS - 1:
                rows_along.append(
                    links.remote(
                        held.at[last, pl.ds(0, back_width)],
                        rows_in.at[s],
                        (fs, links.along(QUARTERS - 1 - s)),
                        rows_in.at[s],
                    )
                )
            q = links.along(2 * QUARTERS - 1 - s)
            for step in range(1, QUARTERS):
                peer = links.along(step)
                start = pl.multiple_of(back_width + peer * out_width, 128)
                q_there = links.along(2 * QUARTERS - 1 - s - step)
                cols_along.append(
                    links.remote(
                        held.at[last, pl.ds(start, out_width)],
                        cols_in.at[step - 1, at_rows(q, quarter)],
                        (fs, peer),
                        cols_in.at[step - 1, at_rows(q_there, quarter)],
                    )
                )

        sub = lax.broadcasted_iota(jnp.int32, (8, SIDE), 0)
        lane = lax.broadcasted_iota(jnp.int32, (8, SIDE), 1)
        mine, common = 2 + fs, 2 + E
        pick_in = (
            ((sub == 0) & ((lane == mine) | (lane == mine + SMALL)))
            | ((sub == 1) & ((lane == common) | (lane == common + SMALL)))
        ).astype(jnp.bfloat16)
        pick_out = (((sub == 0) & (lane == mine)) | ((sub == 1) & (lane == common))).astype(
            jnp.bfloat16
        )

        def one_block(t, index, slot_out, pause):
            first[: 2 * count] = matmul_nt(weights[: 2 * count], two_all[index, :, :width])
            pause(0)
            first[2 * count :] = matmul_nt(weights[2 * count :], cot_all[index])
            scale = matmul_nt(pick_in, two_all[index, :, width:])
            cols = pl.ds(pl.multiple_of(index * rows, rows), rows)
            dots = []
            shared = count - routed
            groups = ((0, 2 * count, routed), (2 * routed, 2 * count + routed, shared))
            for group, (low, last, size) in enumerate(groups):
                gate = first[low : low + size]
                up = first[low + size : low + 2 * size]
                grad = first[last : last + size]
                by = scale[group : group + 1]
                sigmoid = 1.0 / (1.0 + jnp.exp(-gate))
                silu = gate * sigmoid
                active = silu * up
                units[last : last + size, cols] = (by * active).astype(jnp.bfloat16)
                dots.append(jnp.sum(active * grad, axis=0, keepdims=True))
                active_grad = by * grad
                units[low : low + size, cols] = (
                    active_grad * up * sigmoid * (1.0 + gate * (1.0 - sigmoid))
                ).astype(jnp.bfloat16)
                units[low + size : low + 2 * size, cols] = (active_grad * silu).astype(jnp.bfloat16)
            both = jnp.concatenate([*dots, jnp.zeros((6, rows), jnp.float32)], axis=0)
            pause(1)
            tile = 512

            def put(at, value, other):
                if other is not None:
                    value = value + other[:, at].astype(jnp.float32)
                parts[slot_out, :, at] = value.astype(jnp.bfloat16)

            def products(other):
                put(
                    slice(width, back_width), matmul_tn(both.astype(jnp.bfloat16), pick_out), other
                )
                for n in range(width // tile):
                    at = slice(n * tile, (n + 1) * tile)
                    put(at, matmul_tn(units[: 2 * count, cols], weights[: 2 * count, at]), other)
                    beyond = slice(back_width + n * tile, back_width + (n + 1) * tile)
                    put(beyond, matmul_tn(units[2 * count :, cols], weights[2 * count :, at]), other)

            @pl.when(t % 2 == 0)
            def _():
                products(None)

            @pl.when(t % 2 == 1)
            def _():
                products(core_in.at[(t // 2) % 2])

            pause(3)

        def add_in(held, start, size, others):
            chunk = 32

            @pl.loop(0, size // chunk)
            def _(r):
                at = pl.ds(pl.multiple_of(start + r * chunk, chunk), chunk)
                there = pl.ds(pl.multiple_of(r * chunk, chunk), chunk)
                total = parts[held, at, :].astype(jnp.float32)
                for ref in others:
                    total = total + ref[there, :].astype(jnp.float32)
                parts[held, at, :] = total.astype(jnp.bfloat16)

        def to_core(s):
            if s >= 2:
                pl.semaphore_wait(credit, 1)
            core[s][0].start()

        def diagonal(s):
            if s < 2:
                pl.semaphore_signal(
                    credit, inc=1, device_id=(links.peer(CORE_BIT), tp), device_id_type=MESH
                )
            for out, back in diag[s]:
                out.start()

        def sideways(s):
            for h, (out, back) in enumerate(diag[s]):
                back.wait_recv()
                start = (2 - h) * quarter + h * (quarter // 2)
                add_in(2 + s % 3, start, quarter // 2, [diag_in.at[s, h]])
                side[s][h][0].start()

        def finish(s):
            held = 2 + s % 3
            for out, back in side[s]:
                back.wait_recv()
            last = slice(3 * quarter, rows)
            add_in(held, 3 * quarter, quarter, [side_in.at[s, 0], side_in.at[s, 1]])
            if s == QUARTERS - 1:
                own_rows[...] = parts[held, last, :back_width].astype(jnp.float32)
                parts[held, last, back_width:] = (
                    parts[held, last, back_width:].astype(jnp.float32) + residual_ref[...]
                ).astype(jnp.bfloat16)
            else:
                rows_along[s][0].start()
            for out, back in cols_along[3 * s : 3 * s + 3]:
                out.start()
            start = pl.multiple_of(back_width + tp * out_width, 128)
            own_cols[at_rows(links.along(2 * QUARTERS - 1 - s), quarter), :] = parts[
                held, last, pl.ds(start, out_width)
            ].astype(jnp.float32)

        def before_last():
            core[1][0].wait_send()

        def slot_free():
            for out, back in diag[0] + side[0] + cols_along[:3] + rows_along[:1]:
                out.wait_send()

        plan = {
            (0, 0): [gathers[2].third, gathers[3].second],
            (0, 1): [gathers[3].third],
            (0, 3): [lambda: to_core(0), gathers[0].first, gathers[2].last],
            (1, 1): [core[0][1].wait_recv, gathers[0].second],
            (1, 3): [gathers[0].third, lambda: diagonal(0), gathers[3].last],
            (2, 3): [lambda: to_core(1), lambda: sideways(0)],
            (3, 1): [core[1][1].wait_recv],
            (3, 3): [lambda: diagonal(1)],
            (4, 3): [lambda: to_core(2), lambda: sideways(1)],
            (5, 1): [core[2][1].wait_recv],
            (5, 3): [lambda: diagonal(2), gathers[0].last, lambda: finish(0)],
            (6, 3): [lambda: to_core(3), lambda: sideways(2)],
            (7, 1): [core[3][1].wait_recv],
            (7, 3): [lambda: diagonal(3), lambda: finish(1)],
        }
        before = {4: [core[0][0].wait_send], 6: [before_last], 7: [slot_free]}

        gathers[1].third()
        gathers[2].second()
        for load in loads:
            load.wait()
        gathers[1].last()

        @pl.loop(0, 8)
        def _(t):
            s = t // 2
            slot_out = (1 - t % 2) * (s % 2) + (t % 2) * (2 + s % 3)
            for at, steps in before.items():

                @pl.when(t == at)
                def _(steps=steps):
                    for step in steps:
                        step()

            def pause(point):
                for (at, where), steps in plan.items():
                    if where == point:

                        @pl.when(t == at)
                        def _(steps=steps):
                            for step in steps:
                                step()

            one_block(t, 2 * ((s + 1) % QUARTERS) + t % 2, slot_out, pause)

        keeps = []

        pending = [None, None]

        def settle(place):
            if pending[place] is not None:
                pending[place].wait()
            pending[place] = None

        def weight_grads(bits):
            g = links.peer(bits)
            at = pl.ds(pl.multiple_of(g * block, block), block)
            place = len(keeps) % 2
            settle(place)
            hidden_cols = two_all[:, :, at].reshape(E * rows, block)
            staged[place, : 2 * count] = matmul(units[: 2 * count], hidden_cols).astype(
                jnp.bfloat16
            )
            cot_cols = cot_all[:, :, at].reshape(E * rows, block)
            staged[place, 2 * count :] = matmul(units[2 * count :], cot_cols).astype(jnp.bfloat16)
            keep = links.inside(staged.at[place], grads_out.at[g])
            keep.start()
            keeps.append(keep)
            pending[place] = keep

        results = (up_all, shared_up_all, down_all, shared_down_all)
        early = [copy for bits in EARLY for copy in grad_copies(links, grads_out, results, bits)]
        finish(2)
        for bits in EARLY:
            weight_grads(bits)
        sideways(3)
        settle(0)
        settle(1)
        for out, back in early:
            out.start()
        for bits in (6, 7, 3, 5, 1, 0):
            weight_grads(bits)
        finish(3)
        for out, back in rows_along:
            back.wait_recv()
        total = own_rows[...]
        for step in range(1, QUARTERS):
            total = total + rows_in[step - 1].astype(jnp.float32)
        dots = total[:, width : width + SMALL]
        scales = scales_ref[:, :SMALL]
        probs = scales_ref[:, SMALL : 2 * SMALL]
        chosen = scales_ref[:, 2 * SMALL :]
        chosen_grad = chosen * dots
        logit_grad = probs * (chosen_grad - jnp.sum(probs * chosen_grad, axis=1, keepdims=True))
        gate_lane = lax.broadcasted_iota(jnp.int32, (quarter, SMALL), 1) == 2 + E
        logit_grad = jnp.where(gate_lane, dots * scales * (1.0 - scales), logit_grad).astype(
            jnp.bfloat16
        )
        residual = residual_ref[...]
        rstd = lax.rsqrt(jnp.mean(residual * residual, axis=1, keepdims=True) + NORM_EPS)
        mean = jnp.zeros((quarter, 1), jnp.float32)
        for b in range(E):
            at = slice(b * block, (b + 1) * block)
            two_grad = total[:, at] + matmul(logit_grad, small_full[b])
            normed = residual[:, at] * rstd
            gain = small_full[b, 1:2, :].astype(jnp.float32)
            back_ref[:, at] = two_grad
            mean = mean + jnp.sum(two_grad * gain * normed, axis=1, keepdims=True)
            grads = matmul_tn(logit_grad, two_all[1, 3 * quarter :, at])
            line = lax.broadcasted_iota(jnp.int32, (SMALL, block), 0)
            gain_grad = jnp.sum(two_grad * normed, axis=0, keepdims=True)
            small_grad_ref[:, at] = jnp.where(line == 1, gain_grad, grads)
        mean = mean / width
        cot_load.wait()
        for b in range(E):
            at = slice(b * block, (b + 1) * block)
            gain = small_full[b, 1:2, :].astype(jnp.float32)
            normed = residual[:, at] * rstd
            grad = cot_rows[:, at].astype(jnp.float32) + rstd * (
                back_ref[:, at] * gain - normed * mean
            )
            back_ref[:, at] = grad
            branch_ref[:, at] = grad.astype(jnp.bfloat16)
        for out, back in cols_along:
            back.wait_recv()
        total = own_cols[...]
        for step in range(1, QUARTERS):
            total = total + cols_in[step - 1].astype(jnp.float32)
        output_ref[...] = total.astype(jnp.bfloat16)
        for out, back in core[2:] + rows_along[1:] + cols_along[3:]:
            out.wait_send()
        for s in range(1, QUARTERS):
            for out, back in diag[s] + side[s]:
                out.wait_send()
        for gather in gathers:
            gather.sent()
        for out, back in slab_copies + along:
            out.wait_send()
        settle(0)
        settle(1)
        for out, back in early:
            back.wait_recv()
            out.wait_send()

    pl.run_scoped(
        experts,
        pltpu.VMEM((slab_rows, width), bf),
        pltpu.VMEM((E, rows, width), bf),
        pltpu.VMEM((slab_rows, E * rows), bf),
        pltpu.VMEM((slab_rows, rows), f32),
        pltpu.VMEM((5, rows, whole), bf),
        pltpu.VMEM((quarter, back_width), f32),
        pltpu.VMEM((rows, out_width), f32),
        pltpu.VMEM((2, slab_rows, block), bf),
        pltpu.VMEM((quarter, width), bf),
    )


def layer_call(
    tokens,
    cotangent,
    qkv_weight,
    out_weight,
    norm_gains,
    router_weight,
    shared_gate,
    up,
    shared_up,
    down,
    shared_down,
    cosine,
    sine,
    start,
    routes,
):
    rows, width = tokens.shape
    block = width // E
    local_width = qkv_weight.shape[2]
    quarter = rows // QUARTERS
    out_width = width // QUARTERS
    back_width = width + SIDE
    whole = back_width + width
    routed = down.shape[1]
    slabs = (E, 3 * (routed + shared_down.shape[0] // E), block)
    bf, f32 = jnp.bfloat16, jnp.float32
    sds = jax.ShapeDtypeStruct
    vmem = pl.BlockSpec(memory_space=pltpu.VMEM)
    hbm = pl.BlockSpec(memory_space=pl.ANY)
    outs = [
        (sds((rows, out_width), bf), vmem),
        (sds((quarter, width), bf), vmem),
        (sds((quarter, width), f32), vmem),
        (sds((SMALL, width), f32), vmem),
        (sds(slabs, bf), hbm),
        *((sds(shape, bf), hbm) for shape in grad_shapes(routed, shared_down.shape[0] // E, block)),
        (sds((rows, local_width), bf), hbm),
        (sds((rows, local_width), bf), hbm),
        (sds((rows, width), bf), hbm),
        (sds(slabs, bf), hbm),
        (sds((E, rows, CUT), bf), hbm),
        (sds((E, rows, width - CUT), bf), hbm),
        (sds((E, rows, 2 * local_width), bf), hbm),
        (sds((3, width, local_width), bf), hbm),
        (sds((E, local_width, block), bf), hbm),
        (sds((E, SMALL, block), bf), hbm),
        (sds((2, shared_down.shape[0], block), bf), hbm),
    ]
    return pl.pallas_call(
        functools.partial(layer_kernel, routed),
        name="layer",
        out_shape=[o[0] for o in outs],
        in_specs=[hbm] * 4 + [vmem] * 3 + [hbm] * 4 + [vmem] * 4,
        out_specs=[o[1] for o in outs],
        scratch_shapes=[
            pltpu.VMEM((E, SMALL, block), bf),
            pltpu.VMEM((QUARTERS - 1, quarter, width), bf),
            pltpu.VMEM((quarter, back_width), bf),
            pltpu.VMEM((SMALL, block), bf),
            pltpu.VMEM((quarter, 3 * SMALL), f32),
            pltpu.VMEM((quarter, width), f32),
            pltpu.VMEM((E, rows, back_width), bf),
            pltpu.VMEM((2, rows, whole), bf),
            pltpu.VMEM((QUARTERS, 2, quarter // 2, whole), bf),
            pltpu.VMEM((QUARTERS, 2, quarter, whole), bf),
            pltpu.VMEM((QUARTERS - 1, quarter, back_width), bf),
            pltpu.VMEM((QUARTERS - 1, rows, out_width), bf),
            pltpu.SemaphoreType.DMA((192,)),
            pltpu.SemaphoreType.DMA((192,)),
            pltpu.SemaphoreType.DMA((96,)),
            pltpu.SemaphoreType.REGULAR,
        ],
        compiler_params=pltpu.CompilerParams(
            collective_id=1, has_side_effects=True, vmem_limit_bytes=63 * 2**20
        ),
    )(
        tokens,
        cotangent,
        qkv_weight,
        out_weight,
        norm_gains,
        router_weight,
        shared_gate,
        up,
        shared_up,
        down,
        shared_down,
        cosine,
        sine,
        start,
        routes,
    )


LATE = 20


class Scatter:
    def __init__(self, links, parts, core_in, diag_in, side_in):
        self.links, self.parts = links, parts
        self.core_in, self.diag_in, self.side_in = core_in, diag_in, side_in
        self.rows = parts.shape[1]
        p, tp = links.peer, links.tp
        half = self.rows // 2
        self.core = [
            links.remote(
                parts.at[p(bits + CORE_BIT)], core_in.at[i], (p(CORE_BIT), tp), core_in.at[i]
            )
            for i, bits in enumerate((6, 2, 4, 0))
        ]
        self.diag = [
            links.remote(
                parts.at[p(6), pl.ds(h * half, half)], diag_in.at[h], (p(bits), tp), diag_in.at[h]
            )
            for h, bits in enumerate((Y_BIT, X_BIT))
        ]
        self.side = [
            links.remote(parts.at[p(bits)], side_in.at[i], (p(bits), tp), side_in.at[i])
            for i, bits in enumerate((X_BIT, Y_BIT))
        ]

    def add(self, index, first, count, refs, target=None):
        chunk = 32

        @pl.loop(0, count // chunk)
        def _(r):
            here = pl.ds(pl.multiple_of(first + r * chunk, chunk), chunk)
            there = pl.ds(pl.multiple_of(r * chunk, chunk), chunk)
            total = self.parts[index, here, :].astype(jnp.float32)
            for ref in refs:
                total = total + ref[there, :].astype(jnp.float32)
            if target is None:
                self.parts[index, here, :] = total.astype(jnp.bfloat16)
            else:
                target[here, :] = total

    def to_core(self):
        for out, back in self.core:
            out.start()

    def diagonal(self):
        self.core[0][1].wait_recv()
        self.add(self.links.peer(6), 0, self.rows, [self.core_in.at[0]])
        for out, back in self.diag:
            out.start()

    def sideways(self, i):
        index = self.links.peer((X_BIT, Y_BIT)[i])
        self.core[1 + i][1].wait_recv()
        self.add(index, 0, self.rows, [self.core_in.at[1 + i]])
        self.diag[i][1].wait_recv()
        self.add(index, i * (self.rows // 2), self.rows // 2, [self.diag_in.at[i]])
        self.side[i][0].start()

    def finish(self, target):
        self.core[3][1].wait_recv()
        for out, back in self.side:
            back.wait_recv()
        self.add(
            self.links.fs,
            0,
            self.rows,
            [self.core_in.at[3], self.side_in.at[0], self.side_in.at[1]],
            target,
        )

    def sent(self):
        for out, back in self.core + self.diag + self.side:
            out.wait_send()


def backward_kernel(
    branch_ref,
    residual_hbm,
    small_grad_hbm,
    attended_hbm,
    query_ref,
    hidden_hbm,
    tokens_hbm,
    kv_ref,
    qkv_ref,
    out_ref,
    small_ref,
    cos_ref,
    sin_ref,
    start_ref,
    slabs_ref,
    up_in,
    shared_up_in,
    down_in,
    shared_down_in,
    input_grad_ref,
    qkv_own,
    out_own,
    small_own,
    up_all,
    shared_up_all,
    down_all,
    shared_down_all,
    kv_full,
    qkv_full,
    out_full,
    branch_all,
    odds,
    query_grad,
    projected,
    kv_total,
    kv_parts,
    kv_core,
    kv_diag,
    kv_side,
    query_parts,
    query_core,
    query_diag,
    query_side,
    rest_parts,
    rest_core,
    rest_diag,
    rest_side,
    out_parts,
    out_core,
    out_diag,
    out_side,
    one_parts,
    one_in,
    grad_rows,
    small_parts,
    small_in,
    small_column,
    residual_ref,
    small_grad_ref,
    attended_ref,
    hidden_ref,
    token_rows,
    send,
    recv,
    local,
):
    links = Links(send, recv, local)
    fs, tp = links.fs, links.tp
    quarter, width = residual_ref.shape
    rows = quarter * QUARTERS
    block = width // E
    local_width = query_ref.shape[1]
    heads = local_width // HD
    seqs = rows // SEQ_DEV
    length = E * SEQ_DEV
    scale = HD ** (-0.5)

    def at_rows(index, size):
        return pl.ds(pl.multiple_of(index * size, size), size)

    own = at_rows(tp, quarter)
    links.greet(range(1, 8), range(1, QUARTERS))
    branch = []
    for step in range(1, QUARTERS):
        here = branch_all.at[own]
        landing = branch_all.at[at_rows(links.along(QUARTERS - step), quarter)]
        branch.append(links.remote(branch_ref, here, (fs, links.along(step)), landing))
    for out, back in branch:
        out.start()
    branch_all[own, :] = branch_ref[...]
    results = (up_all, shared_up_all, down_all, shared_down_all)
    slab_copies = []
    for bits in (1, 6, 3, 5, 7):
        slab_copies += grad_copies(links, slabs_ref, results, bits)
    for out, back in slab_copies[:LATE]:
        out.start()
    slab_own = [links.inside(*pair) for pair in grad_pieces(slabs_ref, results, fs, fs)]
    for copy in slab_own:
        copy.start()
    kv_load = links.inside(kv_ref, kv_full)
    kv_load.start()
    out_load = links.inside(out_ref, out_full)
    out_load.start()
    qkv_load = links.inside(qkv_ref, qkv_full)
    qkv_load.start()
    operand_loads = [
        links.inside(attended_hbm, attended_ref),
        links.inside(hidden_hbm, hidden_ref),
        links.inside(residual_hbm, residual_ref),
        links.inside(small_grad_hbm, small_grad_ref),
        links.inside(tokens_hbm.at[own], token_rows),
    ]
    for load in operand_loads:
        load.start()
    kv_sum = Scatter(links, kv_parts, kv_core, kv_diag, kv_side)
    query_sum = Scatter(links, query_parts, query_core, query_diag, query_side)
    rest_sum = Scatter(links, rest_parts, rest_core, rest_diag, rest_side)
    out_sum = Scatter(links, out_parts, out_core, out_diag, out_side)

    kv_load.wait()
    key_pos = lax.broadcasted_iota(jnp.int32, (SEQ_DEV, length), 1)
    query_pos = fs * SEQ_DEV + lax.broadcasted_iota(jnp.int32, (SEQ_DEV, length), 0)
    for s in range(seqs):
        here = slice(s * SEQ_DEV, (s + 1) * SEQ_DEV)
        allowed = (key_pos <= query_pos) & (key_pos >= as_column(start_ref[s : s + 1, :]))
        for h in range(heads):
            cols = slice(h * HD, (h + 1) * HD)
            keys = kv_full[:, here, cols].reshape(length, HD)
            scores = matmul_nt(query_ref[here, cols], keys) * scale
            scores = jnp.where(allowed, scores, NEG_FILL)
            top = jnp.max(scores, axis=1, keepdims=True)
            weights = jnp.exp(scores - top)
            odds[s * heads + h] = weights / jnp.sum(weights, axis=1, keepdims=True)
    out_load.wait()
    for out, back in branch:
        back.wait_recv()
    attended_grad = jnp.zeros((rows, local_width), jnp.float32)
    for b in range(E):
        attended_grad = attended_grad + matmul_nt(
            branch_all[:, b * block : (b + 1) * block], out_full[b]
        )
    query_grad[...] = attended_grad.astype(jnp.bfloat16)
    for s in range(seqs):
        here = slice(s * SEQ_DEV, (s + 1) * SEQ_DEV)
        for h in range(heads):
            cols = slice(h * HD, (h + 1) * HD)
            vcols = slice(local_width + h * HD, local_width + (h + 1) * HD)
            keys = kv_full[:, here, cols].reshape(length, HD)
            values = kv_full[:, here, vcols].reshape(length, HD)
            grad = query_grad[here, cols]
            probs = odds[s * heads + h]
            weights_grad = matmul_nt(grad, values)
            delta = jnp.sum(probs * weights_grad, axis=1, keepdims=True)
            score_grad = (probs * (weights_grad - delta)).astype(jnp.bfloat16)
            key_grad = matmul_tn(score_grad, query_ref[here, cols]) * scale
            value_grad = matmul_tn(probs.astype(jnp.bfloat16), grad)
            kv_parts[:, here, cols] = key_grad.astype(jnp.bfloat16).reshape(E, SEQ_DEV, HD)
            kv_parts[:, here, vcols] = value_grad.astype(jnp.bfloat16).reshape(E, SEQ_DEV, HD)
            projected[0, here, cols] = turn(
                matmul(score_grad, keys) * scale, cos_ref[here, :], -sin_ref[here, :]
            ).astype(jnp.bfloat16)
    kv_sum.to_core()
    for load in operand_loads:
        load.wait()
    attended = attended_ref[...]
    for b in range(E):
        cols = slice(b * block, (b + 1) * block)
        out_parts[b] = matmul_tn(attended, branch_all[:, cols]).astype(jnp.bfloat16)
    def weight_grad(j):
        for b in range(E):
            cols = slice(b * block, (b + 1) * block)
            part = matmul_tn(hidden_ref[:, cols], projected[j]).astype(jnp.bfloat16)
            if j == 0:
                query_parts[b] = part
            else:
                rest_parts[b, (j - 1) * block : j * block] = part

    kv_sum.diagonal()
    out_sum.to_core()
    weight_grad(0)
    query_sum.to_core()
    kv_sum.sideways(0)
    kv_sum.sideways(1)
    out_sum.diagonal()
    query_sum.diagonal()
    qkv_load.wait()
    kv_sum.finish(kv_total)
    for out, back in slab_copies[LATE:]:
        out.start()
    projected[1] = turn(kv_total[:, :local_width], cos_ref[...], -sin_ref[...]).astype(jnp.bfloat16)
    projected[2] = kv_total[:, local_width:].astype(jnp.bfloat16)
    for b in range(E):
        cols = slice(b * block, (b + 1) * block)
        part = jnp.zeros((rows, block), jnp.float32)
        for j in range(3):
            part = part + matmul_nt(projected[j], qkv_full[j, cols])
        one_parts[:, cols] = part.astype(jnp.bfloat16)
    column = []
    for step in range(1, QUARTERS):
        peer = links.along(step)
        column.append(
            links.remote(
                one_parts.at[at_rows(peer, quarter)],
                one_in.at[step - 1],
                (fs, peer),
                one_in.at[step - 1],
            )
        )
    for out, back in column:
        out.start()
    weight_grad(1)
    weight_grad(2)
    rest_sum.to_core()
    out_sum.sideways(0)
    out_sum.sideways(1)
    query_sum.sideways(0)
    query_sum.sideways(1)
    rest_sum.diagonal()
    for out, back in column:
        back.wait_recv()
    tokens = token_rows[...].astype(jnp.float32)
    rstd = lax.rsqrt(jnp.mean(tokens * tokens, axis=1, keepdims=True) + NORM_EPS)
    total = one_parts[own, :].astype(jnp.float32)
    for step in range(1, QUARTERS):
        total = total + one_in[step - 1].astype(jnp.float32)
    mean = jnp.zeros((quarter, 1), jnp.float32)
    sub = lax.broadcasted_iota(jnp.int32, (SMALL, block), 0)
    for b in range(E):
        at = slice(b * block, (b + 1) * block)
        gain = small_ref[b, 0:1, :].astype(jnp.float32)
        normed = tokens[:, at] * rstd
        mean = mean + jnp.sum(total[:, at] * gain * normed, axis=1, keepdims=True)
        gain_grad = jnp.sum(total[:, at] * normed, axis=0, keepdims=True)
        small_parts[b] = jnp.where(sub == 0, gain_grad, small_grad_ref[:, at])
    mean = mean / width
    for b in range(E):
        at = slice(b * block, (b + 1) * block)
        gain = small_ref[b, 0:1, :].astype(jnp.float32)
        normed = tokens[:, at] * rstd
        grad_rows[:, at] = (
            residual_ref[:, at] + rstd * (total[:, at] * gain - normed * mean)
        ).astype(jnp.bfloat16)
    spread = []
    for step in range(1, QUARTERS):
        peer = links.along(step)
        landing = input_grad_ref.at[at_rows(links.along(QUARTERS - step), quarter)]
        spread.append(links.remote(grad_rows, input_grad_ref.at[own], (fs, peer), landing))
    for out, back in spread:
        out.start()
    keep = links.inside(grad_rows, input_grad_ref.at[own])
    keep.start()
    small_copies = []
    for bits in range(1, E):
        peer = links.peer(bits)
        small_copies.append(
            links.remote(
                small_parts.at[peer], small_in.at[bits - 1], (peer, tp), small_in.at[bits - 1]
            )
        )
    for out, back in small_copies:
        out.start()
    rest_sum.sideways(0)
    rest_sum.sideways(1)
    out_sum.finish(out_own)
    query_sum.finish(qkv_own.at[pl.ds(0, block)])
    for out, back in small_copies:
        back.wait_recv()
    small_total = small_parts[fs]
    for bits in range(1, E):
        small_total = small_total + small_in[bits - 1]
    small_column[tp] = small_total
    small_spread = []
    for step in range(1, QUARTERS):
        here = small_column.at[tp]
        landing = small_column.at[links.along(QUARTERS - step)]
        small_spread.append(links.remote(here, here, (fs, links.along(step)), landing))
    for out, back in small_spread:
        out.start()
    rest_sum.finish(qkv_own.at[pl.ds(block, 2 * block)])
    for out, back in small_spread:
        back.wait_recv()
    small_own[...] = small_column[0] + small_column[1] + small_column[2] + small_column[3]
    for out, back in spread + slab_copies:
        back.wait_recv()
    for copy in (*slab_own, keep):
        copy.wait()
    for out, back in branch + slab_copies + column + spread + small_copies + small_spread:
        out.wait_send()
    for scatter in (kv_sum, out_sum, query_sum, rest_sum):
        scatter.sent()


def backward_call(
    branch_rows,
    residual_grad,
    small_grad,
    attended,
    query_rows,
    hidden_one,
    tokens,
    kv_all,
    qkv_full,
    out_full,
    small_full,
    cosine,
    sine,
    start,
    slabs,
    *parts,
):
    quarter, width = residual_grad.shape
    rows = quarter * QUARTERS
    block = width // E
    local_width = query_rows.shape[1]
    bf, f32 = jnp.bfloat16, jnp.float32
    sds = jax.ShapeDtypeStruct
    vmem = pl.BlockSpec(memory_space=pltpu.VMEM)
    hbm = pl.BlockSpec(memory_space=pl.ANY)
    outs = [
        (sds((rows, width), bf), hbm),
        (sds((3 * block, local_width), f32), vmem),
        (sds((local_width, block), f32), vmem),
        (sds((SMALL, block), f32), vmem),
        *((sds(part.shape, bf), hbm) for part in parts),
    ]

    def scatter_scratch(count, columns):
        return [
            pltpu.VMEM((E, count, columns), bf),
            pltpu.VMEM((4, count, columns), bf),
            pltpu.VMEM((2, count // 2, columns), bf),
            pltpu.VMEM((2, count, columns), bf),
        ]

    return pl.pallas_call(
        backward_kernel,
        name="attention_backward",
        out_shape=[o[0] for o in outs],
        in_specs=[vmem] + [hbm] * 3 + [vmem] + [hbm] * 5 + [vmem] * 4 + [hbm] * 5,
        out_specs=[o[1] for o in outs],
        input_output_aliases={15 + i: 4 + i for i in range(4)},
        scratch_shapes=[
            pltpu.VMEM((E, rows, 2 * local_width), bf),
            pltpu.VMEM((3, width, local_width), bf),
            pltpu.VMEM((E, local_width, block), bf),
            pltpu.VMEM((rows, width), bf),
            pltpu.VMEM((rows // SEQ_DEV * local_width // HD, SEQ_DEV, E * SEQ_DEV), f32),
            pltpu.VMEM((rows, local_width), bf),
            pltpu.VMEM((3, rows, local_width), bf),
            pltpu.VMEM((rows, 2 * local_width), f32),
            *scatter_scratch(rows, 2 * local_width),
            *scatter_scratch(block, local_width),
            *scatter_scratch(2 * block, local_width),
            *scatter_scratch(local_width, block),
            pltpu.VMEM((rows, width), bf),
            pltpu.VMEM((QUARTERS - 1, quarter, width), bf),
            pltpu.VMEM((quarter, width), bf),
            pltpu.VMEM((E, SMALL, block), f32),
            pltpu.VMEM((E - 1, SMALL, block), f32),
            pltpu.VMEM((QUARTERS, SMALL, block), f32),
            pltpu.VMEM((quarter, width), f32),
            pltpu.VMEM((SMALL, width), f32),
            pltpu.VMEM((rows, local_width), bf),
            pltpu.VMEM((rows, width), bf),
            pltpu.VMEM((quarter, width), bf),
            pltpu.SemaphoreType.DMA((96,)),
            pltpu.SemaphoreType.DMA((96,)),
            pltpu.SemaphoreType.DMA((16,)),
        ],
        compiler_params=pltpu.CompilerParams(
            collective_id=3, has_side_effects=True, vmem_limit_bytes=62 * 2**20
        ),
    )(
        branch_rows,
        residual_grad,
        small_grad,
        attended,
        query_rows,
        hidden_one,
        tokens,
        kv_all,
        qkv_full,
        out_full,
        small_full,
        cosine,
        sine,
        start,
        slabs,
        *parts,
    )


def finish_kernel(
    up_ref,
    down_ref,
    shared_ref,
    grad_ref,
    qkv_ref,
    out_ref,
    output_ref,
    shared_up_ref,
    small_ref,
    up,
    down,
    shared,
    grad,
    qkv,
    out,
    output,
    shared_up,
    gains,
    router,
    gate,
):
    up[...] = up_ref[...].astype(jnp.float32)
    down[...] = down_ref[...].astype(jnp.float32)
    shared[...] = shared_ref[...].astype(jnp.float32)
    grad[...] = grad_ref[...].astype(jnp.float32)
    qkv[...] = qkv_ref[...]
    out[...] = out_ref[...]
    output[...] = output_ref[...]
    for k in range(2):
        shared_up[:, k, :] = shared_up_ref[k].astype(jnp.float32).T
    gains[...] = small_ref[0:2, :]
    router[...] = small_ref[2 : 2 + E, :]
    gate[...] = small_ref[2 + E : 3 + E, :]


def finish_call(up, down, shared, grad, qkv, out, output, shared_up, small):
    steps = 2
    f32 = jnp.float32
    sds = jax.ShapeDtypeStruct
    block = small.shape[1]
    arrays = (up, down, shared, grad, qkv, out, output)
    shared_shape = (block, 2, shared_up.shape[1])

    def split(shape):
        part = (shape[0] // steps, *shape[1:])
        return pl.BlockSpec(part, lambda i: (i,) + (0,) * (len(part) - 1))

    def once(shape):
        return pl.BlockSpec(shape, lambda i: (0, 0))

    specs = [split(array.shape) for array in arrays]
    turned = pl.BlockSpec((*shared_up.shape[:2], block // steps), lambda i: (0, 0, i))
    types = (f32, f32, f32, f32, f32, f32, output.dtype)
    return pl.pallas_call(
        finish_kernel,
        name="finish",
        grid=(steps,),
        out_shape=[sds(a.shape, t) for a, t in zip(arrays, types, strict=True)]
        + [sds(shared_shape, f32)]
        + [sds((n, block), f32) for n in (2, E, 1)],
        in_specs=[*specs, turned, once(small.shape)],
        out_specs=[*specs, split(shared_shape), *(once((n, block)) for n in (2, E, 1))],
        compiler_params=pltpu.CompilerParams(vmem_limit_bytes=60 * 2**20),
    )(*arrays, shared_up, small)


def shards_units(
    tokens,
    cotangent,
    qkv_weight,
    out_weight,
    norm_gains,
    router_weight,
    shared_gate,
    expert_gate_up,
    expert_down,
    shared_gate_up,
    shared_down,
    routes,
    doc_start,
):
    tok_rows, width = tokens.shape
    seq_count = tok_rows // SEQ_DEV
    fs_index = lax.axis_index("fs")
    query_pos = fs_index * SEQ_DEV + jnp.arange(SEQ_DEV, dtype=jnp.int32)
    positions = jnp.tile(query_pos, seq_count)
    half_cos, half_sin = rope_tables(positions)
    cosine = jnp.concatenate([half_cos, half_cos], axis=1)
    sine = jnp.concatenate([-half_sin, half_sin], axis=1)
    routed_units = expert_down.shape[1]
    (
        output,
        branch_rows,
        residual_grad,
        small_grad,
        grad_slabs,
        up_part,
        shared_up_part,
        down_part,
        shared_down_part,
        attended,
        query_rows,
        hidden_one,
        _,
        _,
        _,
        kv_all,
        qkv_full,
        out_full,
        small_full,
        _,
    ) = layer_call(
        tokens,
        cotangent,
        qkv_weight,
        out_weight,
        norm_gains,
        router_weight,
        shared_gate.reshape(2, -1),
        jnp.transpose(expert_gate_up, (0, 2, 3, 1)).reshape(E, 2 * routed_units, -1),
        shared_gate_up,
        expert_down,
        shared_down,
        cosine,
        sine,
        doc_start.reshape(seq_count, SEQ_DEV),
        routes.T,
    )
    input_grad, qkv_own, out_own, small_own, up_own, shared_up_own, down_own, shared_down_own = (
        backward_call(
            branch_rows,
            residual_grad,
            small_grad,
            attended,
            query_rows,
            hidden_one,
            tokens,
            kv_all,
            qkv_full,
            out_full,
            small_full,
            cosine,
            sine,
            doc_start.reshape(seq_count, SEQ_DEV),
            grad_slabs,
            up_part,
            shared_up_part,
            down_part,
            shared_down_part,
        )
    )
    (
        up_own,
        down_own,
        shared_down_own,
        input_grad,
        qkv_own,
        out_own,
        output,
        shared_up_own,
        gains,
        router,
        gate,
    ) = finish_call(
        up_own,
        down_own,
        shared_down_own,
        input_grad,
        qkv_own,
        out_own,
        output,
        shared_up_own,
        small_own,
    )
    up_own = up_own.reshape(E, 2, routed_units, -1)
    return (
        output,
        input_grad,
        qkv_own.reshape(qkv_weight.shape),
        out_own,
        gains,
        router,
        gate[0],
        jnp.transpose(up_own, (0, 3, 1, 2)),
        down_own,
        shared_up_own,
        shared_down_own,
    )


def solution(mesh):
    return jax.shard_map(
        shards_units if dict(mesh.shape) == {"fs": E, "tp": QUARTERS} else shards_gathered,
        mesh=mesh,
        in_specs=(
            P("fs", None),
            P("fs", None),
            P(None, "fs", "tp"),
            P("tp", "fs"),
            P(None, "fs"),
            P(None, "fs"),
            P("fs"),
            P(None, "fs", None, "tp"),
            P(None, "tp", "fs"),
            P("fs", None, "tp"),
            P("tp", "fs"),
            P("fs", None),
            P("fs"),
        ),
        out_specs=(
            P("fs", "tp"),
            P("fs", None),
            P(None, "fs", "tp"),
            P("tp", "fs"),
            P(None, "fs"),
            P(None, "fs"),
            P("fs"),
            P(None, "fs", None, "tp"),
            P(None, "tp", "fs"),
            P("fs", None, "tp"),
            P("tp", "fs"),
        ),
        check_vma=False,
    )
```

```python
import functools
import math

import jax
import jax.numpy as jnp
from jax import lax
from jax.experimental import pallas as pl
from jax.experimental.pallas import tpu as pltpu
from jax.sharding import PartitionSpec as P

HD = 128
E = 8
SEQ_DEV = 128
SIDE = 128


NORM_EPS = 1e-06
NEG_FILL = -1e30
ROPE_BASE = 1000000.0


def rope_tables(positions):
    half_size = HD // 2
    frequency = ROPE_BASE ** (-(jnp.arange(half_size, dtype=jnp.float32) * 2.0 / HD))
    angles = positions.astype(jnp.float32)[:, None] * frequency[None, :]
    return (jnp.cos(angles), jnp.sin(angles))


def rotate(values, cosine, sine_table):
    shaped = values.reshape(values.shape[0], -1, HD)
    half_size = HD // 2
    first_half = shaped[..., :half_size]
    second_half = shaped[..., half_size:]
    cos_part = cosine[:, None, :]
    sin_part = sine_table[:, None, :]
    turned = jnp.concatenate(
        [
            first_half * cos_part - second_half * sin_part,
            second_half * cos_part + first_half * sin_part,
        ],
        axis=-1,
    )
    return turned.reshape(values.shape)


def key_mask(query_pos, query_start, first_dev, group_size):
    key_pos = (first_dev + jnp.arange(group_size, dtype=jnp.int32)[:, None]) * SEQ_DEV + jnp.arange(
        SEQ_DEV, dtype=jnp.int32
    )[None, :]
    key_pos = key_pos[None, None, :, :]
    return (key_pos <= query_pos[None, :, None, None]) & (key_pos >= query_start[:, :, None, None])


def shards_gathered(
    tokens,
    cotangent,
    qkv_weight,
    out_weight,
    norm_gains,
    router_weight,
    shared_gate,
    expert_gate_up,
    expert_down,
    shared_gate_up,
    shared_down,
    routes,
    doc_start,
):
    tok_rows = tokens.shape[0]
    seq_count = tok_rows // SEQ_DEV
    local_width = qkv_weight.shape[2]
    head_count = local_width // HD
    out_width = tokens.shape[1] // lax.axis_size("tp")
    score_scale = HD ** (-0.5)
    fs_index = lax.axis_index("fs")
    tp_index = lax.axis_index("tp")
    query_pos = fs_index * SEQ_DEV + jnp.arange(SEQ_DEV, dtype=jnp.int32)
    positions = jnp.tile(query_pos, seq_count)
    query_start = doc_start.reshape(seq_count, SEQ_DEV)
    cosine, sine_table = rope_tables(positions)
    group_limit = max(1, 512 // SEQ_DEV)
    qkv_full, out_full, gains_full, router_full, shared_gate_full = (
        lax.all_gather(qkv_weight, "fs", axis=1, tiled=True),
        lax.all_gather(out_weight, "fs", axis=1, tiled=True),
        lax.all_gather(norm_gains, "fs", axis=1, tiled=True),
        lax.all_gather(router_weight, "fs", axis=1, tiled=True),
        lax.all_gather(shared_gate, "fs", axis=0, tiled=True),
    )
    token_float = tokens.astype(jnp.float32)
    rstd_one = lax.rsqrt(jnp.mean(token_float * token_float, axis=1, keepdims=True) + NORM_EPS)
    normed_one = token_float * rstd_one
    hidden_one = (normed_one * gains_full[0].astype(jnp.float32)[None, :]).astype(jnp.bfloat16)
    projected = jnp.einsum("td,jdf->jtf", hidden_one, qkv_full, preferred_element_type=jnp.float32)
    query_rows = rotate(projected[0], cosine, sine_table).astype(jnp.bfloat16)
    key_own = rotate(projected[1], cosine, sine_table).astype(jnp.bfloat16)
    value_own = projected[2].astype(jnp.bfloat16)
    query_heads = query_rows.reshape(seq_count, SEQ_DEV, head_count, HD)

    def score_block(key_group, first_dev):
        allowed = key_mask(query_pos, query_start, first_dev, key_group.shape[0])[:, None]
        scores = (
            jnp.einsum(
                "pqhd,gpkhd->phqgk", query_heads, key_group, preferred_element_type=jnp.float32
            )
            * score_scale
        )
        return (jnp.where(allowed, scores, NEG_FILL), allowed)

    def forward_update(running, key_group, value_group, first_dev):
        run_max, run_sum, accumulated = running
        scores, allowed = score_block(key_group, first_dev)
        new_max = jnp.maximum(run_max, jnp.max(scores, axis=(3, 4)))
        weights = jnp.where(allowed, jnp.exp(scores - new_max[..., None, None]), 0.0)
        factor = jnp.exp(run_max - new_max)
        new_sum = run_sum * factor + jnp.sum(weights, axis=(3, 4))
        mixed_part = jnp.einsum(
            "phqgk,gpkhd->pqhd",
            weights.astype(jnp.bfloat16),
            value_group,
            preferred_element_type=jnp.float32,
        )
        new_accum = accumulated * jnp.transpose(factor, (0, 2, 1))[..., None] + mixed_part
        return (new_max, new_sum, new_accum)

    initial = (
        jnp.full((seq_count, head_count, SEQ_DEV), NEG_FILL, jnp.float32),
        jnp.zeros((seq_count, head_count, SEQ_DEV), jnp.float32),
        jnp.zeros((seq_count, SEQ_DEV, head_count, HD), jnp.float32),
    )
    running = initial
    key_piece = lax.all_gather(key_own, "fs", axis=0, tiled=True)
    value_piece = lax.all_gather(value_own, "fs", axis=0, tiled=True)
    shard_count = key_piece.shape[0] // tok_rows
    group_size = math.gcd(shard_count, group_limit)
    step_count = shard_count // group_size
    shaped = (step_count, group_size, seq_count, SEQ_DEV, head_count, HD)
    first_dev = jnp.int32(0) // tok_rows

    def one_step(carried, inputs):
        key_group, value_group, group_index = inputs
        start_dev = group_index * group_size
        updated = lax.cond(
            start_dev <= fs_index,
            lambda state_in: forward_update(state_in, key_group, value_group, start_dev),
            lambda state_in: state_in,
            carried,
        )
        return (updated, None)

    running, ignored = lax.scan(
        one_step,
        running,
        (
            key_piece.reshape(shaped),
            value_piece.reshape(shaped),
            jnp.arange(step_count, dtype=jnp.int32),
        ),
    )
    run_max, run_sum, accumulated = running
    attended_heads = (accumulated / jnp.transpose(run_sum, (0, 2, 1))[..., None]).astype(
        jnp.bfloat16
    )
    log_total = run_max + jnp.log(run_sum)
    attended = attended_heads.reshape(tok_rows, local_width)
    branch_part = jnp.dot(attended, out_full, preferred_element_type=jnp.float32)
    branch = lax.psum(branch_part.astype(jnp.bfloat16), "tp").astype(jnp.float32)
    residual = token_float + branch
    rstd_two = lax.rsqrt(jnp.mean(residual * residual, axis=1, keepdims=True) + NORM_EPS)
    normed_two = residual * rstd_two
    hidden_two = (normed_two * gains_full[1].astype(jnp.float32)[None, :]).astype(jnp.bfloat16)
    expert_gate_all, expert_down_all, shared_up_all, shared_down_all = (
        lax.all_gather(expert_gate_up, "fs", axis=1, tiled=True),
        lax.all_gather(expert_down, "fs", axis=2, tiled=True),
        lax.all_gather(shared_gate_up, "fs", axis=0, tiled=True),
        lax.all_gather(shared_down, "fs", axis=1, tiled=True),
    )
    logits = jnp.einsum("td,ed->te", hidden_two, router_full, preferred_element_type=jnp.float32)
    router_probs = jax.nn.softmax(logits, axis=-1)
    chosen = jnp.sum(
        (routes[:, :, None] == jnp.arange(E, dtype=jnp.int32)[None, None, :]).astype(jnp.float32),
        axis=1,
    )
    gate_weights = router_probs * chosen
    gate_up = jnp.einsum(
        "td,edkf->tekf", hidden_two, expert_gate_all, preferred_element_type=jnp.float32
    )
    gate_part = gate_up[:, :, 0]
    up_part = gate_up[:, :, 1]
    gate_sigmoid = jax.nn.sigmoid(gate_part)
    active = gate_part * gate_sigmoid * up_part
    hidden = (gate_weights[:, :, None] * active).astype(jnp.bfloat16)
    shared_in = jnp.einsum(
        "td,dkf->tkf", hidden_two, shared_up_all, preferred_element_type=jnp.float32
    )
    shared_gate_in = shared_in[:, 0]
    shared_up_in = shared_in[:, 1]
    shared_sigmoid = jax.nn.sigmoid(shared_gate_in)
    shared_active = shared_gate_in * shared_sigmoid * shared_up_in
    gate_logit = jnp.einsum(
        "td,d->t", hidden_two, shared_gate_full, preferred_element_type=jnp.float32
    )
    gate_value = jax.nn.sigmoid(gate_logit)
    shared_hidden = (gate_value[:, None] * shared_active).astype(jnp.bfloat16)
    mixture_part = jnp.einsum(
        "tef,efd->td", hidden, expert_down_all, preferred_element_type=jnp.float32
    ) + jnp.dot(shared_hidden, shared_down_all, preferred_element_type=jnp.float32)
    mixture = lax.psum_scatter(
        mixture_part.astype(jnp.bfloat16), "tp", scatter_dimension=1, tiled=True
    ).astype(jnp.float32)
    output = (
        lax.dynamic_slice_in_dim(residual, tp_index * out_width, out_width, 1) + mixture
    ).astype(jnp.bfloat16)
    qkv_back, out_back, gains_back, router_back, shared_gate_back = (
        lax.all_gather(qkv_weight, "fs", axis=1, tiled=True),
        lax.all_gather(out_weight, "fs", axis=1, tiled=True),
        lax.all_gather(norm_gains, "fs", axis=1, tiled=True),
        lax.all_gather(router_weight, "fs", axis=1, tiled=True),
        lax.all_gather(shared_gate, "fs", axis=0, tiled=True),
    )
    expert_gate_back, expert_down_back, shared_up_back, shared_down_back = (
        lax.all_gather(expert_gate_up, "fs", axis=1, tiled=True),
        lax.all_gather(expert_down, "fs", axis=2, tiled=True),
        lax.all_gather(shared_gate_up, "fs", axis=0, tiled=True),
        lax.all_gather(shared_down, "fs", axis=1, tiled=True),
    )
    hidden_grad = jnp.einsum(
        "td,efd->tef", cotangent, expert_down_back, preferred_element_type=jnp.float32
    )
    expert_down_grad = jnp.einsum(
        "tef,td->efd", hidden, cotangent, preferred_element_type=jnp.float32
    )
    shared_grad = jnp.einsum(
        "td,fd->tf", cotangent, shared_down_back, preferred_element_type=jnp.float32
    )
    shared_down_grad = jnp.einsum(
        "tf,td->fd", shared_hidden, cotangent, preferred_element_type=jnp.float32
    )
    gate_dot = jnp.sum(active * hidden_grad, axis=2)
    shared_dot = jnp.sum(shared_active * shared_grad, axis=1)
    active_grad = gate_weights[:, :, None] * hidden_grad
    gate_grad = active_grad * up_part * gate_sigmoid * (1.0 + gate_part * (1.0 - gate_sigmoid))
    up_grad = active_grad * gate_part * gate_sigmoid
    gate_up_grad = jnp.stack([gate_grad, up_grad], axis=2).astype(jnp.bfloat16)
    shared_active_grad = gate_value[:, None] * shared_grad
    shared_gate_grad = (
        shared_active_grad
        * shared_up_in
        * shared_sigmoid
        * (1.0 + shared_gate_in * (1.0 - shared_sigmoid))
    )
    shared_unit_grad = shared_active_grad * shared_gate_in * shared_sigmoid
    shared_up_grad = jnp.stack([shared_gate_grad, shared_unit_grad], axis=1).astype(jnp.bfloat16)
    expert_gate_grad = jnp.einsum(
        "td,tekf->edkf", hidden_two, gate_up_grad, preferred_element_type=jnp.float32
    )
    shared_proj_grad = jnp.einsum(
        "td,tkf->dkf", hidden_two, shared_up_grad, preferred_element_type=jnp.float32
    )
    input_part = jnp.einsum(
        "tekf,edkf->td", gate_up_grad, expert_gate_back, preferred_element_type=jnp.float32
    ) + jnp.einsum(
        "tkf,dkf->td", shared_up_grad, shared_up_back, preferred_element_type=jnp.float32
    )
    input_sum, gate_sum, shared_sum = (
        lax.psum(input_part.astype(jnp.bfloat16), "tp").astype(jnp.float32),
        lax.psum(gate_dot.astype(jnp.bfloat16), "tp").astype(jnp.float32),
        lax.psum(shared_dot.astype(jnp.bfloat16), "tp").astype(jnp.float32),
    )
    chosen_grad = chosen * gate_sum
    logit_grad = (
        router_probs * (chosen_grad - jnp.sum(router_probs * chosen_grad, axis=1, keepdims=True))
    ).astype(jnp.bfloat16)
    gate_logit_grad = (shared_sum * gate_value * (1.0 - gate_value)).astype(jnp.bfloat16)
    router_grad = jnp.einsum(
        "te,td->ed", logit_grad, hidden_two, preferred_element_type=jnp.float32
    )
    shared_vector_grad = jnp.einsum(
        "t,td->d", gate_logit_grad, hidden_two, preferred_element_type=jnp.float32
    )
    two_grad = (
        input_sum
        + jnp.einsum("te,ed->td", logit_grad, router_back, preferred_element_type=jnp.float32)
        + gate_logit_grad.astype(jnp.float32)[:, None]
        * shared_gate_back.astype(jnp.float32)[None, :]
    )
    scaled_two = two_grad * gains_back[1].astype(jnp.float32)[None, :]
    gain_two_grad = jnp.sum(two_grad * normed_two, axis=0)
    residual_grad = cotangent.astype(jnp.float32) + rstd_two * (
        scaled_two - normed_two * jnp.mean(scaled_two * normed_two, axis=1, keepdims=True)
    )
    branch_grad = residual_grad.astype(jnp.bfloat16)
    out_grad = jnp.einsum("tf,td->fd", attended, branch_grad, preferred_element_type=jnp.float32)
    attended_grad = jnp.einsum(
        "td,fd->tf", branch_grad, out_back, preferred_element_type=jnp.float32
    ).astype(jnp.bfloat16)
    grad_heads = attended_grad.reshape(seq_count, SEQ_DEV, head_count, HD)
    delta_rows = jnp.einsum(
        "pqhd,pqhd->phq", grad_heads, attended_heads, preferred_element_type=jnp.float32
    )
    key_all, value_all = (
        lax.all_gather(key_own, "fs", axis=0, tiled=True),
        lax.all_gather(value_own, "fs", axis=0, tiled=True),
    )
    device_count = key_all.shape[0] // tok_rows
    back_group = math.gcd(device_count, group_limit)
    back_steps = device_count // back_group
    back_shape = (back_steps, back_group, seq_count, SEQ_DEV, head_count, HD)

    def backward_update(key_group, value_group, start_dev):
        scores, allowed = score_block(key_group, start_dev)
        probs_block = jnp.where(allowed, jnp.exp(scores - log_total[..., None, None]), 0.0)
        weights_grad = jnp.einsum(
            "pqhd,gpkhd->phqgk", grad_heads, value_group, preferred_element_type=jnp.float32
        )
        score_grad = (probs_block * (weights_grad - delta_rows[..., None, None])).astype(
            jnp.bfloat16
        )
        query_part = (
            jnp.einsum(
                "phqgk,gpkhd->pqhd", score_grad, key_group, preferred_element_type=jnp.float32
            )
            * score_scale
        )
        key_part = (
            jnp.einsum(
                "phqgk,pqhd->gpkhd", score_grad, query_heads, preferred_element_type=jnp.float32
            )
            * score_scale
        )
        value_part = jnp.einsum(
            "phqgk,pqhd->gpkhd",
            probs_block.astype(jnp.bfloat16),
            grad_heads,
            preferred_element_type=jnp.float32,
        )
        return (query_part, key_part, value_part)

    empty_grads = (
        jnp.zeros((seq_count, SEQ_DEV, head_count, HD), jnp.float32),
        jnp.zeros((back_group, seq_count, SEQ_DEV, head_count, HD), jnp.float32),
        jnp.zeros((back_group, seq_count, SEQ_DEV, head_count, HD), jnp.float32),
    )
    scan_inputs = (
        key_all.reshape(back_shape),
        value_all.reshape(back_shape),
        jnp.arange(back_steps, dtype=jnp.int32),
    )

    def back_step(query_acc, inputs):
        key_group, value_group, group_index = inputs
        start_dev = group_index * back_group
        query_part, key_part, value_part = lax.cond(
            start_dev <= fs_index,
            lambda ignored_in: backward_update(key_group, value_group, start_dev),
            lambda ignored_in: empty_grads,
            key_group,
        )
        term_rows = jnp.concatenate(
            [
                key_part.reshape(back_group * tok_rows, local_width),
                value_part.reshape(back_group * tok_rows, local_width),
            ],
            axis=1,
        )
        return (query_acc + query_part, term_rows)

    query_grad, key_value_terms = lax.scan(back_step, empty_grads[0], scan_inputs)
    key_value_sum = lax.psum_scatter(
        key_value_terms.reshape(device_count * tok_rows, 2 * local_width).astype(jnp.bfloat16),
        "fs",
        scatter_dimension=0,
        tiled=True,
    ).astype(jnp.float32)
    key_grad_rows = key_value_sum[:, :local_width]
    value_grad_rows = key_value_sum[:, local_width:]
    projected_grad = jnp.stack(
        [
            rotate(query_grad.reshape(tok_rows, local_width), cosine, -sine_table),
            rotate(key_grad_rows, cosine, -sine_table),
            value_grad_rows,
        ],
        axis=0,
    ).astype(jnp.bfloat16)
    qkv_grad = jnp.einsum(
        "td,jtf->jdf", hidden_one, projected_grad, preferred_element_type=jnp.float32
    )
    one_part = jnp.einsum(
        "jtf,jdf->td", projected_grad, qkv_back, preferred_element_type=jnp.float32
    )
    one_grad = lax.psum(one_part.astype(jnp.bfloat16), "tp").astype(jnp.float32)
    scaled_one = one_grad * gains_back[0].astype(jnp.float32)[None, :]
    gain_one_grad = jnp.sum(one_grad * normed_one, axis=0)
    input_grad = residual_grad + rstd_one * (
        scaled_one - normed_one * jnp.mean(scaled_one * normed_one, axis=1, keepdims=True)
    )
    gains_grad = jnp.stack([gain_one_grad, gain_two_grad], axis=0)
    reduced = (
        lax.psum_scatter(
            qkv_grad.astype(jnp.bfloat16), "fs", scatter_dimension=1, tiled=True
        ).astype(jnp.float32),
        lax.psum_scatter(
            out_grad.astype(jnp.bfloat16), "fs", scatter_dimension=1, tiled=True
        ).astype(jnp.float32),
        lax.psum_scatter(
            gains_grad.astype(jnp.bfloat16), "fs", scatter_dimension=1, tiled=True
        ).astype(jnp.float32),
        lax.psum_scatter(
            router_grad.astype(jnp.bfloat16), "fs", scatter_dimension=1, tiled=True
        ).astype(jnp.float32),
        lax.psum_scatter(
            shared_vector_grad.astype(jnp.bfloat16), "fs", scatter_dimension=0, tiled=True
        ).astype(jnp.float32),
        lax.psum_scatter(
            expert_gate_grad.astype(jnp.bfloat16), "fs", scatter_dimension=1, tiled=True
        ).astype(jnp.float32),
        lax.psum_scatter(
            expert_down_grad.astype(jnp.bfloat16), "fs", scatter_dimension=2, tiled=True
        ).astype(jnp.float32),
        lax.psum_scatter(
            shared_proj_grad.astype(jnp.bfloat16), "fs", scatter_dimension=0, tiled=True
        ).astype(jnp.float32),
        lax.psum_scatter(
            shared_down_grad.astype(jnp.bfloat16), "fs", scatter_dimension=1, tiled=True
        ).astype(jnp.float32),
    )
    return (
        output,
        input_grad,
        reduced[0],
        reduced[1],
        reduced[2],
        reduced[3],
        reduced[4],
        reduced[5],
        reduced[6],
        reduced[7],
        reduced[8],
    )


MESH = pl.DeviceIdType.MESH
X_BIT, Y_BIT, CORE_BIT = 2, 4, 1
QUARTERS = 4
SMALL = 16
EARLY = (2, 4)
CUT = 1536


def flip(index, bit):
    return index + bit - 2 * bit * ((index // bit) % 2)


class Links:
    def __init__(self, send, recv, local):
        self.fs = lax.axis_index("fs")
        self.tp = lax.axis_index("tp")
        self.send, self.recv, self.local = send, recv, local
        self.used = 0
        self.used_local = 0

    def peer(self, bits):
        where = self.fs
        for bit in (X_BIT, Y_BIT, CORE_BIT):
            if bits & bit:
                where = flip(where, bit)
        return where

    def along(self, step):
        return lax.rem(self.tp + step, QUARTERS)

    def remote(self, source, target, device, landing):
        i = self.used
        self.used += 1
        out = pltpu.make_async_remote_copy(
            src_ref=source,
            dst_ref=target,
            send_sem=self.send.at[i],
            recv_sem=self.recv.at[i],
            device_id=device,
            device_id_type=MESH,
        )
        back = pltpu.make_async_remote_copy(
            src_ref=landing,
            dst_ref=landing,
            send_sem=self.send.at[i],
            recv_sem=self.recv.at[i],
            device_id=device,
            device_id_type=MESH,
        )
        return out, back

    def inside(self, source, target):
        i = self.used_local
        self.used_local += 1
        return pltpu.make_async_copy(source, target, self.local.at[i])

    def greet(self, plane, column):
        barrier = pltpu.get_barrier_semaphore()
        for bits in plane:
            pl.semaphore_signal(
                barrier, inc=1, device_id=(self.peer(bits), self.tp), device_id_type=MESH
            )
        for step in column:
            pl.semaphore_signal(
                barrier, inc=1, device_id=(self.fs, self.along(step)), device_id_type=MESH
            )
        pl.semaphore_wait(barrier, len(plane) + len(column))


class Gather:
    def __init__(self, links, source, place, half):
        self.links = links
        fs, tp = links.fs, links.tp

        def to(bits, what, landing, origin=None):
            return links.remote(
                what if origin is None else origin, what, (links.peer(bits), tp), landing
            )

        p = links.peer
        self.keep = None if source is None else links.inside(source, place(fs))
        self.to_x = to(X_BIT, place(fs), place(p(X_BIT)), source)
        self.to_y = to(Y_BIT, place(fs), place(p(Y_BIT)), source)
        self.to_c = to(CORE_BIT, place(fs), place(p(CORE_BIT)), source)
        xy = X_BIT + Y_BIT
        self.x_on = to(Y_BIT, half(p(X_BIT), 0), half(p(xy), 0))
        self.y_on = to(X_BIT, half(p(Y_BIT), 1), half(p(xy), 1))
        self.x_core = to(CORE_BIT, place(p(X_BIT)), place(p(X_BIT + CORE_BIT)))
        self.y_core = to(CORE_BIT, place(p(Y_BIT)), place(p(Y_BIT + CORE_BIT)))
        self.d_core = [
            to(CORE_BIT, half(p(xy), h), half(p(xy + CORE_BIT), h)) for h in range(2)
        ]

    def first(self):
        self.to_x[0].start()
        self.to_y[0].start()
        self.to_c[0].start()
        if self.keep is not None:
            self.keep.start()

    def second(self):
        self.to_x[1].wait_recv()
        self.x_on[0].start()
        self.x_core[0].start()
        self.to_y[1].wait_recv()
        self.y_on[0].start()
        self.y_core[0].start()

    def third(self):
        self.x_on[1].wait_recv()
        self.d_core[0][0].start()
        self.y_on[1].wait_recv()
        self.d_core[1][0].start()

    def last(self):
        if self.keep is not None:
            self.keep.wait()
        for out, back in (self.to_c, self.x_core, self.y_core, *self.d_core):
            back.wait_recv()
        for out, back in (
            self.to_x,
            self.to_y,
            self.to_c,
            self.x_on,
            self.y_on,
            self.x_core,
            self.y_core,
            *self.d_core,
        ):
            out.wait_send()


class CrossGather:
    def __init__(self, links, source, blocks):
        self.links = links
        tp = links.tp
        size = source.shape[0]

        def slot(k, h=None):
            start, count = (3 - k // 2) * size, size
            if h is not None:
                count = size // 2
                start = start + h * count
            return blocks.at[1, pl.ds(start, count)]

        def to(bits, start, there):
            return links.remote(start, there, (links.peer(bits), tp), there)

        x, y, c = X_BIT, Y_BIT, CORE_BIT
        self.keep = links.inside(source, slot(0))
        self.to_x = to(x, source, slot(x))
        self.to_y = to(y, source, slot(y))
        self.x_on = to(y, slot(x, 0), slot(x + y, 0))
        self.y_on = to(x, slot(y, 1), slot(x + y, 1))
        self.along = []
        for step in range(1, QUARTERS):
            there = blocks.at[2 * step + 1]
            self.along.append(
                links.remote(blocks.at[1], there, (links.fs, links.along(step)), there)
            )
        self.core = [
            to(c, blocks.at[2 * s + 1], blocks.at[2 * s]) for s in range(QUARTERS)
        ]

    def first(self):
        self.to_x[0].start()
        self.to_y[0].start()
        self.keep.start()

    def second(self):
        self.to_x[1].wait_recv()
        self.x_on[0].start()
        self.to_y[1].wait_recv()
        self.y_on[0].start()

    def third(self):
        self.keep.wait()
        self.x_on[1].wait_recv()
        self.y_on[1].wait_recv()
        for out, back in self.along:
            out.start()
        self.core[0][0].start()

    def last(self):
        for s, (out, back) in enumerate(self.along):
            back.wait_recv()
            self.core[s + 1][0].start()
        for out, back in self.core:
            back.wait_recv()
        for out, back in (self.to_x, self.to_y, self.x_on, self.y_on, *self.along, *self.core):
            out.wait_send()


def grad_shapes(routed, shared, block):
    return (
        (E, 2 * routed, block),
        (2, E * shared, block),
        (E, routed, block),
        (E * shared, block),
    )


def grad_pieces(grads, results, index, source):
    up_all, shared_up_all, down_all, shared_down_all = results
    routed, shared = down_all.shape[1], shared_down_all.shape[0] // E
    units = pl.ds(pl.multiple_of(source * shared, 16), shared)
    places = [
        up_all.at[source],
        shared_up_all.at[0, units],
        shared_up_all.at[1, units],
        down_all.at[source],
        shared_down_all.at[units],
    ]
    placed, at = [], 0
    for place, size in zip(places, (2 * routed, shared, shared, routed, shared), strict=True):
        placed.append((grads.at[index, pl.ds(at, size)], place))
        at += size
    return placed


def grad_copies(links, grads, results, bits):
    peer = links.peer(bits)
    pairs = zip(
        grad_pieces(grads, results, peer, links.fs),
        grad_pieces(grads, results, peer, peer),
        strict=True,
    )
    return [
        links.remote(piece, place, (peer, links.tp), landing)
        for (piece, place), (_, landing) in pairs
    ]


def turn(values, cosine, sine_signed):
    parts = []
    for h in range(values.shape[1] // HD):
        v = values[:, h * HD : (h + 1) * HD]
        parts.append(v * cosine + pltpu.roll(v, HD // 2, 1) * sine_signed)
    return jnp.concatenate(parts, axis=1)


def as_column(row):
    size = row.shape[1]
    same = lax.broadcasted_iota(jnp.int32, (size, size), 0) == lax.broadcasted_iota(
        jnp.int32, (size, size), 1
    )
    spread = jnp.where(same, row.astype(jnp.float32), 0.0)
    return jnp.sum(spread, axis=1, keepdims=True).astype(jnp.int32)


def matmul(a, b):
    return jnp.dot(a, b, preferred_element_type=jnp.float32)


def matmul_nt(a, b):
    return lax.dot_general(a, b, (((1,), (1,)), ((), ())), preferred_element_type=jnp.float32)


def matmul_tn(a, b):
    return lax.dot_general(a, b, (((0,), (0,)), ((), ())), preferred_element_type=jnp.float32)


class RowGather:
    def __init__(self, links, source, slot, half):
        self.links = links

        def to(bits, owner, h=None):
            view = slot if h is None else lambda k: half(k, h)
            start = source if owner == 0 and source is not None else view(owner)
            return links.remote(
                start, view(owner ^ bits), (links.peer(bits), links.tp), view(owner ^ bits)
            )

        x, y, c = X_BIT, Y_BIT, CORE_BIT
        self.keep = None if source is None else links.inside(source, slot(0))
        self.own = [to(x, 0), to(y, 0), to(c, 0)]
        self.x_on = [to(y, x, 0), to(c, x)]
        self.y_on = [to(x, y, 1), to(c, y)]
        self.d_on = [to(c, x + y, 0), to(c, x + y, 1)]

    def first(self):
        for out, back in self.own:
            out.start()
        if self.keep is not None:
            self.keep.start()

    def second(self):
        self.own[0][1].wait_recv()
        for out, back in self.x_on:
            out.start()
        self.own[1][1].wait_recv()
        for out, back in self.y_on:
            out.start()

    def third(self):
        self.x_on[0][1].wait_recv()
        self.d_on[0][0].start()
        self.y_on[0][1].wait_recv()
        self.d_on[1][0].start()

    def last(self):
        if self.keep is not None:
            self.keep.wait()
        for out, back in (self.own[2], self.x_on[1], self.y_on[1], *self.d_on):
            back.wait_recv()

    def sent(self):
        for out, back in self.own + self.x_on + self.y_on + self.d_on:
            out.wait_send()


def layer_kernel(
    routed,
    tokens_hbm,
    cotangent_ref,
    qkv_ref,
    out_ref,
    gains_ref,
    router_ref,
    gate_ref,
    up_ref,
    shared_raw,
    down_ref,
    shared_down_ref,
    cos_ref,
    sin_ref,
    start_ref,
    routes_ref,
    output_ref,
    branch_ref,
    back_ref,
    small_grad_ref,
    grads_out,
    up_all,
    shared_up_all,
    down_all,
    shared_down_all,
    attended_out,
    query_out,
    hidden_out,
    slabs_all,
    cotangent_all,
    cotangent_plane,
    kv_out,
    qkv_out,
    out_out,
    small_out,
    shared_up_ref,
    small_full,
    branch_in,
    two_ref,
    small_ref,
    scales_ref,
    residual_ref,
    two_all,
    core_in,
    diag_in,
    side_in,
    rows_in,
    cols_in,
    send,
    recv,
    local,
    credit,
):
    links = Links(send, recv, local)
    fs, tp = links.fs, links.tp
    rows, width = tokens_hbm.shape
    block = width // E
    local_width = qkv_ref.shape[2]
    heads = local_width // HD
    seqs = rows // SEQ_DEV
    quarter = rows // QUARTERS
    out_width = output_ref.shape[1]
    back_width = width + SIDE
    whole = back_width + width
    slab_rows = slabs_all.shape[1]
    count = slab_rows // 3
    bf, f32 = jnp.bfloat16, jnp.float32

    def at_rows(index, size):
        return pl.ds(pl.multiple_of(index * size, size), size)

    small_ref[...] = jnp.concatenate(
        [
            gains_ref[...].astype(f32),
            router_ref[...].astype(f32),
            jnp.concatenate([gate_ref[0:1], gate_ref[1:2]], axis=1).astype(f32),
            jnp.zeros((SMALL - 3 - E, block), f32),
        ],
        axis=0,
    ).astype(jnp.bfloat16)
    links.greet(range(1, 8), range(1, QUARTERS))
    cut = cotangent_all.shape[2]
    cot = CrossGather(
        links, cotangent_ref.at[at_rows(tp, quarter), pl.ds(0, cut)], cotangent_all
    )
    cot_plane = Gather(
        links,
        cotangent_ref.at[:, pl.ds(cut, width - cut)],
        lambda f: cotangent_plane.at[f],
        lambda f, h: cotangent_plane.at[f, pl.ds(h * SEQ_DEV, SEQ_DEV)],
    )
    shared = shared_down_ref.shape[0] // E

    def slab(peer, where):
        units = pl.ds(pl.multiple_of(peer * shared, 16), shared)
        pieces = [
            up_ref.at[peer],
            shared_up_ref.at[0, units],
            shared_up_ref.at[1, units],
            down_ref.at[peer],
            shared_down_ref.at[units],
        ]
        placed, at = [], 0
        for piece, size in zip(pieces, (2 * routed, shared, shared, routed, shared), strict=True):
            placed.append((piece, slabs_all.at[where, pl.ds(at, size)]))
            at += size
        return placed

    slab_copies = []
    for bits in (6, 7, 2, 3, 4, 5, 1):
        peer = links.peer(bits)
        for (piece, place), (_, landing) in zip(slab(peer, fs), slab(peer, peer), strict=True):
            slab_copies.append(links.remote(piece, place, (peer, tp), landing))
    slab_own = [links.inside(piece, place) for piece, place in slab(fs, fs)]
    def slot(s, k, h=None):
        start = (3 - k // 2) * quarter
        size = quarter
        if h is not None:
            size = quarter // 2
            start = start + h * size
        return two_all.at[2 * s + 1 - k % 2, pl.ds(start, size)]

    along = []
    for step in range(1, QUARTERS):
        along.append(
            links.remote(two_ref, slot(step, 0), (fs, links.along(step)), slot(step, 0))
        )
    gathers = []
    for s in range(QUARTERS):
        gathers.append(
            RowGather(
                links,
                two_ref if s == 0 else None,
                lambda k, s=s: slot(s, k),
                lambda k, h, s=s: slot(s, k, h),
            )
        )

    def attention(
        tokens_ref,
        hidden_buf,
        attended_ref,
        query_ref,
        qkv_full,
        out_full,
        kv_own,
        kv_full,
        branch_buf,
        raw,
        by_unit,
    ):
        load = links.inside(tokens_hbm, tokens_ref)
        load.start()
        raw_load = links.inside(shared_raw, raw)
        raw_load.start()
        small = Gather(
            links, small_ref, lambda f: small_full.at[f], lambda f, h: small_full.at[f, :, pl.ds(h * 128, 128)]
        )
        qkv = Gather(
            links,
            qkv_ref,
            lambda f: qkv_out.at[:, at_rows(f, block)],
            lambda f, h: qkv_out.at[:, pl.ds(pl.multiple_of(f * block + h * (block // 2), block // 2), block // 2)],
        )
        outs = Gather(
            links,
            out_ref,
            lambda f: out_out.at[f],
            lambda f, h: out_out.at[f, pl.ds(h * (local_width // 2), local_width // 2)],
        )
        small.first()
        cot.first()
        qkv.first()
        small.second()
        small.third()
        small.last()
        cot.second()
        load.wait()
        tokens = tokens_ref[...].astype(jnp.float32)
        rstd_one = lax.rsqrt(jnp.mean(tokens * tokens, axis=1, keepdims=True) + NORM_EPS)
        for b in range(E):
            cols = slice(b * block, (b + 1) * block)
            gain = small_full[b, 0:1, :].astype(jnp.float32)
            hidden_buf[:, cols] = (tokens[:, cols] * rstd_one * gain).astype(jnp.bfloat16)
        raw_load.wait()
        for k in range(2):
            by_unit[k] = raw[:, k, :].astype(f32).T.astype(bf)
        unit_keep = links.inside(by_unit, shared_up_ref)
        unit_keep.start()
        cot.third()
        qkv.second()
        qkv.third()
        outs.first()
        cot_plane.first()
        qkv.last()
        qkv_load = links.inside(qkv_out, qkv_full)
        qkv_load.start()
        qkv_load.wait()
        hidden = hidden_buf[...]
        cosine, sine = cos_ref[...], sin_ref[...]
        kv_own[:, :local_width] = turn(matmul(hidden, qkv_full[1]), cosine, sine).astype(jnp.bfloat16)
        kv_own[:, local_width:] = matmul(hidden, qkv_full[2]).astype(jnp.bfloat16)
        kv = Gather(
            links,
            kv_own,
            lambda f: kv_out.at[f],
            lambda f, h: kv_out.at[f, pl.ds(h * SEQ_DEV, SEQ_DEV)],
        )
        kv.first()
        query_ref[...] = turn(matmul(hidden, qkv_full[0]), cosine, sine).astype(jnp.bfloat16)
        outs.second()
        kv.second()
        outs.third()
        kv.third()
        cot_plane.second()
        unit_keep.wait()
        for out, back in slab_copies:
            out.start()
        for copy in slab_own:
            copy.start()
        kv.last()
        kv_load = links.inside(kv_out, kv_full)
        kv_load.start()
        kv_load.wait()
        length = E * SEQ_DEV
        key_pos = lax.broadcasted_iota(jnp.int32, (SEQ_DEV, length), 1)
        query_pos = fs * SEQ_DEV + lax.broadcasted_iota(jnp.int32, (SEQ_DEV, length), 0)
        for s in range(seqs):
            here = slice(s * SEQ_DEV, (s + 1) * SEQ_DEV)
            allowed = (key_pos <= query_pos) & (key_pos >= as_column(start_ref[s : s + 1, :]))
            for h in range(heads):
                cols = slice(h * HD, (h + 1) * HD)
                vcols = slice(local_width + h * HD, local_width + (h + 1) * HD)
                keys = kv_full[:, here, cols].reshape(length, HD)
                values = kv_full[:, here, vcols].reshape(length, HD)
                scores = matmul_nt(query_ref[here, cols], keys) * (HD ** (-0.5))
                scores = jnp.where(allowed, scores, NEG_FILL)
                top = jnp.max(scores, axis=1, keepdims=True)
                weights = jnp.exp(scores - top)
                weights = weights / jnp.sum(weights, axis=1, keepdims=True)
                attended_ref[here, cols] = matmul(weights.astype(jnp.bfloat16), values).astype(
                    jnp.bfloat16
                )
        outs.last()
        cot_plane.third()
        out_load = links.inside(out_out, out_full)
        out_load.start()
        small_keep = links.inside(small_full, small_out)
        small_keep.start()
        out_load.wait()
        attended = attended_ref[...]
        for b in range(E):
            branch_buf[:, b * block : (b + 1) * block] = matmul(attended, out_full[b]).astype(
                jnp.bfloat16
            )
        branch = []
        for step in range(1, QUARTERS):
            peer = links.along(step)
            branch.append(
                links.remote(
                    branch_buf.at[at_rows(peer, quarter)],
                    branch_in.at[step - 1],
                    (fs, peer),
                    branch_in.at[step - 1],
                )
            )
        for out, back in branch:
            out.start()
        for out, back in branch:
            back.wait_recv()
        mine = at_rows(tp, quarter)
        total = branch_buf[mine, :].astype(jnp.float32)
        for step in range(1, QUARTERS):
            total = total + branch_in[step - 1].astype(jnp.float32)
        residual = tokens_ref[mine, :].astype(jnp.float32) + total
        residual_ref[...] = residual
        rstd_two = lax.rsqrt(jnp.mean(residual * residual, axis=1, keepdims=True) + NORM_EPS)
        logits = jnp.zeros((quarter, SMALL), jnp.float32)
        for b in range(E):
            cols = slice(b * block, (b + 1) * block)
            gain = small_full[b, 1:2, :].astype(jnp.float32)
            part = (residual[:, cols] * rstd_two * gain).astype(jnp.bfloat16)
            two_ref[:, cols] = part
            logits = logits + matmul_nt(part, small_full[b])
        lane = lax.broadcasted_iota(jnp.int32, (quarter, SMALL), 1)
        real = (lane >= 2) & (lane < 2 + E)
        masked = jnp.where(real, logits, NEG_FILL)
        odds = jnp.exp(masked - jnp.max(masked, axis=1, keepdims=True))
        odds = jnp.where(real, odds, 0.0)
        probs = odds / jnp.sum(odds, axis=1, keepdims=True)
        expert = lax.broadcasted_iota(jnp.int32, (SMALL, rows), 0) - 2
        named = jnp.zeros((SMALL, rows), jnp.float32)
        for k in range(routes_ref.shape[0]):
            named = named + (routes_ref[k : k + 1, :] == expert).astype(jnp.float32)
        pick = lax.broadcasted_iota(jnp.int32, (quarter, rows), 1) == (
            tp * quarter + lax.broadcasted_iota(jnp.int32, (quarter, rows), 0)
        )
        chosen = matmul_nt(pick.astype(jnp.bfloat16), named.astype(jnp.bfloat16))
        gate_value = 1.0 / (1.0 + jnp.exp(-logits))
        scales = jnp.where(lane == 2 + E, gate_value, probs * chosen)
        scales_ref[...] = jnp.concatenate([scales, probs, chosen], axis=1)
        high = scales.astype(jnp.bfloat16)
        low = (scales - high.astype(jnp.float32)).astype(jnp.bfloat16)
        two_ref[:, width:] = jnp.concatenate(
            [high, low, jnp.zeros((quarter, SIDE - 2 * SMALL), jnp.bfloat16)], axis=1
        )
        keeps = [
            links.inside(attended_ref, attended_out),
            links.inside(query_ref, query_out),
            links.inside(hidden_buf, hidden_out),
            small_keep,
        ]
        for keep in keeps[:3]:
            keep.start()
        for out, back in along:
            out.start()
        for out, back in branch:
            out.wait_send()
        for keep in keeps:
            keep.wait()

    pl.run_scoped(
        attention,
        pltpu.VMEM((rows, width), bf),
        pltpu.VMEM((rows, width), bf),
        pltpu.VMEM((rows, local_width), bf),
        pltpu.VMEM((rows, local_width), bf),
        pltpu.VMEM((3, width, local_width), bf),
        pltpu.VMEM((E, local_width, block), bf),
        pltpu.VMEM((rows, 2 * local_width), bf),
        pltpu.VMEM((E, rows, 2 * local_width), bf),
        pltpu.VMEM((rows, width), bf),
        pltpu.VMEM(shared_raw.shape, bf),
        pltpu.VMEM(shared_up_ref.shape, bf),
    )

    def experts(weights, cot_all, units, first, parts, own_rows, own_cols, staged, cot_rows):
        loads = [
            links.inside(slabs_all.at[g], weights.at[:, pl.ds(g * block, block)]) for g in range(E)
        ]
        loads.append(links.inside(cotangent_all, cot_all.at[:, :, pl.ds(0, cut)]))
        for s in range(QUARTERS):
            q = links.along(QUARTERS - s)
            for k in range(E):
                there = cot_all.at[
                    2 * s + 1 - k % 2, pl.ds((3 - k // 2) * quarter, quarter), pl.ds(cut, width - cut)
                ]
                loads.append(
                    links.inside(cotangent_plane.at[links.peer(k), at_rows(q, quarter)], there)
                )
        along[0][1].wait_recv()
        gathers[1].first()
        along[1][1].wait_recv()
        gathers[2].first()
        gathers[1].second()
        along[2][1].wait_recv()
        gathers[3].first()
        cot.last()
        cot_plane.last()
        for load in loads[E:]:
            load.start()
        for out, back in slab_copies:
            back.wait_recv()
        for copy in slab_own:
            copy.wait()
        for load in loads[:E]:
            load.start()

        cot_load = links.inside(cotangent_ref.at[at_rows(tp, quarter)], cot_rows)
        cot_load.start()
        core = [
            links.remote(
                parts.at[s % 2], core_in.at[s % 2], (links.peer(CORE_BIT), tp), core_in.at[s % 2]
            )
            for s in range(QUARTERS)
        ]
        diag, side, rows_along, cols_along = [], [], [], []
        for s in range(QUARTERS):
            held = parts.at[2 + s % 3]
            diag.append(
                [
                    links.remote(
                        held.at[pl.ds(h * (quarter // 2), quarter // 2)],
                        diag_in.at[s, h],
                        (links.peer(bits), tp),
                        diag_in.at[s, h],
                    )
                    for h, bits in enumerate((Y_BIT, X_BIT))
                ]
            )
            side.append(
                [
                    links.remote(
                        held.at[pl.ds((3 - bits // 2) * quarter, quarter)],
                        side_in.at[s, i],
                        (links.peer(bits), tp),
                        side_in.at[s, i],
                    )
                    for i, bits in enumerate((X_BIT, Y_BIT))
                ]
            )
            last = pl.ds(3 * quarter, quarter)
            if s < QUARTERS - 1:
                rows_along.append(
                    links.remote(
                        held.at[last, pl.ds(0, back_width)],
                        rows_in.at[s],
                        (fs, links.along(QUARTERS - 1 - s)),
                        rows_in.at[s],
                    )
                )
            q = links.along(2 * QUARTERS - 1 - s)
            for step in range(1, QUARTERS):
                peer = links.along(step)
                start = pl.multiple_of(back_width + peer * out_width, 128)
                q_there = links.along(2 * QUARTERS - 1 - s - step)
                cols_along.append(
                    links.remote(
                        held.at[last, pl.ds(start, out_width)],
                        cols_in.at[step - 1, at_rows(q, quarter)],
                        (fs, peer),
                        cols_in.at[step - 1, at_rows(q_there, quarter)],
                    )
                )

        sub = lax.broadcasted_iota(jnp.int32, (8, SIDE), 0)
        lane = lax.broadcasted_iota(jnp.int32, (8, SIDE), 1)
        mine, common = 2 + fs, 2 + E
        pick_in = (
            ((sub == 0) & ((lane == mine) | (lane == mine + SMALL)))
            | ((sub == 1) & ((lane == common) | (lane == common + SMALL)))
        ).astype(jnp.bfloat16)
        pick_out = (((sub == 0) & (lane == mine)) | ((sub == 1) & (lane == common))).astype(
            jnp.bfloat16
        )

        def one_block(t, index, slot_out, pause):
            first[: 2 * count] = matmul_nt(weights[: 2 * count], two_all[index, :, :width])
            pause(0)
            first[2 * count :] = matmul_nt(weights[2 * count :], cot_all[index])
            scale = matmul_nt(pick_in, two_all[index, :, width:])
            cols = pl.ds(pl.multiple_of(index * rows, rows), rows)
            dots = []
            shared = count - routed
            groups = ((0, 2 * count, routed), (2 * routed, 2 * count + routed, shared))
            for group, (low, last, size) in enumerate(groups):
                gate = first[low : low + size]
                up = first[low + size : low + 2 * size]
                grad = first[last : last + size]
                by = scale[group : group + 1]
                sigmoid = 1.0 / (1.0 + jnp.exp(-gate))
                silu = gate * sigmoid
                active = silu * up
                units[last : last + size, cols] = (by * active).astype(jnp.bfloat16)
                dots.append(jnp.sum(active * grad, axis=0, keepdims=True))
                active_grad = by * grad
                units[low : low + size, cols] = (
                    active_grad * up * sigmoid * (1.0 + gate * (1.0 - sigmoid))
                ).astype(jnp.bfloat16)
                units[low + size : low + 2 * size, cols] = (active_grad * silu).astype(jnp.bfloat16)
            both = jnp.concatenate([*dots, jnp.zeros((6, rows), jnp.float32)], axis=0)
            pause(1)
            tile = 512

            def put(at, value, other):
                if other is not None:
                    value = value + other[:, at].astype(jnp.float32)
                parts[slot_out, :, at] = value.astype(jnp.bfloat16)

            def products(other):
                put(
                    slice(width, back_width), matmul_tn(both.astype(jnp.bfloat16), pick_out), other
                )
                for n in range(width // tile):
                    at = slice(n * tile, (n + 1) * tile)
                    put(at, matmul_tn(units[: 2 * count, cols], weights[: 2 * count, at]), other)
                    beyond = slice(back_width + n * tile, back_width + (n + 1) * tile)
                    put(beyond, matmul_tn(units[2 * count :, cols], weights[2 * count :, at]), other)

            @pl.when(t % 2 == 0)
            def _():
                products(None)

            @pl.when(t % 2 == 1)
            def _():
                products(core_in.at[(t // 2) % 2])

            pause(3)

        def add_in(held, start, size, others):
            chunk = 32

            @pl.loop(0, size // chunk)
            def _(r):
                at = pl.ds(pl.multiple_of(start + r * chunk, chunk), chunk)
                there = pl.ds(pl.multiple_of(r * chunk, chunk), chunk)
                total = parts[held, at, :].astype(jnp.float32)
                for ref in others:
                    total = total + ref[there, :].astype(jnp.float32)
                parts[held, at, :] = total.astype(jnp.bfloat16)

        def to_core(s):
            if s >= 2:
                pl.semaphore_wait(credit, 1)
            core[s][0].start()

        def diagonal(s):
            if s < 2:
                pl.semaphore_signal(
                    credit, inc=1, device_id=(links.peer(CORE_BIT), tp), device_id_type=MESH
                )
            for out, back in diag[s]:
                out.start()

        def sideways(s):
            for h, (out, back) in enumerate(diag[s]):
                back.wait_recv()
                start = (2 - h) * quarter + h * (quarter // 2)
                add_in(2 + s % 3, start, quarter // 2, [diag_in.at[s, h]])
                side[s][h][0].start()

        def finish(s):
            held = 2 + s % 3
            for out, back in side[s]:
                back.wait_recv()
            last = slice(3 * quarter, rows)
            add_in(held, 3 * quarter, quarter, [side_in.at[s, 0], side_in.at[s, 1]])
            if s == QUARTERS - 1:
                own_rows[...] = parts[held, last, :back_width].astype(jnp.float32)
                parts[held, last, back_width:] = (
                    parts[held, last, back_width:].astype(jnp.float32) + residual_ref[...]
                ).astype(jnp.bfloat16)
            else:
                rows_along[s][0].start()
            for out, back in cols_along[3 * s : 3 * s + 3]:
                out.start()
            start = pl.multiple_of(back_width + tp * out_width, 128)
            own_cols[at_rows(links.along(2 * QUARTERS - 1 - s), quarter), :] = parts[
                held, last, pl.ds(start, out_width)
            ].astype(jnp.float32)

        def before_last():
            core[1][0].wait_send()

        def slot_free():
            for out, back in diag[0] + side[0] + cols_along[:3] + rows_along[:1]:
                out.wait_send()

        plan = {
            (0, 0): [gathers[2].third, gathers[3].second],
            (0, 1): [gathers[3].third],
            (0, 3): [lambda: to_core(0), gathers[0].first, gathers[2].last],
            (1, 1): [core[0][1].wait_recv, gathers[0].second],
            (1, 3): [gathers[0].third, lambda: diagonal(0), gathers[3].last],
            (2, 3): [lambda: to_core(1), lambda: sideways(0)],
            (3, 1): [core[1][1].wait_recv],
            (3, 3): [lambda: diagonal(1)],
            (4, 3): [lambda: to_core(2), lambda: sideways(1)],
            (5, 1): [core[2][1].wait_recv],
            (5, 3): [lambda: diagonal(2), gathers[0].last, lambda: finish(0)],
            (6, 3): [lambda: to_core(3), lambda: sideways(2)],
            (7, 1): [core[3][1].wait_recv],
            (7, 3): [lambda: diagonal(3), lambda: finish(1)],
        }
        before = {4: [core[0][0].wait_send], 6: [before_last], 7: [slot_free]}

        gathers[1].third()
        gathers[2].second()
        for load in loads:
            load.wait()
        gathers[1].last()

        @pl.loop(0, 8)
        def _(t):
            s = t // 2
            slot_out = (1 - t % 2) * (s % 2) + (t % 2) * (2 + s % 3)
            for at, steps in before.items():

                @pl.when(t == at)
                def _(steps=steps):
                    for step in steps:
                        step()

            def pause(point):
                for (at, where), steps in plan.items():
                    if where == point:

                        @pl.when(t == at)
                        def _(steps=steps):
                            for step in steps:
                                step()

            one_block(t, 2 * ((s + 1) % QUARTERS) + t % 2, slot_out, pause)

        keeps = []

        pending = [None, None]

        def settle(place):
            if pending[place] is not None:
                pending[place].wait()
            pending[place] = None

        def weight_grads(bits):
            g = links.peer(bits)
            at = pl.ds(pl.multiple_of(g * block, block), block)
            place = len(keeps) % 2
            settle(place)
            hidden_cols = two_all[:, :, at].reshape(E * rows, block)
            staged[place, : 2 * count] = matmul(units[: 2 * count], hidden_cols).astype(
                jnp.bfloat16
            )
            cot_cols = cot_all[:, :, at].reshape(E * rows, block)
            staged[place, 2 * count :] = matmul(units[2 * count :], cot_cols).astype(jnp.bfloat16)
            keep = links.inside(staged.at[place], grads_out.at[g])
            keep.start()
            keeps.append(keep)
            pending[place] = keep

        results = (up_all, shared_up_all, down_all, shared_down_all)
        early = [copy for bits in EARLY for copy in grad_copies(links, grads_out, results, bits)]
        finish(2)
        for bits in EARLY:
            weight_grads(bits)
        sideways(3)
        settle(0)
        settle(1)
        for out, back in early:
            out.start()
        for bits in (6, 7, 3, 5, 1, 0):
            weight_grads(bits)
        finish(3)
        for out, back in rows_along:
            back.wait_recv()
        total = own_rows[...]
        for step in range(1, QUARTERS):
            total = total + rows_in[step - 1].astype(jnp.float32)
        dots = total[:, width : width + SMALL]
        scales = scales_ref[:, :SMALL]
        probs = scales_ref[:, SMALL : 2 * SMALL]
        chosen = scales_ref[:, 2 * SMALL :]
        chosen_grad = chosen * dots
        logit_grad = probs * (chosen_grad - jnp.sum(probs * chosen_grad, axis=1, keepdims=True))
        gate_lane = lax.broadcasted_iota(jnp.int32, (quarter, SMALL), 1) == 2 + E
        logit_grad = jnp.where(gate_lane, dots * scales * (1.0 - scales), logit_grad).astype(
            jnp.bfloat16
        )
        residual = residual_ref[...]
        rstd = lax.rsqrt(jnp.mean(residual * residual, axis=1, keepdims=True) + NORM_EPS)
        mean = jnp.zeros((quarter, 1), jnp.float32)
        for b in range(E):
            at = slice(b * block, (b + 1) * block)
            two_grad = total[:, at] + matmul(logit_grad, small_full[b])
            normed = residual[:, at] * rstd
            gain = small_full[b, 1:2, :].astype(jnp.float32)
            back_ref[:, at] = two_grad
            mean = mean + jnp.sum(two_grad * gain * normed, axis=1, keepdims=True)
            grads = matmul_tn(logit_grad, two_all[1, 3 * quarter :, at])
            line = lax.broadcasted_iota(jnp.int32, (SMALL, block), 0)
            gain_grad = jnp.sum(two_grad * normed, axis=0, keepdims=True)
            small_grad_ref[:, at] = jnp.where(line == 1, gain_grad, grads)
        mean = mean / width
        cot_load.wait()
        for b in range(E):
            at = slice(b * block, (b + 1) * block)
            gain = small_full[b, 1:2, :].astype(jnp.float32)
            normed = residual[:, at] * rstd
            grad = cot_rows[:, at].astype(jnp.float32) + rstd * (
                back_ref[:, at] * gain - normed * mean
            )
            back_ref[:, at] = grad
            branch_ref[:, at] = grad.astype(jnp.bfloat16)
        for out, back in cols_along:
            back.wait_recv()
        total = own_cols[...]
        for step in range(1, QUARTERS):
            total = total + cols_in[step - 1].astype(jnp.float32)
        output_ref[...] = total.astype(jnp.bfloat16)
        for out, back in core[2:] + rows_along[1:] + cols_along[3:]:
            out.wait_send()
        for s in range(1, QUARTERS):
            for out, back in diag[s] + side[s]:
                out.wait_send()
        for gather in gathers:
            gather.sent()
        for out, back in slab_copies + along:
            out.wait_send()
        settle(0)
        settle(1)
        for out, back in early:
            back.wait_recv()
            out.wait_send()

    pl.run_scoped(
        experts,
        pltpu.VMEM((slab_rows, width), bf),
        pltpu.VMEM((E, rows, width), bf),
        pltpu.VMEM((slab_rows, E * rows), bf),
        pltpu.VMEM((slab_rows, rows), f32),
        pltpu.VMEM((5, rows, whole), bf),
        pltpu.VMEM((quarter, back_width), f32),
        pltpu.VMEM((rows, out_width), f32),
        pltpu.VMEM((2, slab_rows, block), bf),
        pltpu.VMEM((quarter, width), bf),
    )


def layer_call(
    tokens,
    cotangent,
    qkv_weight,
    out_weight,
    norm_gains,
    router_weight,
    shared_gate,
    up,
    shared_up,
    down,
    shared_down,
    cosine,
    sine,
    start,
    routes,
):
    rows, width = tokens.shape
    block = width // E
    local_width = qkv_weight.shape[2]
    quarter = rows // QUARTERS
    out_width = width // QUARTERS
    back_width = width + SIDE
    whole = back_width + width
    routed = down.shape[1]
    slabs = (E, 3 * (routed + shared_down.shape[0] // E), block)
    bf, f32 = jnp.bfloat16, jnp.float32
    sds = jax.ShapeDtypeStruct
    vmem = pl.BlockSpec(memory_space=pltpu.VMEM)
    hbm = pl.BlockSpec(memory_space=pl.ANY)
    outs = [
        (sds((rows, out_width), bf), vmem),
        (sds((quarter, width), bf), vmem),
        (sds((quarter, width), f32), vmem),
        (sds((SMALL, width), f32), vmem),
        (sds(slabs, bf), hbm),
        *((sds(shape, bf), hbm) for shape in grad_shapes(routed, shared_down.shape[0] // E, block)),
        (sds((rows, local_width), bf), hbm),
        (sds((rows, local_width), bf), hbm),
        (sds((rows, width), bf), hbm),
        (sds(slabs, bf), hbm),
        (sds((E, rows, CUT), bf), hbm),
        (sds((E, rows, width - CUT), bf), hbm),
        (sds((E, rows, 2 * local_width), bf), hbm),
        (sds((3, width, local_width), bf), hbm),
        (sds((E, local_width, block), bf), hbm),
        (sds((E, SMALL, block), bf), hbm),
        (sds((2, shared_down.shape[0], block), bf), hbm),
    ]
    return pl.pallas_call(
        functools.partial(layer_kernel, routed),
        name="layer",
        out_shape=[o[0] for o in outs],
        in_specs=[hbm] * 4 + [vmem] * 3 + [hbm] * 4 + [vmem] * 4,
        out_specs=[o[1] for o in outs],
        scratch_shapes=[
            pltpu.VMEM((E, SMALL, block), bf),
            pltpu.VMEM((QUARTERS - 1, quarter, width), bf),
            pltpu.VMEM((quarter, back_width), bf),
            pltpu.VMEM((SMALL, block), bf),
            pltpu.VMEM((quarter, 3 * SMALL), f32),
            pltpu.VMEM((quarter, width), f32),
            pltpu.VMEM((E, rows, back_width), bf),
            pltpu.VMEM((2, rows, whole), bf),
            pltpu.VMEM((QUARTERS, 2, quarter // 2, whole), bf),
            pltpu.VMEM((QUARTERS, 2, quarter, whole), bf),
            pltpu.VMEM((QUARTERS - 1, quarter, back_width), bf),
            pltpu.VMEM((QUARTERS - 1, rows, out_width), bf),
            pltpu.SemaphoreType.DMA((192,)),
            pltpu.SemaphoreType.DMA((192,)),
            pltpu.SemaphoreType.DMA((96,)),
            pltpu.SemaphoreType.REGULAR,
        ],
        compiler_params=pltpu.CompilerParams(
            collective_id=1, has_side_effects=True, vmem_limit_bytes=63 * 2**20
        ),
    )(
        tokens,
        cotangent,
        qkv_weight,
        out_weight,
        norm_gains,
        router_weight,
        shared_gate,
        up,
        shared_up,
        down,
        shared_down,
        cosine,
        sine,
        start,
        routes,
    )


LATE = 20


class Scatter:
    def __init__(self, links, parts, core_in, diag_in, side_in):
        self.links, self.parts = links, parts
        self.core_in, self.diag_in, self.side_in = core_in, diag_in, side_in
        self.rows = parts.shape[1]
        p, tp = links.peer, links.tp
        half = self.rows // 2
        self.core = [
            links.remote(
                parts.at[p(bits + CORE_BIT)], core_in.at[i], (p(CORE_BIT), tp), core_in.at[i]
            )
            for i, bits in enumerate((6, 2, 4, 0))
        ]
        self.diag = [
            links.remote(
                parts.at[p(6), pl.ds(h * half, half)], diag_in.at[h], (p(bits), tp), diag_in.at[h]
            )
            for h, bits in enumerate((Y_BIT, X_BIT))
        ]
        self.side = [
            links.remote(parts.at[p(bits)], side_in.at[i], (p(bits), tp), side_in.at[i])
            for i, bits in enumerate((X_BIT, Y_BIT))
        ]

    def add(self, index, first, count, refs, target=None):
        chunk = 32

        @pl.loop(0, count // chunk)
        def _(r):
            here = pl.ds(pl.multiple_of(first + r * chunk, chunk), chunk)
            there = pl.ds(pl.multiple_of(r * chunk, chunk), chunk)
            total = self.parts[index, here, :].astype(jnp.float32)
            for ref in refs:
                total = total + ref[there, :].astype(jnp.float32)
            if target is None:
                self.parts[index, here, :] = total.astype(jnp.bfloat16)
            else:
                target[here, :] = total

    def to_core(self):
        for out, back in self.core:
            out.start()

    def diagonal(self):
        self.core[0][1].wait_recv()
        self.add(self.links.peer(6), 0, self.rows, [self.core_in.at[0]])
        for out, back in self.diag:
            out.start()

    def sideways(self, i):
        index = self.links.peer((X_BIT, Y_BIT)[i])
        self.core[1 + i][1].wait_recv()
        self.add(index, 0, self.rows, [self.core_in.at[1 + i]])
        self.diag[i][1].wait_recv()
        self.add(index, i * (self.rows // 2), self.rows // 2, [self.diag_in.at[i]])
        self.side[i][0].start()

    def finish(self, target):
        self.core[3][1].wait_recv()
        for out, back in self.side:
            back.wait_recv()
        self.add(
            self.links.fs,
            0,
            self.rows,
            [self.core_in.at[3], self.side_in.at[0], self.side_in.at[1]],
            target,
        )

    def sent(self):
        for out, back in self.core + self.diag + self.side:
            out.wait_send()


def backward_kernel(
    branch_ref,
    residual_hbm,
    small_grad_hbm,
    attended_hbm,
    query_ref,
    hidden_hbm,
    tokens_hbm,
    kv_ref,
    qkv_ref,
    out_ref,
    small_ref,
    cos_ref,
    sin_ref,
    start_ref,
    slabs_ref,
    up_in,
    shared_up_in,
    down_in,
    shared_down_in,
    input_grad_ref,
    qkv_own,
    out_own,
    small_own,
    up_all,
    shared_up_all,
    down_all,
    shared_down_all,
    kv_full,
    qkv_full,
    out_full,
    branch_all,
    odds,
    query_grad,
    projected,
    kv_total,
    kv_parts,
    kv_core,
    kv_diag,
    kv_side,
    query_parts,
    query_core,
    query_diag,
    query_side,
    rest_parts,
    rest_core,
    rest_diag,
    rest_side,
    out_parts,
    out_core,
    out_diag,
    out_side,
    one_parts,
    one_in,
    grad_rows,
    small_parts,
    small_in,
    small_column,
    residual_ref,
    small_grad_ref,
    attended_ref,
    hidden_ref,
    token_rows,
    send,
    recv,
    local,
):
    links = Links(send, recv, local)
    fs, tp = links.fs, links.tp
    quarter, width = residual_ref.shape
    rows = quarter * QUARTERS
    block = width // E
    local_width = query_ref.shape[1]
    heads = local_width // HD
    seqs = rows // SEQ_DEV
    length = E * SEQ_DEV
    scale = HD ** (-0.5)

    def at_rows(index, size):
        return pl.ds(pl.multiple_of(index * size, size), size)

    own = at_rows(tp, quarter)
    links.greet(range(1, 8), range(1, QUARTERS))
    branch = []
    for step in range(1, QUARTERS):
        here = branch_all.at[own]
        landing = branch_all.at[at_rows(links.along(QUARTERS - step), quarter)]
        branch.append(links.remote(branch_ref, here, (fs, links.along(step)), landing))
    for out, back in branch:
        out.start()
    branch_all[own, :] = branch_ref[...]
    results = (up_all, shared_up_all, down_all, shared_down_all)
    slab_copies = []
    for bits in (1, 6, 3, 5, 7):
        slab_copies += grad_copies(links, slabs_ref, results, bits)
    for out, back in slab_copies[:LATE]:
        out.start()
    slab_own = [links.inside(*pair) for pair in grad_pieces(slabs_ref, results, fs, fs)]
    for copy in slab_own:
        copy.start()
    kv_load = links.inside(kv_ref, kv_full)
    kv_load.start()
    out_load = links.inside(out_ref, out_full)
    out_load.start()
    qkv_load = links.inside(qkv_ref, qkv_full)
    qkv_load.start()
    operand_loads = [
        links.inside(attended_hbm, attended_ref),
        links.inside(hidden_hbm, hidden_ref),
        links.inside(residual_hbm, residual_ref),
        links.inside(small_grad_hbm, small_grad_ref),
        links.inside(tokens_hbm.at[own], token_rows),
    ]
    for load in operand_loads:
        load.start()
    kv_sum = Scatter(links, kv_parts, kv_core, kv_diag, kv_side)
    query_sum = Scatter(links, query_parts, query_core, query_diag, query_side)
    rest_sum = Scatter(links, rest_parts, rest_core, rest_diag, rest_side)
    out_sum = Scatter(links, out_parts, out_core, out_diag, out_side)

    kv_load.wait()
    key_pos = lax.broadcasted_iota(jnp.int32, (SEQ_DEV, length), 1)
    query_pos = fs * SEQ_DEV + lax.broadcasted_iota(jnp.int32, (SEQ_DEV, length), 0)
    for s in range(seqs):
        here = slice(s * SEQ_DEV, (s + 1) * SEQ_DEV)
        allowed = (key_pos <= query_pos) & (key_pos >= as_column(start_ref[s : s + 1, :]))
        for h in range(heads):
            cols = slice(h * HD, (h + 1) * HD)
            keys = kv_full[:, here, cols].reshape(length, HD)
            scores = matmul_nt(query_ref[here, cols], keys) * scale
            scores = jnp.where(allowed, scores, NEG_FILL)
            top = jnp.max(scores, axis=1, keepdims=True)
            weights = jnp.exp(scores - top)
            odds[s * heads + h] = weights / jnp.sum(weights, axis=1, keepdims=True)
    out_load.wait()
    for out, back in branch:
        back.wait_recv()
    attended_grad = jnp.zeros((rows, local_width), jnp.float32)
    for b in range(E):
        attended_grad = attended_grad + matmul_nt(
            branch_all[:, b * block : (b + 1) * block], out_full[b]
        )
    query_grad[...] = attended_grad.astype(jnp.bfloat16)
    for s in range(seqs):
        here = slice(s * SEQ_DEV, (s + 1) * SEQ_DEV)
        for h in range(heads):
            cols = slice(h * HD, (h + 1) * HD)
            vcols = slice(local_width + h * HD, local_width + (h + 1) * HD)
            keys = kv_full[:, here, cols].reshape(length, HD)
            values = kv_full[:, here, vcols].reshape(length, HD)
            grad = query_grad[here, cols]
            probs = odds[s * heads + h]
            weights_grad = matmul_nt(grad, values)
            delta = jnp.sum(probs * weights_grad, axis=1, keepdims=True)
            score_grad = (probs * (weights_grad - delta)).astype(jnp.bfloat16)
            key_grad = matmul_tn(score_grad, query_ref[here, cols]) * scale
            value_grad = matmul_tn(probs.astype(jnp.bfloat16), grad)
            kv_parts[:, here, cols] = key_grad.astype(jnp.bfloat16).reshape(E, SEQ_DEV, HD)
            kv_parts[:, here, vcols] = value_grad.astype(jnp.bfloat16).reshape(E, SEQ_DEV, HD)
            projected[0, here, cols] = turn(
                matmul(score_grad, keys) * scale, cos_ref[here, :], -sin_ref[here, :]
            ).astype(jnp.bfloat16)
    kv_sum.to_core()
    for load in operand_loads:
        load.wait()
    attended = attended_ref[...]
    for b in range(E):
        cols = slice(b * block, (b + 1) * block)
        out_parts[b] = matmul_tn(attended, branch_all[:, cols]).astype(jnp.bfloat16)
    def weight_grad(j):
        for b in range(E):
            cols = slice(b * block, (b + 1) * block)
            part = matmul_tn(hidden_ref[:, cols], projected[j]).astype(jnp.bfloat16)
            if j == 0:
                query_parts[b] = part
            else:
                rest_parts[b, (j - 1) * block : j * block] = part

    kv_sum.diagonal()
    out_sum.to_core()
    weight_grad(0)
    query_sum.to_core()
    kv_sum.sideways(0)
    kv_sum.sideways(1)
    out_sum.diagonal()
    query_sum.diagonal()
    qkv_load.wait()
    kv_sum.finish(kv_total)
    for out, back in slab_copies[LATE:]:
        out.start()
    projected[1] = turn(kv_total[:, :local_width], cos_ref[...], -sin_ref[...]).astype(jnp.bfloat16)
    projected[2] = kv_total[:, local_width:].astype(jnp.bfloat16)
    for b in range(E):
        cols = slice(b * block, (b + 1) * block)
        part = jnp.zeros((rows, block), jnp.float32)
        for j in range(3):
            part = part + matmul_nt(projected[j], qkv_full[j, cols])
        one_parts[:, cols] = part.astype(jnp.bfloat16)
    column = []
    for step in range(1, QUARTERS):
        peer = links.along(step)
        column.append(
            links.remote(
                one_parts.at[at_rows(peer, quarter)],
                one_in.at[step - 1],
                (fs, peer),
                one_in.at[step - 1],
            )
        )
    for out, back in column:
        out.start()
    weight_grad(1)
    weight_grad(2)
    rest_sum.to_core()
    out_sum.sideways(0)
    out_sum.sideways(1)
    query_sum.sideways(0)
    query_sum.sideways(1)
    rest_sum.diagonal()
    for out, back in column:
        back.wait_recv()
    tokens = token_rows[...].astype(jnp.float32)
    rstd = lax.rsqrt(jnp.mean(tokens * tokens, axis=1, keepdims=True) + NORM_EPS)
    total = one_parts[own, :].astype(jnp.float32)
    for step in range(1, QUARTERS):
        total = total + one_in[step - 1].astype(jnp.float32)
    mean = jnp.zeros((quarter, 1), jnp.float32)
    sub = lax.broadcasted_iota(jnp.int32, (SMALL, block), 0)
    for b in range(E):
        at = slice(b * block, (b + 1) * block)
        gain = small_ref[b, 0:1, :].astype(jnp.float32)
        normed = tokens[:, at] * rstd
        mean = mean + jnp.sum(total[:, at] * gain * normed, axis=1, keepdims=True)
        gain_grad = jnp.sum(total[:, at] * normed, axis=0, keepdims=True)
        small_parts[b] = jnp.where(sub == 0, gain_grad, small_grad_ref[:, at])
    mean = mean / width
    for b in range(E):
        at = slice(b * block, (b + 1) * block)
        gain = small_ref[b, 0:1, :].astype(jnp.float32)
        normed = tokens[:, at] * rstd
        grad_rows[:, at] = (
            residual_ref[:, at] + rstd * (total[:, at] * gain - normed * mean)
        ).astype(jnp.bfloat16)
    spread = []
    for step in range(1, QUARTERS):
        peer = links.along(step)
        landing = input_grad_ref.at[at_rows(links.along(QUARTERS - step), quarter)]
        spread.append(links.remote(grad_rows, input_grad_ref.at[own], (fs, peer), landing))
    for out, back in spread:
        out.start()
    keep = links.inside(grad_rows, input_grad_ref.at[own])
    keep.start()
    small_copies = []
    for bits in range(1, E):
        peer = links.peer(bits)
        small_copies.append(
            links.remote(
                small_parts.at[peer], small_in.at[bits - 1], (peer, tp), small_in.at[bits - 1]
            )
        )
    for out, back in small_copies:
        out.start()
    rest_sum.sideways(0)
    rest_sum.sideways(1)
    out_sum.finish(out_own)
    query_sum.finish(qkv_own.at[pl.ds(0, block)])
    for out, back in small_copies:
        back.wait_recv()
    small_total = small_parts[fs]
    for bits in range(1, E):
        small_total = small_total + small_in[bits - 1]
    small_column[tp] = small_total
    small_spread = []
    for step in range(1, QUARTERS):
        here = small_column.at[tp]
        landing = small_column.at[links.along(QUARTERS - step)]
        small_spread.append(links.remote(here, here, (fs, links.along(step)), landing))
    for out, back in small_spread:
        out.start()
    rest_sum.finish(qkv_own.at[pl.ds(block, 2 * block)])
    for out, back in small_spread:
        back.wait_recv()
    small_own[...] = small_column[0] + small_column[1] + small_column[2] + small_column[3]
    for out, back in spread + slab_copies:
        back.wait_recv()
    for copy in (*slab_own, keep):
        copy.wait()
    for out, back in branch + slab_copies + column + spread + small_copies + small_spread:
        out.wait_send()
    for scatter in (kv_sum, out_sum, query_sum, rest_sum):
        scatter.sent()


def backward_call(
    branch_rows,
    residual_grad,
    small_grad,
    attended,
    query_rows,
    hidden_one,
    tokens,
    kv_all,
    qkv_full,
    out_full,
    small_full,
    cosine,
    sine,
    start,
    slabs,
    *parts,
):
    quarter, width = residual_grad.shape
    rows = quarter * QUARTERS
    block = width // E
    local_width = query_rows.shape[1]
    bf, f32 = jnp.bfloat16, jnp.float32
    sds = jax.ShapeDtypeStruct
    vmem = pl.BlockSpec(memory_space=pltpu.VMEM)
    hbm = pl.BlockSpec(memory_space=pl.ANY)
    outs = [
        (sds((rows, width), bf), hbm),
        (sds((3 * block, local_width), f32), vmem),
        (sds((local_width, block), f32), vmem),
        (sds((SMALL, block), f32), vmem),
        *((sds(part.shape, bf), hbm) for part in parts),
    ]

    def scatter_scratch(count, columns):
        return [
            pltpu.VMEM((E, count, columns), bf),
            pltpu.VMEM((4, count, columns), bf),
            pltpu.VMEM((2, count // 2, columns), bf),
            pltpu.VMEM((2, count, columns), bf),
        ]

    return pl.pallas_call(
        backward_kernel,
        name="attention_backward",
        out_shape=[o[0] for o in outs],
        in_specs=[vmem] + [hbm] * 3 + [vmem] + [hbm] * 5 + [vmem] * 4 + [hbm] * 5,
        out_specs=[o[1] for o in outs],
        input_output_aliases={15 + i: 4 + i for i in range(4)},
        scratch_shapes=[
            pltpu.VMEM((E, rows, 2 * local_width), bf),
            pltpu.VMEM((3, width, local_width), bf),
            pltpu.VMEM((E, local_width, block), bf),
            pltpu.VMEM((rows, width), bf),
            pltpu.VMEM((rows // SEQ_DEV * local_width // HD, SEQ_DEV, E * SEQ_DEV), f32),
            pltpu.VMEM((rows, local_width), bf),
            pltpu.VMEM((3, rows, local_width), bf),
            pltpu.VMEM((rows, 2 * local_width), f32),
            *scatter_scratch(rows, 2 * local_width),
            *scatter_scratch(block, local_width),
            *scatter_scratch(2 * block, local_width),
            *scatter_scratch(local_width, block),
            pltpu.VMEM((rows, width), bf),
            pltpu.VMEM((QUARTERS - 1, quarter, width), bf),
            pltpu.VMEM((quarter, width), bf),
            pltpu.VMEM((E, SMALL, block), f32),
            pltpu.VMEM((E - 1, SMALL, block), f32),
            pltpu.VMEM((QUARTERS, SMALL, block), f32),
            pltpu.VMEM((quarter, width), f32),
            pltpu.VMEM((SMALL, width), f32),
            pltpu.VMEM((rows, local_width), bf),
            pltpu.VMEM((rows, width), bf),
            pltpu.VMEM((quarter, width), bf),
            pltpu.SemaphoreType.DMA((96,)),
            pltpu.SemaphoreType.DMA((96,)),
            pltpu.SemaphoreType.DMA((16,)),
        ],
        compiler_params=pltpu.CompilerParams(
            collective_id=3, has_side_effects=True, vmem_limit_bytes=62 * 2**20
        ),
    )(
        branch_rows,
        residual_grad,
        small_grad,
        attended,
        query_rows,
        hidden_one,
        tokens,
        kv_all,
        qkv_full,
        out_full,
        small_full,
        cosine,
        sine,
        start,
        slabs,
        *parts,
    )


def finish_kernel(
    up_ref,
    down_ref,
    shared_ref,
    grad_ref,
    qkv_ref,
    out_ref,
    output_ref,
    shared_up_ref,
    small_ref,
    up,
    down,
    shared,
    grad,
    qkv,
    out,
    output,
    shared_up,
    gains,
    router,
    gate,
):
    up[...] = up_ref[...].astype(jnp.float32)
    down[...] = down_ref[...].astype(jnp.float32)
    shared[...] = shared_ref[...].astype(jnp.float32)
    grad[...] = grad_ref[...].astype(jnp.float32)
    qkv[...] = qkv_ref[...]
    out[...] = out_ref[...]
    output[...] = output_ref[...]
    for k in range(2):
        shared_up[:, k, :] = shared_up_ref[k].astype(jnp.float32).T
    gains[...] = small_ref[0:2, :]
    router[...] = small_ref[2 : 2 + E, :]
    gate[...] = small_ref[2 + E : 3 + E, :]


def finish_call(up, down, shared, grad, qkv, out, output, shared_up, small):
    steps = 2
    f32 = jnp.float32
    sds = jax.ShapeDtypeStruct
    block = small.shape[1]
    arrays = (up, down, shared, grad, qkv, out, output)
    shared_shape = (block, 2, shared_up.shape[1])

    def split(shape):
        part = (shape[0] // steps, *shape[1:])
        return pl.BlockSpec(part, lambda i: (i,) + (0,) * (len(part) - 1))

    def once(shape):
        return pl.BlockSpec(shape, lambda i: (0, 0))

    specs = [split(array.shape) for array in arrays]
    turned = pl.BlockSpec((*shared_up.shape[:2], block // steps), lambda i: (0, 0, i))
    types = (f32, f32, f32, f32, f32, f32, output.dtype)
    return pl.pallas_call(
        finish_kernel,
        name="finish",
        grid=(steps,),
        out_shape=[sds(a.shape, t) for a, t in zip(arrays, types, strict=True)]
        + [sds(shared_shape, f32)]
        + [sds((n, block), f32) for n in (2, E, 1)],
        in_specs=[*specs, turned, once(small.shape)],
        out_specs=[*specs, split(shared_shape), *(once((n, block)) for n in (2, E, 1))],
        compiler_params=pltpu.CompilerParams(vmem_limit_bytes=60 * 2**20),
    )(*arrays, shared_up, small)


def shards_units(
    tokens,
    cotangent,
    qkv_weight,
    out_weight,
    norm_gains,
    router_weight,
    shared_gate,
    expert_gate_up,
    expert_down,
    shared_gate_up,
    shared_down,
    routes,
    doc_start,
):
    tok_rows, width = tokens.shape
    seq_count = tok_rows // SEQ_DEV
    fs_index = lax.axis_index("fs")
    query_pos = fs_index * SEQ_DEV + jnp.arange(SEQ_DEV, dtype=jnp.int32)
    positions = jnp.tile(query_pos, seq_count)
    half_cos, half_sin = rope_tables(positions)
    cosine = jnp.concatenate([half_cos, half_cos], axis=1)
    sine = jnp.concatenate([-half_sin, half_sin], axis=1)
    routed_units = expert_down.shape[1]
    (
        output,
        branch_rows,
        residual_grad,
        small_grad,
        grad_slabs,
        up_part,
        shared_up_part,
        down_part,
        shared_down_part,
        attended,
        query_rows,
        hidden_one,
        _,
        _,
        _,
        kv_all,
        qkv_full,
        out_full,
        small_full,
        _,
    ) = layer_call(
        tokens,
        cotangent,
        qkv_weight,
        out_weight,
        norm_gains,
        router_weight,
        shared_gate.reshape(2, -1),
        jnp.transpose(expert_gate_up, (0, 2, 3, 1)).reshape(E, 2 * routed_units, -1),
        shared_gate_up,
        expert_down,
        shared_down,
        cosine,
        sine,
        doc_start.reshape(seq_count, SEQ_DEV),
        routes.T,
    )
    input_grad, qkv_own, out_own, small_own, up_own, shared_up_own, down_own, shared_down_own = (
        backward_call(
            branch_rows,
            residual_grad,
            small_grad,
            attended,
            query_rows,
            hidden_one,
            tokens,
            kv_all,
            qkv_full,
            out_full,
            small_full,
            cosine,
            sine,
            doc_start.reshape(seq_count, SEQ_DEV),
            grad_slabs,
            up_part,
            shared_up_part,
            down_part,
            shared_down_part,
        )
    )
    (
        up_own,
        down_own,
        shared_down_own,
        input_grad,
        qkv_own,
        out_own,
        output,
        shared_up_own,
        gains,
        router,
        gate,
    ) = finish_call(
        up_own,
        down_own,
        shared_down_own,
        input_grad,
        qkv_own,
        out_own,
        output,
        shared_up_own,
        small_own,
    )
    up_own = up_own.reshape(E, 2, routed_units, -1)
    return (
        output,
        input_grad,
        qkv_own.reshape(qkv_weight.shape),
        out_own,
        gains,
        router,
        gate[0],
        jnp.transpose(up_own, (0, 3, 1, 2)),
        down_own,
        shared_up_own,
        shared_down_own,
    )


def solution(mesh):
    return jax.shard_map(
        shards_units if dict(mesh.shape) == {"fs": E, "tp": QUARTERS} else shards_gathered,
        mesh=mesh,
        in_specs=(
            P("fs", None),
            P("fs", None),
            P(None, "fs", "tp"),
            P("tp", "fs"),
            P(None, "fs"),
            P(None, "fs"),
            P("fs"),
            P(None, "fs", None, "tp"),
            P(None, "tp", "fs"),
            P("fs", None, "tp"),
            P("tp", "fs"),
            P("fs", None),
            P("fs"),
        ),
        out_specs=(
            P("fs", "tp"),
            P("fs", None),
            P(None, "fs", "tp"),
            P("tp", "fs"),
            P(None, "fs"),
            P(None, "fs"),
            P("fs"),
            P(None, "fs", None, "tp"),
            P(None, "tp", "fs"),
            P("fs", None, "tp"),
            P("tp", "fs"),
        ),
        check_vma=False,
    )
```
